32 devices in a mesh: dp: 16 (over z, y, core), tensor: 2 (over x).
Axes of the slice: x: 2, y: 2, z: 4, core: 2. Of those that a mesh axis runs over, the one named last changes fastest.
Arguments:
- tokens: bfloat16 [32768, 1536], P(('dp', 'tensor')), may hold values from -6 to 6
- norm_gains: float32 [1536], replicated, may hold values from 0.5 to 1.5
- w_query: bfloat16 [1536, 1536], P(None, 'tensor'), may hold values from -0.15625 to 0.15625
- w_key: bfloat16 [1536, 512], P(None, 'tensor'), may hold values from -0.15625 to 0.15625
- w_value: bfloat16 [1536, 512], P(None, 'tensor'), may hold values from -0.15625 to 0.15625
- w_out: bfloat16 [1536, 1536], P('tensor'), may hold values from -2.5 to 2.5
- mix_gains: float32 [1536], replicated, may hold values from 0.5 to 1.5
- w_router: bfloat16 [1536, 40], replicated, may hold values from -0.078125 to 0.078125
- w_gate: bfloat16 [40, 1536, 512], P('tensor'), may hold values from -0.15625 to 0.15625
- w_up: bfloat16 [40, 1536, 512], P('tensor'), may hold values from -0.15625 to 0.15625
- w_down: bfloat16 [40, 512, 1536], P('tensor'), may hold values from -1 to 1
- routes: int32 [32768, 8], P('dp'), may hold values from 0 to 39, all different within a row; in each aligned block of 2048 rows (0 to 2047, 2048 to 4095, ...) at most 614 rows name the same one
- starts: int32 [32, 2], P('dp'), may hold values from 0 to 768, as said below
- cotangent: bfloat16 [32768, 1536], P(('dp', 'tensor')), may hold values from -6 to 6
Outputs:
- output: bfloat16 [32768, 1536], P(('dp', 'tensor'))
- balance: float32 [40], replicated
- input_grad: float32 [32768, 1536], P(('dp', 'tensor'))
- norm_gain_grad: float32 [1536], replicated
- query_weight_grad: float32 [1536, 1536], P('dp', 'tensor')
- key_weight_grad: float32 [1536, 512], P('dp', 'tensor')
- value_weight_grad: float32 [1536, 512], P('dp', 'tensor')
- out_weight_grad: float32 [1536, 1536], P('tensor', 'dp')
- mix_gain_grad: float32 [1536], replicated
- router_grad: float32 [1536, 40], replicated
- gate_weight_grad: float32 [40, 1536, 512], P('tensor', 'dp')
- up_weight_grad: float32 [40, 1536, 512], P('tensor', 'dp')
- down_weight_grad: float32 [40, 512, 1536], P('tensor', None, 'dp')
The draws below stay inside these ranges and needn't reach their ends.
Inputs may be any that keep to these rules, and one draw needn't show every extreme that they name: `routes`: each row names 8 different experts. In each aligned block of 2048 rows (the tokens of one index of dp) no expert is named by more than 614 rows, a bound that some block reaches. Row s holds the first positions of the 2 picture pieces of sequence s, each 256 tokens long; piece k starts between k * 512 and (k + 1) * 512 - 256.
All inputs are finite; a program needn't handle non-finite values.
Results may differ from the reference program's by a relative error of at most 0.02.
Values may be sent and summed in bfloat16 or wider, within the bound.
No kernel may reach another device: no remote copies, remote signals or barrier semaphores. Data moves between devices by JAX's collectives and lax.ppermute only.
A program may use at most 896 MiB of HBM per device.

```python
import math
import jax
import jax.numpy as jnp
import numpy as np
from jax import lax

D = 1536
HEADS = 24
KV = 8
HD = 64
EXPERTS = 40
EF = 512
TOPK = 8
LEN = 1024
PIECE = 256
PIECES = 2
SEQS = 2
TOK_DEV = 2048
SEQUENCES = 32
TOKENS = 32768
CAP = 614
N_DP = 16


def draw_starts(key, part):
    span_width = LEN // PIECES
    offsets = jax.random.randint(jax.random.fold_in(key, 1), (SEQUENCES, PIECES), 0, span_width - PIECE + 1, dtype=jnp.int32)
    chosen_row = jax.random.randint(jax.random.fold_in(key, 2), (), 0, SEQUENCES, dtype=jnp.int32)
    row_index = jnp.arange(SEQUENCES, dtype=jnp.int32)[:, None]
    piece_index = jnp.arange(PIECES, dtype=jnp.int32)[None, :]
    extremes = jnp.where(piece_index == PIECES - 1, span_width - PIECE, 0).astype(jnp.int32)
    offsets = jnp.where(row_index == chosen_row, extremes, offsets)
    return offsets + piece_index * span_width


def with_spikes(values, own_key, source, target, shards_of, factor):
    owner, partner = [(jnp.arange(values.shape[dim]) // (values.shape[dim] // shards_of)).reshape([-1 if axis == dim else 1 for axis in range(values.ndim)]) for dim in (source, target)]
    chosen = jax.random.permutation(own_key, shards_of)[partner]
    strong = (owner == chosen) | (owner == (partner + shards_of // 2) % shards_of)
    return jnp.where(strong, factor * values, values)


def shard_levels(own_key, shape, pieces, least, top_value):
    def one(dim, blocks):
        draws = jax.random.uniform(jax.random.fold_in(jax.random.fold_in(own_key, 6), dim), (blocks,), jnp.float32, least / len(pieces), top_value / len(pieces))
        return jnp.repeat(jnp.exp(draws), shape[dim] // blocks).reshape((-1,) + (1,) * (len(shape) - dim - 1))

    loudness = one(*pieces[0])
    for cut in pieces[1:]:
        loudness = loudness * one(*cut)
    return loudness


def assign_block(own_key, own, number, rows, count, top, limit, lean):
    order = jax.random.permutation(own_key, count)
    packed, common = shares(count, rows * top, limit, lean, True), shares(count, rows * top, limit, lean, False)
    places = jnp.arange(count)

    def named(lengths, turn):
        used = int((lengths > 0).sum())
        fixed = max(1, used // 4)
        moved = fixed + (places - fixed + turn * (used - fixed)) % max(1, count - fixed)
        return jnp.zeros((count,), jnp.int32).at[order[jnp.where(places < fixed, places, moved)]].set(jnp.asarray(lengths, jnp.int32))

    lengths = jnp.where(number % 4 == 0, named(packed, number // 4), named(common, number - number // 4 - 1))
    mixed = jax.random.permutation(jax.random.fold_in(own, 3), count)
    giver, sink = mixed[0:count // 2 * 2:2], mixed[1:count // 2 * 2:2]
    slack = jnp.minimum(lengths[giver] - 1, limit - lengths[sink]) // 2
    slack = jnp.where((giver == order[0]) | (sink == order[0]) | (lengths[sink] == 0), 0, jnp.maximum(slack, 0))
    moved = jax.random.randint(jax.random.fold_in(own, 4), (count // 2,), 0, 1 << 20) % (slack + 1)
    lengths = lengths.at[giver].add(-moved).at[sink].add(moved)
    members = jnp.searchsorted(jnp.cumsum(lengths), jnp.arange(rows * top), side="right").astype(jnp.int32)
    grid = members.reshape(top, rows).T
    grid = grid[jax.random.permutation(jax.random.fold_in(own, 1), rows)]
    turn = jax.random.randint(jax.random.fold_in(own, 2), (rows, 1), 0, top)
    return jnp.take_along_axis(grid, (jnp.arange(top)[None, :] + turn) % top, axis=1)


def shares(amount, total, most, slope, full):
    portions = [(1 << 20) // math.isqrt(standing ** slope) + 1 for standing in range(1, amount + 1)]
    largest = most if full else min(most, max(-(-total // amount), total * portions[0] // sum(portions)))
    least = 1 if total - largest >= amount - 1 else 0
    given, rest = [largest] + [least] * (amount - 1), total - largest - least * (amount - 1)
    while rest > 0:
        free = [i for i in range(1, amount) if given[i] < largest] or [i for i in range(1, amount) if given[i] < most]
        pool, left = sum([portions[i] for i in free]), rest
        for i in free:
            more = min(most - given[i], max(1, left * portions[i] // pool), rest)
            given[i] = given[i] + more
            rest = rest - more
    return np.array(given)


def normal_values(key, dims, deviation, reach, pieces=(), kind=jnp.bfloat16):
    values = jax.random.normal(key, dims, jnp.float32) * deviation
    if len(pieces) > 0:
        values = shard_levels(key, dims, pieces, -0.22, 0.18) * values
    return jnp.clip(values, min=-reach, max=reach).astype(kind)


def bell_draw_with(key, extent, scale, most, shards, heavy, kind=jnp.bfloat16):
    values = scale * jax.random.normal(key, extent, jnp.float32)
    if shards:
        values = values * shard_levels(key, extent, shards, -0.22, 0.18)
    return jnp.clip(with_spikes(values, jax.random.fold_in(key, 3), *heavy), -most, most).astype(kind)


def setup_inputs(seed: int = 0) -> dict:
    key_list = jax.random.split(jax.random.key(seed), 15)
    tokens = bell_draw_with(key_list[0], (TOKENS, D), 1.0, 6.0, ((0, 32),), (0, 1, 32, 2.75))
    norm_gains = jnp.clip(1.0 + 0.1 * jax.random.normal(key_list[1], (D,), jnp.float32), 0.5, 1.5)
    w_query = normal_values(key_list[2], (D, HEADS * HD), D ** -0.5, 0.15625, ((1, 2),))
    w_key = normal_values(key_list[3], (D, KV * HD), D ** -0.5, 0.15625, ((1, 2),))
    w_value = normal_values(key_list[4], (D, KV * HD), D ** -0.5, 0.15625, ((1, 2),))
    w_out = normal_values(key_list[5], (HEADS * HD, D), (HEADS * HD * 4 // LEN) ** -0.5, 2.5, ((0, 2),))
    mix_gains = jnp.clip(1.0 + 0.1 * jax.random.normal(key_list[6], (D,), jnp.float32), 0.5, 1.5)
    w_router = normal_values(key_list[7], (D, EXPERTS), (4 * D) ** -0.5, 0.078125)
    w_gate = normal_values(key_list[8], (EXPERTS, D, EF), D ** -0.5, 0.15625, ((0, 2),))
    w_up = normal_values(key_list[9], (EXPERTS, D, EF), D ** -0.5, 0.15625, ((0, 2),))
    w_down = normal_values(key_list[10], (EXPERTS, EF, D), (EF // 16) ** -0.5, 1.0, ((0, 2),))
    routes_keys = jax.random.split(jax.random.fold_in(key_list[11], 1), TOKENS // TOK_DEV)
    routes_turns = jax.random.permutation(jax.random.fold_in(key_list[11], 3), TOKENS // TOK_DEV)
    routes = jax.vmap(lambda own, number: assign_block(jax.random.fold_in(key_list[11], 2), own, number, TOK_DEV, EXPERTS, TOPK, CAP, 1))(routes_keys, routes_turns).reshape((TOKENS, TOPK))
    starts = draw_starts(jax.random.fold_in(key_list[14], 71), 0)
    cotangent = bell_draw_with(key_list[13], (TOKENS, D), 1.0, 6.0, ((0, 32),), (0, 1, 32, 2.75))
    return dict(tokens=tokens, norm_gains=norm_gains, w_query=w_query, w_key=w_key, w_value=w_value, w_out=w_out, mix_gains=mix_gains, w_router=w_router, w_gate=w_gate, w_up=w_up, w_down=w_down, routes=routes, starts=starts, cotangent=cotangent)


@jax.custom_vjp
def low(v):
    return lax.optimization_barrier(v.astype(jnp.bfloat16)).astype(jnp.float32)

@jax.custom_vjp
def low_back(v):
    return v

def low_keep(v):
    return (low(v), None)

def low_pass(kept, grad):
    return (grad,)

def back_keep(v):
    return (v, None)

def back_low(kept, grad):
    return (low(grad),)
low.defvjp(low_keep, low_pass)
low_back.defvjp(back_keep, back_low)
EPSILON = 1e-06
ALPHA = 0.01
HIGHEST = lax.Precision.HIGHEST

def matmul(left, right):
    return jnp.dot(left, right, precision=HIGHEST, preferred_element_type=jnp.float32)

def normalize(values, gains):
    return values * lax.rsqrt(lax.optimization_barrier(jnp.mean(values * values, axis=-1, keepdims=True)) + EPSILON) * gains

def softmax_rows(values):
    shifted = jnp.exp(values - lax.optimization_barrier(jnp.max(values, axis=-1, keepdims=True)))
    return shifted / lax.optimization_barrier(jnp.sum(shifted, axis=-1, keepdims=True))

def rope_tables():
    half_width = HD // 2
    frequency = 10000.0 ** (-(jnp.arange(half_width, dtype=jnp.float32) * 2.0 / HD))
    angles = jnp.arange(LEN, dtype=jnp.float32)[:, None] * frequency[None, :]
    return (jnp.cos(angles), jnp.sin(angles))

def rotate(values, cosine, sine_table):
    half_width = values.shape[-1] // 2
    first_half = values[..., :half_width]
    second_half = values[..., half_width:]
    cosine_rows = cosine[:, None, :]
    sine_rows = sine_table[:, None, :]
    return jnp.concatenate([first_half * cosine_rows - second_half * sine_rows, second_half * cosine_rows + first_half * sine_rows], axis=-1)

def allowed_pairs(starts_row):
    position = jnp.arange(LEN, dtype=jnp.int32)
    labels = jnp.full((LEN,), -1, jnp.int32)
    for piece_index in range(PIECES):
        inside = (position >= starts_row[piece_index]) & (position < starts_row[piece_index] + PIECE)
        labels = jnp.where(inside, piece_index, labels)
    causal = position[None, :] <= position[:, None]
    shared = (labels[:, None] == labels[None, :]) & (labels[:, None] >= 0)
    return causal | shared

def attend(hidden, starts_row, w_query, w_key, w_value):
    cosine, sine_table = rope_tables()
    query_rows = low_back(matmul(hidden, w_query)).reshape(LEN, HEADS, HD)
    key_rows = low_back(matmul(hidden, w_key)).reshape(LEN, KV, HD)
    value_rows = low(low_back(matmul(hidden, w_value))).reshape(LEN, KV, HD)
    query_rows = low(rotate(query_rows, cosine, sine_table)).reshape(LEN, KV, HEADS // KV, HD)
    key_rows = low(rotate(key_rows, cosine, sine_table))
    scores = low_back(jnp.einsum('qkgd,skd->kgqs', query_rows, key_rows, precision=HIGHEST) * HD ** (-0.5))
    scores = jnp.where(allowed_pairs(starts_row), scores, -1e+30)
    weights = low(softmax_rows(scores))
    mixed_values = jnp.einsum('kgqs,skd->qkgd', weights, value_rows, precision=HIGHEST)
    return low(low_back(mixed_values.reshape(LEN, HEADS * HD)))

def slot_table(routes_group):
    flattened = routes_group.reshape(-1)
    onehot = (flattened[:, None] == jnp.arange(EXPERTS, dtype=jnp.int32)[None, :]).astype(jnp.int32)
    placed = lax.optimization_barrier(jnp.sum((jnp.cumsum(onehot, axis=0) - 1) * onehot, axis=1))
    entries = jnp.arange(TOK_DEV * TOPK, dtype=jnp.int32)
    return jnp.full((EXPERTS * CAP,), TOK_DEV * TOPK, jnp.int32).at[flattened * CAP + placed].set(entries)

def expert_mix(hidden, gate_values, routes_group, w_gate, w_up, w_down):
    slots = slot_table(routes_group)
    owners = slots // TOPK
    padded_rows = jnp.concatenate([hidden, jnp.zeros((1, D), hidden.dtype)], axis=0)
    padded_gates = jnp.concatenate([gate_values.reshape(-1), jnp.zeros((1,), gate_values.dtype)], axis=0)
    expert_inputs = padded_rows[owners].reshape(EXPERTS, CAP, D)
    gate_proj = low_back(jnp.einsum('ecd,edf->ecf', expert_inputs, w_gate, precision=HIGHEST))
    up_proj = low_back(jnp.einsum('ecd,edf->ecf', expert_inputs, w_up, precision=HIGHEST))
    activated = low(gate_proj * jax.nn.sigmoid(gate_proj) * up_proj)
    returned = low_back(jnp.einsum('ecf,efd->ecd', activated, w_down, precision=HIGHEST)).reshape(EXPERTS * CAP, D)
    weighted = padded_gates[slots][:, None] * returned
    return jax.ops.segment_sum(weighted, owners, num_segments=TOK_DEV + 1)[:TOK_DEV]

def block_forward(tokens, norm_gains, w_query, w_key, w_value, w_out, mix_gains, w_router, w_gate, w_up, w_down, routes, starts):

    def one_group(group_args):
        group_tokens, group_routes, group_starts = group_args
        normed = low(normalize(group_tokens, norm_gains))

        def one_sequence(sequence_args):
            return attend(sequence_args[0], sequence_args[1], w_query, w_key, w_value)
        attended = lax.map(jax.checkpoint(one_sequence), (normed.reshape(SEQS, LEN, D), group_starts))
        middle = group_tokens + low_back(matmul(attended.reshape(TOK_DEV, HEADS * HD), w_out))
        mixed = low(normalize(middle, mix_gains))
        logits = matmul(mixed, w_router)
        chosen = jnp.take_along_axis(logits, group_routes, axis=1)
        gate_values = low(softmax_rows(chosen))
        result = middle + expert_mix(mixed, gate_values, group_routes, w_gate, w_up, w_down)
        return (result, lax.optimization_barrier(jnp.sum(softmax_rows(logits), axis=0)))
    results, prob_sums = lax.map(jax.checkpoint(one_group), (tokens.reshape(N_DP, TOK_DEV, D), routes.reshape(N_DP, TOK_DEV, TOPK), starts.reshape(N_DP, SEQS, PIECES)))
    counts = lax.optimization_barrier(jnp.sum((routes.reshape(-1)[:, None] == jnp.arange(EXPERTS, dtype=jnp.int32)[None, :]).astype(jnp.float32), axis=0))
    fractions = counts / (TOKENS * TOPK)
    balance = EXPERTS * EXPERTS * fractions * lax.optimization_barrier(jnp.sum(prob_sums, axis=0)) / TOKENS
    return (results.reshape(TOKENS, D), balance)

def reference(tokens, norm_gains, w_query, w_key, w_value, w_out, mix_gains, w_router, w_gate, w_up, w_down, routes, starts, cotangent):
    floats = tuple((array.astype(jnp.float32) for array in (tokens, norm_gains, w_query, w_key, w_value, w_out, mix_gains, w_router, w_gate, w_up, w_down)))

    def objective(*weights):
        return block_forward(*weights, routes, starts)
    (result, balance), pullback = jax.vjp(objective, *floats)
    gradients = pullback((cotangent.astype(jnp.float32), jnp.full_like(balance, ALPHA / EXPERTS)))
    return (result.astype(jnp.bfloat16), balance, gradients[0], gradients[1], gradients[2], gradients[3], gradients[4], gradients[5], gradients[6], gradients[7], gradients[8], gradients[9], gradients[10])
```

```python
import functools

import jax
import jax.numpy as jnp
from jax import lax
from jax.experimental import pallas as pl
from jax.experimental.pallas import tpu as pltpu
from jax.sharding import PartitionSpec as P

HD = 64
PIECE = 256
CAP = 614


EPSILON = 1e-06
ALPHA = 0.01
HIGHEST = lax.Precision.HIGHEST


def normalize(values, gains):
    return values * lax.rsqrt(jnp.mean(values * values, axis=-1, keepdims=True) + EPSILON) * gains


def softmax_rows(values):
    shifted = jnp.exp(values - jnp.max(values, axis=-1, keepdims=True))
    return shifted / jnp.sum(shifted, axis=-1, keepdims=True)


def contract_rows(left, right):
    return lax.dot_general(
        left, right, (((0,), (0,)), ((), ())), preferred_element_type=jnp.float32
    )


def contract_cols(left, right):
    return lax.dot_general(
        left, right, (((1,), (1,)), ((), ())), preferred_element_type=jnp.float32
    )


def rope_tables(sequence_length, head_width):
    half_width = head_width // 2
    frequency = 10000.0 ** (-(jnp.arange(half_width, dtype=jnp.float32) * 2.0 / head_width))
    angles = jnp.arange(sequence_length, dtype=jnp.float32)[:, None] * frequency[None, :]
    return (jnp.cos(angles), jnp.sin(angles))


def rotate(values, cosine, sine_table):
    half_width = values.shape[-1] // 2
    first_half = values[..., :half_width]
    second_half = values[..., half_width:]
    cosine_rows = cosine[:, None, :]
    sine_rows = sine_table[:, None, :]
    return jnp.concatenate(
        [
            first_half * cosine_rows - second_half * sine_rows,
            second_half * cosine_rows + first_half * sine_rows,
        ],
        axis=-1,
    )


def allowed_pairs(starts_row, sequence_length, piece_length):
    position = jnp.arange(sequence_length, dtype=jnp.int32)
    labels = jnp.full((sequence_length,), -1, jnp.int32)
    for piece_index in range(starts_row.shape[0]):
        inside = (position >= starts_row[piece_index]) & (
            position < starts_row[piece_index] + piece_length
        )
        labels = jnp.where(inside, piece_index, labels)
    causal = position[None, :] <= position[:, None]
    shared = (labels[:, None] == labels[None, :]) & (labels[:, None] >= 0)
    return causal | shared


def scores_of(query_block, key_block, allowed, score_scale):
    raw_scores = (
        jnp.einsum("qkgd,skd->kgqs", query_block, key_block, preferred_element_type=jnp.float32)
        * score_scale
    )
    return jnp.where(allowed, raw_scores, -1e30)


BLOCK = 256
PART = 128
PIECE_ROWS = 64
GROUP = BLOCK // PIECE_ROWS
VMEM_LIMIT = 60 * 1024 * 1024


def dot_nt(left, right):
    return lax.dot_general(
        left, right, (((1,), (1,)), ((), ())), preferred_element_type=jnp.float32
    )


def dot_tn(left, right):
    return lax.dot_general(
        left, right, (((0,), (0,)), ((), ())), preferred_element_type=jnp.float32
    )


def round_up(value, multiple):
    return -(-value // multiple) * multiple


def placement(routes_rows, gates_rows, first_expert, experts):
    rows = routes_rows.shape[0]
    tiles = rows // BLOCK
    turned = routes_rows.T
    names = first_expert + jnp.arange(experts, dtype=jnp.int32)
    hit = turned[None, :, :] == names[:, None, None]
    member = jnp.any(hit, axis=1)
    upper = jnp.triu(jnp.ones((BLOCK, BLOCK), jnp.bfloat16))
    inside = jnp.dot(
        member.astype(jnp.bfloat16).reshape(experts * tiles, BLOCK),
        upper,
        preferred_element_type=jnp.float32,
    ).astype(jnp.int32).reshape(experts, tiles, BLOCK)
    sums = inside[:, :, -1]
    ends = jnp.cumsum(sums, axis=1)
    begins = ends - sums
    place = jnp.where(
        member.reshape(experts, tiles, BLOCK), begins[:, :, None] + inside - 1, -1
    )
    place = jnp.concatenate(
        [place, jnp.full((1, tiles, BLOCK), -1, jnp.int32)], axis=0
    ).reshape(experts + 1, tiles, 1, BLOCK)
    gates = None
    if gates_rows is not None:
        gates = jnp.sum(
            jnp.where(hit, gates_rows.astype(jnp.float32).T[None, :, :], 0.0), axis=1
        ).reshape(experts, tiles, 1, BLOCK)
    return place, begins, ends, gates


def gather_tables(begins, ends, slots):
    counts = ends[:, -1]
    parts = jnp.arange(slots // PART, dtype=jnp.int32) * PART
    low = jnp.sum((ends[:, None, :] <= parts[None, :, None]).astype(jnp.int32), axis=2)
    high = jnp.sum((begins[:, None, :] < parts[None, :, None] + PART).astype(jnp.int32), axis=2)
    high = jnp.where(parts[None, :] < counts[:, None], high, low)
    blocks = jnp.maximum(-(-counts // BLOCK), 1)
    return low, high, blocks


def combine_tables(begins, ends, slots):
    experts, tiles = begins.shape
    width = round_up(experts * (BLOCK // PIECE_ROWS + 1), GROUP)
    first = begins // PIECE_ROWS
    amount = jnp.where(ends > begins, (ends - 1) // PIECE_ROWS - first + 1, 0)
    stop = jnp.cumsum(amount, axis=0)
    place = jnp.arange(width, dtype=jnp.int32)
    owner = jnp.sum(
        (stop.T[:, None, :] <= place[None, :, None]).astype(jnp.int32), axis=2
    )
    chosen = owner[:, :, None] == jnp.arange(experts, dtype=jnp.int32)[None, None, :]
    offset = jnp.sum(
        jnp.where(chosen, (first - (stop - amount)).T[:, None, :], 0), axis=2
    )
    valid = owner < experts
    piece = jnp.where(valid, offset + place[None, :], 0)
    source = jnp.where(valid, owner, 0) * (slots // PIECE_ROWS) + piece
    groups = jnp.maximum(-(-stop[-1] // GROUP), 1)
    return owner, piece, source, groups, width


def gather_kernel(
    experts, slots, sources, with_gates, low_ref, high_ref, blocks_ref, place_ref, *rest
):
    if with_gates:
        gates_ref, rest = rest[0], rest[1:]
    inputs, rest = rest[:sources], rest[sources:]
    if with_gates:
        out_ref, gate_out_ref, rest = rest[0], rest[1], rest[2:]
    else:
        out_ref, rest = rest[0], rest[1:]
    held, total, gate_total, sems = rest
    expert = pl.program_id(0)
    part = pl.program_id(1)
    share = inputs[0].shape[0]

    @pl.when((expert == 0) & (part == 0))
    def _():
        copies = [
            pltpu.make_async_copy(ref, held.at[pl.ds(i * share, share)], sems.at[i])
            for i, ref in enumerate(inputs)
        ]
        for copy in copies:
            copy.start()
        for copy in copies:
            copy.wait()

    @pl.when(part * PART < blocks_ref[expert] * BLOCK)
    def _():
        total[...] = jnp.zeros_like(total)
        if with_gates:
            gate_total[...] = jnp.zeros_like(gate_total)
        rows = lax.broadcasted_iota(jnp.int32, (PART, BLOCK), 0) + part * PART

        def step(tile, carry):
            match = rows == place_ref[expert, tile]
            pick = jnp.where(match, 1.0, 0.0)
            start = pl.multiple_of(tile * BLOCK, BLOCK)
            total[...] += jnp.dot(
                pick.astype(jnp.bfloat16),
                held[pl.ds(start, BLOCK), :],
                preferred_element_type=jnp.float32,
            )
            if with_gates:
                weighted = pick * gates_ref[expert, tile]
                gate_total[...] += jnp.broadcast_to(
                    jnp.sum(weighted, axis=1, keepdims=True), gate_total.shape
                )
            return carry

        lax.fori_loop(low_ref[expert, part], high_ref[expert, part], step, 0)
        out_ref[...] = total[...].astype(out_ref.dtype)
        if with_gates:
            gate_out_ref[...] = gate_total[...]


def gather_rows(tables, place, gates, sources, slots, first, count):
    low, high, blocks = tables
    low, high, blocks = (t[first : first + count] for t in (low, high, blocks))
    place = place[first : first + count]
    tiles = place.shape[1]
    rows = tiles * BLOCK
    width = sources[0].shape[1]
    with_gates = gates is not None
    if with_gates:
        gates = gates[first : first + count]
    parts = slots // PART

    def out_index(expert, part, low, high, blocks):
        return (expert * parts + jnp.minimum(part, blocks[expert] * (BLOCK // PART) - 1), 0)

    def whole(array):
        zeros = (0,) * array.ndim
        return pl.BlockSpec(array.shape, lambda *_: zeros)

    operands = [place] + ([gates] if with_gates else [])
    in_specs = [whole(a) for a in operands] + [pl.BlockSpec(memory_space=pl.ANY)] * len(sources)
    out_shape = [jax.ShapeDtypeStruct((count * slots, width), jnp.bfloat16)]
    out_specs = [pl.BlockSpec((PART, width), out_index)]
    if with_gates:
        out_shape.append(jax.ShapeDtypeStruct((count * slots, 128), jnp.float32))
        out_specs.append(pl.BlockSpec((PART, 128), out_index))
    return pl.pallas_call(
        functools.partial(gather_kernel, count, slots, len(sources), with_gates),
        grid_spec=pltpu.PrefetchScalarGridSpec(
            num_scalar_prefetch=3,
            grid=(count, parts),
            in_specs=in_specs,
            out_specs=out_specs,
            scratch_shapes=[
                pltpu.VMEM((rows, width), jnp.bfloat16),
                pltpu.VMEM((PART, width), jnp.float32),
                pltpu.VMEM((PART, 128), jnp.float32),
                pltpu.SemaphoreType.DMA((len(sources),)),
            ],
        ),
        out_shape=out_shape,
        compiler_params=pltpu.CompilerParams(vmem_limit_bytes=VMEM_LIMIT),
        cost_estimate=pl.CostEstimate(
            flops=count * rows * 6 * PART * width, bytes_accessed=rows * width * 6, transcendentals=0
        ),
    )(low, high, blocks, *operands, *sources)


def expert_kernel(
    first, split, depth, blocks_ref, misc_ref, x_ref, c_ref, sg_ref, wg_ref, wu_ref, wd_ref, *rest
):
    if len(rest) == 3 + (2 if split else 1) + 2 + 3:
        rest = rest[3:]
    y_ref, dx_ref, gg_ref = rest[:3]
    rest = rest[3:]
    if split:
        send_ref, keep_ref = rest[:2]
        rest = rest[2:]
    else:
        grads_ref = rest[0]
        rest = rest[1:]
    total_gu, total_d = rest
    block = pl.program_id(1)
    hidden = wg_ref.shape[2]

    @pl.when(block == 0)
    def _():
        total_gu[...] = jnp.zeros_like(total_gu)
        total_d[...] = jnp.zeros_like(total_d)

    @pl.when(block < blocks_ref[first + pl.program_id(0)])
    def _():
        x = x_ref[...]
        c = c_ref[...]
        gate = jnp.concatenate([sg_ref[...]] * (hidden // 128), axis=1)
        gate_proj = jnp.dot(x, wg_ref[0], preferred_element_type=jnp.float32)
        up_proj = jnp.dot(x, wu_ref[0], preferred_element_type=jnp.float32)
        sigmoid = 1.0 / (1.0 + jnp.exp(-gate_proj))
        silu = gate_proj * sigmoid
        activated = (silu * up_proj).astype(jnp.bfloat16).astype(jnp.float32)
        pulled = dot_nt(c, wd_ref[0])
        gate_grad = jnp.sum(activated * pulled, axis=1, keepdims=True)
        gg_ref[...] = jnp.broadcast_to(gate_grad, gg_ref.shape)
        gated = (gate * activated).astype(jnp.bfloat16)
        y_ref[...] = jnp.dot(gated, wd_ref[0], preferred_element_type=jnp.float32).astype(
            y_ref.dtype
        )
        activated_grad = gate * pulled
        gate_low = (
            activated_grad * up_proj * sigmoid * (1.0 + gate_proj * (1.0 - sigmoid))
        ).astype(jnp.bfloat16)
        up_low = (activated_grad * silu).astype(jnp.bfloat16)
        dx_ref[...] = (dot_nt(gate_low, wg_ref[0]) + dot_nt(up_low, wu_ref[0])).astype(
            dx_ref.dtype
        )
        total_gu[...] += dot_tn(x, jnp.concatenate([gate_low, up_low], axis=1))
        total_d[...] += dot_tn(c, gated)

    @pl.when(block == pl.num_programs(1) - 1)
    def _():
        parts = (
            (total_gu, 0),
            (total_gu, hidden),
            (total_d, 0),
        )
        for which, (ref, column) in enumerate(parts):
            if split:
                side = misc_ref[1]
                for index in range(keep_ref.shape[2]):
                    for out, chosen in ((keep_ref, side), (send_ref, 1 - side)):
                        start = pl.multiple_of((2 * index + chosen) * depth, 64)
                        out[0, which, index] = ref[
                            pl.ds(start, depth), pl.ds(column, hidden)
                        ].astype(out.dtype)
            else:
                grads_ref[0, which] = ref[:, pl.ds(column, hidden)].astype(grads_ref.dtype)


def expert_call(blocks, misc, x, c, sg, weights, carried, slots, first, count, x_first, c_first, depth):
    w_gate, w_up, w_down = weights
    experts = blocks.shape[0]
    width = x.shape[1]
    hidden = w_gate.shape[2]
    most = slots // BLOCK
    split = depth is not None

    def rows_index(base):
        def index(expert, block, blocks, misc):
            limit = blocks[first + expert] - 1
            return ((first - base + expert) * most + jnp.minimum(block, limit), 0)

        return index

    def weight_index(expert, block, blocks, misc):
        return (misc[0] + first + expert, 0, 0)

    def grads_index(expert, block, blocks, misc):
        return (expert, 0, 0, 0, 0)

    out_shape = [
        jax.ShapeDtypeStruct((experts * slots, width), jnp.bfloat16),
        jax.ShapeDtypeStruct((experts * slots, width), jnp.bfloat16),
        jax.ShapeDtypeStruct((experts * slots, 128), jnp.float32),
    ]
    out_specs = [
        pl.BlockSpec((BLOCK, width), rows_index(0)),
        pl.BlockSpec((BLOCK, width), rows_index(0)),
        pl.BlockSpec((BLOCK, 128), rows_index(0)),
    ]
    if split:
        cuts = width // depth // 2
        out_shape += [jax.ShapeDtypeStruct((count, 3, cuts, depth, hidden), jnp.bfloat16)] * 2
        out_specs += [pl.BlockSpec((1, 3, cuts, depth, hidden), grads_index)] * 2
    else:
        out_shape += [jax.ShapeDtypeStruct((count, 3, width, hidden), jnp.bfloat16)]
        out_specs += [pl.BlockSpec((1, 3, width, hidden), lambda e, b, *_: (e, 0, 0, 0))]
    operands = [x, c, sg, w_gate, w_up, w_down]
    in_specs = [
        pl.BlockSpec((BLOCK, width), rows_index(x_first)),
        pl.BlockSpec((BLOCK, width), rows_index(c_first)),
        pl.BlockSpec((BLOCK, 128), rows_index(x_first)),
        pl.BlockSpec((1, width, hidden), weight_index),
        pl.BlockSpec((1, width, hidden), weight_index),
        pl.BlockSpec((1, hidden, width), weight_index),
    ]
    aliases = {}
    if carried is not None:
        operands += list(carried)
        in_specs += [pl.BlockSpec(memory_space=pl.ANY)] * 3
        aliases = {8: 0, 9: 1, 10: 2}
    rows = count * 820
    return pl.pallas_call(
        functools.partial(expert_kernel, first, split, depth),
        grid_spec=pltpu.PrefetchScalarGridSpec(
            num_scalar_prefetch=2,
            grid=(count, most),
            in_specs=in_specs,
            out_specs=out_specs,
            scratch_shapes=[
                pltpu.VMEM((width, 2 * hidden), jnp.float32),
                pltpu.VMEM((width, hidden), jnp.float32),
            ],
        ),
        out_shape=out_shape,
        input_output_aliases=aliases,
        compiler_params=pltpu.CompilerParams(vmem_limit_bytes=VMEM_LIMIT),
        cost_estimate=pl.CostEstimate(
            flops=18 * rows * width * hidden,
            bytes_accessed=8 * rows * width + 12 * count * width * hidden,
            transcendentals=rows * hidden,
        ),
    )(blocks, misc, *operands)


def combine_kernel(
    first, width, owner_ref, piece_ref, source_ref, groups_ref, begin_ref, place_ref, y_ref, dx_ref,
    gg_ref, y_out, dx_out, gate_out, y_buf, dx_buf, gg_buf, y_total, dx_total, sems,
):
    step = pl.program_id(0)
    tile = first + step

    def copies(which_tile, group, slot):
        made = []
        for i in range(GROUP):
            source = pl.multiple_of(
                source_ref[which_tile, group * GROUP + i] * PIECE_ROWS, PIECE_ROWS
            )
            for kind, (ref, buf) in enumerate(((y_ref, y_buf), (dx_ref, dx_buf), (gg_ref, gg_buf))):
                made.append(
                    pltpu.make_async_copy(
                        ref.at[pl.ds(source, PIECE_ROWS)],
                        buf.at[slot, pl.ds(i * PIECE_ROWS, PIECE_ROWS)],
                        sems.at[slot, kind, i],
                    )
                )
        return made

    @pl.when(step == 0)
    def _():
        for copy in copies(tile, 0, begin_ref[tile] % 2):
            copy.start()

    y_total[...] = jnp.zeros_like(y_total)
    dx_total[...] = jnp.zeros_like(dx_total)
    gate_out[...] = jnp.zeros_like(gate_out)

    def one(group, carry):
        slot = (begin_ref[tile] + group) % 2
        last = group + 1 == groups_ref[tile]
        next_tile = jnp.where(last, tile + 1, tile)
        next_group = jnp.where(last, 0, group + 1)

        @pl.when(jnp.logical_not(last & (step == pl.num_programs(0) - 1)))
        def _():
            for copy in copies(next_tile, next_group, 1 - slot):
                copy.start()

        for copy in copies(tile, group, slot):
            copy.wait()
        picks = []
        for i in range(GROUP):
            entry = group * GROUP + i
            expert = owner_ref[tile, entry]
            rows = (
                lax.broadcasted_iota(jnp.int32, (PIECE_ROWS, BLOCK), 0)
                + piece_ref[tile, entry] * PIECE_ROWS
            )
            pick = jnp.where(rows == place_ref[expert, step], 1.0, 0.0)
            picks.append(pick.astype(jnp.bfloat16))
            grads = gg_buf[slot, pl.ds(i * PIECE_ROWS, PIECE_ROWS), :]
            grads = jnp.concatenate([grads] * (BLOCK // 128), axis=1)
            gate_out[expert, 0] += jnp.sum(pick * grads, axis=0, keepdims=True)
        picked = jnp.concatenate(picks, axis=0)
        y_total[...] += dot_tn(picked, y_buf[slot])
        dx_total[...] += dot_tn(picked, dx_buf[slot])
        return carry

    lax.fori_loop(0, groups_ref[tile], one, 0)
    y_out[...] = y_total[...].astype(y_out.dtype)
    dx_out[...] = dx_total[...].astype(dx_out.dtype)


def combine_rows(tables, place, y, dx, gg, first, count):
    owner, piece, source, groups, width = tables
    begin = jnp.cumsum(groups) - groups
    experts = place.shape[0]
    columns = y.shape[1]
    return pl.pallas_call(
        functools.partial(combine_kernel, first, width),
        grid_spec=pltpu.PrefetchScalarGridSpec(
            num_scalar_prefetch=5,
            grid=(count,),
            in_specs=[pl.BlockSpec((experts, count, 1, BLOCK), lambda *_: (0, first // count, 0, 0))]
            + [pl.BlockSpec(memory_space=pl.ANY)] * 3,
            out_specs=[
                pl.BlockSpec((BLOCK, columns), lambda t, *_: (t, 0)),
                pl.BlockSpec((BLOCK, columns), lambda t, *_: (t, 0)),
                pl.BlockSpec((experts, 1, 1, BLOCK), lambda t, *_: (0, t, 0, 0)),
            ],
            scratch_shapes=[
                pltpu.VMEM((2, BLOCK, columns), jnp.bfloat16),
                pltpu.VMEM((2, BLOCK, columns), jnp.bfloat16),
                pltpu.VMEM((2, BLOCK, 128), jnp.float32),
                pltpu.VMEM((BLOCK, columns), jnp.float32),
                pltpu.VMEM((BLOCK, columns), jnp.float32),
                pltpu.SemaphoreType.DMA((2, 3, GROUP)),
            ],
        ),
        out_shape=[
            jax.ShapeDtypeStruct((count * BLOCK, columns), jnp.bfloat16),
            jax.ShapeDtypeStruct((count * BLOCK, columns), jnp.bfloat16),
            jax.ShapeDtypeStruct((experts, count, 1, BLOCK), jnp.float32),
        ],
        compiler_params=pltpu.CompilerParams(vmem_limit_bytes=VMEM_LIMIT),
        cost_estimate=pl.CostEstimate(
            flops=count * 20 * PIECE_ROWS * BLOCK * columns * 4,
            bytes_accessed=count * 20 * PIECE_ROWS * columns * 4,
            transcendentals=0,
        ),
    )(owner, piece, source, groups, begin, place, y, dx, gg)


def flip(value, bit):
    size = lax.axis_size("dp")
    return lax.ppermute(value, "dp", [(i, i ^ bit) for i in range(size)])


def swap(value):
    return lax.ppermute(value, "tensor", [(0, 1), (1, 0)])


def add_low(left, right):
    return (left.astype(jnp.float32) + right.astype(jnp.float32)).astype(jnp.bfloat16)


def pick_index(value, index, axis):
    return lax.dynamic_index_in_dim(value, index, axis, keepdims=False)


def chip_sum(send, keep, rank):
    low_bit, high_bit = (rank // 4) % 2, rank // 8
    count, kinds, cuts, depth, hidden = keep.shape
    got = flip(send, 2)
    view = (count, kinds, cuts // 2, 2, depth, hidden)
    keep, got = keep.reshape(view), got.reshape(view)
    send = add_low(pick_index(keep, 1 - low_bit, 3), pick_index(got, 1 - low_bit, 3))
    keep = add_low(pick_index(keep, low_bit, 3), pick_index(got, low_bit, 3))
    got = flip(send, 4)
    send = add_low(pick_index(keep, 1 - high_bit, 2), pick_index(got, 1 - high_bit, 2))
    keep = add_low(pick_index(keep, high_bit, 2), pick_index(got, high_bit, 2))
    got = flip(send, 8)
    return add_low(keep, got)


def attend_half(normed, joined_weights, sizes, tables, allowed, score_scale):
    query_width, key_width, head_width = sizes
    rows = normed.shape[0]
    heads_here = query_width // head_width
    groups_here = key_width // head_width
    per_group = heads_here // groups_here
    cosine, sine_table = tables
    projected = jnp.dot(normed, joined_weights, preferred_element_type=jnp.float32)
    query_rows = rotate(
        projected[:, :query_width].reshape(rows, heads_here, head_width), cosine, sine_table
    ).astype(jnp.bfloat16)
    key_rows = rotate(
        projected[:, query_width : query_width + key_width].reshape(rows, groups_here, head_width),
        cosine,
        sine_table,
    ).astype(jnp.bfloat16)
    value_rows = (
        projected[:, query_width + key_width :]
        .astype(jnp.bfloat16)
        .reshape(rows, groups_here, head_width)
    )
    query_block = query_rows.reshape(rows, groups_here, per_group, head_width)
    scores = scores_of(query_block, key_rows, allowed, score_scale)
    highest = jnp.max(scores, axis=-1, keepdims=True)
    shifted = jnp.exp(scores - highest)
    totals = jnp.sum(shifted, axis=-1, keepdims=True)
    weights = (shifted / totals).astype(jnp.bfloat16)
    mixed_values = jnp.einsum(
        "kgqs,skd->qkgd", weights, value_rows, preferred_element_type=jnp.float32
    )
    attended = mixed_values.reshape(rows, query_width).astype(jnp.bfloat16)
    return attended, (query_block, key_rows, value_rows, highest + jnp.log(totals))


def attend_half_back(saved, attended_grad, sizes, tables, allowed, score_scale):
    query_width, key_width, head_width = sizes
    query_block, key_block, value_block, logsum = saved
    rows = key_block.shape[0]
    cosine, sine_table = tables
    scores = scores_of(query_block, key_block, allowed, score_scale)
    weights_full = jnp.exp(scores - logsum)
    weights_low = weights_full.astype(jnp.bfloat16)
    grad_block = attended_grad.reshape(query_block.shape)
    value_grad = jnp.einsum(
        "kgqs,qkgd->skd", weights_low, grad_block, preferred_element_type=jnp.float32
    )
    weight_grad = jnp.einsum(
        "qkgd,skd->kgqs", grad_block, value_block, preferred_element_type=jnp.float32
    )
    score_low = (
        weights_full * (weight_grad - jnp.sum(weights_full * weight_grad, axis=-1, keepdims=True))
    ).astype(jnp.bfloat16)
    query_grad = (
        jnp.einsum("kgqs,skd->qkgd", score_low, key_block, preferred_element_type=jnp.float32)
        * score_scale
    )
    key_grad = (
        jnp.einsum("kgqs,qkgd->skd", score_low, query_block, preferred_element_type=jnp.float32)
        * score_scale
    )
    query_grads = (
        rotate(query_grad.reshape(rows, -1, head_width), cosine, -sine_table)
        .astype(jnp.bfloat16)
        .reshape(rows, query_width)
    )
    key_grads = (
        rotate(key_grad, cosine, -sine_table).astype(jnp.bfloat16).reshape(rows, key_width)
    )
    value_grads = value_grad.astype(jnp.bfloat16).reshape(rows, key_width)
    return jnp.concatenate([query_grads, key_grads, value_grads], axis=1)


def slot_table(routes, expert_count, capacity):
    flattened = routes.reshape(-1)
    onehot = (flattened[:, None] == jnp.arange(expert_count, dtype=jnp.int32)[None, :]).astype(
        jnp.int32
    )
    placed = jnp.sum((jnp.cumsum(onehot, axis=0) - 1) * onehot, axis=1)
    entries = jnp.arange(flattened.shape[0], dtype=jnp.int32)
    return (
        jnp.full((expert_count * capacity,), flattened.shape[0], jnp.int32)
        .at[flattened * capacity + placed]
        .set(entries)
    )


def expert_forward(expert_inputs, w_gate, w_up, w_down):
    gate_proj = jnp.einsum(
        "ecd,edf->ecf", expert_inputs, w_gate, preferred_element_type=jnp.float32
    )
    up_proj = jnp.einsum("ecd,edf->ecf", expert_inputs, w_up, preferred_element_type=jnp.float32)
    activated = (gate_proj * jax.nn.sigmoid(gate_proj) * up_proj).astype(jnp.bfloat16)
    returned = jnp.einsum("ecf,efd->ecd", activated, w_down, preferred_element_type=jnp.float32)
    return (gate_proj, up_proj, activated, returned)


def shards_wide(
    tokens,
    norm_gains,
    w_query,
    w_key,
    w_value,
    w_out,
    mix_gains,
    w_router,
    w_gate,
    w_up,
    w_down,
    routes,
    starts,
    cotangent,
):
    share_rows = tokens.shape[0]
    model_width = tokens.shape[1]
    head_width = HD
    query_width = w_query.shape[1]
    key_width = w_key.shape[1]
    heads_here = query_width // head_width
    groups_here = key_width // head_width
    per_group = heads_here // groups_here
    experts_here = w_gate.shape[0]
    group_rows = routes.shape[0]
    choices_count = routes.shape[1]
    sequences_here = starts.shape[0]
    sequence_length = group_rows // sequences_here
    expert_count = w_router.shape[1]
    tensor_rank = lax.axis_index("tensor")
    total_tokens = group_rows * lax.axis_size("dp")
    score_scale = head_width ** (-0.5)
    inputs_share = tokens.astype(jnp.float32)
    normed_share = normalize(inputs_share, norm_gains).astype(jnp.bfloat16)
    normed = lax.all_gather(normed_share, "tensor", axis=0, tiled=True)
    joined_weights = jnp.concatenate([w_query, w_key, w_value], axis=1)
    projected = jnp.dot(normed, joined_weights, preferred_element_type=jnp.float32)
    cosine, sine_table = rope_tables(sequence_length, head_width)
    cosine_rows = jnp.tile(cosine, (sequences_here, 1))
    sine_rows = jnp.tile(sine_table, (sequences_here, 1))
    query_rows = rotate(
        projected[:, :query_width].reshape(group_rows, heads_here, head_width),
        cosine_rows,
        sine_rows,
    ).astype(jnp.bfloat16)
    key_rows = rotate(
        projected[:, query_width : query_width + key_width].reshape(
            group_rows, groups_here, head_width
        ),
        cosine_rows,
        sine_rows,
    ).astype(jnp.bfloat16)
    value_rows = (
        projected[:, query_width + key_width :]
        .astype(jnp.bfloat16)
        .reshape(group_rows, groups_here, head_width)
    )
    attended_parts = []
    logsum_parts = []
    for sequence in range(sequences_here):
        first_row = sequence * sequence_length
        query_block = query_rows[first_row : first_row + sequence_length].reshape(
            sequence_length, groups_here, per_group, head_width
        )
        key_block = key_rows[first_row : first_row + sequence_length]
        value_block = value_rows[first_row : first_row + sequence_length]
        allowed = allowed_pairs(starts[sequence], sequence_length, PIECE)
        scores = scores_of(query_block, key_block, allowed, score_scale)
        highest = jnp.max(scores, axis=-1, keepdims=True)
        shifted = jnp.exp(scores - highest)
        totals = jnp.sum(shifted, axis=-1, keepdims=True)
        weights = (shifted / totals).astype(jnp.bfloat16)
        mixed_values = jnp.einsum(
            "kgqs,skd->qkgd", weights, value_block, preferred_element_type=jnp.float32
        )
        attended_parts.append(
            mixed_values.reshape(sequence_length, query_width).astype(jnp.bfloat16)
        )
        logsum_parts.append(highest + jnp.log(totals))
    attended = jnp.concatenate(attended_parts, axis=0)
    attention_share = lax.psum_scatter(
        jnp.dot(attended, w_out, preferred_element_type=jnp.float32),
        "tensor",
        scatter_dimension=0,
        tiled=True,
    )
    middle_share = inputs_share + attention_share
    mixed_share = normalize(middle_share, mix_gains).astype(jnp.bfloat16)
    share_routes = lax.dynamic_slice_in_dim(routes, tensor_rank * share_rows, share_rows, 0)
    route_onehot = (
        share_routes[:, :, None] == jnp.arange(expert_count, dtype=jnp.int32)[None, None, :]
    ).astype(jnp.float32)
    logits = jnp.dot(mixed_share, w_router, preferred_element_type=jnp.float32)
    probabilities = softmax_rows(logits)
    chosen = jnp.sum(logits[:, None, :] * route_onehot, axis=-1)
    gate_soft = softmax_rows(chosen)
    gate_low = gate_soft.astype(jnp.bfloat16)
    counts, prob_sums = lax.psum(
        (jnp.sum(route_onehot, axis=(0, 1)), jnp.sum(probabilities, axis=0)), ("dp", "tensor")
    )
    fractions = counts / (total_tokens * choices_count)
    balance = expert_count * expert_count * fractions * prob_sums / total_tokens
    mixed_rows, gate_rows = (
        lax.all_gather(mixed_share, "tensor", axis=0, tiled=True),
        lax.all_gather(gate_low, "tensor", axis=0, tiled=True),
    )
    slots_all = slot_table(routes, expert_count, CAP)
    slots = lax.dynamic_slice_in_dim(
        slots_all, tensor_rank * experts_here * CAP, experts_here * CAP, 0
    )
    owners = slots // choices_count
    padded_rows = jnp.concatenate([mixed_rows, jnp.zeros((1, model_width), jnp.bfloat16)], axis=0)
    padded_gates = jnp.concatenate(
        [gate_rows.reshape(-1).astype(jnp.float32), jnp.zeros((1,), jnp.float32)], axis=0
    )
    slot_gates = padded_gates[slots]
    expert_inputs = padded_rows[owners].reshape(experts_here, CAP, model_width)
    gate_proj, up_proj, activated, returned = expert_forward(expert_inputs, w_gate, w_up, w_down)
    returned_flat = returned.reshape(experts_here * CAP, model_width)
    expert_partial = jax.ops.segment_sum(
        slot_gates[:, None] * returned_flat, owners, num_segments=group_rows + 1
    )[:group_rows]
    expert_share = lax.psum_scatter(
        expert_partial.astype(jnp.bfloat16), "tensor", scatter_dimension=0, tiled=True
    ).astype(jnp.float32)
    output_share = (middle_share + expert_share).astype(jnp.bfloat16)
    upstream = cotangent.astype(jnp.float32)
    upstream_rows = lax.all_gather(cotangent, "tensor", axis=0, tiled=True)
    padded_upstream = jnp.concatenate(
        [upstream_rows, jnp.zeros((1, model_width), jnp.bfloat16)], axis=0
    )
    slot_upstream = padded_upstream[owners].astype(jnp.float32)
    slot_cotangent = (
        (slot_gates[:, None] * slot_upstream)
        .astype(jnp.bfloat16)
        .reshape(experts_here, CAP, model_width)
    )
    slot_gate_grad = jnp.sum(slot_upstream * returned_flat, axis=1)
    activated_grad = jnp.einsum(
        "ecd,efd->ecf", slot_cotangent, w_down, preferred_element_type=jnp.float32
    )
    down_grad = jnp.einsum(
        "ecf,ecd->efd", activated, slot_cotangent, preferred_element_type=jnp.float32
    )
    sigmoid_gate = jax.nn.sigmoid(gate_proj)
    gate_proj_low = (
        activated_grad * up_proj * sigmoid_gate * (1.0 + gate_proj * (1.0 - sigmoid_gate))
    ).astype(jnp.bfloat16)
    up_proj_low = (activated_grad * gate_proj * sigmoid_gate).astype(jnp.bfloat16)
    inputs_grad = jnp.einsum(
        "ecf,edf->ecd", gate_proj_low, w_gate, preferred_element_type=jnp.float32
    ) + jnp.einsum("ecf,edf->ecd", up_proj_low, w_up, preferred_element_type=jnp.float32)
    gate_grad = jnp.einsum(
        "ecd,ecf->edf", expert_inputs, gate_proj_low, preferred_element_type=jnp.float32
    )
    up_grad = jnp.einsum(
        "ecd,ecf->edf", expert_inputs, up_proj_low, preferred_element_type=jnp.float32
    )
    mixed_partial = jax.ops.segment_sum(
        inputs_grad.reshape(experts_here * CAP, model_width), owners, num_segments=group_rows + 1
    )[:group_rows]
    gate_partial = jax.ops.segment_sum(
        slot_gate_grad, slots, num_segments=group_rows * choices_count + 1
    )[: group_rows * choices_count].reshape(group_rows, choices_count)
    mixed_grad_share, gates_grad_share = (
        lax.psum_scatter(mixed_partial, "tensor", scatter_dimension=0, tiled=True),
        lax.psum_scatter(gate_partial, "tensor", scatter_dimension=0, tiled=True),
    )
    gate_total, up_total = (
        lax.psum_scatter(
            gate_grad.astype(jnp.bfloat16), "dp", scatter_dimension=1, tiled=True
        ).astype(jnp.float32),
        lax.psum_scatter(
            up_grad.astype(jnp.bfloat16), "dp", scatter_dimension=1, tiled=True
        ).astype(jnp.float32),
    )
    down_total = lax.psum_scatter(
        down_grad.astype(jnp.bfloat16), "dp", scatter_dimension=2, tiled=True
    ).astype(jnp.float32)
    chosen_grad = gate_soft * (
        gates_grad_share - jnp.sum(gate_soft * gates_grad_share, axis=-1, keepdims=True)
    )
    logit_grad = jnp.sum(chosen_grad[:, :, None] * route_onehot, axis=1)
    prob_target = ALPHA * expert_count * fractions / total_tokens
    logit_grad = logit_grad + probabilities * (
        prob_target[None, :] - jnp.sum(probabilities * prob_target[None, :], axis=-1, keepdims=True)
    )
    mixed_float = mixed_share.astype(jnp.float32)
    router_grad = jnp.dot(
        mixed_float.T, logit_grad, precision=HIGHEST, preferred_element_type=jnp.float32
    )
    mixed_grad_share = mixed_grad_share + jnp.dot(
        logit_grad,
        w_router.astype(jnp.float32).T,
        precision=HIGHEST,
        preferred_element_type=jnp.float32,
    )
    mix_pullback = jax.vjp(normalize, middle_share, mix_gains)[1]
    middle_from_norm, mix_gain_grad = mix_pullback(mixed_grad_share)
    middle_grad = upstream + middle_from_norm
    middle_low = middle_grad.astype(jnp.bfloat16)
    middle_rows = lax.all_gather(middle_low, "tensor", axis=0, tiled=True)
    out_grad = contract_rows(attended, middle_rows)
    attended_grad = contract_cols(middle_rows, w_out).astype(jnp.bfloat16)
    query_parts = []
    key_parts = []
    value_parts = []
    for sequence in range(sequences_here):
        first_row = sequence * sequence_length
        query_block = query_rows[first_row : first_row + sequence_length].reshape(
            sequence_length, groups_here, per_group, head_width
        )
        key_block = key_rows[first_row : first_row + sequence_length]
        value_block = value_rows[first_row : first_row + sequence_length]
        allowed = allowed_pairs(starts[sequence], sequence_length, PIECE)
        scores = scores_of(query_block, key_block, allowed, score_scale)
        weights_full = jnp.exp(scores - logsum_parts[sequence])
        weights_low = weights_full.astype(jnp.bfloat16)
        grad_block = attended_grad[first_row : first_row + sequence_length].reshape(
            sequence_length, groups_here, per_group, head_width
        )
        value_parts.append(
            jnp.einsum(
                "kgqs,qkgd->skd", weights_low, grad_block, preferred_element_type=jnp.float32
            )
        )
        weight_grad = jnp.einsum(
            "qkgd,skd->kgqs", grad_block, value_block, preferred_element_type=jnp.float32
        )
        score_low = (
            weights_full
            * (weight_grad - jnp.sum(weights_full * weight_grad, axis=-1, keepdims=True))
        ).astype(jnp.bfloat16)
        query_parts.append(
            jnp.einsum("kgqs,skd->qkgd", score_low, key_block, preferred_element_type=jnp.float32)
            * score_scale
        )
        key_parts.append(
            jnp.einsum("kgqs,qkgd->skd", score_low, query_block, preferred_element_type=jnp.float32)
            * score_scale
        )
    query_grads = (
        rotate(
            jnp.concatenate(query_parts, axis=0).reshape(group_rows, heads_here, head_width),
            cosine_rows,
            -sine_rows,
        )
        .astype(jnp.bfloat16)
        .reshape(group_rows, query_width)
    )
    key_grads = (
        rotate(jnp.concatenate(key_parts, axis=0), cosine_rows, -sine_rows)
        .astype(jnp.bfloat16)
        .reshape(group_rows, key_width)
    )
    value_grads = (
        jnp.concatenate(value_parts, axis=0).astype(jnp.bfloat16).reshape(group_rows, key_width)
    )
    joined_grads = jnp.concatenate([query_grads, key_grads, value_grads], axis=1)
    joined_weight_grad = contract_rows(normed, joined_grads)
    normed_grad_share = lax.psum_scatter(
        contract_cols(joined_grads, joined_weights).astype(jnp.bfloat16),
        "tensor",
        scatter_dimension=0,
        tiled=True,
    ).astype(jnp.float32)
    input_pullback = jax.vjp(normalize, inputs_share, norm_gains)[1]
    input_from_norm, norm_gain_grad = input_pullback(normed_grad_share)
    input_grad_share = middle_grad + input_from_norm
    query_total, key_total, value_total, out_turned = (
        lax.psum_scatter(
            joined_weight_grad[:, :query_width].astype(jnp.bfloat16),
            "dp",
            scatter_dimension=0,
            tiled=True,
        ).astype(jnp.float32),
        lax.psum_scatter(
            joined_weight_grad[:, query_width : query_width + key_width].astype(jnp.bfloat16),
            "dp",
            scatter_dimension=0,
            tiled=True,
        ).astype(jnp.float32),
        lax.psum_scatter(
            joined_weight_grad[:, query_width + key_width :].astype(jnp.bfloat16),
            "dp",
            scatter_dimension=0,
            tiled=True,
        ).astype(jnp.float32),
        lax.psum_scatter(
            out_grad.T.astype(jnp.bfloat16), "dp", scatter_dimension=0, tiled=True
        ).astype(jnp.float32),
    )
    out_total = out_turned.T
    norm_gain_total, mix_gain_total, router_total = lax.psum(
        (norm_gain_grad, mix_gain_grad, router_grad), ("dp", "tensor")
    )
    return (
        output_share,
        balance,
        input_grad_share,
        norm_gain_total,
        query_total,
        key_total,
        value_total,
        out_total,
        mix_gain_total,
        router_total,
        gate_total,
        up_total,
        down_total,
    )


def all_sum(value):
    for bit in (1, 2, 4, 8):
        value = value + flip(value, bit)
    return value + swap(value)


def spread(value):
    across = swap(value)
    return [value, across, flip(value, 1), flip(across, 1)]


CHUNK = 2


def shards_pair(
    tokens,
    norm_gains,
    w_query,
    w_key,
    w_value,
    w_out,
    mix_gains,
    w_router,
    w_gate,
    w_up,
    w_down,
    routes,
    starts,
    cotangent,
):
    share_rows, model_width = tokens.shape
    query_width = w_query.shape[1]
    key_width = w_key.shape[1]
    sizes = (query_width, key_width, HD)
    experts_here = w_gate.shape[0]
    experts = experts_here // 2
    choices_count = routes.shape[1]
    expert_count = w_router.shape[1]
    dp_size = lax.axis_size("dp")
    rank = lax.axis_index("dp")
    core, side = rank % 2, (rank // 2) % 2
    tensor_rank = lax.axis_index("tensor")
    total_tokens = routes.shape[0] * dp_size
    score_scale = HD ** (-0.5)
    depth = model_width // dp_size * 2
    slots = round_up(2 * CAP, BLOCK)

    joined_own = jnp.concatenate([w_query, w_key, w_value], axis=1)
    part_rows = model_width // dp_size
    out_rows = query_width // dp_size
    joined_other = lax.all_gather(
        swap(lax.dynamic_slice_in_dim(joined_own, rank * part_rows, part_rows, 0)),
        "dp",
        axis=0,
        tiled=True,
    )
    out_other = lax.all_gather(
        swap(lax.dynamic_slice_in_dim(w_out, rank * out_rows, out_rows, 0)),
        "dp",
        axis=0,
        tiled=True,
    )

    own_routes = lax.dynamic_slice_in_dim(routes, tensor_rank * share_rows, share_rows, 0)
    across_routes = lax.dynamic_slice_in_dim(routes, (1 - tensor_rank) * share_rows, share_rows, 0)
    both_routes = jnp.concatenate([own_routes, across_routes], axis=0)
    group_routes = jnp.concatenate([both_routes, flip(both_routes, 1)], axis=0)
    first_expert = tensor_rank * experts_here + core * experts

    cotangent_rows = spread(cotangent)

    inputs_share = tokens.astype(jnp.float32)
    normed = normalize(inputs_share, norm_gains).astype(jnp.bfloat16)
    tables = rope_tables(share_rows, HD)
    starts_row = lax.dynamic_index_in_dim(starts, tensor_rank, 0, keepdims=False)
    allowed = allowed_pairs(starts_row, share_rows, PIECE)
    attended_own, saved_own = attend_half(normed, joined_own, sizes, tables, allowed, score_scale)
    attended_other, saved_other = attend_half(
        normed, joined_other, sizes, tables, allowed, score_scale
    )
    middle_share = (
        inputs_share
        + jnp.dot(attended_own, w_out, preferred_element_type=jnp.float32)
        + jnp.dot(attended_other, out_other, preferred_element_type=jnp.float32)
    )
    mixed_share = normalize(middle_share, mix_gains).astype(jnp.bfloat16)

    route_onehot = (
        own_routes[:, :, None] == jnp.arange(expert_count, dtype=jnp.int32)[None, None, :]
    ).astype(jnp.float32)
    logits = jnp.dot(mixed_share, w_router, preferred_element_type=jnp.float32)
    probabilities = softmax_rows(logits)
    chosen = jnp.sum(logits[:, None, :] * route_onehot, axis=-1)
    gate_soft = softmax_rows(chosen)
    gate_low = gate_soft.astype(jnp.bfloat16)
    counts = all_sum(jnp.sum(route_onehot, axis=(0, 1)))
    prob_sums = all_sum(jnp.sum(probabilities, axis=0))
    fractions = counts / (total_tokens * choices_count)
    balance = expert_count * expert_count * fractions * prob_sums / total_tokens

    mixed_rows = spread(mixed_share)
    group_gates = jnp.concatenate(spread(gate_low), axis=0)
    place, begins, ends, gates = placement(group_routes, group_gates, first_expert, experts)
    gather_from = gather_tables(begins, ends, slots)
    blocks = gather_from[2]
    cot_slots = gather_rows(gather_from, place, None, cotangent_rows, slots, 0, experts)[0]
    misc = jnp.stack([core * experts, side])
    weights = (w_gate, w_up, w_down)
    carried = None
    sums = []
    first_part = gather_rows(gather_from, place, gates, mixed_rows, slots, 0, CHUNK)
    later_part = gather_rows(gather_from, place, gates, mixed_rows, slots, CHUNK, experts - CHUNK)
    for first in range(0, experts, CHUNK):
        (x_slots, slot_gates), x_first = (
            (first_part, 0) if first == 0 else (later_part, CHUNK)
        )
        *carried, send, keep = expert_call(
            blocks, misc, x_slots, cot_slots, slot_gates, weights, carried, slots,
            first, CHUNK, x_first, 0, depth,
        )
        sums.append(chip_sum(send, keep, rank))

    combine_from = combine_tables(begins, ends, slots)
    tiles = place.shape[1] // 2
    turned_routes = group_routes.T
    names = first_expert + jnp.arange(experts, dtype=jnp.int32)

    def combined(half):
        y, dx, gate_grads = combine_rows(combine_from, place, *carried, half * tiles, tiles)
        gate_grads = gate_grads[:experts].reshape(experts, 1, tiles * BLOCK)
        rows = turned_routes[:, half * tiles * BLOCK : (half + 1) * tiles * BLOCK]
        hit = rows[None, :, :] == names[:, None, None]
        return y, dx, jnp.sum(jnp.where(hit, gate_grads, 0.0), axis=0)

    y_far, dx_far, gg_far = combined(1)
    y_far, dx_far, gg_far = flip(y_far, 1), flip(dx_far, 1), flip(gg_far, 1)
    y_near, dx_near, gg_near = combined(0)
    dx_across = swap(add_low(dx_near[share_rows:], dx_far[share_rows:]))
    gg_across = swap(gg_near[:, share_rows:] + gg_far[:, share_rows:])
    y_across = swap(add_low(y_near[share_rows:], y_far[share_rows:]))
    mixed_grad_share = (
        dx_near[:share_rows].astype(jnp.float32)
        + dx_far[:share_rows].astype(jnp.float32)
        + dx_across.astype(jnp.float32)
    )
    gates_grad_share = (gg_near[:, :share_rows] + gg_far[:, :share_rows] + gg_across).T
    expert_share = (
        y_near[:share_rows].astype(jnp.float32)
        + y_far[:share_rows].astype(jnp.float32)
        + y_across.astype(jnp.float32)
    )
    output_share = (middle_share + expert_share).astype(jnp.bfloat16)

    upstream = cotangent.astype(jnp.float32)
    chosen_grad = gate_soft * (
        gates_grad_share - jnp.sum(gate_soft * gates_grad_share, axis=-1, keepdims=True)
    )
    logit_grad = jnp.sum(chosen_grad[:, :, None] * route_onehot, axis=1)
    prob_target = ALPHA * expert_count * fractions / total_tokens
    logit_grad = logit_grad + probabilities * (
        prob_target[None, :] - jnp.sum(probabilities * prob_target[None, :], axis=-1, keepdims=True)
    )
    router_grad = jnp.dot(
        mixed_share.astype(jnp.float32).T,
        logit_grad,
        precision=HIGHEST,
        preferred_element_type=jnp.float32,
    )
    mixed_grad_share = mixed_grad_share + jnp.dot(
        logit_grad,
        w_router.astype(jnp.float32).T,
        precision=HIGHEST,
        preferred_element_type=jnp.float32,
    )
    mix_pullback = jax.vjp(normalize, middle_share, mix_gains)[1]
    middle_from_norm, mix_gain_grad = mix_pullback(mixed_grad_share)
    middle_grad = upstream + middle_from_norm
    middle_low = middle_grad.astype(jnp.bfloat16)

    def half_back(saved, attended, joined_weights, out_weights):
        attended_grad = dot_nt(middle_low, out_weights).astype(jnp.bfloat16)
        joined_grads = attend_half_back(saved, attended_grad, sizes, tables, allowed, score_scale)
        weight_grads = jnp.concatenate(
            [dot_tn(normed, joined_grads), dot_tn(middle_low, attended)], axis=1
        )
        return weight_grads.astype(jnp.bfloat16), dot_nt(joined_grads, joined_weights)

    other_grads, other_normed = half_back(saved_other, attended_other, joined_other, out_other)
    own_grads, own_normed = half_back(saved_own, attended_own, joined_own, w_out)
    attention_grads = add_low(own_grads, swap(other_grads))
    attention_total = lax.psum_scatter(
        attention_grads, "dp", scatter_dimension=0, tiled=True
    ).astype(jnp.float32)
    input_pullback = jax.vjp(normalize, inputs_share, norm_gains)[1]
    input_from_norm, norm_gain_grad = input_pullback(other_normed + own_normed)
    input_grad_share = middle_grad + input_from_norm
    key_end = query_width + key_width
    joined_end = key_end + key_width

    router_total = all_sum(router_grad)
    mix_gain_total = all_sum(mix_gain_grad)
    norm_gain_total = all_sum(norm_gain_grad)

    mine = jnp.concatenate(sums, axis=0).reshape(experts, 3, 2, depth // 2, -1)
    theirs = flip(pick_index(mine, 1 - core, 2), 1)
    mine = pick_index(mine, core, 2)
    expert_total = jnp.where(
        core == 0,
        jnp.concatenate([mine, theirs], axis=0),
        jnp.concatenate([theirs, mine], axis=0),
    ).astype(jnp.float32)
    return (
        output_share,
        balance,
        input_grad_share,
        norm_gain_total,
        attention_total[:, :query_width],
        attention_total[:, query_width:key_end],
        attention_total[:, key_end:joined_end],
        attention_total[:, joined_end:].T,
        mix_gain_total,
        router_total,
        expert_total[:, 0],
        expert_total[:, 1],
        expert_total[:, 2].transpose(0, 2, 1),
    )


def solution(mesh):
    sizes = dict(mesh.shape)
    paired = sizes["tensor"] == 2 and sizes["dp"] == 16
    return jax.shard_map(
        shards_pair if paired else shards_wide,
        mesh=mesh,
        in_specs=(
            P(("dp", "tensor"), None),
            P(),
            P(None, "tensor"),
            P(None, "tensor"),
            P(None, "tensor"),
            P("tensor", None),
            P(),
            P(),
            P("tensor", None, None),
            P("tensor", None, None),
            P("tensor", None, None),
            P("dp", None),
            P("dp", None),
            P(("dp", "tensor"), None),
        ),
        out_specs=(
            P(("dp", "tensor"), None),
            P(),
            P(("dp", "tensor"), None),
            P(),
            P("dp", "tensor"),
            P("dp", "tensor"),
            P("dp", "tensor"),
            P("tensor", "dp"),
            P(),
            P(),
            P("tensor", "dp", None),
            P("tensor", "dp", None),
            P("tensor", None, "dp"),
        ),
        check_vma=False,
    )
```

```python
import functools

import jax
import jax.numpy as jnp
from jax import lax
from jax.experimental import pallas as pl
from jax.experimental.pallas import tpu as pltpu
from jax.sharding import PartitionSpec as P

HD = 64
PIECE = 256
CAP = 614


EPSILON = 1e-06
ALPHA = 0.01
HIGHEST = lax.Precision.HIGHEST


def normalize(values, gains):
    return values * lax.rsqrt(jnp.mean(values * values, axis=-1, keepdims=True) + EPSILON) * gains


def softmax_rows(values):
    shifted = jnp.exp(values - jnp.max(values, axis=-1, keepdims=True))
    return shifted / jnp.sum(shifted, axis=-1, keepdims=True)


def contract_rows(left, right):
    return lax.dot_general(
        left, right, (((0,), (0,)), ((), ())), preferred_element_type=jnp.float32
    )


def contract_cols(left, right):
    return lax.dot_general(
        left, right, (((1,), (1,)), ((), ())), preferred_element_type=jnp.float32
    )


def rope_tables(sequence_length, head_width):
    half_width = head_width // 2
    frequency = 10000.0 ** (-(jnp.arange(half_width, dtype=jnp.float32) * 2.0 / head_width))
    angles = jnp.arange(sequence_length, dtype=jnp.float32)[:, None] * frequency[None, :]
    return (jnp.cos(angles), jnp.sin(angles))


def rotate(values, cosine, sine_table):
    half_width = values.shape[-1] // 2
    first_half = values[..., :half_width]
    second_half = values[..., half_width:]
    cosine_rows = cosine[:, None, :]
    sine_rows = sine_table[:, None, :]
    return jnp.concatenate(
        [
            first_half * cosine_rows - second_half * sine_rows,
            second_half * cosine_rows + first_half * sine_rows,
        ],
        axis=-1,
    )


def allowed_pairs(starts_row, sequence_length, piece_length):
    position = jnp.arange(sequence_length, dtype=jnp.int32)
    labels = jnp.full((sequence_length,), -1, jnp.int32)
    for piece_index in range(starts_row.shape[0]):
        inside = (position >= starts_row[piece_index]) & (
            position < starts_row[piece_index] + piece_length
        )
        labels = jnp.where(inside, piece_index, labels)
    causal = position[None, :] <= position[:, None]
    shared = (labels[:, None] == labels[None, :]) & (labels[:, None] >= 0)
    return causal | shared


def scores_of(query_block, key_block, allowed, score_scale):
    raw_scores = (
        jnp.einsum("qkgd,skd->kgqs", query_block, key_block, preferred_element_type=jnp.float32)
        * score_scale
    )
    return jnp.where(allowed, raw_scores, -1e30)


BLOCK = 256
PART = 256
PIECE_ROWS = 64
GROUP = BLOCK // PIECE_ROWS
VMEM_LIMIT = 60 * 1024 * 1024
COST = 0.6


def cost(micros):
    return pl.CostEstimate(flops=0, bytes_accessed=int(micros * 3e6), transcendentals=0)


def dot_nt(left, right):
    return lax.dot_general(
        left, right, (((1,), (1,)), ((), ())), preferred_element_type=jnp.float32
    )


def dot_tn(left, right):
    return lax.dot_general(
        left, right, (((0,), (0,)), ((), ())), preferred_element_type=jnp.float32
    )


def round_up(value, multiple):
    return -(-value // multiple) * multiple


def placement(routes_rows, gates_rows, first_expert, experts):
    rows = routes_rows.shape[0]
    tiles = rows // BLOCK
    turned = routes_rows.T
    names = first_expert + jnp.arange(experts, dtype=jnp.int32)
    hit = turned[None, :, :] == names[:, None, None]
    member = jnp.any(hit, axis=1)
    upper = jnp.triu(jnp.ones((BLOCK, BLOCK), jnp.bfloat16))
    inside = jnp.dot(
        member.astype(jnp.bfloat16).reshape(experts * tiles, BLOCK),
        upper,
        preferred_element_type=jnp.float32,
    ).astype(jnp.int32).reshape(experts, tiles, BLOCK)
    sums = inside[:, :, -1]
    ends = jnp.cumsum(sums, axis=1)
    begins = ends - sums
    place = jnp.where(
        member.reshape(experts, tiles, BLOCK), begins[:, :, None] + inside - 1, -1
    )
    place = jnp.concatenate(
        [place, jnp.full((1, tiles, BLOCK), -1, jnp.int32)], axis=0
    ).reshape(experts + 1, tiles, 1, BLOCK)
    gates = None
    if gates_rows is not None:
        gates = jnp.sum(
            jnp.where(hit, gates_rows.astype(jnp.float32).T[None, :, :], 0.0), axis=1
        ).reshape(experts, tiles, 1, BLOCK)
    return place, begins, ends, gates


def gather_tables(begins, ends, slots):
    counts = ends[:, -1]
    parts = jnp.arange(slots // PART, dtype=jnp.int32) * PART
    low = jnp.sum((ends[:, None, :] <= parts[None, :, None]).astype(jnp.int32), axis=2)
    high = jnp.sum((begins[:, None, :] < parts[None, :, None] + PART).astype(jnp.int32), axis=2)
    high = jnp.where(parts[None, :] < counts[:, None], high, low)
    blocks = jnp.maximum(-(-counts // BLOCK), 1)
    return low, high, blocks


def combine_tables(begins, ends, slots):
    experts, tiles = begins.shape
    width = round_up(experts * (BLOCK // PIECE_ROWS + 1), GROUP)
    first = begins // PIECE_ROWS
    amount = jnp.where(ends > begins, (ends - 1) // PIECE_ROWS - first + 1, 0)
    stop = jnp.cumsum(amount, axis=0)
    place = jnp.arange(width, dtype=jnp.int32)
    owner = jnp.sum(
        (stop.T[:, None, :] <= place[None, :, None]).astype(jnp.int32), axis=2
    )
    chosen = owner[:, :, None] == jnp.arange(experts, dtype=jnp.int32)[None, None, :]
    offset = jnp.sum(
        jnp.where(chosen, (first - (stop - amount)).T[:, None, :], 0), axis=2
    )
    valid = owner < experts
    piece = jnp.where(valid, offset + place[None, :], 0)
    source = jnp.where(valid, owner, 0) * (slots // PIECE_ROWS) + piece
    groups = jnp.maximum(-(-stop[-1] // GROUP), 1)
    return owner, piece, source, groups, width


def gather_kernel(
    experts, slots, sources, with_gates, after, low_ref, high_ref, blocks_ref, place_ref, *rest
):
    if with_gates:
        gates_ref, rest = rest[0], rest[1:]
    inputs, rest = rest[:sources], rest[sources + after :]
    if with_gates:
        out_ref, gate_out_ref, rest = rest[0], rest[1], rest[2:]
    else:
        out_ref, rest = rest[0], rest[1:]
    held, total, gate_total, sems = rest
    expert = pl.program_id(0)
    part = pl.program_id(1)
    share = inputs[0].shape[0]

    @pl.when((expert == 0) & (part == 0))
    def _():
        copies = [
            pltpu.make_async_copy(ref, held.at[pl.ds(i * share, share)], sems.at[i])
            for i, ref in enumerate(inputs)
        ]
        for copy in copies:
            copy.start()
        for copy in copies:
            copy.wait()

    @pl.when(part * PART < blocks_ref[expert] * BLOCK)
    def _():
        total[...] = jnp.zeros_like(total)
        if with_gates:
            gate_total[...] = jnp.zeros_like(gate_total)
        rows = lax.broadcasted_iota(jnp.int32, (PART, BLOCK), 0) + part * PART

        def step(tile, carry):
            match = rows == place_ref[expert, tile]
            pick = jnp.where(match, 1.0, 0.0)
            start = pl.multiple_of(tile * BLOCK, BLOCK)
            total[...] += jnp.dot(
                pick.astype(jnp.bfloat16),
                held[pl.ds(start, BLOCK), :],
                preferred_element_type=jnp.float32,
            )
            if with_gates:
                weighted = pick * gates_ref[expert, tile]
                gate_total[...] += jnp.broadcast_to(
                    jnp.sum(weighted, axis=1, keepdims=True), gate_total.shape
                )
            return carry

        lax.fori_loop(low_ref[expert, part], high_ref[expert, part], step, 0)
        out_ref[...] = total[...].astype(out_ref.dtype)
        if with_gates:
            gate_out_ref[...] = gate_total[...]


def gather_rows(tables, place, gates, sources, slots, first, count, after=()):
    low, high, blocks = tables
    low, high, blocks = (t[first : first + count] for t in (low, high, blocks))
    place = place[first : first + count]
    tiles = place.shape[1]
    rows = tiles * BLOCK
    width = sources[0].shape[1]
    with_gates = gates is not None
    if with_gates:
        gates = gates[first : first + count]
    parts = slots // PART

    def out_index(expert, part, low, high, blocks):
        return (expert * parts + jnp.minimum(part, blocks[expert] * (BLOCK // PART) - 1), 0)

    def whole(array):
        zeros = (0,) * array.ndim
        return pl.BlockSpec(array.shape, lambda *_: zeros)

    operands = [place] + ([gates] if with_gates else [])
    in_specs = [whole(a) for a in operands] + [pl.BlockSpec(memory_space=pl.ANY)] * (
        len(sources) + len(after)
    )
    out_shape = [jax.ShapeDtypeStruct((count * slots, width), jnp.bfloat16)]
    out_specs = [pl.BlockSpec((PART, width), out_index)]
    if with_gates:
        out_shape.append(jax.ShapeDtypeStruct((count * slots, 128), jnp.float32))
        out_specs.append(pl.BlockSpec((PART, 128), out_index))
    return pl.pallas_call(
        functools.partial(gather_kernel, count, slots, len(sources), with_gates, len(after)),
        grid_spec=pltpu.PrefetchScalarGridSpec(
            num_scalar_prefetch=3,
            grid=(count, parts),
            in_specs=in_specs,
            out_specs=out_specs,
            scratch_shapes=[
                pltpu.VMEM((rows, width), jnp.bfloat16),
                pltpu.VMEM((PART, width), jnp.float32),
                pltpu.VMEM((PART, 128), jnp.float32),
                pltpu.SemaphoreType.DMA((len(sources),)),
            ],
        ),
        out_shape=out_shape,
        compiler_params=pltpu.CompilerParams(vmem_limit_bytes=VMEM_LIMIT),
        cost_estimate=cost(COST * count * 5.5),
    )(low, high, blocks, *operands, *sources, *after)


def expert_kernel(
    first, split, depth, far_first, extra, blocks_ref, misc_ref, x_ref, c_ref, sg_ref, wg_ref, wu_ref, wd_ref, *rest
):
    yd_ref, gg_ref = rest[extra : extra + 2]
    rest = rest[extra + 2 :]
    width = x_ref.shape[1]
    if split:
        send_ref, keep_ref = rest[:2]
        rest = rest[2:]
    else:
        grads_ref = rest[0]
        rest = rest[1:]
    total_gu, total_d = rest
    block = pl.program_id(1)
    hidden = wg_ref.shape[2]

    @pl.when(block == 0)
    def _():
        total_gu[...] = jnp.zeros_like(total_gu)
        total_d[...] = jnp.zeros_like(total_d)

    @pl.when(block < blocks_ref[first + pl.program_id(0)])
    def _():
        x = x_ref[...]
        c = c_ref[...]
        gate = jnp.concatenate([sg_ref[...]] * (hidden // 128), axis=1)
        gate_proj = jnp.dot(x, wg_ref[0], preferred_element_type=jnp.float32)
        up_proj = jnp.dot(x, wu_ref[0], preferred_element_type=jnp.float32)
        sigmoid = 1.0 / (1.0 + jnp.exp(-gate_proj))
        silu = gate_proj * sigmoid
        activated = (silu * up_proj).astype(jnp.bfloat16).astype(jnp.float32)
        pulled = dot_nt(c, wd_ref[0])
        gate_grad = jnp.sum(activated * pulled, axis=1, keepdims=True)
        gg_ref[...] = jnp.broadcast_to(gate_grad, gg_ref.shape)
        gated = (gate * activated).astype(jnp.bfloat16)
        yd_ref[:, :width] = jnp.dot(
            gated, wd_ref[0], preferred_element_type=jnp.float32
        ).astype(yd_ref.dtype)
        activated_grad = gate * pulled
        gate_low = (
            activated_grad * up_proj * sigmoid * (1.0 + gate_proj * (1.0 - sigmoid))
        ).astype(jnp.bfloat16)
        up_low = (activated_grad * silu).astype(jnp.bfloat16)
        yd_ref[:, width:] = (dot_nt(gate_low, wg_ref[0]) + dot_nt(up_low, wu_ref[0])).astype(
            yd_ref.dtype
        )
        total_gu[...] += dot_tn(x, jnp.concatenate([gate_low, up_low], axis=1))
        total_d[...] += dot_tn(c, gated)

    @pl.when(block == pl.num_programs(1) - 1)
    def _():
        parts = (
            (total_gu, 0),
            (total_gu, hidden),
            (total_d, 0),
        )
        for which, (ref, column) in enumerate(parts):
            if split:
                side = misc_ref[1 + far_first]
                for high in range(2):
                    for low in range(2):
                        for out, chosen in ((keep_ref, side), (send_ref, 1 - side)):
                            middle, last = (chosen, low) if far_first else (low, chosen)
                            start = ((high * 2 + middle) * 2 + last) * depth
                            out[0, which, high, low] = ref[
                                pl.ds(pl.multiple_of(start, 64), depth), pl.ds(column, hidden)
                            ].astype(out.dtype)
            else:
                grads_ref[0, which] = ref[:, pl.ds(column, hidden)].astype(grads_ref.dtype)


def expert_call(
    blocks, misc, x, c, sg, weights, carried, slots, first, count, x_first, c_first, depth, far_first=0, after=()
):
    w_gate, w_up, w_down = weights
    experts = blocks.shape[0]
    width = x.shape[1]
    hidden = w_gate.shape[2]
    most = slots // BLOCK
    split = depth is not None

    def rows_index(base):
        def index(expert, block, blocks, misc):
            limit = blocks[first + expert] - 1
            return ((first - base + expert) * most + jnp.minimum(block, limit), 0)

        return index

    def weight_index(expert, block, blocks, misc):
        return (misc[0] + first + expert, 0, 0)

    def grads_index(expert, block, blocks, misc):
        return (expert, 0, 0, 0, 0, 0)

    out_shape = [
        jax.ShapeDtypeStruct((experts * slots, 2 * width), jnp.bfloat16),
        jax.ShapeDtypeStruct((experts * slots, 128), jnp.float32),
    ]
    out_specs = [
        pl.BlockSpec((BLOCK, 2 * width), rows_index(0)),
        pl.BlockSpec((BLOCK, 128), rows_index(0)),
    ]
    if split:
        out_shape += [jax.ShapeDtypeStruct((count, 3, 2, 2, depth, hidden), jnp.bfloat16)] * 2
        out_specs += [pl.BlockSpec((1, 3, 2, 2, depth, hidden), grads_index)] * 2
    else:
        out_shape += [jax.ShapeDtypeStruct((count, 3, width, hidden), jnp.bfloat16)]
        out_specs += [pl.BlockSpec((1, 3, width, hidden), lambda e, b, *_: (e, 0, 0, 0))]
    operands = [x, c, sg, w_gate, w_up, w_down]
    in_specs = [
        pl.BlockSpec((BLOCK, width), rows_index(x_first)),
        pl.BlockSpec((BLOCK, width), rows_index(c_first)),
        pl.BlockSpec((BLOCK, 128), rows_index(x_first)),
        pl.BlockSpec((1, width, hidden), weight_index),
        pl.BlockSpec((1, width, hidden), weight_index),
        pl.BlockSpec((1, hidden, width), weight_index),
    ]
    aliases = {}
    if carried is not None:
        operands += list(carried)
        aliases = {8: 0, 9: 1}
    operands += list(after)
    extra = len(operands) - 6
    in_specs += [pl.BlockSpec(memory_space=pl.ANY)] * extra
    return pl.pallas_call(
        functools.partial(expert_kernel, first, split, depth, far_first, extra),
        grid_spec=pltpu.PrefetchScalarGridSpec(
            num_scalar_prefetch=2,
            grid=(count, most),
            in_specs=in_specs,
            out_specs=out_specs,
            scratch_shapes=[
                pltpu.VMEM((width, 2 * hidden), jnp.float32),
                pltpu.VMEM((width, hidden), jnp.float32),
            ],
        ),
        out_shape=out_shape,
        input_output_aliases=aliases,
        compiler_params=pltpu.CompilerParams(vmem_limit_bytes=VMEM_LIMIT),
        cost_estimate=cost(COST * count * 21.0),
    )(blocks, misc, *operands)


def combine_kernel(
    first, owner_ref, piece_ref, source_ref, groups_ref, begin_ref, place_ref, yd_ref, gg_ref, *rest
):
    y_out, dx_out, gate_out, yd_buf, gg_buf, total, sems = rest[-7:]
    columns = y_out.shape[1]
    step = pl.program_id(0)
    tile = first + step

    def copies(which_tile, group, slot):
        made = []
        for i in range(GROUP):
            source = pl.multiple_of(
                source_ref[which_tile, group * GROUP + i] * PIECE_ROWS, PIECE_ROWS
            )
            for kind, (ref, buf) in enumerate(((yd_ref, yd_buf), (gg_ref, gg_buf))):
                made.append(
                    pltpu.make_async_copy(
                        ref.at[pl.ds(source, PIECE_ROWS)],
                        buf.at[slot, pl.ds(i * PIECE_ROWS, PIECE_ROWS)],
                        sems.at[slot, kind, i],
                    )
                )
        return made

    @pl.when(step == 0)
    def _():
        for copy in copies(tile, 0, begin_ref[tile] % 2):
            copy.start()

    total[...] = jnp.zeros_like(total)
    gate_out[...] = jnp.zeros_like(gate_out)

    def one(group, carry):
        slot = (begin_ref[tile] + group) % 2
        last = group + 1 == groups_ref[tile]
        next_tile = jnp.where(last, tile + 1, tile)
        next_group = jnp.where(last, 0, group + 1)

        @pl.when(jnp.logical_not(last & (step == pl.num_programs(0) - 1)))
        def _():
            for copy in copies(next_tile, next_group, 1 - slot):
                copy.start()

        for copy in copies(tile, group, slot):
            copy.wait()
        picks = []
        for i in range(GROUP):
            entry = group * GROUP + i
            expert = owner_ref[tile, entry]
            rows = (
                lax.broadcasted_iota(jnp.int32, (PIECE_ROWS, BLOCK), 0)
                + piece_ref[tile, entry] * PIECE_ROWS
            )
            pick = jnp.where(rows == place_ref[expert, step], 1.0, 0.0)
            picks.append(pick.astype(jnp.bfloat16))
            grads = gg_buf[slot, pl.ds(i * PIECE_ROWS, PIECE_ROWS), :]
            grads = jnp.concatenate([grads] * (BLOCK // 128), axis=1)
            gate_out[expert, 0] += jnp.sum(pick * grads, axis=0, keepdims=True)
        picked = jnp.concatenate(picks, axis=0)
        total[...] += dot_tn(picked, yd_buf[slot])
        return carry

    lax.fori_loop(0, groups_ref[tile], one, 0)
    y_out[...] = total[:, :columns].astype(y_out.dtype)
    dx_out[...] = total[:, columns:].astype(dx_out.dtype)


def combine_rows(tables, place, yd, gg, first, count, after=()):
    owner, piece, source, groups, width = tables
    begin = jnp.cumsum(groups) - groups
    experts = place.shape[0]
    columns = yd.shape[1] // 2
    return pl.pallas_call(
        functools.partial(combine_kernel, first),
        grid_spec=pltpu.PrefetchScalarGridSpec(
            num_scalar_prefetch=5,
            grid=(count,),
            in_specs=[pl.BlockSpec((experts, count, 1, BLOCK), lambda *_: (0, first // count, 0, 0))]
            + [pl.BlockSpec(memory_space=pl.ANY)] * (2 + len(after)),
            out_specs=[
                pl.BlockSpec((BLOCK, columns), lambda t, *_: (t, 0)),
                pl.BlockSpec((BLOCK, columns), lambda t, *_: (t, 0)),
                pl.BlockSpec((experts, 1, 1, BLOCK), lambda t, *_: (0, t, 0, 0)),
            ],
            scratch_shapes=[
                pltpu.VMEM((2, BLOCK, 2 * columns), jnp.bfloat16),
                pltpu.VMEM((2, BLOCK, 128), jnp.float32),
                pltpu.VMEM((BLOCK, 2 * columns), jnp.float32),
                pltpu.SemaphoreType.DMA((2, 2, GROUP)),
            ],
        ),
        out_shape=[
            jax.ShapeDtypeStruct((count * BLOCK, columns), jnp.bfloat16),
            jax.ShapeDtypeStruct((count * BLOCK, columns), jnp.bfloat16),
            jax.ShapeDtypeStruct((experts, count, 1, BLOCK), jnp.float32),
        ],
        compiler_params=pltpu.CompilerParams(vmem_limit_bytes=VMEM_LIMIT),
        cost_estimate=cost(COST * 45.0),
    )(owner, piece, source, groups, begin, place, yd, gg, *after)


def flip(value, bit):
    size = lax.axis_size("dp")
    return lax.ppermute(value, "dp", [(i, i ^ bit) for i in range(size)])


def swap(value):
    return lax.ppermute(value, "tensor", [(0, 1), (1, 0)])


def order(value, *after):
    return lax.optimization_barrier((value, *after))[0] if after else value


def add_low(left, right):
    return (left.astype(jnp.float32) + right.astype(jnp.float32)).astype(jnp.bfloat16)


def pick_index(value, index, axis):
    return lax.dynamic_index_in_dim(value, index, axis, keepdims=False)


def sum_stage(parts, bit, axis, chosen, after):
    send, keep = parts
    got = order(flip(send, bit), *after)
    return (
        add_low(pick_index(keep, 1 - chosen, axis), pick_index(got, 1 - chosen, axis)),
        add_low(pick_index(keep, chosen, axis), pick_index(got, chosen, axis)),
    )


class ChipSum:
    def __init__(self, parts, rank, far_first):
        side, low_bit, high_bit = (rank // 2) % 2, (rank // 4) % 2, rank // 8
        self.parts = parts
        self.first = (4, 2, high_bit) if far_first else (2, 3, low_bit)
        self.second = (8, 2, side) if far_first else (4, 2, high_bit)
        self.last = 2 if far_first else 8

    def one(self, *after):
        self.parts = sum_stage(self.parts, *self.first, after)
        return self.parts[0]

    def two(self, *after):
        self.parts = sum_stage(self.parts, *self.second, after)
        return self.parts[0]

    def three(self, *after):
        send, keep = self.parts
        return add_low(keep, order(flip(send, self.last), *after))


def sum_heads(own, other, rank, marks=((), (), ())):
    core, side = rank % 2, (rank // 2) % 2
    low_bit, high_bit = (rank // 4) % 2, rank // 8
    rows, columns = own.shape
    part = rows // 16
    view = (8, 2, part, columns)
    parts = []
    for value in (other, own):
        value = value.reshape(view)
        got = order(flip(pick_index(value, 1 - core, 1).astype(jnp.bfloat16), 1), *marks[0])
        parts.append(add_low(pick_index(value, core, 1), got))
    held = parts[0]
    total = add_low(parts[1], order(swap(parts[0]), *marks[1])).reshape(4, 2, part, columns)
    got = order(flip(pick_index(total, 1 - side, 1), 2), *marks[2])
    total = add_low(pick_index(total, side, 1), got).reshape(2, 2, part, columns)
    got = flip(pick_index(total, 1 - low_bit, 1), 4)
    total = add_low(pick_index(total, low_bit, 1), got)
    got = flip(pick_index(total, 1 - high_bit, 0), 8)
    return pick_index(total, high_bit, 0).astype(jnp.float32) + got.astype(jnp.float32), held


def fetch_other(weights, core, side):
    rows = weights.shape[0] // 4
    pieces = swap(lax.dynamic_slice_in_dim(weights, (side * 2 + core) * rows, rows, 0))
    turned = flip(pieces, 2)
    result = jnp.zeros_like(weights)
    first = pieces
    for value, place in (
        (pieces, side * 2 + core),
        (turned, (1 - side) * 2 + core),
        (flip(pieces, 1), side * 2 + 1 - core),
        (flip(turned, 1), (1 - side) * 2 + 1 - core),
    ):
        result = lax.dynamic_update_slice_in_dim(result, value, place * rows, 0)
    return result, first


ROWS = 256
HALF = 512


def lane_swap(values):
    width = values.shape[1]
    lane = lax.broadcasted_iota(jnp.int32, values.shape, 1) % HD
    ahead = pltpu.roll(values, width - HD // 2, 1)
    behind = pltpu.roll(values, HD // 2, 1)
    return jnp.where(lane < HD // 2, ahead, behind)


def turn_tables(rows):
    cosine, sine = rope_tables(rows, HD)
    return (
        jnp.concatenate([cosine] * 4, axis=1),
        jnp.concatenate([-sine, sine, -sine, sine], axis=1),
    )


def project_kernel(sizes, score_scale, normed_ref, weights_ref, cosine_ref, sine_ref, *outs):
    query_ref, key_ref, value_ref = outs
    query_width, key_width = sizes
    projected = jnp.dot(normed_ref[...], weights_ref[...], preferred_element_type=jnp.float32)
    cosine, sine = cosine_ref[...], sine_ref[...]
    for start in range(0, query_width + key_width, 128):
        piece = projected[:, start : start + 128]
        turned = piece * cosine + lane_swap(piece) * sine
        if start < query_width:
            query_ref[:, start : start + 128] = (turned * score_scale).astype(jnp.bfloat16)
        else:
            begin = start - query_width
            key_ref[:, begin : begin + 128] = turned.astype(jnp.bfloat16)
    value_ref[...] = projected[:, query_width + key_width :].astype(jnp.bfloat16)


def project(normed, weights, tables, query_width, key_width, score_scale):
    rows, depth = normed.shape
    width = weights.shape[1]
    row_spec = lambda columns: pl.BlockSpec((ROWS, columns), lambda i: (i, 0))
    return pl.pallas_call(
        functools.partial(project_kernel, (query_width, key_width), score_scale),
        grid=(rows // ROWS,),
        in_specs=[
            row_spec(depth),
            pl.BlockSpec((depth, width), lambda i: (0, 0)),
            row_spec(128),
            row_spec(128),
        ],
        out_specs=[row_spec(query_width), row_spec(key_width), row_spec(key_width)],
        out_shape=[
            jax.ShapeDtypeStruct((rows, query_width), jnp.bfloat16),
            jax.ShapeDtypeStruct((rows, key_width), jnp.bfloat16),
            jax.ShapeDtypeStruct((rows, key_width), jnp.bfloat16),
        ],
        compiler_params=pltpu.CompilerParams(vmem_limit_bytes=VMEM_LIMIT),
        cost_estimate=cost(COST * 9.0),
    )(normed, weights, *tables)


def attend_kernel(per_pair, query_ref, key_ref, value_ref, limit_ref, out_ref, lse_ref):
    step = pl.program_id(1)

    def work(keys):
        columns = lax.broadcasted_iota(jnp.int32, (ROWS, HALF), 1) + (keys - HALF)
        allowed = columns <= limit_ref[...]
        lanes = lax.broadcasted_iota(jnp.int32, (ROWS, 128), 1)
        sums = jnp.zeros((ROWS, 128), jnp.float32)
        pieces = []
        for head in range(per_pair):
            group = head // (per_pair // 2)
            query = query_ref[:, head * HD : (head + 1) * HD]
            key = key_ref[:keys, group * HD : (group + 1) * HD]
            value = value_ref[:keys, group * HD : (group + 1) * HD]
            scores = dot_nt(query, key)
            last = jnp.where(allowed, scores[:, keys - HALF :], -1e30)
            scores = last if keys == HALF else jnp.concatenate([scores[:, : keys - HALF], last], 1)
            highest = jnp.max(scores, axis=1, keepdims=True)
            shifted = jnp.exp(scores - highest)
            total = jnp.sum(shifted, axis=1, keepdims=True)
            mixed = jnp.dot(
                shifted.astype(jnp.bfloat16), value, preferred_element_type=jnp.float32
            )
            pieces.append((mixed / total).astype(jnp.bfloat16))
            sums = jnp.where(lanes == head, highest + jnp.log(total), sums)
        out_ref[...] = jnp.concatenate(pieces, axis=1)
        lse_ref[0] = sums

    halfway = pl.num_programs(1) // 2

    @pl.when(step < halfway)
    def _():
        work(HALF)

    @pl.when(step >= halfway)
    def _():
        work(2 * HALF)


def attend(query, key, value, limits):
    rows, query_width = query.shape
    pairs = key.shape[1] // 128
    wide = query_width // pairs
    return pl.pallas_call(
        functools.partial(attend_kernel, wide // HD),
        grid=(pairs, rows // ROWS),
        in_specs=[
            pl.BlockSpec((ROWS, wide), lambda p, i: (i, p)),
            pl.BlockSpec((rows, 128), lambda p, i: (0, p)),
            pl.BlockSpec((rows, 128), lambda p, i: (0, p)),
            pl.BlockSpec((ROWS, 1), lambda p, i: (i, 0)),
        ],
        out_specs=[
            pl.BlockSpec((ROWS, wide), lambda p, i: (i, p)),
            pl.BlockSpec((1, ROWS, 128), lambda p, i: (p, i, 0)),
        ],
        out_shape=[
            jax.ShapeDtypeStruct((rows, query_width), jnp.bfloat16),
            jax.ShapeDtypeStruct((pairs, rows, 128), jnp.float32),
        ],
        compiler_params=pltpu.CompilerParams(vmem_limit_bytes=VMEM_LIMIT),
        cost_estimate=cost(COST * 24.0),
    )(query, key, value, limits)


def back_kernel(
    per_pair, score_scale, after, query_ref, key_ref, value_ref, turned_key_ref, grad_ref, lse_ref,
    limit_ref, cosine_ref, sine_ref, all_cosine_ref, all_sine_ref, *rest
):
    query_out, key_out, value_out, key_total, value_total = rest[after:]
    step = pl.program_id(1)
    halfway = pl.num_programs(1) // 2

    @pl.when(step == 0)
    def _():
        key_total[...] = jnp.zeros_like(key_total)
        value_total[...] = jnp.zeros_like(value_total)

    def work(keys):
        rows = lax.broadcasted_iota(jnp.int32, (HALF, ROWS), 0) + (keys - HALF)
        allowed = rows <= limit_ref[...]
        made = []
        key_parts, value_parts = [], []
        for group in range(2):
            span = slice(group * HD, (group + 1) * HD)
            key, value = key_ref[:keys, span], value_ref[:keys, span]
            key_part = value_part = 0.0
            for head in range(group * per_pair // 2, (group + 1) * per_pair // 2):
                query = query_ref[:, head * HD : (head + 1) * HD]
                grad = grad_ref[:, head * HD : (head + 1) * HD]
                scores = dot_nt(key, query)
                last = jnp.where(allowed, scores[keys - HALF :], -1e30)
                scores = (
                    last
                    if keys == HALF
                    else jnp.concatenate([scores[: keys - HALF], last], axis=0)
                )
                weights = jnp.exp(scores - lse_ref[0, head : head + 1, :])
                pulled = dot_nt(value, grad)
                inner = jnp.sum(weights * pulled, axis=0, keepdims=True)
                score_low = (weights * (pulled - inner)).astype(jnp.bfloat16)
                value_part += jnp.dot(
                    weights.astype(jnp.bfloat16), grad, preferred_element_type=jnp.float32
                )
                key_part += jnp.dot(score_low, query, preferred_element_type=jnp.float32)
                made.append(
                    jnp.dot(
                        turned_key_ref[0, span, :keys],
                        score_low,
                        preferred_element_type=jnp.float32,
                    )
                )
            key_parts.append(key_part)
            value_parts.append(value_part)
        key_total[:keys] += jnp.concatenate(key_parts, axis=1)
        value_total[:keys] += jnp.concatenate(value_parts, axis=1)
        cosine, sine = cosine_ref[...], sine_ref[...]
        for index in range(per_pair // 2):
            both = jnp.concatenate(made[2 * index : 2 * index + 2], axis=0).T * score_scale
            query_out[:, index * 128 : (index + 1) * 128] = (
                both * cosine - lane_swap(both) * sine
            ).astype(jnp.bfloat16)

    @pl.when(step < halfway)
    def _():
        work(HALF)

    @pl.when(step >= halfway)
    def _():
        work(2 * HALF)

    @pl.when(step == pl.num_programs(1) - 1)
    def _():
        total = key_total[...]
        key_out[...] = (
            total * all_cosine_ref[...] - lane_swap(total) * all_sine_ref[...]
        ).astype(jnp.bfloat16)
        value_out[...] = value_total[...].astype(jnp.bfloat16)


def attend_back(saved, attended_grad, limits, tables, score_scale, after=()):
    query, key, value, lse = saved
    rows, query_width = query.shape
    pairs = key.shape[1] // 128
    wide = query_width // pairs
    turned_key = key.T.reshape(pairs, 128, rows)
    lse_rows = lse[:, :, :8].transpose(0, 2, 1)
    cosine, sine = tables
    block = lambda columns: pl.BlockSpec((ROWS, columns), lambda p, i: (i, p))
    whole = pl.BlockSpec((rows, 128), lambda p, i: (0, p))
    table = pl.BlockSpec((ROWS, 128), lambda p, i: (i, 0))
    full_table = pl.BlockSpec((rows, 128), lambda p, i: (0, 0))
    return pl.pallas_call(
        functools.partial(back_kernel, wide // HD, score_scale, len(after)),
        grid=(pairs, rows // ROWS),
        in_specs=[
            block(wide),
            whole,
            whole,
            pl.BlockSpec((1, 128, rows), lambda p, i: (p, 0, 0)),
            block(wide),
            pl.BlockSpec((1, 8, ROWS), lambda p, i: (p, 0, i)),
            pl.BlockSpec((1, ROWS), lambda p, i: (0, i)),
            table,
            table,
            full_table,
            full_table,
        ]
        + [pl.BlockSpec(memory_space=pl.ANY)] * len(after),
        out_specs=[block(wide), whole, whole],
        out_shape=[
            jax.ShapeDtypeStruct((rows, query_width), jnp.bfloat16),
            jax.ShapeDtypeStruct((rows, key.shape[1]), jnp.bfloat16),
            jax.ShapeDtypeStruct((rows, key.shape[1]), jnp.bfloat16),
        ],
        scratch_shapes=[
            pltpu.VMEM((rows, 128), jnp.float32),
            pltpu.VMEM((rows, 128), jnp.float32),
        ],
        compiler_params=pltpu.CompilerParams(vmem_limit_bytes=VMEM_LIMIT),
        cost_estimate=cost(COST * 40.0),
    )(
        query, key, value, turned_key, attended_grad, lse_rows, limits.T, cosine, sine, cosine,
        sine, *after,
    )


def piece_limits(starts_row, rows):
    position = jnp.arange(rows, dtype=jnp.int32)
    limits = position
    for index in range(starts_row.shape[0]):
        start = starts_row[index]
        inside = (position >= start) & (position < start + PIECE)
        limits = jnp.where(inside, start + PIECE - 1, limits)
    return limits[:, None]


def slot_table(routes, expert_count, capacity):
    flattened = routes.reshape(-1)
    onehot = (flattened[:, None] == jnp.arange(expert_count, dtype=jnp.int32)[None, :]).astype(
        jnp.int32
    )
    placed = jnp.sum((jnp.cumsum(onehot, axis=0) - 1) * onehot, axis=1)
    entries = jnp.arange(flattened.shape[0], dtype=jnp.int32)
    return (
        jnp.full((expert_count * capacity,), flattened.shape[0], jnp.int32)
        .at[flattened * capacity + placed]
        .set(entries)
    )


def expert_forward(expert_inputs, w_gate, w_up, w_down):
    gate_proj = jnp.einsum(
        "ecd,edf->ecf", expert_inputs, w_gate, preferred_element_type=jnp.float32
    )
    up_proj = jnp.einsum("ecd,edf->ecf", expert_inputs, w_up, preferred_element_type=jnp.float32)
    activated = (gate_proj * jax.nn.sigmoid(gate_proj) * up_proj).astype(jnp.bfloat16)
    returned = jnp.einsum("ecf,efd->ecd", activated, w_down, preferred_element_type=jnp.float32)
    return (gate_proj, up_proj, activated, returned)


def shards_wide(
    tokens,
    norm_gains,
    w_query,
    w_key,
    w_value,
    w_out,
    mix_gains,
    w_router,
    w_gate,
    w_up,
    w_down,
    routes,
    starts,
    cotangent,
):
    share_rows = tokens.shape[0]
    model_width = tokens.shape[1]
    head_width = HD
    query_width = w_query.shape[1]
    key_width = w_key.shape[1]
    heads_here = query_width // head_width
    groups_here = key_width // head_width
    per_group = heads_here // groups_here
    experts_here = w_gate.shape[0]
    group_rows = routes.shape[0]
    choices_count = routes.shape[1]
    sequences_here = starts.shape[0]
    sequence_length = group_rows // sequences_here
    expert_count = w_router.shape[1]
    tensor_rank = lax.axis_index("tensor")
    total_tokens = group_rows * lax.axis_size("dp")
    score_scale = head_width ** (-0.5)
    inputs_share = tokens.astype(jnp.float32)
    normed_share = normalize(inputs_share, norm_gains).astype(jnp.bfloat16)
    normed = lax.all_gather(normed_share, "tensor", axis=0, tiled=True)
    joined_weights = jnp.concatenate([w_query, w_key, w_value], axis=1)
    projected = jnp.dot(normed, joined_weights, preferred_element_type=jnp.float32)
    cosine, sine_table = rope_tables(sequence_length, head_width)
    cosine_rows = jnp.tile(cosine, (sequences_here, 1))
    sine_rows = jnp.tile(sine_table, (sequences_here, 1))
    query_rows = rotate(
        projected[:, :query_width].reshape(group_rows, heads_here, head_width),
        cosine_rows,
        sine_rows,
    ).astype(jnp.bfloat16)
    key_rows = rotate(
        projected[:, query_width : query_width + key_width].reshape(
            group_rows, groups_here, head_width
        ),
        cosine_rows,
        sine_rows,
    ).astype(jnp.bfloat16)
    value_rows = (
        projected[:, query_width + key_width :]
        .astype(jnp.bfloat16)
        .reshape(group_rows, groups_here, head_width)
    )
    attended_parts = []
    logsum_parts = []
    for sequence in range(sequences_here):
        first_row = sequence * sequence_length
        query_block = query_rows[first_row : first_row + sequence_length].reshape(
            sequence_length, groups_here, per_group, head_width
        )
        key_block = key_rows[first_row : first_row + sequence_length]
        value_block = value_rows[first_row : first_row + sequence_length]
        allowed = allowed_pairs(starts[sequence], sequence_length, PIECE)
        scores = scores_of(query_block, key_block, allowed, score_scale)
        highest = jnp.max(scores, axis=-1, keepdims=True)
        shifted = jnp.exp(scores - highest)
        totals = jnp.sum(shifted, axis=-1, keepdims=True)
        weights = (shifted / totals).astype(jnp.bfloat16)
        mixed_values = jnp.einsum(
            "kgqs,skd->qkgd", weights, value_block, preferred_element_type=jnp.float32
        )
        attended_parts.append(
            mixed_values.reshape(sequence_length, query_width).astype(jnp.bfloat16)
        )
        logsum_parts.append(highest + jnp.log(totals))
    attended = jnp.concatenate(attended_parts, axis=0)
    attention_share = lax.psum_scatter(
        jnp.dot(attended, w_out, preferred_element_type=jnp.float32),
        "tensor",
        scatter_dimension=0,
        tiled=True,
    )
    middle_share = inputs_share + attention_share
    mixed_share = normalize(middle_share, mix_gains).astype(jnp.bfloat16)
    share_routes = lax.dynamic_slice_in_dim(routes, tensor_rank * share_rows, share_rows, 0)
    route_onehot = (
        share_routes[:, :, None] == jnp.arange(expert_count, dtype=jnp.int32)[None, None, :]
    ).astype(jnp.float32)
    logits = jnp.dot(mixed_share, w_router, preferred_element_type=jnp.float32)
    probabilities = softmax_rows(logits)
    chosen = jnp.sum(logits[:, None, :] * route_onehot, axis=-1)
    gate_soft = softmax_rows(chosen)
    gate_low = gate_soft.astype(jnp.bfloat16)
    counts, prob_sums = lax.psum(
        (jnp.sum(route_onehot, axis=(0, 1)), jnp.sum(probabilities, axis=0)), ("dp", "tensor")
    )
    fractions = counts / (total_tokens * choices_count)
    balance = expert_count * expert_count * fractions * prob_sums / total_tokens
    mixed_rows, gate_rows = (
        lax.all_gather(mixed_share, "tensor", axis=0, tiled=True),
        lax.all_gather(gate_low, "tensor", axis=0, tiled=True),
    )
    slots_all = slot_table(routes, expert_count, CAP)
    slots = lax.dynamic_slice_in_dim(
        slots_all, tensor_rank * experts_here * CAP, experts_here * CAP, 0
    )
    owners = slots // choices_count
    padded_rows = jnp.concatenate([mixed_rows, jnp.zeros((1, model_width), jnp.bfloat16)], axis=0)
    padded_gates = jnp.concatenate(
        [gate_rows.reshape(-1).astype(jnp.float32), jnp.zeros((1,), jnp.float32)], axis=0
    )
    slot_gates = padded_gates[slots]
    expert_inputs = padded_rows[owners].reshape(experts_here, CAP, model_width)
    gate_proj, up_proj, activated, returned = expert_forward(expert_inputs, w_gate, w_up, w_down)
    returned_flat = returned.reshape(experts_here * CAP, model_width)
    expert_partial = jax.ops.segment_sum(
        slot_gates[:, None] * returned_flat, owners, num_segments=group_rows + 1
    )[:group_rows]
    expert_share = lax.psum_scatter(
        expert_partial.astype(jnp.bfloat16), "tensor", scatter_dimension=0, tiled=True
    ).astype(jnp.float32)
    output_share = (middle_share + expert_share).astype(jnp.bfloat16)
    upstream = cotangent.astype(jnp.float32)
    upstream_rows = lax.all_gather(cotangent, "tensor", axis=0, tiled=True)
    padded_upstream = jnp.concatenate(
        [upstream_rows, jnp.zeros((1, model_width), jnp.bfloat16)], axis=0
    )
    slot_upstream = padded_upstream[owners].astype(jnp.float32)
    slot_cotangent = (
        (slot_gates[:, None] * slot_upstream)
        .astype(jnp.bfloat16)
        .reshape(experts_here, CAP, model_width)
    )
    slot_gate_grad = jnp.sum(slot_upstream * returned_flat, axis=1)
    activated_grad = jnp.einsum(
        "ecd,efd->ecf", slot_cotangent, w_down, preferred_element_type=jnp.float32
    )
    down_grad = jnp.einsum(
        "ecf,ecd->efd", activated, slot_cotangent, preferred_element_type=jnp.float32
    )
    sigmoid_gate = jax.nn.sigmoid(gate_proj)
    gate_proj_low = (
        activated_grad * up_proj * sigmoid_gate * (1.0 + gate_proj * (1.0 - sigmoid_gate))
    ).astype(jnp.bfloat16)
    up_proj_low = (activated_grad * gate_proj * sigmoid_gate).astype(jnp.bfloat16)
    inputs_grad = jnp.einsum(
        "ecf,edf->ecd", gate_proj_low, w_gate, preferred_element_type=jnp.float32
    ) + jnp.einsum("ecf,edf->ecd", up_proj_low, w_up, preferred_element_type=jnp.float32)
    gate_grad = jnp.einsum(
        "ecd,ecf->edf", expert_inputs, gate_proj_low, preferred_element_type=jnp.float32
    )
    up_grad = jnp.einsum(
        "ecd,ecf->edf", expert_inputs, up_proj_low, preferred_element_type=jnp.float32
    )
    mixed_partial = jax.ops.segment_sum(
        inputs_grad.reshape(experts_here * CAP, model_width), owners, num_segments=group_rows + 1
    )[:group_rows]
    gate_partial = jax.ops.segment_sum(
        slot_gate_grad, slots, num_segments=group_rows * choices_count + 1
    )[: group_rows * choices_count].reshape(group_rows, choices_count)
    mixed_grad_share, gates_grad_share = (
        lax.psum_scatter(mixed_partial, "tensor", scatter_dimension=0, tiled=True),
        lax.psum_scatter(gate_partial, "tensor", scatter_dimension=0, tiled=True),
    )
    gate_total, up_total = (
        lax.psum_scatter(
            gate_grad.astype(jnp.bfloat16), "dp", scatter_dimension=1, tiled=True
        ).astype(jnp.float32),
        lax.psum_scatter(
            up_grad.astype(jnp.bfloat16), "dp", scatter_dimension=1, tiled=True
        ).astype(jnp.float32),
    )
    down_total = lax.psum_scatter(
        down_grad.astype(jnp.bfloat16), "dp", scatter_dimension=2, tiled=True
    ).astype(jnp.float32)
    chosen_grad = gate_soft * (
        gates_grad_share - jnp.sum(gate_soft * gates_grad_share, axis=-1, keepdims=True)
    )
    logit_grad = jnp.sum(chosen_grad[:, :, None] * route_onehot, axis=1)
    prob_target = ALPHA * expert_count * fractions / total_tokens
    logit_grad = logit_grad + probabilities * (
        prob_target[None, :] - jnp.sum(probabilities * prob_target[None, :], axis=-1, keepdims=True)
    )
    mixed_float = mixed_share.astype(jnp.float32)
    router_grad = jnp.dot(
        mixed_float.T, logit_grad, precision=HIGHEST, preferred_element_type=jnp.float32
    )
    mixed_grad_share = mixed_grad_share + jnp.dot(
        logit_grad,
        w_router.astype(jnp.float32).T,
        precision=HIGHEST,
        preferred_element_type=jnp.float32,
    )
    mix_pullback = jax.vjp(normalize, middle_share, mix_gains)[1]
    middle_from_norm, mix_gain_grad = mix_pullback(mixed_grad_share)
    middle_grad = upstream + middle_from_norm
    middle_low = middle_grad.astype(jnp.bfloat16)
    middle_rows = lax.all_gather(middle_low, "tensor", axis=0, tiled=True)
    out_grad = contract_rows(attended, middle_rows)
    attended_grad = contract_cols(middle_rows, w_out).astype(jnp.bfloat16)
    query_parts = []
    key_parts = []
    value_parts = []
    for sequence in range(sequences_here):
        first_row = sequence * sequence_length
        query_block = query_rows[first_row : first_row + sequence_length].reshape(
            sequence_length, groups_here, per_group, head_width
        )
        key_block = key_rows[first_row : first_row + sequence_length]
        value_block = value_rows[first_row : first_row + sequence_length]
        allowed = allowed_pairs(starts[sequence], sequence_length, PIECE)
        scores = scores_of(query_block, key_block, allowed, score_scale)
        weights_full = jnp.exp(scores - logsum_parts[sequence])
        weights_low = weights_full.astype(jnp.bfloat16)
        grad_block = attended_grad[first_row : first_row + sequence_length].reshape(
            sequence_length, groups_here, per_group, head_width
        )
        value_parts.append(
            jnp.einsum(
                "kgqs,qkgd->skd", weights_low, grad_block, preferred_element_type=jnp.float32
            )
        )
        weight_grad = jnp.einsum(
            "qkgd,skd->kgqs", grad_block, value_block, preferred_element_type=jnp.float32
        )
        score_low = (
            weights_full
            * (weight_grad - jnp.sum(weights_full * weight_grad, axis=-1, keepdims=True))
        ).astype(jnp.bfloat16)
        query_parts.append(
            jnp.einsum("kgqs,skd->qkgd", score_low, key_block, preferred_element_type=jnp.float32)
            * score_scale
        )
        key_parts.append(
            jnp.einsum("kgqs,qkgd->skd", score_low, query_block, preferred_element_type=jnp.float32)
            * score_scale
        )
    query_grads = (
        rotate(
            jnp.concatenate(query_parts, axis=0).reshape(group_rows, heads_here, head_width),
            cosine_rows,
            -sine_rows,
        )
        .astype(jnp.bfloat16)
        .reshape(group_rows, query_width)
    )
    key_grads = (
        rotate(jnp.concatenate(key_parts, axis=0), cosine_rows, -sine_rows)
        .astype(jnp.bfloat16)
        .reshape(group_rows, key_width)
    )
    value_grads = (
        jnp.concatenate(value_parts, axis=0).astype(jnp.bfloat16).reshape(group_rows, key_width)
    )
    joined_grads = jnp.concatenate([query_grads, key_grads, value_grads], axis=1)
    joined_weight_grad = contract_rows(normed, joined_grads)
    normed_grad_share = lax.psum_scatter(
        contract_cols(joined_grads, joined_weights).astype(jnp.bfloat16),
        "tensor",
        scatter_dimension=0,
        tiled=True,
    ).astype(jnp.float32)
    input_pullback = jax.vjp(normalize, inputs_share, norm_gains)[1]
    input_from_norm, norm_gain_grad = input_pullback(normed_grad_share)
    input_grad_share = middle_grad + input_from_norm
    query_total, key_total, value_total, out_turned = (
        lax.psum_scatter(
            joined_weight_grad[:, :query_width].astype(jnp.bfloat16),
            "dp",
            scatter_dimension=0,
            tiled=True,
        ).astype(jnp.float32),
        lax.psum_scatter(
            joined_weight_grad[:, query_width : query_width + key_width].astype(jnp.bfloat16),
            "dp",
            scatter_dimension=0,
            tiled=True,
        ).astype(jnp.float32),
        lax.psum_scatter(
            joined_weight_grad[:, query_width + key_width :].astype(jnp.bfloat16),
            "dp",
            scatter_dimension=0,
            tiled=True,
        ).astype(jnp.float32),
        lax.psum_scatter(
            out_grad.T.astype(jnp.bfloat16), "dp", scatter_dimension=0, tiled=True
        ).astype(jnp.float32),
    )
    out_total = out_turned.T
    norm_gain_total, mix_gain_total, router_total = lax.psum(
        (norm_gain_grad, mix_gain_grad, router_grad), ("dp", "tensor")
    )
    return (
        output_share,
        balance,
        input_grad_share,
        norm_gain_total,
        query_total,
        key_total,
        value_total,
        out_total,
        mix_gain_total,
        router_total,
        gate_total,
        up_total,
        down_total,
    )


def all_sum(value):
    for bit in (1, 2, 4, 8):
        value = value + flip(value, bit)
    return value + swap(value)


def spread(value):
    across = swap(value)
    return [value, across, flip(value, 1), flip(across, 1)]


FIRST_PART = 2
FAR_FIRST = (2, 5)


def shards_pair(
    tokens,
    norm_gains,
    w_query,
    w_key,
    w_value,
    w_out,
    mix_gains,
    w_router,
    w_gate,
    w_up,
    w_down,
    routes,
    starts,
    cotangent,
):
    share_rows, model_width = tokens.shape
    query_width = w_query.shape[1]
    key_width = w_key.shape[1]
    sizes = (query_width, key_width, HD)
    experts_here = w_gate.shape[0]
    experts = experts_here // 2
    choices_count = routes.shape[1]
    expert_count = w_router.shape[1]
    dp_size = lax.axis_size("dp")
    rank = lax.axis_index("dp")
    core, side = rank % 2, (rank // 2) % 2
    tensor_rank = lax.axis_index("tensor")
    total_tokens = routes.shape[0] * dp_size
    score_scale = HD ** (-0.5)
    depth = model_width // dp_size * 2
    slots = round_up(2 * CAP, BLOCK)

    joined_own = jnp.concatenate([w_query, w_key, w_value], axis=1)
    joined_other, joined_piece = fetch_other(joined_own, core, side)
    out_other, out_piece = fetch_other(w_out, core, side)

    own_routes = lax.dynamic_slice_in_dim(routes, tensor_rank * share_rows, share_rows, 0)
    across_routes = lax.dynamic_slice_in_dim(routes, (1 - tensor_rank) * share_rows, share_rows, 0)
    both_routes = jnp.concatenate([own_routes, across_routes], axis=0)
    group_routes = jnp.concatenate([both_routes, flip(both_routes, 1)], axis=0)
    first_expert = tensor_rank * experts_here + core * experts

    route_onehot = (
        own_routes[:, :, None] == jnp.arange(expert_count, dtype=jnp.int32)[None, None, :]
    ).astype(jnp.float32)
    counts = all_sum(jnp.sum(route_onehot, axis=(0, 1)))
    cotangent_rows = spread(order(cotangent, joined_piece, out_piece))

    inputs_share = tokens.astype(jnp.float32)
    normed = normalize(inputs_share, norm_gains).astype(jnp.bfloat16)
    tables = turn_tables(share_rows)
    starts_row = lax.dynamic_index_in_dim(starts, tensor_rank, 0, keepdims=False)
    limits = piece_limits(starts_row, share_rows)

    def half_forward(joined_weights):
        query, key, value = project(
            normed, joined_weights, tables, query_width, key_width, score_scale
        )
        attended, lse = attend(query, key, value, limits)
        return attended, (query, key, value, lse)

    attended_own, saved_own = half_forward(joined_own)
    attended_other, saved_other = half_forward(joined_other)
    middle_share = (
        inputs_share
        + jnp.dot(attended_own, w_out, preferred_element_type=jnp.float32)
        + jnp.dot(attended_other, out_other, preferred_element_type=jnp.float32)
    )
    mixed_share = normalize(middle_share, mix_gains).astype(jnp.bfloat16)

    logits = jnp.dot(mixed_share, w_router, preferred_element_type=jnp.float32)
    probabilities = softmax_rows(logits)
    chosen = jnp.sum(logits[:, None, :] * route_onehot, axis=-1)
    gate_soft = softmax_rows(chosen)
    gate_low = gate_soft.astype(jnp.bfloat16)
    fractions = counts / (total_tokens * choices_count)

    group_gates = jnp.concatenate(spread(gate_low), axis=0)
    place, begins, ends, gates = placement(group_routes, group_gates, first_expert, experts)
    gather_from = gather_tables(begins, ends, slots)
    blocks = gather_from[2]
    cot_slots = gather_rows(gather_from, place, None, cotangent_rows, slots, 0, experts)[0]
    mixed_across = order(swap(mixed_share), cot_slots)
    mixed_rows = [mixed_share, mixed_across, flip(mixed_share, 1), flip(mixed_across, 1)]
    misc = jnp.stack([core * experts, side, (rank // 4) % 2])
    weights = (w_gate, w_up, w_down)
    first_part = gather_rows(
        gather_from, place, gates, mixed_rows, slots, 0, FIRST_PART, (cot_slots, counts)
    )
    later_part = None
    carried = None
    chips = []
    for index in range(experts):
        if index == FIRST_PART:
            later_part = gather_rows(
                gather_from, place, gates, mixed_rows, slots, FIRST_PART, experts - FIRST_PART,
                (carried[1],),
            )
        if later_part is None:
            (x_slots, slot_gates), x_first = first_part, 0
        else:
            (x_slots, slot_gates), x_first = later_part, FIRST_PART
        waits = []
        if index == 2:
            waits = [chips[0].one(slot_gates)]
        elif index == 4:
            waits = [chips[1].one(carried[1]), chips[0].two(carried[1])]
        elif index == 6:
            waits = [chips[2].one(carried[1])]
        elif index == 7:
            waits = [chips[3].one(carried[1]), chips[1].two(carried[1])]
        elif index == 9:
            waits = [chips[4].one(carried[1])]
        far_first = int(index in FAR_FIRST)
        *carried, send, keep = expert_call(
            blocks, misc, x_slots, cot_slots, slot_gates, weights, carried, slots,
            index, 1, x_first, 0, depth, far_first, waits,
        )
        chips.append(ChipSum((send, keep), rank, far_first))
    waits = [chips[5].one(carried[1])] + [chips[i].two(carried[1]) for i in (2, 3)]

    combine_from = combine_tables(begins, ends, slots)
    tiles = place.shape[1] // 4
    turned_routes = group_routes.T
    names = first_expert + jnp.arange(experts, dtype=jnp.int32)

    def combined(start, count, after):
        y, dx, gate_grads = combine_rows(combine_from, place, *carried, start, count, after)
        gate_grads = gate_grads[:experts].reshape(experts, 1, count * BLOCK)
        rows = turned_routes[:, start * BLOCK : (start + count) * BLOCK]
        hit = rows[None, :, :] == names[:, None, None]
        return y, dx, jnp.sum(jnp.where(hit, gate_grads, 0.0), axis=0)

    y_far, dx_far, gg_far = combined(2 * tiles, 2 * tiles, waits)
    waits = [chips[6].one(dx_far), chips[4].two(dx_far)]
    dx_far, y_far, gg_far = flip(dx_far, 1), flip(y_far, 1), flip(gg_far, 1)
    y_cross, dx_cross, gg_cross = combined(tiles, tiles, waits)
    dx_send = add_low(dx_cross, dx_far[share_rows:])
    dx_across = swap(dx_send)
    gg_across = swap(gg_cross + gg_far[:, share_rows:])
    y_near, dx_near, gg_near = combined(0, tiles, [dx_send])
    waits = [chips[7].one(dx_near)] + [chips[i].two(dx_near) for i in (5, 6)]
    waits.append(chips[8].one(dx_near))
    mixed_grad_share = (
        dx_near.astype(jnp.float32)
        + dx_far[:share_rows].astype(jnp.float32)
        + dx_across.astype(jnp.float32)
    )
    gates_grad_share = (gg_near + gg_far[:, :share_rows] + gg_across).T

    upstream = cotangent.astype(jnp.float32)
    chosen_grad = gate_soft * (
        gates_grad_share - jnp.sum(gate_soft * gates_grad_share, axis=-1, keepdims=True)
    )
    logit_grad = jnp.sum(chosen_grad[:, :, None] * route_onehot, axis=1)
    prob_target = ALPHA * expert_count * fractions / total_tokens
    logit_grad = logit_grad + probabilities * (
        prob_target[None, :] - jnp.sum(probabilities * prob_target[None, :], axis=-1, keepdims=True)
    )
    router_grad = jnp.dot(
        mixed_share.astype(jnp.float32).T,
        logit_grad,
        precision=HIGHEST,
        preferred_element_type=jnp.float32,
    )
    mixed_grad_share = mixed_grad_share + jnp.dot(
        logit_grad,
        w_router.astype(jnp.float32).T,
        precision=HIGHEST,
        preferred_element_type=jnp.float32,
    )
    mix_pullback = jax.vjp(normalize, middle_share, mix_gains)[1]
    middle_from_norm, mix_gain_grad = mix_pullback(mixed_grad_share)
    middle_grad = upstream + middle_from_norm
    middle_low = middle_grad.astype(jnp.bfloat16)

    def half_back(saved, out_weights, after):
        attended_grad = dot_nt(middle_low, out_weights).astype(jnp.bfloat16)
        grads = attend_back(saved, attended_grad, limits, tables, score_scale, after)
        return jnp.concatenate(grads, axis=1)

    other_grads = half_back(saved_other, out_other, waits)
    y_across = swap(order(add_low(y_cross, y_far[share_rows:]), other_grads))
    expert_share = (
        y_near.astype(jnp.float32)
        + y_far[:share_rows].astype(jnp.float32)
        + y_across.astype(jnp.float32)
    )
    output_share = (middle_share + expert_share).astype(jnp.bfloat16)
    other_weight_grads = dot_tn(normed, other_grads)
    waits = [chips[9].one(other_grads)] + [chips[i].two(other_grads) for i in (7, 8)]
    out_grads = (
        dot_tn(middle_low, attended_own),
        dot_tn(order(middle_low, other_grads), attended_other),
    )
    own_grads = half_back(saved_own, w_out, waits)
    out_total, _ = sum_heads(*out_grads, rank, ((), (), (own_grads,)))
    own_weight_grads = dot_tn(normed, own_grads)
    joined_total, _ = sum_heads(own_weight_grads, other_weight_grads, rank)
    chips[9].two(own_weight_grads)
    sums = [chip.three(own_weight_grads) for chip in chips]
    other_normed = dot_nt(other_grads, joined_other)
    own_normed = dot_nt(own_grads, joined_own)
    input_pullback = jax.vjp(normalize, inputs_share, norm_gains)[1]
    input_from_norm, norm_gain_grad = input_pullback(other_normed + own_normed)
    input_grad_share = middle_grad + input_from_norm
    key_end = query_width + key_width
    small = all_sum(
        jnp.concatenate(
            [jnp.sum(probabilities, axis=0), mix_gain_grad, norm_gain_grad, router_grad.reshape(-1)]
        )
    )
    prob_sums = small[:expert_count]
    mix_gain_total = small[expert_count : expert_count + model_width]
    norm_gain_total = small[expert_count + model_width : expert_count + 2 * model_width]
    router_total = small[expert_count + 2 * model_width :].reshape(router_grad.shape)
    balance = expert_count * expert_count * fractions * prob_sums / total_tokens

    mine = jnp.concatenate(sums, axis=0).reshape(experts, 3, 2, depth // 2, -1)
    theirs = flip(pick_index(mine, 1 - core, 2), 1)
    mine = pick_index(mine, core, 2)
    expert_total = jnp.where(
        core == 0,
        jnp.concatenate([mine, theirs], axis=0),
        jnp.concatenate([theirs, mine], axis=0),
    ).astype(jnp.float32)
    return (
        output_share,
        balance,
        input_grad_share,
        norm_gain_total,
        joined_total[:, :query_width],
        joined_total[:, query_width:key_end],
        joined_total[:, key_end:],
        out_total.T,
        mix_gain_total,
        router_total,
        expert_total[:, 0],
        expert_total[:, 1],
        expert_total[:, 2].transpose(0, 2, 1),
    )


def solution(mesh):
    sizes = dict(mesh.shape)
    paired = sizes["tensor"] == 2 and sizes["dp"] == 16
    return jax.shard_map(
        shards_pair if paired else shards_wide,
        mesh=mesh,
        in_specs=(
            P(("dp", "tensor"), None),
            P(),
            P(None, "tensor"),
            P(None, "tensor"),
            P(None, "tensor"),
            P("tensor", None),
            P(),
            P(),
            P("tensor", None, None),
            P("tensor", None, None),
            P("tensor", None, None),
            P("dp", None),
            P("dp", None),
            P(("dp", "tensor"), None),
        ),
        out_specs=(
            P(("dp", "tensor"), None),
            P(),
            P(("dp", "tensor"), None),
            P(),
            P("dp", "tensor"),
            P("dp", "tensor"),
            P("dp", "tensor"),
            P("tensor", "dp"),
            P(),
            P(),
            P("tensor", "dp", None),
            P("tensor", "dp", None),
            P("tensor", None, "dp"),
        ),
        check_vma=False,
    )
```

```python
import functools

import jax
import jax.numpy as jnp
from jax import lax
from jax.experimental import pallas as pl
from jax.experimental.pallas import tpu as pltpu
from jax.sharding import PartitionSpec as P

HD = 64
PIECE = 256
CAP = 614


EPSILON = 1e-06
ALPHA = 0.01
HIGHEST = lax.Precision.HIGHEST


def normalize(values, gains):
    return values * lax.rsqrt(jnp.mean(values * values, axis=-1, keepdims=True) + EPSILON) * gains


def softmax_rows(values):
    shifted = jnp.exp(values - jnp.max(values, axis=-1, keepdims=True))
    return shifted / jnp.sum(shifted, axis=-1, keepdims=True)


def contract_rows(left, right):
    return lax.dot_general(
        left, right, (((0,), (0,)), ((), ())), preferred_element_type=jnp.float32
    )


def contract_cols(left, right):
    return lax.dot_general(
        left, right, (((1,), (1,)), ((), ())), preferred_element_type=jnp.float32
    )


def rope_tables(sequence_length, head_width):
    half_width = head_width // 2
    frequency = 10000.0 ** (-(jnp.arange(half_width, dtype=jnp.float32) * 2.0 / head_width))
    angles = jnp.arange(sequence_length, dtype=jnp.float32)[:, None] * frequency[None, :]
    return (jnp.cos(angles), jnp.sin(angles))


def rotate(values, cosine, sine_table):
    half_width = values.shape[-1] // 2
    first_half = values[..., :half_width]
    second_half = values[..., half_width:]
    cosine_rows = cosine[:, None, :]
    sine_rows = sine_table[:, None, :]
    return jnp.concatenate(
        [
            first_half * cosine_rows - second_half * sine_rows,
            second_half * cosine_rows + first_half * sine_rows,
        ],
        axis=-1,
    )


def allowed_pairs(starts_row, sequence_length, piece_length):
    position = jnp.arange(sequence_length, dtype=jnp.int32)
    labels = jnp.full((sequence_length,), -1, jnp.int32)
    for piece_index in range(starts_row.shape[0]):
        inside = (position >= starts_row[piece_index]) & (
            position < starts_row[piece_index] + piece_length
        )
        labels = jnp.where(inside, piece_index, labels)
    causal = position[None, :] <= position[:, None]
    shared = (labels[:, None] == labels[None, :]) & (labels[:, None] >= 0)
    return causal | shared


def scores_of(query_block, key_block, allowed, score_scale):
    raw_scores = (
        jnp.einsum("qkgd,skd->kgqs", query_block, key_block, preferred_element_type=jnp.float32)
        * score_scale
    )
    return jnp.where(allowed, raw_scores, -1e30)


BLOCK = 256
PART = 256
PIECE_ROWS = 32
GROUP = 8
VMEM_LIMIT = 60 * 1024 * 1024


def dot_nt(left, right):
    return lax.dot_general(
        left, right, (((1,), (1,)), ((), ())), preferred_element_type=jnp.float32
    )


def dot_tn(left, right):
    return lax.dot_general(
        left, right, (((0,), (0,)), ((), ())), preferred_element_type=jnp.float32
    )


def round_up(value, multiple):
    return -(-value // multiple) * multiple


def placement(routes_rows, first_expert, experts):
    rows = routes_rows.shape[0]
    tiles = rows // BLOCK
    turned = routes_rows.T
    names = first_expert + jnp.arange(experts, dtype=jnp.int32)
    hit = turned[None, :, :] == names[:, None, None]
    member = jnp.any(hit, axis=1)
    upper = jnp.triu(jnp.ones((BLOCK, BLOCK), jnp.bfloat16))
    inside = jnp.dot(
        member.astype(jnp.bfloat16).reshape(experts * tiles, BLOCK),
        upper,
        preferred_element_type=jnp.float32,
    ).astype(jnp.int32).reshape(experts, tiles, BLOCK)
    sums = inside[:, :, -1]
    ends = jnp.cumsum(sums, axis=1)
    begins = ends - sums
    place = jnp.where(
        member.reshape(experts, tiles, BLOCK), begins[:, :, None] + inside - 1, -1
    )
    place = jnp.concatenate(
        [place, jnp.full((1, tiles, BLOCK), -1, jnp.int32)], axis=0
    ).reshape(experts + 1, tiles, 1, BLOCK)
    return place, begins, ends


def gate_table(routes_rows, gates_rows, first_expert, experts):
    names = first_expert + jnp.arange(experts, dtype=jnp.int32)
    hit = routes_rows.T[None, :, :] == names[:, None, None]
    table = jnp.sum(jnp.where(hit, gates_rows.astype(jnp.float32).T[None, :, :], 0.0), axis=1)
    return jnp.pad(table, ((0, 128 - experts), (0, 0))).T.astype(jnp.bfloat16)


def gather_tables(begins, ends, slots):
    counts = ends[:, -1]
    parts = jnp.arange(slots // PART, dtype=jnp.int32) * PART
    low = jnp.sum((ends[:, None, :] <= parts[None, :, None]).astype(jnp.int32), axis=2)
    high = jnp.sum((begins[:, None, :] < parts[None, :, None] + PART).astype(jnp.int32), axis=2)
    high = jnp.where(parts[None, :] < counts[:, None], high, low)
    blocks = jnp.maximum(-(-counts // BLOCK), 1)
    return low, high, blocks


def combine_tables(begins, ends, slots):
    experts, tiles = begins.shape
    width = round_up(experts * (BLOCK // PIECE_ROWS + 1), GROUP)
    first = begins // PIECE_ROWS
    amount = jnp.where(ends > begins, (ends - 1) // PIECE_ROWS - first + 1, 0)
    stop = jnp.cumsum(amount, axis=0)
    place = jnp.arange(width, dtype=jnp.int32)
    owner = jnp.sum(
        (stop.T[:, None, :] <= place[None, :, None]).astype(jnp.int32), axis=2
    )
    chosen = owner[:, :, None] == jnp.arange(experts, dtype=jnp.int32)[None, None, :]
    offset = jnp.sum(
        jnp.where(chosen, (first - (stop - amount)).T[:, None, :], 0), axis=2
    )
    valid = owner < experts
    piece = jnp.where(valid, offset + place[None, :], 0)
    source = jnp.where(valid, owner, 0) * (slots // PIECE_ROWS) + piece
    groups = jnp.maximum(-(-stop[-1] // GROUP), 1)
    return owner, piece, source, groups, width


def gather_kernel(sources, with_gates, after, low_ref, high_ref, blocks_ref, place_ref, *rest):
    if with_gates:
        gates_ref, rest = rest[0], rest[1:]
    inputs, rest = rest[:sources], rest[sources + after :]
    if with_gates:
        out_ref, gate_out_ref, held, buffer, gate_buffer, sems, out_sems = rest
    else:
        out_ref, held, buffer, sems, out_sems = rest
    expert = pl.program_id(0)
    share = inputs[0].shape[0]
    slots = out_ref.shape[0] // pl.num_programs(0)

    @pl.when(expert == 0)
    def _():
        copies = [
            pltpu.make_async_copy(ref, held.at[pl.ds(i * share, share)], sems.at[i])
            for i, ref in enumerate(inputs)
        ]
        for copy in copies:
            copy.start()
        for copy in copies:
            copy.wait()

    def copies_of(part, slot):
        start = pl.multiple_of(expert * slots + part * PART, PART)
        made = [
            pltpu.make_async_copy(
                buffer.at[slot], out_ref.at[pl.ds(start, PART)], out_sems.at[0, slot]
            )
        ]
        if with_gates:
            made.append(
                pltpu.make_async_copy(
                    gate_buffer.at[slot], gate_out_ref.at[pl.ds(start, PART)], out_sems.at[1, slot]
                )
            )
        return made

    parts = blocks_ref[expert] * (BLOCK // PART)

    def one(part, carry):
        slot = part % 2

        @pl.when(part >= 2)
        def _():
            for copy in copies_of(part - 2, slot):
                copy.wait()

        buffer[slot] = jnp.zeros(buffer.shape[1:], buffer.dtype)
        if with_gates:
            gate_buffer[slot] = jnp.zeros(gate_buffer.shape[1:], gate_buffer.dtype)
        rows = lax.broadcasted_iota(jnp.int32, (PART, BLOCK), 0) + part * PART

        def step(pair, carry):
            pick = jnp.concatenate(
                [
                    jnp.where(rows == place_ref[expert, 2 * pair + i], 1.0, 0.0)
                    for i in range(2)
                ],
                axis=1,
            ).astype(jnp.bfloat16)
            start = pl.multiple_of(pair * 2 * BLOCK, 2 * BLOCK)
            buffer[slot] += jnp.dot(
                pick, held[pl.ds(start, 2 * BLOCK), :], preferred_element_type=jnp.float32
            ).astype(buffer.dtype)
            if with_gates:
                gate_buffer[slot] += jnp.dot(
                    pick, gates_ref[pl.ds(start, 2 * BLOCK), :], preferred_element_type=jnp.float32
                )
            return carry

        lax.fori_loop(
            low_ref[expert, part] // 2, (high_ref[expert, part] + 1) // 2, step, 0
        )
        for copy in copies_of(part, slot):
            copy.start()
        return carry

    lax.fori_loop(0, parts, one, 0)
    for back in (2, 1):
        for copy in copies_of(parts - back, (parts - back) % 2):
            copy.wait()


def gather_rows(tables, place, gates, sources, slots, first, count, after=()):
    low, high, blocks = tables
    low, high, blocks = (t[first : first + count] for t in (low, high, blocks))
    place = place[first : first + count]
    rows = place.shape[1] * BLOCK
    width = sources[0].shape[1]
    with_gates = gates is not None

    def whole(array):
        zeros = (0,) * array.ndim
        return pl.BlockSpec(array.shape, lambda *_: zeros)

    operands = [place] + ([gates] if with_gates else [])
    anywhere = pl.BlockSpec(memory_space=pl.ANY)
    in_specs = [whole(a) for a in operands] + [anywhere] * (len(sources) + len(after))
    out_shape = [jax.ShapeDtypeStruct((count * slots, width), jnp.bfloat16)]
    scratch = [
        pltpu.VMEM((rows, width), jnp.bfloat16),
        pltpu.VMEM((2, PART, width), jnp.bfloat16),
    ]
    if with_gates:
        out_shape.append(jax.ShapeDtypeStruct((count * slots, 128), jnp.float32))
        scratch.append(pltpu.VMEM((2, PART, 128), jnp.float32))
    return pl.pallas_call(
        functools.partial(gather_kernel, len(sources), with_gates, len(after)),
        grid_spec=pltpu.PrefetchScalarGridSpec(
            num_scalar_prefetch=3,
            grid=(count,),
            in_specs=in_specs,
            out_specs=[anywhere] * len(out_shape),
            scratch_shapes=scratch
            + [pltpu.SemaphoreType.DMA((len(sources),)), pltpu.SemaphoreType.DMA((2, 2))],
        ),
        out_shape=out_shape,
        compiler_params=pltpu.CompilerParams(vmem_limit_bytes=VMEM_LIMIT),
    )(low, high, blocks, *operands, *sources, *after)


def expert_kernel(
    first, split, depth, far_first, extra, blocks_ref, misc_ref, x_ref, c_ref, sg_ref, wg_ref,
    wu_ref, wd_ref, *rest
):
    yd_ref = rest[extra]
    rest = rest[extra + 1 :]
    width = x_ref.shape[1]
    if split:
        send_ref, keep_ref = rest[:2]
        rest = rest[2:]
    else:
        grads_ref = rest[0]
        rest = rest[1:]
    total_gu, total_d, x_held, c_held, low_held, gated_held = rest
    expert = first + pl.program_id(0)
    block = pl.program_id(1)
    hidden = wg_ref.shape[2]
    blocks = blocks_ref[expert]
    lanes = lax.broadcasted_iota(jnp.int32, (BLOCK, 128), 1)

    @pl.when(block < blocks)
    def _():
        x = x_ref[...]
        c = c_ref[...]
        gate = jnp.sum(jnp.where(lanes == expert, sg_ref[...], 0.0), axis=1, keepdims=True)
        gate_proj = jnp.dot(x, wg_ref[0], preferred_element_type=jnp.float32)
        up_proj = jnp.dot(x, wu_ref[0], preferred_element_type=jnp.float32)
        pulled = dot_nt(c, wd_ref[0])
        sigmoid = 1.0 / (1.0 + jnp.exp(-gate_proj))
        silu = gate_proj * sigmoid
        activated = (silu * up_proj).astype(jnp.bfloat16).astype(jnp.float32)
        gate_grad = jnp.sum(activated * pulled, axis=1, keepdims=True)
        coarse = gate_grad.astype(jnp.bfloat16).astype(jnp.float32)
        yd_ref[:, 2 * width :] = jnp.where(
            lanes == expert, coarse, jnp.where(lanes == expert + 64, gate_grad - coarse, 0.0)
        ).astype(yd_ref.dtype)
        gated = (gate * activated).astype(jnp.bfloat16)
        yd_ref[:, :width] = jnp.dot(
            gated, wd_ref[0], preferred_element_type=jnp.float32
        ).astype(yd_ref.dtype)
        activated_grad = gate * pulled
        gate_low = (
            activated_grad * up_proj * sigmoid * (1.0 + gate_proj * (1.0 - sigmoid))
        ).astype(jnp.bfloat16)
        up_low = (activated_grad * silu).astype(jnp.bfloat16)
        yd_ref[:, width : 2 * width] = (
            dot_nt(gate_low, wg_ref[0]) + dot_nt(up_low, wu_ref[0])
        ).astype(yd_ref.dtype)
        start = pl.multiple_of((block % 2) * BLOCK, BLOCK)
        held = pl.ds(start, BLOCK)
        x_held[held, :] = x
        c_held[held, :] = c
        low_held[held, :hidden] = gate_low
        low_held[held, hidden:] = up_low
        gated_held[held, :] = gated

    def gather(rows, fresh):
        for begin in range(0, width, BLOCK):
            span = slice(begin, begin + BLOCK)
            for total, left, right in (
                (total_gu, x_held, low_held),
                (total_d, c_held, gated_held),
            ):
                term = dot_tn(left[:rows, span], right[:rows, :])
                total[span, :] = term if fresh else total[span, :] + term

    odd = block % 2 == 1
    last = block == blocks - 1

    @pl.when((block == 0) & last)
    def _():
        gather(BLOCK, True)

    @pl.when((block == 1) & (block < blocks))
    def _():
        gather(2 * BLOCK, True)

    @pl.when((block > 1) & odd & (block < blocks))
    def _():
        gather(2 * BLOCK, False)

    @pl.when((block > 1) & jnp.logical_not(odd) & last)
    def _():
        gather(BLOCK, False)

    @pl.when(block == pl.num_programs(1) - 1)
    def _():
        parts = (
            (total_gu, 0),
            (total_gu, hidden),
            (total_d, 0),
        )
        for which, (ref, column) in enumerate(parts):
            if split:
                side = misc_ref[1 + far_first]
                for high in range(2):
                    for low in range(2):
                        for out, chosen in ((keep_ref, side), (send_ref, 1 - side)):
                            if far_first:
                                start = ((high * 2 + chosen) * 2 + low) * depth
                                place = (high, low, which)
                            else:
                                start = ((high * 2 + low) * 2 + chosen) * depth
                                place = (low, high, which)
                            out[place] = ref[
                                pl.ds(pl.multiple_of(start, 64), depth), pl.ds(column, hidden)
                            ].astype(out.dtype)
            else:
                grads_ref[0, which] = ref[:, pl.ds(column, hidden)].astype(grads_ref.dtype)


def expert_call(
    blocks, misc, x, c, sg, weights, carried, slots, first, count, x_first, c_first, depth,
    far_first=0, after=()
):
    w_gate, w_up, w_down = weights
    experts = blocks.shape[0]
    width = x.shape[1]
    hidden = w_gate.shape[2]
    most = slots // BLOCK
    split = depth is not None

    def rows_index(base):
        def index(expert, block, blocks, misc):
            limit = blocks[first + expert] - 1
            return ((first - base + expert) * most + jnp.minimum(block, limit), 0)

        return index

    def weight_index(expert, block, blocks, misc):
        return (misc[0] + first + expert, 0, 0)

    def grads_index(expert, block, blocks, misc):
        return (0, 0, 0, 0, 0)

    out_shape = [jax.ShapeDtypeStruct((experts * slots, 2 * width + 128), jnp.bfloat16)]
    out_specs = [pl.BlockSpec((BLOCK, 2 * width + 128), rows_index(0))]
    if split:
        out_shape += [jax.ShapeDtypeStruct((2, 2, 3, depth, hidden), jnp.bfloat16)] * 2
        out_specs += [pl.BlockSpec((2, 2, 3, depth, hidden), grads_index)] * 2
    else:
        out_shape += [jax.ShapeDtypeStruct((count, 3, width, hidden), jnp.bfloat16)]
        out_specs += [pl.BlockSpec((1, 3, width, hidden), lambda e, b, *_: (e, 0, 0, 0))]
    operands = [x, c, sg, w_gate, w_up, w_down]
    in_specs = [
        pl.BlockSpec((BLOCK, width), rows_index(x_first)),
        pl.BlockSpec((BLOCK, width), rows_index(c_first)),
        pl.BlockSpec((BLOCK, 128), rows_index(x_first)),
        pl.BlockSpec((1, width, hidden), weight_index),
        pl.BlockSpec((1, width, hidden), weight_index),
        pl.BlockSpec((1, hidden, width), weight_index),
    ]
    aliases = {}
    if carried is not None:
        operands.append(carried)
        aliases = {8: 0}
    operands += list(after)
    extra = len(operands) - 6
    in_specs += [pl.BlockSpec(memory_space=pl.ANY)] * extra
    return pl.pallas_call(
        functools.partial(expert_kernel, first, split, depth, far_first, extra),
        grid_spec=pltpu.PrefetchScalarGridSpec(
            num_scalar_prefetch=2,
            grid=(count, most),
            in_specs=in_specs,
            out_specs=out_specs,
            scratch_shapes=[
                pltpu.VMEM((width, 2 * hidden), jnp.float32),
                pltpu.VMEM((width, hidden), jnp.float32),
                pltpu.VMEM((2 * BLOCK, width), jnp.bfloat16),
                pltpu.VMEM((2 * BLOCK, width), jnp.bfloat16),
                pltpu.VMEM((2 * BLOCK, 2 * hidden), jnp.bfloat16),
                pltpu.VMEM((2 * BLOCK, hidden), jnp.bfloat16),
            ],
        ),
        out_shape=out_shape,
        input_output_aliases=aliases,
        compiler_params=pltpu.CompilerParams(vmem_limit_bytes=VMEM_LIMIT),
    )(blocks, misc, *operands)


def combine_kernel(
    first, owner_ref, piece_ref, source_ref, groups_ref, begin_ref, place_ref, yd_ref, *rest
):
    y_out, dx_out, gate_out, buffer, total, sems = rest[-6:]
    columns = y_out.shape[1]
    step = pl.program_id(0)
    tile = first + step

    def copies(which_tile, group, slot):
        made = []
        for i in range(GROUP):
            source = pl.multiple_of(
                source_ref[which_tile, group * GROUP + i] * PIECE_ROWS, PIECE_ROWS
            )
            made.append(
                pltpu.make_async_copy(
                    yd_ref.at[pl.ds(source, PIECE_ROWS)],
                    buffer.at[slot, pl.ds(i * PIECE_ROWS, PIECE_ROWS)],
                    sems.at[slot, i],
                )
            )
        return made

    @pl.when(step == 0)
    def _():
        for copy in copies(tile, 0, begin_ref[tile] % 2):
            copy.start()

    def one(group, carry):
        slot = (begin_ref[tile] + group) % 2
        last = group + 1 == groups_ref[tile]
        next_tile = jnp.where(last, tile + 1, tile)
        next_group = jnp.where(last, 0, group + 1)

        @pl.when(jnp.logical_not(last & (step == pl.num_programs(0) - 1)))
        def _():
            for copy in copies(next_tile, next_group, 1 - slot):
                copy.start()

        picks = []
        for i in range(GROUP):
            entry = group * GROUP + i
            rows = (
                lax.broadcasted_iota(jnp.int32, (PIECE_ROWS, BLOCK), 0)
                + piece_ref[tile, entry] * PIECE_ROWS
            )
            picks.append(jnp.where(rows == place_ref[owner_ref[tile, entry], step], 1.0, 0.0))
        picked = jnp.concatenate(picks, axis=0).T.astype(jnp.bfloat16)
        for copy in copies(tile, group, slot):
            copy.wait()
        fresh = group == 0
        for begin in range(0, total.shape[1], 640):
            span = slice(begin, begin + 640)
            term = jnp.dot(picked, buffer[slot, :, span], preferred_element_type=jnp.float32)
            total[:, span] = jnp.where(fresh, 0.0, total[:, span]) + term
        return carry

    lax.fori_loop(0, groups_ref[tile], one, 0)
    y_out[...] = total[:, :columns].astype(y_out.dtype)
    dx_out[...] = total[:, columns : 2 * columns].astype(dx_out.dtype)
    gate_out[...] = total[:, 2 * columns :]


def combine_rows(tables, place, yd, first, count, after=()):
    owner, piece, source, groups, width = tables
    begin = jnp.cumsum(groups) - groups
    experts = place.shape[0]
    whole_width = yd.shape[1]
    columns = (whole_width - 128) // 2
    row_block = lambda wide: pl.BlockSpec((BLOCK, wide), lambda t, *_: (t, 0))
    return pl.pallas_call(
        functools.partial(combine_kernel, first),
        grid_spec=pltpu.PrefetchScalarGridSpec(
            num_scalar_prefetch=5,
            grid=(count,),
            in_specs=[pl.BlockSpec((experts, count, 1, BLOCK), lambda *_: (0, first // count, 0, 0))]
            + [pl.BlockSpec(memory_space=pl.ANY)] * (1 + len(after)),
            out_specs=[row_block(columns), row_block(columns), row_block(128)],
            scratch_shapes=[
                pltpu.VMEM((2, GROUP * PIECE_ROWS, whole_width), jnp.bfloat16),
                pltpu.VMEM((BLOCK, whole_width), jnp.float32),
                pltpu.SemaphoreType.DMA((2, GROUP)),
            ],
        ),
        out_shape=[
            jax.ShapeDtypeStruct((count * BLOCK, columns), jnp.bfloat16),
            jax.ShapeDtypeStruct((count * BLOCK, columns), jnp.bfloat16),
            jax.ShapeDtypeStruct((count * BLOCK, 128), jnp.float32),
        ],
        compiler_params=pltpu.CompilerParams(vmem_limit_bytes=VMEM_LIMIT),
    )(owner, piece, source, groups, begin, place, yd, *after)


def flip(value, bit):
    size = lax.axis_size("dp")
    return lax.ppermute(value, "dp", [(i, i ^ bit) for i in range(size)])


def swap(value):
    return lax.ppermute(value, "tensor", [(0, 1), (1, 0)])


def order(value, *after):
    return lax.optimization_barrier((value, *after))[0] if after else value


def add_low(left, right):
    return (left.astype(jnp.float32) + right.astype(jnp.float32)).astype(jnp.bfloat16)


def pick_index(value, index, axis):
    return lax.dynamic_index_in_dim(value, index, axis, keepdims=False)


def sum_stage(parts, bit, chosen, after):
    send, keep = parts
    got = order(flip(send, bit), *after)
    return tuple(
        add_low(pick_index(keep, which, 0), pick_index(got, which, 0))
        for which in (1 - chosen, chosen)
    )


class ChipSum:
    def __init__(self, parts, rank, far_first):
        side, low_bit, high_bit = (rank // 2) % 2, (rank // 4) % 2, rank // 8
        self.parts = parts
        self.first = (4, high_bit) if far_first else (2, low_bit)
        self.second = (8, side) if far_first else (4, high_bit)
        self.last = 2 if far_first else 8

    def one(self, *after):
        self.parts = sum_stage(self.parts, *self.first, after)
        return self.parts[0]

    def two(self, *after):
        self.parts = sum_stage(self.parts, *self.second, after)
        return self.parts[0]

    def three(self, *after):
        send, keep = self.parts
        return add_low(keep, order(flip(send, self.last), *after))


def core_sum(value, core):
    rows, columns = value.shape
    value = value.reshape(8, 2, rows // 16, columns)
    got = flip(pick_index(value, 1 - core, 1).astype(jnp.bfloat16), 1)
    return add_low(pick_index(value, core, 1), got)


def plane_sum(total, rank, *after):
    side, low_bit, high_bit = (rank // 2) % 2, (rank // 4) % 2, rank // 8
    part, columns = total.shape[1:]
    total = total.reshape(4, 2, part, columns)
    got = order(flip(pick_index(total, 1 - side, 1), 2), *after)
    total = add_low(pick_index(total, side, 1), got).reshape(2, 2, part, columns)
    got = flip(pick_index(total, 1 - low_bit, 1), 4)
    total = add_low(pick_index(total, low_bit, 1), got)
    got = flip(pick_index(total, 1 - high_bit, 0), 8)
    return pick_index(total, high_bit, 0).astype(jnp.float32) + got.astype(jnp.float32)


def fetch_other(weights, core, side, after=()):
    rows = weights[0].shape[0] // 4
    start = (side * 2 + core) * rows
    own = jnp.concatenate(
        [lax.dynamic_slice_in_dim(w, start, rows, 0) for w in weights], axis=1
    )
    pieces = swap(order(own, *after))
    turned = flip(pieces, 2)
    result = jnp.zeros((4 * rows, own.shape[1]), own.dtype)
    for value, place in (
        (pieces, side * 2 + core),
        (turned, (1 - side) * 2 + core),
        (flip(pieces, 1), side * 2 + 1 - core),
        (flip(turned, 1), (1 - side) * 2 + 1 - core),
    ):
        result = lax.dynamic_update_slice_in_dim(result, value, place * rows, 0)
    return result, own, pieces


ROWS = 256
HALF = 512


def lane_swap(values):
    width = values.shape[1]
    lane = lax.broadcasted_iota(jnp.int32, values.shape, 1) % HD
    ahead = pltpu.roll(values, width - HD // 2, 1)
    behind = pltpu.roll(values, HD // 2, 1)
    return jnp.where(lane < HD // 2, ahead, behind)


def turn_tables(rows):
    cosine, sine = rope_tables(rows, HD)
    return (
        jnp.concatenate([cosine] * 4, axis=1),
        jnp.concatenate([-sine, sine, -sine, sine], axis=1),
    )


def project_kernel(sizes, score_scale, normed_ref, weights_ref, cosine_ref, sine_ref, *outs):
    query_ref, key_ref, value_ref = outs[-3:]
    query_width, key_width = sizes
    projected = jnp.dot(normed_ref[...], weights_ref[...], preferred_element_type=jnp.float32)
    cosine, sine = cosine_ref[...], sine_ref[...]
    for start in range(0, query_width + key_width, 128):
        piece = projected[:, start : start + 128]
        turned = piece * cosine + lane_swap(piece) * sine
        if start < query_width:
            query_ref[:, start : start + 128] = (turned * score_scale).astype(jnp.bfloat16)
        else:
            begin = start - query_width
            key_ref[:, begin : begin + 128] = turned.astype(jnp.bfloat16)
    value_ref[...] = projected[:, query_width + key_width :].astype(jnp.bfloat16)


def project(normed, weights, tables, query_width, key_width, score_scale, after=()):
    rows, depth = normed.shape
    width = weights.shape[1]
    row_spec = lambda columns: pl.BlockSpec((ROWS, columns), lambda i: (i, 0))
    return pl.pallas_call(
        functools.partial(project_kernel, (query_width, key_width), score_scale),
        grid=(rows // ROWS,),
        in_specs=[
            row_spec(depth),
            pl.BlockSpec((depth, width), lambda i: (0, 0)),
            row_spec(128),
            row_spec(128),
        ]
        + [pl.BlockSpec(memory_space=pl.ANY)] * len(after),
        out_specs=[row_spec(query_width), row_spec(key_width), row_spec(key_width)],
        out_shape=[
            jax.ShapeDtypeStruct((rows, query_width), jnp.bfloat16),
            jax.ShapeDtypeStruct((rows, key_width), jnp.bfloat16),
            jax.ShapeDtypeStruct((rows, key_width), jnp.bfloat16),
        ],
        compiler_params=pltpu.CompilerParams(vmem_limit_bytes=VMEM_LIMIT),
    )(normed, weights, *tables, *after)


def attend_kernel(per_pair, query_ref, key_ref, value_ref, limit_ref, out_ref, lse_ref):
    step = pl.program_id(1)

    def work(keys):
        columns = lax.broadcasted_iota(jnp.int32, (ROWS, HALF), 1) + (keys - HALF)
        allowed = columns <= limit_ref[...]
        lanes = lax.broadcasted_iota(jnp.int32, (ROWS, 128), 1)
        sums = jnp.zeros((ROWS, 128), jnp.float32)
        pieces = []
        for head in range(per_pair):
            group = head // (per_pair // 2)
            query = query_ref[:, head * HD : (head + 1) * HD]
            key = key_ref[:keys, group * HD : (group + 1) * HD]
            value = value_ref[:keys, group * HD : (group + 1) * HD]
            scores = dot_nt(query, key)
            last = jnp.where(allowed, scores[:, keys - HALF :], -1e30)
            scores = last if keys == HALF else jnp.concatenate([scores[:, : keys - HALF], last], 1)
            highest = jnp.max(scores, axis=1, keepdims=True)
            shifted = jnp.exp(scores - highest)
            total = jnp.sum(shifted, axis=1, keepdims=True)
            mixed = jnp.dot(
                shifted.astype(jnp.bfloat16), value, preferred_element_type=jnp.float32
            )
            pieces.append((mixed / total).astype(jnp.bfloat16))
            sums = jnp.where(lanes == head, highest + jnp.log(total), sums)
        out_ref[...] = jnp.concatenate(pieces, axis=1)
        lse_ref[0] = sums

    halfway = pl.num_programs(1) // 2

    @pl.when(step < halfway)
    def _():
        work(HALF)

    @pl.when(step >= halfway)
    def _():
        work(2 * HALF)


def attend(query, key, value, limits):
    rows, query_width = query.shape
    pairs = key.shape[1] // 128
    wide = query_width // pairs
    return pl.pallas_call(
        functools.partial(attend_kernel, wide // HD),
        grid=(pairs, rows // ROWS),
        in_specs=[
            pl.BlockSpec((ROWS, wide), lambda p, i: (i, p)),
            pl.BlockSpec((rows, 128), lambda p, i: (0, p)),
            pl.BlockSpec((rows, 128), lambda p, i: (0, p)),
            pl.BlockSpec((ROWS, 1), lambda p, i: (i, 0)),
        ],
        out_specs=[
            pl.BlockSpec((ROWS, wide), lambda p, i: (i, p)),
            pl.BlockSpec((1, ROWS, 128), lambda p, i: (p, i, 0)),
        ],
        out_shape=[
            jax.ShapeDtypeStruct((rows, query_width), jnp.bfloat16),
            jax.ShapeDtypeStruct((pairs, rows, 128), jnp.float32),
        ],
        compiler_params=pltpu.CompilerParams(vmem_limit_bytes=VMEM_LIMIT),
    )(query, key, value, limits)


def back_kernel(
    per_pair, score_scale, after, query_ref, key_ref, value_ref, turned_key_ref, grad_ref, lse_ref,
    limit_ref, cosine_ref, sine_ref, all_cosine_ref, all_sine_ref, *rest
):
    query_out, key_out, value_out, key_total, value_total = rest[after:]
    step = pl.program_id(1)
    halfway = pl.num_programs(1) // 2

    @pl.when(step == 0)
    def _():
        key_total[...] = jnp.zeros_like(key_total)
        value_total[...] = jnp.zeros_like(value_total)

    def work(keys):
        rows = lax.broadcasted_iota(jnp.int32, (HALF, ROWS), 0) + (keys - HALF)
        allowed = rows <= limit_ref[...]
        made = []
        key_parts, value_parts = [], []
        for group in range(2):
            span = slice(group * HD, (group + 1) * HD)
            key, value = key_ref[:keys, span], value_ref[:keys, span]
            key_part = value_part = 0.0
            for head in range(group * per_pair // 2, (group + 1) * per_pair // 2):
                query = query_ref[:, head * HD : (head + 1) * HD]
                grad = grad_ref[:, head * HD : (head + 1) * HD]
                scores = dot_nt(key, query)
                last = jnp.where(allowed, scores[keys - HALF :], -1e30)
                scores = (
                    last
                    if keys == HALF
                    else jnp.concatenate([scores[: keys - HALF], last], axis=0)
                )
                weights = jnp.exp(scores - lse_ref[0, head : head + 1, :])
                pulled = dot_nt(value, grad)
                inner = jnp.sum(weights * pulled, axis=0, keepdims=True)
                score_low = (weights * (pulled - inner)).astype(jnp.bfloat16)
                value_part += jnp.dot(
                    weights.astype(jnp.bfloat16), grad, preferred_element_type=jnp.float32
                )
                key_part += jnp.dot(score_low, query, preferred_element_type=jnp.float32)
                made.append(
                    jnp.dot(
                        turned_key_ref[0, span, :keys],
                        score_low,
                        preferred_element_type=jnp.float32,
                    )
                )
            key_parts.append(key_part)
            value_parts.append(value_part)
        key_total[:keys] += jnp.concatenate(key_parts, axis=1)
        value_total[:keys] += jnp.concatenate(value_parts, axis=1)
        cosine, sine = cosine_ref[...], sine_ref[...]
        for index in range(per_pair // 2):
            both = jnp.concatenate(made[2 * index : 2 * index + 2], axis=0).T * score_scale
            query_out[:, index * 128 : (index + 1) * 128] = (
                both * cosine - lane_swap(both) * sine
            ).astype(jnp.bfloat16)

    @pl.when(step < halfway)
    def _():
        work(HALF)

    @pl.when(step >= halfway)
    def _():
        work(2 * HALF)

    @pl.when(step == pl.num_programs(1) - 1)
    def _():
        total = key_total[...]
        key_out[...] = (
            total * all_cosine_ref[...] - lane_swap(total) * all_sine_ref[...]
        ).astype(jnp.bfloat16)
        value_out[...] = value_total[...].astype(jnp.bfloat16)


def attend_back(saved, attended_grad, limits, tables, score_scale, chosen, after=()):
    query, key, value, lse = saved
    rows, query_width = query.shape
    pairs = key.shape[1] // 128
    wide = query_width // pairs
    turned_key = key.T.reshape(pairs, 128, rows)
    lse_rows = lse[:, :, :8].transpose(0, 2, 1)
    cosine, sine = tables
    begin, count = chosen
    block = lambda columns: pl.BlockSpec((ROWS, columns), lambda p, i: (i, p + begin))
    whole = pl.BlockSpec((rows, 128), lambda p, i: (0, p + begin))
    block_out = pl.BlockSpec((ROWS, wide), lambda p, i: (i, p))
    whole_out = pl.BlockSpec((rows, 128), lambda p, i: (0, p))
    table = pl.BlockSpec((ROWS, 128), lambda p, i: (i, 0))
    full_table = pl.BlockSpec((rows, 128), lambda p, i: (0, 0))
    return pl.pallas_call(
        functools.partial(back_kernel, wide // HD, score_scale, len(after)),
        grid=(count, rows // ROWS),
        in_specs=[
            block(wide),
            whole,
            whole,
            pl.BlockSpec((1, 128, rows), lambda p, i: (p + begin, 0, 0)),
            block(wide),
            pl.BlockSpec((1, 8, ROWS), lambda p, i: (p + begin, 0, i)),
            pl.BlockSpec((1, ROWS), lambda p, i: (0, i)),
            table,
            table,
            full_table,
            full_table,
        ]
        + [pl.BlockSpec(memory_space=pl.ANY)] * len(after),
        out_specs=[block_out, whole_out, whole_out],
        out_shape=[
            jax.ShapeDtypeStruct((rows, count * wide), jnp.bfloat16),
            jax.ShapeDtypeStruct((rows, count * 128), jnp.bfloat16),
            jax.ShapeDtypeStruct((rows, count * 128), jnp.bfloat16),
        ],
        scratch_shapes=[
            pltpu.VMEM((rows, 128), jnp.float32),
            pltpu.VMEM((rows, 128), jnp.float32),
        ],
        compiler_params=pltpu.CompilerParams(vmem_limit_bytes=VMEM_LIMIT),
    )(
        query, key, value, turned_key, attended_grad, lse_rows, limits.T, cosine, sine, cosine,
        sine, *after,
    )


def piece_limits(starts_row, rows):
    position = jnp.arange(rows, dtype=jnp.int32)
    limits = position
    for index in range(starts_row.shape[0]):
        start = starts_row[index]
        inside = (position >= start) & (position < start + PIECE)
        limits = jnp.where(inside, start + PIECE - 1, limits)
    return limits[:, None]


def slot_table(routes, expert_count, capacity):
    flattened = routes.reshape(-1)
    onehot = (flattened[:, None] == jnp.arange(expert_count, dtype=jnp.int32)[None, :]).astype(
        jnp.int32
    )
    placed = jnp.sum((jnp.cumsum(onehot, axis=0) - 1) * onehot, axis=1)
    entries = jnp.arange(flattened.shape[0], dtype=jnp.int32)
    return (
        jnp.full((expert_count * capacity,), flattened.shape[0], jnp.int32)
        .at[flattened * capacity + placed]
        .set(entries)
    )


def expert_forward(expert_inputs, w_gate, w_up, w_down):
    gate_proj = jnp.einsum(
        "ecd,edf->ecf", expert_inputs, w_gate, preferred_element_type=jnp.float32
    )
    up_proj = jnp.einsum("ecd,edf->ecf", expert_inputs, w_up, preferred_element_type=jnp.float32)
    activated = (gate_proj * jax.nn.sigmoid(gate_proj) * up_proj).astype(jnp.bfloat16)
    returned = jnp.einsum("ecf,efd->ecd", activated, w_down, preferred_element_type=jnp.float32)
    return (gate_proj, up_proj, activated, returned)


def shards_wide(
    tokens,
    norm_gains,
    w_query,
    w_key,
    w_value,
    w_out,
    mix_gains,
    w_router,
    w_gate,
    w_up,
    w_down,
    routes,
    starts,
    cotangent,
):
    share_rows = tokens.shape[0]
    model_width = tokens.shape[1]
    head_width = HD
    query_width = w_query.shape[1]
    key_width = w_key.shape[1]
    heads_here = query_width // head_width
    groups_here = key_width // head_width
    per_group = heads_here // groups_here
    experts_here = w_gate.shape[0]
    group_rows = routes.shape[0]
    choices_count = routes.shape[1]
    sequences_here = starts.shape[0]
    sequence_length = group_rows // sequences_here
    expert_count = w_router.shape[1]
    tensor_rank = lax.axis_index("tensor")
    total_tokens = group_rows * lax.axis_size("dp")
    score_scale = head_width ** (-0.5)
    inputs_share = tokens.astype(jnp.float32)
    normed_share = normalize(inputs_share, norm_gains).astype(jnp.bfloat16)
    normed = lax.all_gather(normed_share, "tensor", axis=0, tiled=True)
    joined_weights = jnp.concatenate([w_query, w_key, w_value], axis=1)
    projected = jnp.dot(normed, joined_weights, preferred_element_type=jnp.float32)
    cosine, sine_table = rope_tables(sequence_length, head_width)
    cosine_rows = jnp.tile(cosine, (sequences_here, 1))
    sine_rows = jnp.tile(sine_table, (sequences_here, 1))
    query_rows = rotate(
        projected[:, :query_width].reshape(group_rows, heads_here, head_width),
        cosine_rows,
        sine_rows,
    ).astype(jnp.bfloat16)
    key_rows = rotate(
        projected[:, query_width : query_width + key_width].reshape(
            group_rows, groups_here, head_width
        ),
        cosine_rows,
        sine_rows,
    ).astype(jnp.bfloat16)
    value_rows = (
        projected[:, query_width + key_width :]
        .astype(jnp.bfloat16)
        .reshape(group_rows, groups_here, head_width)
    )
    attended_parts = []
    logsum_parts = []
    for sequence in range(sequences_here):
        first_row = sequence * sequence_length
        query_block = query_rows[first_row : first_row + sequence_length].reshape(
            sequence_length, groups_here, per_group, head_width
        )
        key_block = key_rows[first_row : first_row + sequence_length]
        value_block = value_rows[first_row : first_row + sequence_length]
        allowed = allowed_pairs(starts[sequence], sequence_length, PIECE)
        scores = scores_of(query_block, key_block, allowed, score_scale)
        highest = jnp.max(scores, axis=-1, keepdims=True)
        shifted = jnp.exp(scores - highest)
        totals = jnp.sum(shifted, axis=-1, keepdims=True)
        weights = (shifted / totals).astype(jnp.bfloat16)
        mixed_values = jnp.einsum(
            "kgqs,skd->qkgd", weights, value_block, preferred_element_type=jnp.float32
        )
        attended_parts.append(
            mixed_values.reshape(sequence_length, query_width).astype(jnp.bfloat16)
        )
        logsum_parts.append(highest + jnp.log(totals))
    attended = jnp.concatenate(attended_parts, axis=0)
    attention_share = lax.psum_scatter(
        jnp.dot(attended, w_out, preferred_element_type=jnp.float32),
        "tensor",
        scatter_dimension=0,
        tiled=True,
    )
    middle_share = inputs_share + attention_share
    mixed_share = normalize(middle_share, mix_gains).astype(jnp.bfloat16)
    share_routes = lax.dynamic_slice_in_dim(routes, tensor_rank * share_rows, share_rows, 0)
    route_onehot = (
        share_routes[:, :, None] == jnp.arange(expert_count, dtype=jnp.int32)[None, None, :]
    ).astype(jnp.float32)
    logits = jnp.dot(mixed_share, w_router, preferred_element_type=jnp.float32)
    probabilities = softmax_rows(logits)
    chosen = jnp.sum(logits[:, None, :] * route_onehot, axis=-1)
    gate_soft = softmax_rows(chosen)
    gate_low = gate_soft.astype(jnp.bfloat16)
    counts, prob_sums = lax.psum(
        (jnp.sum(route_onehot, axis=(0, 1)), jnp.sum(probabilities, axis=0)), ("dp", "tensor")
    )
    fractions = counts / (total_tokens * choices_count)
    balance = expert_count * expert_count * fractions * prob_sums / total_tokens
    mixed_rows, gate_rows = (
        lax.all_gather(mixed_share, "tensor", axis=0, tiled=True),
        lax.all_gather(gate_low, "tensor", axis=0, tiled=True),
    )
    slots_all = slot_table(routes, expert_count, CAP)
    slots = lax.dynamic_slice_in_dim(
        slots_all, tensor_rank * experts_here * CAP, experts_here * CAP, 0
    )
    owners = slots // choices_count
    padded_rows = jnp.concatenate([mixed_rows, jnp.zeros((1, model_width), jnp.bfloat16)], axis=0)
    padded_gates = jnp.concatenate(
        [gate_rows.reshape(-1).astype(jnp.float32), jnp.zeros((1,), jnp.float32)], axis=0
    )
    slot_gates = padded_gates[slots]
    expert_inputs = padded_rows[owners].reshape(experts_here, CAP, model_width)
    gate_proj, up_proj, activated, returned = expert_forward(expert_inputs, w_gate, w_up, w_down)
    returned_flat = returned.reshape(experts_here * CAP, model_width)
    expert_partial = jax.ops.segment_sum(
        slot_gates[:, None] * returned_flat, owners, num_segments=group_rows + 1
    )[:group_rows]
    expert_share = lax.psum_scatter(
        expert_partial.astype(jnp.bfloat16), "tensor", scatter_dimension=0, tiled=True
    ).astype(jnp.float32)
    output_share = (middle_share + expert_share).astype(jnp.bfloat16)
    upstream = cotangent.astype(jnp.float32)
    upstream_rows = lax.all_gather(cotangent, "tensor", axis=0, tiled=True)
    padded_upstream = jnp.concatenate(
        [upstream_rows, jnp.zeros((1, model_width), jnp.bfloat16)], axis=0
    )
    slot_upstream = padded_upstream[owners].astype(jnp.float32)
    slot_cotangent = (
        (slot_gates[:, None] * slot_upstream)
        .astype(jnp.bfloat16)
        .reshape(experts_here, CAP, model_width)
    )
    slot_gate_grad = jnp.sum(slot_upstream * returned_flat, axis=1)
    activated_grad = jnp.einsum(
        "ecd,efd->ecf", slot_cotangent, w_down, preferred_element_type=jnp.float32
    )
    down_grad = jnp.einsum(
        "ecf,ecd->efd", activated, slot_cotangent, preferred_element_type=jnp.float32
    )
    sigmoid_gate = jax.nn.sigmoid(gate_proj)
    gate_proj_low = (
        activated_grad * up_proj * sigmoid_gate * (1.0 + gate_proj * (1.0 - sigmoid_gate))
    ).astype(jnp.bfloat16)
    up_proj_low = (activated_grad * gate_proj * sigmoid_gate).astype(jnp.bfloat16)
    inputs_grad = jnp.einsum(
        "ecf,edf->ecd", gate_proj_low, w_gate, preferred_element_type=jnp.float32
    ) + jnp.einsum("ecf,edf->ecd", up_proj_low, w_up, preferred_element_type=jnp.float32)
    gate_grad = jnp.einsum(
        "ecd,ecf->edf", expert_inputs, gate_proj_low, preferred_element_type=jnp.float32
    )
    up_grad = jnp.einsum(
        "ecd,ecf->edf", expert_inputs, up_proj_low, preferred_element_type=jnp.float32
    )
    mixed_partial = jax.ops.segment_sum(
        inputs_grad.reshape(experts_here * CAP, model_width), owners, num_segments=group_rows + 1
    )[:group_rows]
    gate_partial = jax.ops.segment_sum(
        slot_gate_grad, slots, num_segments=group_rows * choices_count + 1
    )[: group_rows * choices_count].reshape(group_rows, choices_count)
    mixed_grad_share, gates_grad_share = (
        lax.psum_scatter(mixed_partial, "tensor", scatter_dimension=0, tiled=True),
        lax.psum_scatter(gate_partial, "tensor", scatter_dimension=0, tiled=True),
    )
    gate_total, up_total = (
        lax.psum_scatter(
            gate_grad.astype(jnp.bfloat16), "dp", scatter_dimension=1, tiled=True
        ).astype(jnp.float32),
        lax.psum_scatter(
            up_grad.astype(jnp.bfloat16), "dp", scatter_dimension=1, tiled=True
        ).astype(jnp.float32),
    )
    down_total = lax.psum_scatter(
        down_grad.astype(jnp.bfloat16), "dp", scatter_dimension=2, tiled=True
    ).astype(jnp.float32)
    chosen_grad = gate_soft * (
        gates_grad_share - jnp.sum(gate_soft * gates_grad_share, axis=-1, keepdims=True)
    )
    logit_grad = jnp.sum(chosen_grad[:, :, None] * route_onehot, axis=1)
    prob_target = ALPHA * expert_count * fractions / total_tokens
    logit_grad = logit_grad + probabilities * (
        prob_target[None, :] - jnp.sum(probabilities * prob_target[None, :], axis=-1, keepdims=True)
    )
    mixed_float = mixed_share.astype(jnp.float32)
    router_grad = jnp.dot(
        mixed_float.T, logit_grad, precision=HIGHEST, preferred_element_type=jnp.float32
    )
    mixed_grad_share = mixed_grad_share + jnp.dot(
        logit_grad,
        w_router.astype(jnp.float32).T,
        precision=HIGHEST,
        preferred_element_type=jnp.float32,
    )
    mix_pullback = jax.vjp(normalize, middle_share, mix_gains)[1]
    middle_from_norm, mix_gain_grad = mix_pullback(mixed_grad_share)
    middle_grad = upstream + middle_from_norm
    middle_low = middle_grad.astype(jnp.bfloat16)
    middle_rows = lax.all_gather(middle_low, "tensor", axis=0, tiled=True)
    out_grad = contract_rows(attended, middle_rows)
    attended_grad = contract_cols(middle_rows, w_out).astype(jnp.bfloat16)
    query_parts = []
    key_parts = []
    value_parts = []
    for sequence in range(sequences_here):
        first_row = sequence * sequence_length
        query_block = query_rows[first_row : first_row + sequence_length].reshape(
            sequence_length, groups_here, per_group, head_width
        )
        key_block = key_rows[first_row : first_row + sequence_length]
        value_block = value_rows[first_row : first_row + sequence_length]
        allowed = allowed_pairs(starts[sequence], sequence_length, PIECE)
        scores = scores_of(query_block, key_block, allowed, score_scale)
        weights_full = jnp.exp(scores - logsum_parts[sequence])
        weights_low = weights_full.astype(jnp.bfloat16)
        grad_block = attended_grad[first_row : first_row + sequence_length].reshape(
            sequence_length, groups_here, per_group, head_width
        )
        value_parts.append(
            jnp.einsum(
                "kgqs,qkgd->skd", weights_low, grad_block, preferred_element_type=jnp.float32
            )
        )
        weight_grad = jnp.einsum(
            "qkgd,skd->kgqs", grad_block, value_block, preferred_element_type=jnp.float32
        )
        score_low = (
            weights_full
            * (weight_grad - jnp.sum(weights_full * weight_grad, axis=-1, keepdims=True))
        ).astype(jnp.bfloat16)
        query_parts.append(
            jnp.einsum("kgqs,skd->qkgd", score_low, key_block, preferred_element_type=jnp.float32)
            * score_scale
        )
        key_parts.append(
            jnp.einsum("kgqs,qkgd->skd", score_low, query_block, preferred_element_type=jnp.float32)
            * score_scale
        )
    query_grads = (
        rotate(
            jnp.concatenate(query_parts, axis=0).reshape(group_rows, heads_here, head_width),
            cosine_rows,
            -sine_rows,
        )
        .astype(jnp.bfloat16)
        .reshape(group_rows, query_width)
    )
    key_grads = (
        rotate(jnp.concatenate(key_parts, axis=0), cosine_rows, -sine_rows)
        .astype(jnp.bfloat16)
        .reshape(group_rows, key_width)
    )
    value_grads = (
        jnp.concatenate(value_parts, axis=0).astype(jnp.bfloat16).reshape(group_rows, key_width)
    )
    joined_grads = jnp.concatenate([query_grads, key_grads, value_grads], axis=1)
    joined_weight_grad = contract_rows(normed, joined_grads)
    normed_grad_share = lax.psum_scatter(
        contract_cols(joined_grads, joined_weights).astype(jnp.bfloat16),
        "tensor",
        scatter_dimension=0,
        tiled=True,
    ).astype(jnp.float32)
    input_pullback = jax.vjp(normalize, inputs_share, norm_gains)[1]
    input_from_norm, norm_gain_grad = input_pullback(normed_grad_share)
    input_grad_share = middle_grad + input_from_norm
    query_total, key_total, value_total, out_turned = (
        lax.psum_scatter(
            joined_weight_grad[:, :query_width].astype(jnp.bfloat16),
            "dp",
            scatter_dimension=0,
            tiled=True,
        ).astype(jnp.float32),
        lax.psum_scatter(
            joined_weight_grad[:, query_width : query_width + key_width].astype(jnp.bfloat16),
            "dp",
            scatter_dimension=0,
            tiled=True,
        ).astype(jnp.float32),
        lax.psum_scatter(
            joined_weight_grad[:, query_width + key_width :].astype(jnp.bfloat16),
            "dp",
            scatter_dimension=0,
            tiled=True,
        ).astype(jnp.float32),
        lax.psum_scatter(
            out_grad.T.astype(jnp.bfloat16), "dp", scatter_dimension=0, tiled=True
        ).astype(jnp.float32),
    )
    out_total = out_turned.T
    norm_gain_total, mix_gain_total, router_total = lax.psum(
        (norm_gain_grad, mix_gain_grad, router_grad), ("dp", "tensor")
    )
    return (
        output_share,
        balance,
        input_grad_share,
        norm_gain_total,
        query_total,
        key_total,
        value_total,
        out_total,
        mix_gain_total,
        router_total,
        gate_total,
        up_total,
        down_total,
    )


def all_sum(value):
    for bit in (1, 2, 4, 8):
        value = value + flip(value, bit)
    return value + swap(value)


def spread(value):
    across = swap(value)
    return [value, across, flip(value, 1), flip(across, 1)]


FIRST_PART = 2
FAR_FIRST = (2, 5)


def shards_pair(
    tokens,
    norm_gains,
    w_query,
    w_key,
    w_value,
    w_out,
    mix_gains,
    w_router,
    w_gate,
    w_up,
    w_down,
    routes,
    starts,
    cotangent,
):
    share_rows, model_width = tokens.shape
    query_width = w_query.shape[1]
    key_width = w_key.shape[1]
    sizes = (query_width, key_width, HD)
    experts_here = w_gate.shape[0]
    experts = experts_here // 2
    choices_count = routes.shape[1]
    expert_count = w_router.shape[1]
    dp_size = lax.axis_size("dp")
    rank = lax.axis_index("dp")
    core, side = rank % 2, (rank // 2) % 2
    tensor_rank = lax.axis_index("tensor")
    total_tokens = routes.shape[0] * dp_size
    score_scale = HD ** (-0.5)
    depth = model_width // dp_size * 2
    slots = round_up(2 * CAP, BLOCK)

    joined_own = jnp.concatenate([w_query, w_key, w_value], axis=1)
    joined_other, joined_send, joined_piece = fetch_other([w_query, w_key, w_value], core, side)
    out_other, _, out_piece = fetch_other([w_out], core, side, (joined_send,))

    own_routes = lax.dynamic_slice_in_dim(routes, tensor_rank * share_rows, share_rows, 0)
    across_routes = lax.dynamic_slice_in_dim(routes, (1 - tensor_rank) * share_rows, share_rows, 0)
    both_routes = jnp.concatenate([own_routes, across_routes], axis=0)
    group_routes = jnp.concatenate([both_routes, flip(both_routes, 1)], axis=0)
    first_expert = tensor_rank * experts_here + core * experts

    route_onehot = (
        own_routes[:, :, None] == jnp.arange(expert_count, dtype=jnp.int32)[None, None, :]
    ).astype(jnp.float32)
    counts = all_sum(jnp.sum(route_onehot, axis=(0, 1)))
    cotangent_rows = spread(order(cotangent, joined_piece, out_piece))

    inputs_share = tokens.astype(jnp.float32)
    normed = normalize(inputs_share, norm_gains).astype(jnp.bfloat16)
    tables = turn_tables(share_rows)
    starts_row = lax.dynamic_index_in_dim(starts, tensor_rank, 0, keepdims=False)
    limits = piece_limits(starts_row, share_rows)

    def half_forward(joined_weights, after=()):
        query, key, value = project(
            normed, joined_weights, tables, query_width, key_width, score_scale, after
        )
        attended, lse = attend(query, key, value, limits)
        return attended, (query, key, value, lse)

    attended_own, saved_own = half_forward(joined_own)
    attended_other, saved_other = half_forward(joined_other, (counts,))
    middle_share = (
        inputs_share
        + jnp.dot(attended_own, w_out, preferred_element_type=jnp.float32)
        + jnp.dot(attended_other, out_other, preferred_element_type=jnp.float32)
    )
    mixed_share = normalize(middle_share, mix_gains).astype(jnp.bfloat16)

    logits = jnp.dot(mixed_share, w_router, preferred_element_type=jnp.float32)
    probabilities = softmax_rows(logits)
    chosen = jnp.sum(logits[:, None, :] * route_onehot, axis=-1)
    gate_soft = softmax_rows(chosen)
    gate_low = gate_soft.astype(jnp.bfloat16)
    fractions = counts / (total_tokens * choices_count)

    group_gates = jnp.concatenate(spread(gate_low), axis=0)
    gates = gate_table(group_routes, group_gates, first_expert, experts)
    place, begins, ends = placement(group_routes, first_expert, experts)
    gather_from = gather_tables(begins, ends, slots)
    blocks = gather_from[2]
    cot_slots = gather_rows(gather_from, place, None, cotangent_rows, slots, 0, experts)[0]
    mixed_across = order(swap(mixed_share), cot_slots)
    mixed_rows = [mixed_share, mixed_across, flip(mixed_share, 1), flip(mixed_across, 1)]
    misc = jnp.stack([core * experts, side, (rank // 4) % 2])
    weights = (w_gate, w_up, w_down)
    first_part = gather_rows(
        gather_from, place, gates, mixed_rows, slots, 0, FIRST_PART, (cot_slots, counts)
    )
    later_part = None
    carried = None
    chips = []
    for index in range(experts):
        if index == FIRST_PART:
            later_part = gather_rows(
                gather_from, place, gates, mixed_rows, slots, FIRST_PART, experts - FIRST_PART,
                (carried,),
            )
        if later_part is None:
            (x_slots, slot_gates), x_first = first_part, 0
        else:
            (x_slots, slot_gates), x_first = later_part, FIRST_PART
        waits = []
        if index == 2:
            waits = [chips[0].one(slot_gates)]
        elif index == 4:
            waits = [chips[0].two(carried)]
        elif index == 5:
            waits = [chips[1].one(carried)]
        elif index == 6:
            waits = [chips[2].one(carried)]
        elif index == 8:
            waits = [chips[3].one(carried), chips[1].two(carried)]
        far_first = int(index in FAR_FIRST)
        carried, send, keep = expert_call(
            blocks, misc, x_slots, cot_slots, slot_gates, weights, carried, slots,
            index, 1, x_first, 0, depth, far_first, waits,
        )
        chips.append(ChipSum((send, keep), rank, far_first))
    waits = [chips[4].one(carried), chips[5].one(carried)]
    done = [chips[0].three(carried)]
    waits += done

    combine_from = combine_tables(begins, ends, slots)
    tiles = place.shape[1] // 4
    names = first_expert + jnp.arange(experts, dtype=jnp.int32)

    def combined(quarter, after):
        y, dx, gate_grads = combine_rows(
            combine_from, place, carried, quarter * tiles, tiles, after
        )
        gate_grads = gate_grads[:, :experts] + gate_grads[:, 64 : 64 + experts]
        rows = group_routes[quarter * share_rows : (quarter + 1) * share_rows]
        hit = rows[:, :, None] == names[None, None, :]
        return y, dx, jnp.sum(jnp.where(hit, gate_grads[:, None, :], 0.0), axis=2)

    far = combined(3, waits)
    waits = [chips[2].two(far[1])]
    done.append(chips[1].three(far[1]))
    waits.append(done[1])
    far_y, far_dx, far_gg = (flip(value, 1) for value in far)
    cross = combined(1, waits)
    dx_send = add_low(cross[1], far_dx)
    dx_across = swap(dx_send)
    gg_across = swap(cross[2] + far_gg)
    waits = [dx_send, chips[6].one(cross[1]), chips[3].two(cross[1])]
    next_door = combined(2, waits)
    door_y, door_dx, door_gg = (flip(value, 1) for value in next_door)
    y_send = add_low(cross[0], far_y)
    y_across = swap(order(y_send, dx_send))
    near = combined(0, [y_send, next_door[1]])
    waits = [chips[7].one(near[1]), chips[5].two(near[1])]
    done += [chips[2].three(near[1]), chips[3].three(near[1])]
    waits += done[2:]
    mixed_grad_share = (
        near[1].astype(jnp.float32) + door_dx.astype(jnp.float32) + dx_across.astype(jnp.float32)
    )
    gates_grad_share = near[2] + door_gg + gg_across

    upstream = cotangent.astype(jnp.float32)
    chosen_grad = gate_soft * (
        gates_grad_share - jnp.sum(gate_soft * gates_grad_share, axis=-1, keepdims=True)
    )
    logit_grad = jnp.sum(chosen_grad[:, :, None] * route_onehot, axis=1)
    prob_target = ALPHA * expert_count * fractions / total_tokens
    logit_grad = logit_grad + probabilities * (
        prob_target[None, :] - jnp.sum(probabilities * prob_target[None, :], axis=-1, keepdims=True)
    )
    router_grad = jnp.dot(
        mixed_share.astype(jnp.float32).T,
        logit_grad,
        precision=HIGHEST,
        preferred_element_type=jnp.float32,
    )
    mixed_grad_share = mixed_grad_share + jnp.dot(
        logit_grad,
        w_router.astype(jnp.float32).T,
        precision=HIGHEST,
        preferred_element_type=jnp.float32,
    )
    mix_pullback = jax.vjp(normalize, middle_share, mix_gains)[1]
    middle_from_norm, mix_gain_grad = mix_pullback(mixed_grad_share)
    middle_grad = upstream + middle_from_norm
    middle_low = middle_grad.astype(jnp.bfloat16)

    def half_back(saved, out_weights):
        attended_grad = dot_nt(middle_low, out_weights).astype(jnp.bfloat16)

        def part(chosen, after):
            return attend_back(
                saved, attended_grad, limits, tables, score_scale, chosen, after
            )

        return part

    waits += [chips[8].one(middle_low), chips[4].two(middle_low), chips[6].two(middle_low)]
    pairs = key_width // 128
    other_grads = jnp.concatenate(
        half_back(saved_other, out_other)((0, pairs), waits), axis=1
    )
    expert_share = (
        near[0].astype(jnp.float32)
        + door_y.astype(jnp.float32)
        + order(y_across, other_grads).astype(jnp.float32)
    )
    output_share = (middle_share + expert_share).astype(jnp.bfloat16)
    joined_held = core_sum(dot_tn(normed, other_grads), core)
    joined_across = swap(joined_held)
    marked = order(middle_low, other_grads)
    out_held = core_sum(dot_tn(marked, attended_other), core)
    out_across = swap(order(out_held, joined_held))
    out_kept = core_sum(dot_tn(marked, attended_own), core)
    waits = [chips[9].one(other_grads), chips[7].two(other_grads)]
    done += [chips[i].three(other_grads) for i in (4, 5, 6)]
    waits += done[4:]
    waits += [joined_held, out_held, out_kept, output_share]
    own_part = half_back(saved_own, w_out)
    front = own_part((0, pairs // 2), waits)
    back = own_part((pairs // 2, pairs - pairs // 2), [joined_across, front[0]])
    own_grads = jnp.concatenate(
        [part for both in zip(front, back) for part in both], axis=1
    )
    out_half = add_low(out_kept, order(out_across, own_grads))
    own_weight_grads = dot_tn(normed, own_grads)
    joined_total = plane_sum(add_low(core_sum(own_weight_grads, core), joined_across), rank)
    out_total = plane_sum(out_half, rank, own_weight_grads)
    chips[8].two(own_grads)
    chips[9].two(own_grads)
    sums = done + [chips[i].three(own_weight_grads) for i in (7, 8, 9)]
    other_normed = dot_nt(other_grads, joined_other)
    own_normed = dot_nt(own_grads, joined_own)
    input_pullback = jax.vjp(normalize, inputs_share, norm_gains)[1]
    input_from_norm, norm_gain_grad = input_pullback(other_normed + own_normed)
    input_grad_share = middle_grad + input_from_norm
    key_end = query_width + key_width
    small = all_sum(
        jnp.concatenate(
            [jnp.sum(probabilities, axis=0), mix_gain_grad, norm_gain_grad, router_grad.reshape(-1)]
        )
    )
    prob_sums = small[:expert_count]
    mix_gain_total = small[expert_count : expert_count + model_width]
    norm_gain_total = small[expert_count + model_width : expert_count + 2 * model_width]
    router_total = small[expert_count + 2 * model_width :].reshape(router_grad.shape)
    balance = expert_count * expert_count * fractions * prob_sums / total_tokens

    mine = jnp.stack(sums, axis=0).reshape(experts, 3, 2, depth // 2, -1)
    theirs = flip(pick_index(mine, 1 - core, 2), 1)
    mine = pick_index(mine, core, 2)
    expert_total = jnp.where(
        core == 0,
        jnp.concatenate([mine, theirs], axis=0),
        jnp.concatenate([theirs, mine], axis=0),
    ).astype(jnp.float32)
    return (
        output_share,
        balance,
        input_grad_share,
        norm_gain_total,
        joined_total[:, :query_width],
        joined_total[:, query_width:key_end],
        joined_total[:, key_end:],
        out_total.T,
        mix_gain_total,
        router_total,
        expert_total[:, 0],
        expert_total[:, 1],
        expert_total[:, 2].transpose(0, 2, 1),
    )


def solution(mesh):
    sizes = dict(mesh.shape)
    paired = sizes["tensor"] == 2 and sizes["dp"] == 16
    return jax.shard_map(
        shards_pair if paired else shards_wide,
        mesh=mesh,
        in_specs=(
            P(("dp", "tensor"), None),
            P(),
            P(None, "tensor"),
            P(None, "tensor"),
            P(None, "tensor"),
            P("tensor", None),
            P(),
            P(),
            P("tensor", None, None),
            P("tensor", None, None),
            P("tensor", None, None),
            P("dp", None),
            P("dp", None),
            P(("dp", "tensor"), None),
        ),
        out_specs=(
            P(("dp", "tensor"), None),
            P(),
            P(("dp", "tensor"), None),
            P(),
            P("dp", "tensor"),
            P("dp", "tensor"),
            P("dp", "tensor"),
            P("tensor", "dp"),
            P(),
            P(),
            P("tensor", "dp", None),
            P("tensor", "dp", None),
            P("tensor", None, "dp"),
        ),
        check_vma=False,
    )
```

```python
import functools

import jax
import jax.numpy as jnp
from jax import lax
from jax.experimental import pallas as pl
from jax.experimental.pallas import tpu as pltpu
from jax.sharding import PartitionSpec as P

HD = 64
PIECE = 256
CAP = 614


EPSILON = 1e-06
ALPHA = 0.01
HIGHEST = lax.Precision.HIGHEST


def normalize(values, gains):
    return values * lax.rsqrt(jnp.mean(values * values, axis=-1, keepdims=True) + EPSILON) * gains


def softmax_rows(values):
    shifted = jnp.exp(values - jnp.max(values, axis=-1, keepdims=True))
    return shifted / jnp.sum(shifted, axis=-1, keepdims=True)


def contract_rows(left, right):
    return lax.dot_general(
        left, right, (((0,), (0,)), ((), ())), preferred_element_type=jnp.float32
    )


def contract_cols(left, right):
    return lax.dot_general(
        left, right, (((1,), (1,)), ((), ())), preferred_element_type=jnp.float32
    )


def rope_tables(sequence_length, head_width):
    half_width = head_width // 2
    frequency = 10000.0 ** (-(jnp.arange(half_width, dtype=jnp.float32) * 2.0 / head_width))
    angles = jnp.arange(sequence_length, dtype=jnp.float32)[:, None] * frequency[None, :]
    return (jnp.cos(angles), jnp.sin(angles))


def rotate(values, cosine, sine_table):
    half_width = values.shape[-1] // 2
    first_half = values[..., :half_width]
    second_half = values[..., half_width:]
    cosine_rows = cosine[:, None, :]
    sine_rows = sine_table[:, None, :]
    return jnp.concatenate(
        [
            first_half * cosine_rows - second_half * sine_rows,
            second_half * cosine_rows + first_half * sine_rows,
        ],
        axis=-1,
    )


def allowed_pairs(starts_row, sequence_length, piece_length):
    position = jnp.arange(sequence_length, dtype=jnp.int32)
    labels = jnp.full((sequence_length,), -1, jnp.int32)
    for piece_index in range(starts_row.shape[0]):
        inside = (position >= starts_row[piece_index]) & (
            position < starts_row[piece_index] + piece_length
        )
        labels = jnp.where(inside, piece_index, labels)
    causal = position[None, :] <= position[:, None]
    shared = (labels[:, None] == labels[None, :]) & (labels[:, None] >= 0)
    return causal | shared


def scores_of(query_block, key_block, allowed, score_scale):
    raw_scores = (
        jnp.einsum("qkgd,skd->kgqs", query_block, key_block, preferred_element_type=jnp.float32)
        * score_scale
    )
    return jnp.where(allowed, raw_scores, -1e30)


BLOCK = 256
PART = 128
PIECE_ROWS = 32
GROUP = 8
DEEP = 4
VMEM_LIMIT = 60 * 1024 * 1024


def dot_nt(left, right):
    return lax.dot_general(
        left, right, (((1,), (1,)), ((), ())), preferred_element_type=jnp.float32
    )


def dot_tn(left, right):
    return lax.dot_general(
        left, right, (((0,), (0,)), ((), ())), preferred_element_type=jnp.float32
    )


def round_up(value, multiple):
    return -(-value // multiple) * multiple


def placement(routes_rows, first_expert, experts):
    rows = routes_rows.shape[0]
    tiles = rows // BLOCK
    turned = routes_rows.T
    names = first_expert + jnp.arange(experts, dtype=jnp.int32)
    hit = turned[None, :, :] == names[:, None, None]
    member = jnp.any(hit, axis=1)
    upper = jnp.triu(jnp.ones((BLOCK, BLOCK), jnp.bfloat16))
    inside = jnp.dot(
        member.astype(jnp.bfloat16).reshape(experts * tiles, BLOCK),
        upper,
        preferred_element_type=jnp.float32,
    ).astype(jnp.int32).reshape(experts, tiles, BLOCK)
    sums = inside[:, :, -1]
    ends = jnp.cumsum(sums, axis=1)
    begins = ends - sums
    place = jnp.where(
        member.reshape(experts, tiles, BLOCK), begins[:, :, None] + inside - 1, -1
    )
    place = jnp.concatenate(
        [place, jnp.full((1, tiles, BLOCK), -1, jnp.int32)], axis=0
    ).reshape(experts + 1, tiles, 1, BLOCK)
    return place, begins, ends


def gate_table(routes_rows, gates_rows, first_expert, experts):
    names = first_expert + jnp.arange(experts, dtype=jnp.int32)
    hit = routes_rows.T[None, :, :] == names[:, None, None]
    table = jnp.sum(jnp.where(hit, gates_rows.astype(jnp.float32).T[None, :, :], 0.0), axis=1)
    return jnp.pad(table, ((0, 128 - experts), (0, 0))).T.astype(jnp.bfloat16)


def gather_tables(begins, ends, slots):
    counts = ends[:, -1]
    parts = jnp.arange(slots // PART, dtype=jnp.int32) * PART
    low = jnp.sum((ends[:, None, :] <= parts[None, :, None]).astype(jnp.int32), axis=2)
    high = jnp.sum((begins[:, None, :] < parts[None, :, None] + PART).astype(jnp.int32), axis=2)
    high = jnp.where(parts[None, :] < counts[:, None], high, low)
    blocks = jnp.maximum(-(-counts // BLOCK), 1)
    return low, high, blocks


def combine_tables(begins, ends, slots):
    experts, tiles = begins.shape
    width = round_up(experts * (BLOCK // PIECE_ROWS + 1), GROUP)
    first = begins // PIECE_ROWS
    amount = jnp.where(ends > begins, (ends - 1) // PIECE_ROWS - first + 1, 0)
    stop = jnp.cumsum(amount, axis=0)
    place = jnp.arange(width, dtype=jnp.int32)
    owner = jnp.sum(
        (stop.T[:, None, :] <= place[None, :, None]).astype(jnp.int32), axis=2
    )
    chosen = owner[:, :, None] == jnp.arange(experts, dtype=jnp.int32)[None, None, :]
    offset = jnp.sum(
        jnp.where(chosen, (first - (stop - amount)).T[:, None, :], 0), axis=2
    )
    valid = owner < experts
    piece = jnp.where(valid, offset + place[None, :], 0)
    source = jnp.where(valid, owner, 0) * (slots // PIECE_ROWS) + piece
    groups = jnp.maximum(-(-stop[-1] // GROUP), 1)
    return owner, piece, source, groups, width


def gather_kernel(sources, with_gates, after, low_ref, high_ref, blocks_ref, place_ref, *rest):
    if with_gates:
        gates_ref, rest = rest[0], rest[1:]
    inputs, rest = rest[:sources], rest[sources + after :]
    if with_gates:
        out_ref, gate_out_ref, held, buffer, gate_buffer, sems, out_sems = rest
    else:
        out_ref, held, buffer, sems, out_sems = rest
    expert = pl.program_id(0)
    share = inputs[0].shape[0]
    slots = out_ref.shape[0] // pl.num_programs(0)

    @pl.when(expert == 0)
    def _():
        copies = [
            pltpu.make_async_copy(ref, held.at[pl.ds(i * share, share)], sems.at[i])
            for i, ref in enumerate(inputs)
        ]
        for copy in copies:
            copy.start()
        for copy in copies:
            copy.wait()

    def copies_of(part, slot):
        start = pl.multiple_of(expert * slots + part * PART, PART)
        made = [
            pltpu.make_async_copy(
                buffer.at[slot], out_ref.at[pl.ds(start, PART)], out_sems.at[0, slot]
            )
        ]
        if with_gates:
            made.append(
                pltpu.make_async_copy(
                    gate_buffer.at[slot], gate_out_ref.at[pl.ds(start, PART)], out_sems.at[1, slot]
                )
            )
        return made

    parts = blocks_ref[expert] * (BLOCK // PART)

    def one(part, carry):
        slot = part % 2

        @pl.when(part >= 2)
        def _():
            for copy in copies_of(part - 2, slot):
                copy.wait()

        buffer[slot] = jnp.zeros(buffer.shape[1:], buffer.dtype)
        if with_gates:
            gate_buffer[slot] = jnp.zeros(gate_buffer.shape[1:], gate_buffer.dtype)
        rows = lax.broadcasted_iota(jnp.int32, (PART, BLOCK), 0) + part * PART

        def step(tile, carry):
            pick = jnp.where(rows == place_ref[expert, tile], 1.0, 0.0).astype(jnp.bfloat16)
            start = pl.multiple_of(tile * BLOCK, BLOCK)
            buffer[slot] += jnp.dot(
                pick, held[pl.ds(start, BLOCK), :], preferred_element_type=jnp.float32
            ).astype(buffer.dtype)
            if with_gates:
                gate_buffer[slot] += jnp.dot(
                    pick, gates_ref[pl.ds(start, BLOCK), :], preferred_element_type=jnp.float32
                )
            return carry

        lax.fori_loop(low_ref[expert, part], high_ref[expert, part], step, 0)
        for copy in copies_of(part, slot):
            copy.start()
        return carry

    lax.fori_loop(0, parts, one, 0)
    for back in (2, 1):
        for copy in copies_of(parts - back, (parts - back) % 2):
            copy.wait()


def gather_rows(tables, place, gates, sources, slots, first, count, after=()):
    low, high, blocks = tables
    low, high, blocks = (t[first : first + count] for t in (low, high, blocks))
    place = place[first : first + count]
    rows = place.shape[1] * BLOCK
    width = sources[0].shape[1]
    with_gates = gates is not None

    def whole(array):
        zeros = (0,) * array.ndim
        return pl.BlockSpec(array.shape, lambda *_: zeros)

    operands = [place] + ([gates] if with_gates else [])
    anywhere = pl.BlockSpec(memory_space=pl.ANY)
    in_specs = [whole(a) for a in operands] + [anywhere] * (len(sources) + len(after))
    out_shape = [jax.ShapeDtypeStruct((count * slots, width), jnp.bfloat16)]
    scratch = [
        pltpu.VMEM((rows, width), jnp.bfloat16),
        pltpu.VMEM((2, PART, width), jnp.bfloat16),
    ]
    if with_gates:
        out_shape.append(jax.ShapeDtypeStruct((count * slots, 128), jnp.float32))
        scratch.append(pltpu.VMEM((2, PART, 128), jnp.float32))
    return pl.pallas_call(
        functools.partial(gather_kernel, len(sources), with_gates, len(after)),
        grid_spec=pltpu.PrefetchScalarGridSpec(
            num_scalar_prefetch=3,
            grid=(count,),
            in_specs=in_specs,
            out_specs=[anywhere] * len(out_shape),
            scratch_shapes=scratch
            + [pltpu.SemaphoreType.DMA((len(sources),)), pltpu.SemaphoreType.DMA((2, 2))],
        ),
        out_shape=out_shape,
        compiler_params=pltpu.CompilerParams(vmem_limit_bytes=VMEM_LIMIT),
    )(low, high, blocks, *operands, *sources, *after)


def expert_kernel(
    first, split, depth, far_first, extra, blocks_ref, misc_ref, x_ref, c_ref, sg_ref, wg_ref,
    wu_ref, wd_ref, *rest
):
    yd_ref = rest[extra]
    rest = rest[extra + 1 :]
    width = x_ref.shape[1]
    if split:
        send_ref, keep_ref = rest[:2]
        rest = rest[2:]
    else:
        grads_ref = rest[0]
        rest = rest[1:]
    total_gu, total_d, x_held, c_held, low_held, gated_held = rest
    expert = first + pl.program_id(0)
    block = pl.program_id(1)
    hidden = wg_ref.shape[2]
    blocks = blocks_ref[expert]
    lanes = lax.broadcasted_iota(jnp.int32, (BLOCK, 128), 1)

    @pl.when(block < blocks)
    def _():
        x = x_ref[...]
        c = c_ref[...]
        gate = jnp.sum(jnp.where(lanes == expert, sg_ref[...], 0.0), axis=1, keepdims=True)
        gate_proj = jnp.dot(x, wg_ref[0], preferred_element_type=jnp.float32)
        up_proj = jnp.dot(x, wu_ref[0], preferred_element_type=jnp.float32)
        pulled = dot_nt(c, wd_ref[0])
        sigmoid = 1.0 / (1.0 + jnp.exp(-gate_proj))
        silu = gate_proj * sigmoid
        activated = (silu * up_proj).astype(jnp.bfloat16).astype(jnp.float32)
        gate_grad = jnp.sum(activated * pulled, axis=1, keepdims=True)
        coarse = gate_grad.astype(jnp.bfloat16).astype(jnp.float32)
        yd_ref[:, 2 * width :] = jnp.where(
            lanes == expert, coarse, jnp.where(lanes == expert + 64, gate_grad - coarse, 0.0)
        ).astype(yd_ref.dtype)
        gated = (gate * activated).astype(jnp.bfloat16)
        yd_ref[:, :width] = jnp.dot(
            gated, wd_ref[0], preferred_element_type=jnp.float32
        ).astype(yd_ref.dtype)
        activated_grad = gate * pulled
        gate_low = (
            activated_grad * up_proj * sigmoid * (1.0 + gate_proj * (1.0 - sigmoid))
        ).astype(jnp.bfloat16)
        up_low = (activated_grad * silu).astype(jnp.bfloat16)
        yd_ref[:, width : 2 * width] = (
            dot_nt(gate_low, wg_ref[0]) + dot_nt(up_low, wu_ref[0])
        ).astype(yd_ref.dtype)
        start = pl.multiple_of((block % 2) * BLOCK, BLOCK)
        held = pl.ds(start, BLOCK)
        x_held[held, :] = x
        c_held[held, :] = c
        low_held[held, :hidden] = gate_low
        low_held[held, hidden:] = up_low
        gated_held[held, :] = gated

    def gather(rows, fresh):
        for begin in range(0, width, BLOCK):
            span = slice(begin, begin + BLOCK)
            for total, left, right in (
                (total_gu, x_held, low_held),
                (total_d, c_held, gated_held),
            ):
                term = dot_tn(left[:rows, span], right[:rows, :])
                total[span, :] = term if fresh else total[span, :] + term

    odd = block % 2 == 1
    last = block == blocks - 1

    @pl.when((block == 0) & last)
    def _():
        gather(BLOCK, True)

    @pl.when((block == 1) & (block < blocks))
    def _():
        gather(2 * BLOCK, True)

    @pl.when((block > 1) & odd & (block < blocks))
    def _():
        gather(2 * BLOCK, False)

    @pl.when((block > 1) & jnp.logical_not(odd) & last)
    def _():
        gather(BLOCK, False)

    @pl.when(block == pl.num_programs(1) - 1)
    def _():
        parts = (
            (total_gu, 0),
            (total_gu, hidden),
            (total_d, 0),
        )
        for which, (ref, column) in enumerate(parts):
            if split:
                side = misc_ref[1 + far_first]
                for high in range(2):
                    for low in range(2):
                        for out, chosen in ((keep_ref, side), (send_ref, 1 - side)):
                            if far_first:
                                start = ((high * 2 + chosen) * 2 + low) * depth
                                place = (high, low, which)
                            else:
                                start = ((high * 2 + low) * 2 + chosen) * depth
                                place = (low, high, which)
                            out[place] = ref[
                                pl.ds(pl.multiple_of(start, 64), depth), pl.ds(column, hidden)
                            ].astype(out.dtype)
            else:
                grads_ref[0, which] = ref[:, pl.ds(column, hidden)].astype(grads_ref.dtype)


def expert_call(
    blocks, misc, x, c, sg, weights, carried, slots, first, count, x_first, c_first, depth,
    far_first=0, after=()
):
    w_gate, w_up, w_down = weights
    experts = blocks.shape[0]
    width = x.shape[1]
    hidden = w_gate.shape[2]
    most = slots // BLOCK
    split = depth is not None

    def rows_index(base):
        def index(expert, block, blocks, misc):
            limit = blocks[first + expert] - 1
            return ((first - base + expert) * most + jnp.minimum(block, limit), 0)

        return index

    def weight_index(expert, block, blocks, misc):
        return (misc[0] + first + expert, 0, 0)

    def grads_index(expert, block, blocks, misc):
        return (0, 0, expert, 0, 0)

    out_shape = [jax.ShapeDtypeStruct((experts * slots, 2 * width + 128), jnp.bfloat16)]
    out_specs = [pl.BlockSpec((BLOCK, 2 * width + 128), rows_index(0))]
    if split:
        out_shape += [jax.ShapeDtypeStruct((2, 2, 3 * count, depth, hidden), jnp.bfloat16)] * 2
        out_specs += [pl.BlockSpec((2, 2, 3, depth, hidden), grads_index)] * 2
    else:
        out_shape += [jax.ShapeDtypeStruct((count, 3, width, hidden), jnp.bfloat16)]
        out_specs += [pl.BlockSpec((1, 3, width, hidden), lambda e, b, *_: (e, 0, 0, 0))]
    operands = [x, c, sg, w_gate, w_up, w_down]
    in_specs = [
        pl.BlockSpec((BLOCK, width), rows_index(x_first)),
        pl.BlockSpec((BLOCK, width), rows_index(c_first)),
        pl.BlockSpec((BLOCK, 128), rows_index(x_first)),
        pl.BlockSpec((1, width, hidden), weight_index),
        pl.BlockSpec((1, width, hidden), weight_index),
        pl.BlockSpec((1, hidden, width), weight_index),
    ]
    aliases = {}
    if carried is not None:
        operands.append(carried)
        aliases = {8: 0}
    operands += list(after)
    extra = len(operands) - 6
    in_specs += [pl.BlockSpec(memory_space=pl.ANY)] * extra
    return pl.pallas_call(
        functools.partial(expert_kernel, first, split, depth, far_first, extra),
        grid_spec=pltpu.PrefetchScalarGridSpec(
            num_scalar_prefetch=2,
            grid=(count, most),
            in_specs=in_specs,
            out_specs=out_specs,
            scratch_shapes=[
                pltpu.VMEM((width, 2 * hidden), jnp.float32),
                pltpu.VMEM((width, hidden), jnp.float32),
                pltpu.VMEM((2 * BLOCK, width), jnp.bfloat16),
                pltpu.VMEM((2 * BLOCK, width), jnp.bfloat16),
                pltpu.VMEM((2 * BLOCK, 2 * hidden), jnp.bfloat16),
                pltpu.VMEM((2 * BLOCK, hidden), jnp.bfloat16),
            ],
        ),
        out_shape=out_shape,
        input_output_aliases=aliases,
        compiler_params=pltpu.CompilerParams(vmem_limit_bytes=VMEM_LIMIT),
    )(blocks, misc, *operands)


def combine_kernel(
    first, owner_ref, piece_ref, source_ref, groups_ref, begin_ref, tile_ref, place_ref, yd_ref, *rest
):
    yd_out, gate_out, buffer, total, sems = rest[-5:]
    columns = yd_out.shape[1]
    step = pl.program_id(0)
    tile = first + step

    head = begin_ref[first]
    final = first + pl.num_programs(0) - 1
    stop = begin_ref[final] + groups_ref[final]

    def copies(place):
        which_tile = tile_ref[place]
        group = place - begin_ref[which_tile]
        slot = (place - head) % DEEP
        made = []
        for i in range(GROUP):
            source = pl.multiple_of(
                source_ref[which_tile, group * GROUP + i] * PIECE_ROWS, PIECE_ROWS
            )
            made.append(
                pltpu.make_async_copy(
                    yd_ref.at[pl.ds(source, PIECE_ROWS)],
                    buffer.at[slot, pl.ds(i * PIECE_ROWS, PIECE_ROWS)],
                    sems.at[slot, i],
                )
            )
        return made

    @pl.when(step == 0)
    def _():
        for ahead in range(DEEP - 1):

            @pl.when(head + ahead < stop)
            def _():
                for copy in copies(head + ahead):
                    copy.start()

    def one(group, carry):
        place = begin_ref[tile] + group
        slot = (place - head) % DEEP

        @pl.when(place + DEEP - 1 < stop)
        def _():
            for copy in copies(place + DEEP - 1):
                copy.start()

        picks = []
        for i in range(GROUP):
            entry = group * GROUP + i
            rows = (
                lax.broadcasted_iota(jnp.int32, (PIECE_ROWS, BLOCK), 0)
                + piece_ref[tile, entry] * PIECE_ROWS
            )
            picks.append(jnp.where(rows == place_ref[owner_ref[tile, entry], step], 1.0, 0.0))
        picked = jnp.concatenate(picks, axis=0).T.astype(jnp.bfloat16)
        for copy in copies(place):
            copy.wait()
        fresh = group == 0
        for begin in range(0, total.shape[1], 640):
            span = slice(begin, begin + 640)
            term = jnp.dot(picked, buffer[slot, :, span], preferred_element_type=jnp.float32)
            total[:, span] = jnp.where(fresh, 0.0, total[:, span]) + term
        return carry

    lax.fori_loop(0, groups_ref[tile], one, 0)
    yd_out[...] = total[:, :columns].astype(yd_out.dtype)
    gate_out[...] = total[:, columns:]


def combine_rows(tables, place, yd, first, count, after=()):
    owner, piece, source, groups, width = tables
    ends = jnp.cumsum(groups)
    begin = ends - groups
    most = groups.shape[0] * (width // GROUP)
    tile_of = jnp.minimum(
        jnp.sum((ends[None, :] <= jnp.arange(most)[:, None]).astype(jnp.int32), axis=1),
        groups.shape[0] - 1,
    )
    experts = place.shape[0]
    whole_width = yd.shape[1]
    columns = whole_width - 128
    row_block = lambda wide: pl.BlockSpec((BLOCK, wide), lambda t, *_: (t, 0))
    return pl.pallas_call(
        functools.partial(combine_kernel, first),
        grid_spec=pltpu.PrefetchScalarGridSpec(
            num_scalar_prefetch=6,
            grid=(count,),
            in_specs=[pl.BlockSpec((experts, count, 1, BLOCK), lambda *_: (0, first // count, 0, 0))]
            + [pl.BlockSpec(memory_space=pl.ANY)] * (1 + len(after)),
            out_specs=[row_block(columns), row_block(128)],
            scratch_shapes=[
                pltpu.VMEM((DEEP, GROUP * PIECE_ROWS, whole_width), jnp.bfloat16),
                pltpu.VMEM((BLOCK, whole_width), jnp.float32),
                pltpu.SemaphoreType.DMA((DEEP, GROUP)),
            ],
        ),
        out_shape=[
            jax.ShapeDtypeStruct((count * BLOCK, columns), jnp.bfloat16),
            jax.ShapeDtypeStruct((count * BLOCK, 128), jnp.float32),
        ],
        compiler_params=pltpu.CompilerParams(vmem_limit_bytes=VMEM_LIMIT),
    )(owner, piece, source, groups, begin, tile_of, place, yd, *after)


def flip(value, bit):
    size = lax.axis_size("dp")
    return lax.ppermute(value, "dp", [(i, i ^ bit) for i in range(size)])


def swap(value):
    return lax.ppermute(value, "tensor", [(0, 1), (1, 0)])


def order(value, *after):
    return lax.optimization_barrier((value, *after))[0] if after else value


def add_low(left, right):
    return (left.astype(jnp.float32) + right.astype(jnp.float32)).astype(jnp.bfloat16)


def pick_index(value, index, axis):
    return lax.dynamic_index_in_dim(value, index, axis, keepdims=False)


def sum_stage(parts, bit, chosen, after):
    send, keep = parts
    got = order(flip(send, bit), *after)
    return tuple(
        add_low(pick_index(keep, which, 0), pick_index(got, which, 0))
        for which in (1 - chosen, chosen)
    )


class ChipSum:
    def __init__(self, parts, rank, far_first):
        side, low_bit, high_bit = (rank // 2) % 2, (rank // 4) % 2, rank // 8
        self.parts = parts
        self.first = (4, high_bit) if far_first else (2, low_bit)
        self.second = (8, side) if far_first else (4, high_bit)
        self.last = 2 if far_first else 8

    def one(self, *after):
        self.parts = sum_stage(self.parts, *self.first, after)
        return self.parts[0]

    def two(self, *after):
        self.parts = sum_stage(self.parts, *self.second, after)
        return self.parts[0]

    def three(self, *after):
        send, keep = self.parts
        return add_low(keep, order(flip(send, self.last), *after))


def core_sum(value, core):
    rows, columns = value.shape
    value = value.reshape(8, 2, rows // 16, columns)
    got = flip(pick_index(value, 1 - core, 1).astype(jnp.bfloat16), 1)
    return add_low(pick_index(value, core, 1), got)


def plane_sum(total, rank, *after):
    side, low_bit, high_bit = (rank // 2) % 2, (rank // 4) % 2, rank // 8
    part, columns = total.shape[1:]
    total = total.reshape(4, 2, part, columns)
    got = order(flip(pick_index(total, 1 - side, 1), 2), *after)
    total = add_low(pick_index(total, side, 1), got).reshape(2, 2, part, columns)
    got = flip(pick_index(total, 1 - low_bit, 1), 4)
    total = add_low(pick_index(total, low_bit, 1), got)
    got = flip(pick_index(total, 1 - high_bit, 0), 8)
    return pick_index(total, high_bit, 0).astype(jnp.float32) + got.astype(jnp.float32)


def fetch_other(weights, core, side, after=()):
    rows = weights[0].shape[0] // 4
    start = (side * 2 + core) * rows
    own = jnp.concatenate(
        [lax.dynamic_slice_in_dim(w, start, rows, 0) for w in weights], axis=1
    )
    pieces = swap(order(own, *after))
    turned = flip(pieces, 2)
    result = jnp.zeros((4 * rows, own.shape[1]), own.dtype)
    for value, place in (
        (pieces, side * 2 + core),
        (turned, (1 - side) * 2 + core),
        (flip(pieces, 1), side * 2 + 1 - core),
        (flip(turned, 1), (1 - side) * 2 + 1 - core),
    ):
        result = lax.dynamic_update_slice_in_dim(result, value, place * rows, 0)
    return result, own, pieces


ROWS = 256
HALF = 512


def lane_swap(values):
    width = values.shape[1]
    lane = lax.broadcasted_iota(jnp.int32, values.shape, 1) % HD
    ahead = pltpu.roll(values, width - HD // 2, 1)
    behind = pltpu.roll(values, HD // 2, 1)
    return jnp.where(lane < HD // 2, ahead, behind)


def turn_tables(rows):
    cosine, sine = rope_tables(rows, HD)
    return (
        jnp.concatenate([cosine] * 4, axis=1),
        jnp.concatenate([-sine, sine, -sine, sine], axis=1),
    )


def project_kernel(sizes, score_scale, normed_ref, weights_ref, cosine_ref, sine_ref, *outs):
    query_ref, key_ref, value_ref = outs[-3:]
    query_width, key_width = sizes
    projected = jnp.dot(normed_ref[...], weights_ref[...], preferred_element_type=jnp.float32)
    cosine, sine = cosine_ref[...], sine_ref[...]
    for start in range(0, query_width + key_width, 128):
        piece = projected[:, start : start + 128]
        turned = piece * cosine + lane_swap(piece) * sine
        if start < query_width:
            query_ref[:, start : start + 128] = (turned * score_scale).astype(jnp.bfloat16)
        else:
            begin = start - query_width
            key_ref[:, begin : begin + 128] = turned.astype(jnp.bfloat16)
    value_ref[...] = projected[:, query_width + key_width :].astype(jnp.bfloat16)


def project(normed, weights, tables, query_width, key_width, score_scale, after=()):
    rows, depth = normed.shape
    width = weights.shape[1]
    row_spec = lambda columns: pl.BlockSpec((ROWS, columns), lambda i: (i, 0))
    return pl.pallas_call(
        functools.partial(project_kernel, (query_width, key_width), score_scale),
        grid=(rows // ROWS,),
        in_specs=[
            row_spec(depth),
            pl.BlockSpec((depth, width), lambda i: (0, 0)),
            row_spec(128),
            row_spec(128),
        ]
        + [pl.BlockSpec(memory_space=pl.ANY)] * len(after),
        out_specs=[row_spec(query_width), row_spec(key_width), row_spec(key_width)],
        out_shape=[
            jax.ShapeDtypeStruct((rows, query_width), jnp.bfloat16),
            jax.ShapeDtypeStruct((rows, key_width), jnp.bfloat16),
            jax.ShapeDtypeStruct((rows, key_width), jnp.bfloat16),
        ],
        compiler_params=pltpu.CompilerParams(vmem_limit_bytes=VMEM_LIMIT),
    )(normed, weights, *tables, *after)


def attend_kernel(per_pair, query_ref, key_ref, value_ref, limit_ref, *rest):
    out_ref, lse_ref = rest[-2:]
    step = pl.program_id(1)

    def work(keys):
        columns = lax.broadcasted_iota(jnp.int32, (ROWS, HALF), 1) + (keys - HALF)
        allowed = columns <= limit_ref[...]
        lanes = lax.broadcasted_iota(jnp.int32, (ROWS, 128), 1)
        sums = jnp.zeros((ROWS, 128), jnp.float32)
        pieces = []
        for head in range(per_pair):
            group = head // (per_pair // 2)
            query = query_ref[:, head * HD : (head + 1) * HD]
            key = key_ref[:keys, group * HD : (group + 1) * HD]
            value = value_ref[:keys, group * HD : (group + 1) * HD]
            scores = dot_nt(query, key)
            last = jnp.where(allowed, scores[:, keys - HALF :], -1e30)
            scores = last if keys == HALF else jnp.concatenate([scores[:, : keys - HALF], last], 1)
            highest = jnp.max(scores, axis=1, keepdims=True)
            shifted = jnp.exp(scores - highest)
            total = jnp.sum(shifted, axis=1, keepdims=True)
            mixed = jnp.dot(
                shifted.astype(jnp.bfloat16), value, preferred_element_type=jnp.float32
            )
            pieces.append((mixed / total).astype(jnp.bfloat16))
            sums = jnp.where(lanes == head, highest + jnp.log(total), sums)
        out_ref[...] = jnp.concatenate(pieces, axis=1)
        lse_ref[0] = sums

    halfway = pl.num_programs(1) // 2

    @pl.when(step < halfway)
    def _():
        work(HALF)

    @pl.when(step >= halfway)
    def _():
        work(2 * HALF)


def attend(query, key, value, limits, after=()):
    rows, query_width = query.shape
    pairs = key.shape[1] // 128
    wide = query_width // pairs
    return pl.pallas_call(
        functools.partial(attend_kernel, wide // HD),
        grid=(pairs, rows // ROWS),
        in_specs=[
            pl.BlockSpec((ROWS, wide), lambda p, i: (i, p)),
            pl.BlockSpec((rows, 128), lambda p, i: (0, p)),
            pl.BlockSpec((rows, 128), lambda p, i: (0, p)),
            pl.BlockSpec((ROWS, 1), lambda p, i: (i, 0)),
        ]
        + [pl.BlockSpec(memory_space=pl.ANY)] * len(after),
        out_specs=[
            pl.BlockSpec((ROWS, wide), lambda p, i: (i, p)),
            pl.BlockSpec((1, ROWS, 128), lambda p, i: (p, i, 0)),
        ],
        out_shape=[
            jax.ShapeDtypeStruct((rows, query_width), jnp.bfloat16),
            jax.ShapeDtypeStruct((pairs, rows, 128), jnp.float32),
        ],
        compiler_params=pltpu.CompilerParams(vmem_limit_bytes=VMEM_LIMIT),
    )(query, key, value, limits, *after)


def back_kernel(
    per_pair, score_scale, after, query_ref, key_ref, value_ref, turned_key_ref, grad_ref, lse_ref,
    limit_ref, cosine_ref, sine_ref, all_cosine_ref, all_sine_ref, *rest
):
    query_out, key_out, value_out, key_total, value_total = rest[after:]
    step = pl.program_id(1)
    halfway = pl.num_programs(1) // 2

    @pl.when(step == 0)
    def _():
        key_total[...] = jnp.zeros_like(key_total)
        value_total[...] = jnp.zeros_like(value_total)

    def work(keys):
        rows = lax.broadcasted_iota(jnp.int32, (HALF, ROWS), 0) + (keys - HALF)
        allowed = rows <= limit_ref[...]
        made = []
        key_parts, value_parts = [], []
        for group in range(2):
            span = slice(group * HD, (group + 1) * HD)
            key, value = key_ref[:keys, span], value_ref[:keys, span]
            key_part = value_part = 0.0
            for head in range(group * per_pair // 2, (group + 1) * per_pair // 2):
                query = query_ref[:, head * HD : (head + 1) * HD]
                grad = grad_ref[:, head * HD : (head + 1) * HD]
                scores = dot_nt(key, query)
                last = jnp.where(allowed, scores[keys - HALF :], -1e30)
                scores = (
                    last
                    if keys == HALF
                    else jnp.concatenate([scores[: keys - HALF], last], axis=0)
                )
                weights = jnp.exp(scores - lse_ref[0, head : head + 1, :])
                pulled = dot_nt(value, grad)
                inner = jnp.sum(weights * pulled, axis=0, keepdims=True)
                score_low = (weights * (pulled - inner)).astype(jnp.bfloat16)
                value_part += jnp.dot(
                    weights.astype(jnp.bfloat16), grad, preferred_element_type=jnp.float32
                )
                key_part += jnp.dot(score_low, query, preferred_element_type=jnp.float32)
                made.append(
                    jnp.dot(
                        turned_key_ref[0, span, :keys],
                        score_low,
                        preferred_element_type=jnp.float32,
                    )
                )
            key_parts.append(key_part)
            value_parts.append(value_part)
        key_total[:keys] += jnp.concatenate(key_parts, axis=1)
        value_total[:keys] += jnp.concatenate(value_parts, axis=1)
        cosine, sine = cosine_ref[...], sine_ref[...]
        for index in range(per_pair // 2):
            both = jnp.concatenate(made[2 * index : 2 * index + 2], axis=0).T * score_scale
            query_out[:, index * 128 : (index + 1) * 128] = (
                both * cosine - lane_swap(both) * sine
            ).astype(jnp.bfloat16)

    @pl.when(step < halfway)
    def _():
        work(HALF)

    @pl.when(step >= halfway)
    def _():
        work(2 * HALF)

    @pl.when(step == pl.num_programs(1) - 1)
    def _():
        total = key_total[...]
        key_out[...] = (
            total * all_cosine_ref[...] - lane_swap(total) * all_sine_ref[...]
        ).astype(jnp.bfloat16)
        value_out[...] = value_total[...].astype(jnp.bfloat16)


def attend_back(saved, attended_grad, limits, tables, score_scale, chosen, after=()):
    query, key, value, lse = saved
    rows, query_width = query.shape
    pairs = key.shape[1] // 128
    wide = query_width // pairs
    turned_key = key.T.reshape(pairs, 128, rows)
    lse_rows = lse[:, :, :8].transpose(0, 2, 1)
    cosine, sine = tables
    begin, count = chosen
    block = lambda columns: pl.BlockSpec((ROWS, columns), lambda p, i: (i, p + begin))
    whole = pl.BlockSpec((rows, 128), lambda p, i: (0, p + begin))
    block_out = pl.BlockSpec((ROWS, wide), lambda p, i: (i, p))
    whole_out = pl.BlockSpec((rows, 128), lambda p, i: (0, p))
    table = pl.BlockSpec((ROWS, 128), lambda p, i: (i, 0))
    full_table = pl.BlockSpec((rows, 128), lambda p, i: (0, 0))
    return pl.pallas_call(
        functools.partial(back_kernel, wide // HD, score_scale, len(after)),
        grid=(count, rows // ROWS),
        in_specs=[
            block(wide),
            whole,
            whole,
            pl.BlockSpec((1, 128, rows), lambda p, i: (p + begin, 0, 0)),
            block(wide),
            pl.BlockSpec((1, 8, ROWS), lambda p, i: (p + begin, 0, i)),
            pl.BlockSpec((1, ROWS), lambda p, i: (0, i)),
            table,
            table,
            full_table,
            full_table,
        ]
        + [pl.BlockSpec(memory_space=pl.ANY)] * len(after),
        out_specs=[block_out, whole_out, whole_out],
        out_shape=[
            jax.ShapeDtypeStruct((rows, count * wide), jnp.bfloat16),
            jax.ShapeDtypeStruct((rows, count * 128), jnp.bfloat16),
            jax.ShapeDtypeStruct((rows, count * 128), jnp.bfloat16),
        ],
        scratch_shapes=[
            pltpu.VMEM((rows, 128), jnp.float32),
            pltpu.VMEM((rows, 128), jnp.float32),
        ],
        compiler_params=pltpu.CompilerParams(vmem_limit_bytes=VMEM_LIMIT),
    )(
        query, key, value, turned_key, attended_grad, lse_rows, limits.T, cosine, sine, cosine,
        sine, *after,
    )


def piece_limits(starts_row, rows):
    position = jnp.arange(rows, dtype=jnp.int32)
    limits = position
    for index in range(starts_row.shape[0]):
        start = starts_row[index]
        inside = (position >= start) & (position < start + PIECE)
        limits = jnp.where(inside, start + PIECE - 1, limits)
    return limits[:, None]


def slot_table(routes, expert_count, capacity):
    flattened = routes.reshape(-1)
    onehot = (flattened[:, None] == jnp.arange(expert_count, dtype=jnp.int32)[None, :]).astype(
        jnp.int32
    )
    placed = jnp.sum((jnp.cumsum(onehot, axis=0) - 1) * onehot, axis=1)
    entries = jnp.arange(flattened.shape[0], dtype=jnp.int32)
    return (
        jnp.full((expert_count * capacity,), flattened.shape[0], jnp.int32)
        .at[flattened * capacity + placed]
        .set(entries)
    )


def expert_forward(expert_inputs, w_gate, w_up, w_down):
    gate_proj = jnp.einsum(
        "ecd,edf->ecf", expert_inputs, w_gate, preferred_element_type=jnp.float32
    )
    up_proj = jnp.einsum("ecd,edf->ecf", expert_inputs, w_up, preferred_element_type=jnp.float32)
    activated = (gate_proj * jax.nn.sigmoid(gate_proj) * up_proj).astype(jnp.bfloat16)
    returned = jnp.einsum("ecf,efd->ecd", activated, w_down, preferred_element_type=jnp.float32)
    return (gate_proj, up_proj, activated, returned)


def shards_wide(
    tokens,
    norm_gains,
    w_query,
    w_key,
    w_value,
    w_out,
    mix_gains,
    w_router,
    w_gate,
    w_up,
    w_down,
    routes,
    starts,
    cotangent,
):
    share_rows = tokens.shape[0]
    model_width = tokens.shape[1]
    head_width = HD
    query_width = w_query.shape[1]
    key_width = w_key.shape[1]
    heads_here = query_width // head_width
    groups_here = key_width // head_width
    per_group = heads_here // groups_here
    experts_here = w_gate.shape[0]
    group_rows = routes.shape[0]
    choices_count = routes.shape[1]
    sequences_here = starts.shape[0]
    sequence_length = group_rows // sequences_here
    expert_count = w_router.shape[1]
    tensor_rank = lax.axis_index("tensor")
    total_tokens = group_rows * lax.axis_size("dp")
    score_scale = head_width ** (-0.5)
    inputs_share = tokens.astype(jnp.float32)
    normed_share = normalize(inputs_share, norm_gains).astype(jnp.bfloat16)
    normed = lax.all_gather(normed_share, "tensor", axis=0, tiled=True)
    joined_weights = jnp.concatenate([w_query, w_key, w_value], axis=1)
    projected = jnp.dot(normed, joined_weights, preferred_element_type=jnp.float32)
    cosine, sine_table = rope_tables(sequence_length, head_width)
    cosine_rows = jnp.tile(cosine, (sequences_here, 1))
    sine_rows = jnp.tile(sine_table, (sequences_here, 1))
    query_rows = rotate(
        projected[:, :query_width].reshape(group_rows, heads_here, head_width),
        cosine_rows,
        sine_rows,
    ).astype(jnp.bfloat16)
    key_rows = rotate(
        projected[:, query_width : query_width + key_width].reshape(
            group_rows, groups_here, head_width
        ),
        cosine_rows,
        sine_rows,
    ).astype(jnp.bfloat16)
    value_rows = (
        projected[:, query_width + key_width :]
        .astype(jnp.bfloat16)
        .reshape(group_rows, groups_here, head_width)
    )
    attended_parts = []
    logsum_parts = []
    for sequence in range(sequences_here):
        first_row = sequence * sequence_length
        query_block = query_rows[first_row : first_row + sequence_length].reshape(
            sequence_length, groups_here, per_group, head_width
        )
        key_block = key_rows[first_row : first_row + sequence_length]
        value_block = value_rows[first_row : first_row + sequence_length]
        allowed = allowed_pairs(starts[sequence], sequence_length, PIECE)
        scores = scores_of(query_block, key_block, allowed, score_scale)
        highest = jnp.max(scores, axis=-1, keepdims=True)
        shifted = jnp.exp(scores - highest)
        totals = jnp.sum(shifted, axis=-1, keepdims=True)
        weights = (shifted / totals).astype(jnp.bfloat16)
        mixed_values = jnp.einsum(
            "kgqs,skd->qkgd", weights, value_block, preferred_element_type=jnp.float32
        )
        attended_parts.append(
            mixed_values.reshape(sequence_length, query_width).astype(jnp.bfloat16)
        )
        logsum_parts.append(highest + jnp.log(totals))
    attended = jnp.concatenate(attended_parts, axis=0)
    attention_share = lax.psum_scatter(
        jnp.dot(attended, w_out, preferred_element_type=jnp.float32),
        "tensor",
        scatter_dimension=0,
        tiled=True,
    )
    middle_share = inputs_share + attention_share
    mixed_share = normalize(middle_share, mix_gains).astype(jnp.bfloat16)
    share_routes = lax.dynamic_slice_in_dim(routes, tensor_rank * share_rows, share_rows, 0)
    route_onehot = (
        share_routes[:, :, None] == jnp.arange(expert_count, dtype=jnp.int32)[None, None, :]
    ).astype(jnp.float32)
    logits = jnp.dot(mixed_share, w_router, preferred_element_type=jnp.float32)
    probabilities = softmax_rows(logits)
    chosen = jnp.sum(logits[:, None, :] * route_onehot, axis=-1)
    gate_soft = softmax_rows(chosen)
    gate_low = gate_soft.astype(jnp.bfloat16)
    counts, prob_sums = lax.psum(
        (jnp.sum(route_onehot, axis=(0, 1)), jnp.sum(probabilities, axis=0)), ("dp", "tensor")
    )
    fractions = counts / (total_tokens * choices_count)
    balance = expert_count * expert_count * fractions * prob_sums / total_tokens
    mixed_rows, gate_rows = (
        lax.all_gather(mixed_share, "tensor", axis=0, tiled=True),
        lax.all_gather(gate_low, "tensor", axis=0, tiled=True),
    )
    slots_all = slot_table(routes, expert_count, CAP)
    slots = lax.dynamic_slice_in_dim(
        slots_all, tensor_rank * experts_here * CAP, experts_here * CAP, 0
    )
    owners = slots // choices_count
    padded_rows = jnp.concatenate([mixed_rows, jnp.zeros((1, model_width), jnp.bfloat16)], axis=0)
    padded_gates = jnp.concatenate(
        [gate_rows.reshape(-1).astype(jnp.float32), jnp.zeros((1,), jnp.float32)], axis=0
    )
    slot_gates = padded_gates[slots]
    expert_inputs = padded_rows[owners].reshape(experts_here, CAP, model_width)
    gate_proj, up_proj, activated, returned = expert_forward(expert_inputs, w_gate, w_up, w_down)
    returned_flat = returned.reshape(experts_here * CAP, model_width)
    expert_partial = jax.ops.segment_sum(
        slot_gates[:, None] * returned_flat, owners, num_segments=group_rows + 1
    )[:group_rows]
    expert_share = lax.psum_scatter(
        expert_partial.astype(jnp.bfloat16), "tensor", scatter_dimension=0, tiled=True
    ).astype(jnp.float32)
    output_share = (middle_share + expert_share).astype(jnp.bfloat16)
    upstream = cotangent.astype(jnp.float32)
    upstream_rows = lax.all_gather(cotangent, "tensor", axis=0, tiled=True)
    padded_upstream = jnp.concatenate(
        [upstream_rows, jnp.zeros((1, model_width), jnp.bfloat16)], axis=0
    )
    slot_upstream = padded_upstream[owners].astype(jnp.float32)
    slot_cotangent = (
        (slot_gates[:, None] * slot_upstream)
        .astype(jnp.bfloat16)
        .reshape(experts_here, CAP, model_width)
    )
    slot_gate_grad = jnp.sum(slot_upstream * returned_flat, axis=1)
    activated_grad = jnp.einsum(
        "ecd,efd->ecf", slot_cotangent, w_down, preferred_element_type=jnp.float32
    )
    down_grad = jnp.einsum(
        "ecf,ecd->efd", activated, slot_cotangent, preferred_element_type=jnp.float32
    )
    sigmoid_gate = jax.nn.sigmoid(gate_proj)
    gate_proj_low = (
        activated_grad * up_proj * sigmoid_gate * (1.0 + gate_proj * (1.0 - sigmoid_gate))
    ).astype(jnp.bfloat16)
    up_proj_low = (activated_grad * gate_proj * sigmoid_gate).astype(jnp.bfloat16)
    inputs_grad = jnp.einsum(
        "ecf,edf->ecd", gate_proj_low, w_gate, preferred_element_type=jnp.float32
    ) + jnp.einsum("ecf,edf->ecd", up_proj_low, w_up, preferred_element_type=jnp.float32)
    gate_grad = jnp.einsum(
        "ecd,ecf->edf", expert_inputs, gate_proj_low, preferred_element_type=jnp.float32
    )
    up_grad = jnp.einsum(
        "ecd,ecf->edf", expert_inputs, up_proj_low, preferred_element_type=jnp.float32
    )
    mixed_partial = jax.ops.segment_sum(
        inputs_grad.reshape(experts_here * CAP, model_width), owners, num_segments=group_rows + 1
    )[:group_rows]
    gate_partial = jax.ops.segment_sum(
        slot_gate_grad, slots, num_segments=group_rows * choices_count + 1
    )[: group_rows * choices_count].reshape(group_rows, choices_count)
    mixed_grad_share, gates_grad_share = (
        lax.psum_scatter(mixed_partial, "tensor", scatter_dimension=0, tiled=True),
        lax.psum_scatter(gate_partial, "tensor", scatter_dimension=0, tiled=True),
    )
    gate_total, up_total = (
        lax.psum_scatter(
            gate_grad.astype(jnp.bfloat16), "dp", scatter_dimension=1, tiled=True
        ).astype(jnp.float32),
        lax.psum_scatter(
            up_grad.astype(jnp.bfloat16), "dp", scatter_dimension=1, tiled=True
        ).astype(jnp.float32),
    )
    down_total = lax.psum_scatter(
        down_grad.astype(jnp.bfloat16), "dp", scatter_dimension=2, tiled=True
    ).astype(jnp.float32)
    chosen_grad = gate_soft * (
        gates_grad_share - jnp.sum(gate_soft * gates_grad_share, axis=-1, keepdims=True)
    )
    logit_grad = jnp.sum(chosen_grad[:, :, None] * route_onehot, axis=1)
    prob_target = ALPHA * expert_count * fractions / total_tokens
    logit_grad = logit_grad + probabilities * (
        prob_target[None, :] - jnp.sum(probabilities * prob_target[None, :], axis=-1, keepdims=True)
    )
    mixed_float = mixed_share.astype(jnp.float32)
    router_grad = jnp.dot(
        mixed_float.T, logit_grad, precision=HIGHEST, preferred_element_type=jnp.float32
    )
    mixed_grad_share = mixed_grad_share + jnp.dot(
        logit_grad,
        w_router.astype(jnp.float32).T,
        precision=HIGHEST,
        preferred_element_type=jnp.float32,
    )
    mix_pullback = jax.vjp(normalize, middle_share, mix_gains)[1]
    middle_from_norm, mix_gain_grad = mix_pullback(mixed_grad_share)
    middle_grad = upstream + middle_from_norm
    middle_low = middle_grad.astype(jnp.bfloat16)
    middle_rows = lax.all_gather(middle_low, "tensor", axis=0, tiled=True)
    out_grad = contract_rows(attended, middle_rows)
    attended_grad = contract_cols(middle_rows, w_out).astype(jnp.bfloat16)
    query_parts = []
    key_parts = []
    value_parts = []
    for sequence in range(sequences_here):
        first_row = sequence * sequence_length
        query_block = query_rows[first_row : first_row + sequence_length].reshape(
            sequence_length, groups_here, per_group, head_width
        )
        key_block = key_rows[first_row : first_row + sequence_length]
        value_block = value_rows[first_row : first_row + sequence_length]
        allowed = allowed_pairs(starts[sequence], sequence_length, PIECE)
        scores = scores_of(query_block, key_block, allowed, score_scale)
        weights_full = jnp.exp(scores - logsum_parts[sequence])
        weights_low = weights_full.astype(jnp.bfloat16)
        grad_block = attended_grad[first_row : first_row + sequence_length].reshape(
            sequence_length, groups_here, per_group, head_width
        )
        value_parts.append(
            jnp.einsum(
                "kgqs,qkgd->skd", weights_low, grad_block, preferred_element_type=jnp.float32
            )
        )
        weight_grad = jnp.einsum(
            "qkgd,skd->kgqs", grad_block, value_block, preferred_element_type=jnp.float32
        )
        score_low = (
            weights_full
            * (weight_grad - jnp.sum(weights_full * weight_grad, axis=-1, keepdims=True))
        ).astype(jnp.bfloat16)
        query_parts.append(
            jnp.einsum("kgqs,skd->qkgd", score_low, key_block, preferred_element_type=jnp.float32)
            * score_scale
        )
        key_parts.append(
            jnp.einsum("kgqs,qkgd->skd", score_low, query_block, preferred_element_type=jnp.float32)
            * score_scale
        )
    query_grads = (
        rotate(
            jnp.concatenate(query_parts, axis=0).reshape(group_rows, heads_here, head_width),
            cosine_rows,
            -sine_rows,
        )
        .astype(jnp.bfloat16)
        .reshape(group_rows, query_width)
    )
    key_grads = (
        rotate(jnp.concatenate(key_parts, axis=0), cosine_rows, -sine_rows)
        .astype(jnp.bfloat16)
        .reshape(group_rows, key_width)
    )
    value_grads = (
        jnp.concatenate(value_parts, axis=0).astype(jnp.bfloat16).reshape(group_rows, key_width)
    )
    joined_grads = jnp.concatenate([query_grads, key_grads, value_grads], axis=1)
    joined_weight_grad = contract_rows(normed, joined_grads)
    normed_grad_share = lax.psum_scatter(
        contract_cols(joined_grads, joined_weights).astype(jnp.bfloat16),
        "tensor",
        scatter_dimension=0,
        tiled=True,
    ).astype(jnp.float32)
    input_pullback = jax.vjp(normalize, inputs_share, norm_gains)[1]
    input_from_norm, norm_gain_grad = input_pullback(normed_grad_share)
    input_grad_share = middle_grad + input_from_norm
    query_total, key_total, value_total, out_turned = (
        lax.psum_scatter(
            joined_weight_grad[:, :query_width].astype(jnp.bfloat16),
            "dp",
            scatter_dimension=0,
            tiled=True,
        ).astype(jnp.float32),
        lax.psum_scatter(
            joined_weight_grad[:, query_width : query_width + key_width].astype(jnp.bfloat16),
            "dp",
            scatter_dimension=0,
            tiled=True,
        ).astype(jnp.float32),
        lax.psum_scatter(
            joined_weight_grad[:, query_width + key_width :].astype(jnp.bfloat16),
            "dp",
            scatter_dimension=0,
            tiled=True,
        ).astype(jnp.float32),
        lax.psum_scatter(
            out_grad.T.astype(jnp.bfloat16), "dp", scatter_dimension=0, tiled=True
        ).astype(jnp.float32),
    )
    out_total = out_turned.T
    norm_gain_total, mix_gain_total, router_total = lax.psum(
        (norm_gain_grad, mix_gain_grad, router_grad), ("dp", "tensor")
    )
    return (
        output_share,
        balance,
        input_grad_share,
        norm_gain_total,
        query_total,
        key_total,
        value_total,
        out_total,
        mix_gain_total,
        router_total,
        gate_total,
        up_total,
        down_total,
    )


def all_sum(value):
    for bit in (1, 2, 4, 8):
        value = value + flip(value, bit)
    return value + swap(value)


def spread(value):
    across = swap(value)
    return [value, across, flip(value, 1), flip(across, 1)]


CHUNK = 2
FAR_FIRST = -1


def shards_pair(
    tokens,
    norm_gains,
    w_query,
    w_key,
    w_value,
    w_out,
    mix_gains,
    w_router,
    w_gate,
    w_up,
    w_down,
    routes,
    starts,
    cotangent,
):
    share_rows, model_width = tokens.shape
    query_width = w_query.shape[1]
    key_width = w_key.shape[1]
    sizes = (query_width, key_width, HD)
    experts_here = w_gate.shape[0]
    experts = experts_here // 2
    choices_count = routes.shape[1]
    expert_count = w_router.shape[1]
    dp_size = lax.axis_size("dp")
    rank = lax.axis_index("dp")
    core, side = rank % 2, (rank // 2) % 2
    tensor_rank = lax.axis_index("tensor")
    total_tokens = routes.shape[0] * dp_size
    score_scale = HD ** (-0.5)
    depth = model_width // dp_size * 2
    slots = round_up(2 * CAP, BLOCK)

    joined_own = jnp.concatenate([w_query, w_key, w_value], axis=1)
    joined_other, joined_send, joined_piece = fetch_other([w_query, w_key, w_value], core, side)
    out_other, _, out_piece = fetch_other([w_out], core, side, (joined_send,))

    own_routes = lax.dynamic_slice_in_dim(routes, tensor_rank * share_rows, share_rows, 0)
    across_routes = lax.dynamic_slice_in_dim(routes, (1 - tensor_rank) * share_rows, share_rows, 0)
    both_routes = jnp.concatenate([own_routes, across_routes], axis=0)
    group_routes = jnp.concatenate([both_routes, flip(both_routes, 1)], axis=0)
    first_expert = tensor_rank * experts_here + core * experts

    route_onehot = (
        own_routes[:, :, None] == jnp.arange(expert_count, dtype=jnp.int32)[None, None, :]
    ).astype(jnp.float32)
    counts = all_sum(jnp.sum(route_onehot, axis=(0, 1)))
    cotangent_rows = spread(order(cotangent, joined_piece))

    inputs_share = tokens.astype(jnp.float32)
    normed = normalize(inputs_share, norm_gains).astype(jnp.bfloat16)
    tables = turn_tables(share_rows)
    starts_row = lax.dynamic_index_in_dim(starts, tensor_rank, 0, keepdims=False)
    limits = piece_limits(starts_row, share_rows)

    def half_forward(joined_weights, after=(), later=()):
        query, key, value = project(
            normed, joined_weights, tables, query_width, key_width, score_scale, after
        )
        attended, lse = attend(query, key, value, limits, later)
        return attended, (query, key, value, lse)

    attended_own, saved_own = half_forward(joined_own, (), (joined_piece,))
    attended_other, saved_other = half_forward(joined_other, (counts,))
    middle_share = (
        inputs_share
        + jnp.dot(attended_own, w_out, preferred_element_type=jnp.float32)
        + jnp.dot(attended_other, out_other, preferred_element_type=jnp.float32)
    )
    mixed_share = normalize(middle_share, mix_gains).astype(jnp.bfloat16)

    logits = jnp.dot(mixed_share, w_router, preferred_element_type=jnp.float32)
    probabilities = softmax_rows(logits)
    chosen = jnp.sum(logits[:, None, :] * route_onehot, axis=-1)
    gate_soft = softmax_rows(chosen)
    gate_low = gate_soft.astype(jnp.bfloat16)
    fractions = counts / (total_tokens * choices_count)

    group_gates = jnp.concatenate(spread(gate_low), axis=0)
    gates = gate_table(group_routes, group_gates, first_expert, experts)
    place, begins, ends = placement(group_routes, first_expert, experts)
    gather_from = gather_tables(begins, ends, slots)
    blocks = gather_from[2]
    cot_slots = gather_rows(gather_from, place, None, cotangent_rows, slots, 0, experts)[0]
    mixed_across = order(swap(mixed_share), cot_slots)
    mixed_rows = [mixed_share, mixed_across, flip(mixed_share, 1), flip(mixed_across, 1)]
    misc = jnp.stack([core * experts, side, (rank // 4) % 2])
    weights = (w_gate, w_up, w_down)
    first_part = gather_rows(
        gather_from, place, gates, mixed_rows, slots, 0, CHUNK, (cot_slots, counts)
    )
    later_part = None
    carried = None
    chips = []
    for index in range(experts // CHUNK):
        if index == 1:
            later_part = gather_rows(
                gather_from, place, gates, mixed_rows, slots, CHUNK, experts - CHUNK, (carried,)
            )
        (x_slots, slot_gates), x_first = (later_part, CHUNK) if index else (first_part, 0)
        waits = []
        if index == 2:
            waits = [chips[0].one(carried)]
        elif index == 4:
            waits = [chips[0].two(carried)]
        far_first = int(index == FAR_FIRST)
        carried, send, keep = expert_call(
            blocks, misc, x_slots, cot_slots, slot_gates, weights, carried, slots,
            index * CHUNK, CHUNK, x_first, 0, depth, far_first, waits,
        )
        chips.append(ChipSum((send, keep), rank, far_first))
    waits = [chips[1].one(carried)]

    combine_from = combine_tables(begins, ends, slots)
    tiles = place.shape[1] // 4
    names = first_expert + jnp.arange(experts, dtype=jnp.int32)

    def combined(quarter, after):
        yd, gate_grads = combine_rows(combine_from, place, carried, quarter * tiles, tiles, after)
        gate_grads = gate_grads[:, :experts] + gate_grads[:, 64 : 64 + experts]
        rows = group_routes[quarter * share_rows : (quarter + 1) * share_rows]
        hit = rows[:, :, None] == names[None, None, :]
        return yd, jnp.sum(jnp.where(hit, gate_grads[:, None, :], 0.0), axis=2)

    far = combined(3, waits)
    far_yd, far_gg = (flip(value, 1) for value in far)
    cross = combined(1, [far[0]])
    dx_send = add_low(cross[0][:, model_width:], far_yd[:, model_width:])
    dx_across = swap(dx_send)
    gg_across = swap(cross[1] + far_gg)
    next_door = combined(2, [dx_send])
    door_yd, door_gg = (flip(value, 1) for value in next_door)
    y_send = add_low(cross[0][:, :model_width], far_yd[:, :model_width])
    near = combined(0, [next_door[0]])
    y_across = swap(order(y_send, near[0]))
    waits = [chips[2].one(near[0]), chips[1].two(near[0])]
    done = [chips[0].three(near[0])]
    waits += done
    near_yd = order(near[0], *waits)
    mixed_grad_share = (
        near_yd[:, model_width:].astype(jnp.float32)
        + door_yd[:, model_width:].astype(jnp.float32)
        + dx_across.astype(jnp.float32)
    )
    gates_grad_share = near[1] + door_gg + gg_across

    upstream = cotangent.astype(jnp.float32)
    chosen_grad = gate_soft * (
        gates_grad_share - jnp.sum(gate_soft * gates_grad_share, axis=-1, keepdims=True)
    )
    logit_grad = jnp.sum(chosen_grad[:, :, None] * route_onehot, axis=1)
    prob_target = ALPHA * expert_count * fractions / total_tokens
    logit_grad = logit_grad + probabilities * (
        prob_target[None, :] - jnp.sum(probabilities * prob_target[None, :], axis=-1, keepdims=True)
    )
    router_grad = jnp.dot(
        mixed_share.astype(jnp.float32).T,
        logit_grad,
        precision=HIGHEST,
        preferred_element_type=jnp.float32,
    )
    mixed_grad_share = mixed_grad_share + jnp.dot(
        logit_grad,
        w_router.astype(jnp.float32).T,
        precision=HIGHEST,
        preferred_element_type=jnp.float32,
    )
    mix_pullback = jax.vjp(normalize, middle_share, mix_gains)[1]
    middle_from_norm, mix_gain_grad = mix_pullback(mixed_grad_share)
    middle_grad = upstream + middle_from_norm
    middle_low = middle_grad.astype(jnp.bfloat16)

    def half_back(saved, out_weights):
        attended_grad = dot_nt(middle_low, out_weights).astype(jnp.bfloat16)

        def part(chosen, after):
            return attend_back(
                saved, attended_grad, limits, tables, score_scale, chosen, after
            )

        return part

    pairs = key_width // 128
    other_grads = jnp.concatenate(
        half_back(saved_other, out_other)((0, pairs), waits), axis=1
    )
    waits = [chips[3].one(other_grads), chips[2].two(other_grads)]
    done.append(chips[1].three(other_grads))
    waits.append(done[1])
    other_grads = order(other_grads, *waits)
    expert_share = (
        near[0][:, :model_width].astype(jnp.float32)
        + door_yd[:, :model_width].astype(jnp.float32)
        + order(y_across, other_grads).astype(jnp.float32)
    )
    output_share = (middle_share + expert_share).astype(jnp.bfloat16)
    joined_held = core_sum(dot_tn(normed, other_grads), core)
    joined_across = swap(joined_held)
    marked = order(middle_low, other_grads)
    out_held = core_sum(dot_tn(marked, attended_other), core)
    out_across = swap(order(out_held, joined_held))
    out_kept = core_sum(dot_tn(marked, attended_own), core)
    waits = [joined_held, out_held, out_kept, output_share]
    own_part = half_back(saved_own, w_out)
    front = own_part((0, pairs // 2), waits)
    back = own_part((pairs // 2, pairs - pairs // 2), [joined_across, front[0]])
    own_grads = jnp.concatenate(
        [part for both in zip(front, back) for part in both], axis=1
    )
    out_half = add_low(out_kept, order(out_across, own_grads))
    own_weight_grads = dot_tn(normed, own_grads)
    own_held = core_sum(own_weight_grads, core)
    joined_total = plane_sum(add_low(own_held, joined_across), rank)
    out_total = plane_sum(out_half, rank, own_weight_grads)
    chips[4].one(own_weight_grads)
    chips[3].two(own_grads)
    chips[4].two(own_weight_grads)
    sums = done + [chips[i].three(own_weight_grads) for i in (2, 3, 4)]
    other_normed = dot_nt(other_grads, joined_other)
    own_normed = dot_nt(order(own_grads, own_held), joined_own)
    input_pullback = jax.vjp(normalize, inputs_share, norm_gains)[1]
    input_from_norm, norm_gain_grad = input_pullback(other_normed + own_normed)
    input_grad_share = middle_grad + input_from_norm
    key_end = query_width + key_width
    small = all_sum(
        jnp.concatenate(
            [jnp.sum(probabilities, axis=0), mix_gain_grad, norm_gain_grad, router_grad.reshape(-1)]
        )
    )
    prob_sums = small[:expert_count]
    mix_gain_total = small[expert_count : expert_count + model_width]
    norm_gain_total = small[expert_count + model_width : expert_count + 2 * model_width]
    router_total = small[expert_count + 2 * model_width :].reshape(router_grad.shape)
    balance = expert_count * expert_count * fractions * prob_sums / total_tokens

    mine = jnp.concatenate(sums, axis=0).reshape(experts, 3, 2, depth // 2, -1)
    theirs = flip(pick_index(mine, 1 - core, 2), 1)
    mine = pick_index(mine, core, 2)
    def placed(kind):
        own_kind, other_kind = mine[:, kind], theirs[:, kind]
        return jnp.where(
            core == 0,
            jnp.concatenate([own_kind, other_kind], axis=0),
            jnp.concatenate([other_kind, own_kind], axis=0),
        ).astype(jnp.float32)

    return (
        output_share,
        balance,
        input_grad_share,
        norm_gain_total,
        joined_total[:, :query_width],
        joined_total[:, query_width:key_end],
        joined_total[:, key_end:],
        out_total.T,
        mix_gain_total,
        router_total,
        placed(0),
        placed(1),
        placed(2).transpose(0, 2, 1),
    )


def solution(mesh):
    sizes = dict(mesh.shape)
    paired = sizes["tensor"] == 2 and sizes["dp"] == 16
    return jax.shard_map(
        shards_pair if paired else shards_wide,
        mesh=mesh,
        in_specs=(
            P(("dp", "tensor"), None),
            P(),
            P(None, "tensor"),
            P(None, "tensor"),
            P(None, "tensor"),
            P("tensor", None),
            P(),
            P(),
            P("tensor", None, None),
            P("tensor", None, None),
            P("tensor", None, None),
            P("dp", None),
            P("dp", None),
            P(("dp", "tensor"), None),
        ),
        out_specs=(
            P(("dp", "tensor"), None),
            P(),
            P(("dp", "tensor"), None),
            P(),
            P("dp", "tensor"),
            P("dp", "tensor"),
            P("dp", "tensor"),
            P("tensor", "dp"),
            P(),
            P(),
            P("tensor", "dp", None),
            P("tensor", "dp", None),
            P("tensor", None, "dp"),
        ),
        check_vma=False,
    )
```

```python
import functools

import jax
import jax.numpy as jnp
from jax import lax
from jax.experimental import pallas as pl
from jax.experimental.pallas import tpu as pltpu
from jax.sharding import PartitionSpec as P

HD = 64
PIECE = 256
CAP = 614


EPSILON = 1e-06
ALPHA = 0.01
HIGHEST = lax.Precision.HIGHEST


def normalize(values, gains):
    return values * lax.rsqrt(jnp.mean(values * values, axis=-1, keepdims=True) + EPSILON) * gains


def softmax_rows(values):
    shifted = jnp.exp(values - jnp.max(values, axis=-1, keepdims=True))
    return shifted / jnp.sum(shifted, axis=-1, keepdims=True)


def contract_rows(left, right):
    return lax.dot_general(
        left, right, (((0,), (0,)), ((), ())), preferred_element_type=jnp.float32
    )


def contract_cols(left, right):
    return lax.dot_general(
        left, right, (((1,), (1,)), ((), ())), preferred_element_type=jnp.float32
    )


def rope_tables(sequence_length, head_width):
    half_width = head_width // 2
    frequency = 10000.0 ** (-(jnp.arange(half_width, dtype=jnp.float32) * 2.0 / head_width))
    angles = jnp.arange(sequence_length, dtype=jnp.float32)[:, None] * frequency[None, :]
    return (jnp.cos(angles), jnp.sin(angles))


def rotate(values, cosine, sine_table):
    half_width = values.shape[-1] // 2
    first_half = values[..., :half_width]
    second_half = values[..., half_width:]
    cosine_rows = cosine[:, None, :]
    sine_rows = sine_table[:, None, :]
    return jnp.concatenate(
        [
            first_half * cosine_rows - second_half * sine_rows,
            second_half * cosine_rows + first_half * sine_rows,
        ],
        axis=-1,
    )


def allowed_pairs(starts_row, sequence_length, piece_length):
    position = jnp.arange(sequence_length, dtype=jnp.int32)
    labels = jnp.full((sequence_length,), -1, jnp.int32)
    for piece_index in range(starts_row.shape[0]):
        inside = (position >= starts_row[piece_index]) & (
            position < starts_row[piece_index] + piece_length
        )
        labels = jnp.where(inside, piece_index, labels)
    causal = position[None, :] <= position[:, None]
    shared = (labels[:, None] == labels[None, :]) & (labels[:, None] >= 0)
    return causal | shared


def scores_of(query_block, key_block, allowed, score_scale):
    raw_scores = (
        jnp.einsum("qkgd,skd->kgqs", query_block, key_block, preferred_element_type=jnp.float32)
        * score_scale
    )
    return jnp.where(allowed, raw_scores, -1e30)


BLOCK = 256
PART = 128
PIECE_ROWS = 32
GROUP = 8
DEEP = 4
VMEM_LIMIT = 60 * 1024 * 1024


def dot_nt(left, right):
    return lax.dot_general(
        left, right, (((1,), (1,)), ((), ())), preferred_element_type=jnp.float32
    )


def dot_tn(left, right):
    return lax.dot_general(
        left, right, (((0,), (0,)), ((), ())), preferred_element_type=jnp.float32
    )


def round_up(value, multiple):
    return -(-value // multiple) * multiple


def placement(routes_rows, first_expert, experts):
    rows = routes_rows.shape[0]
    tiles = rows // BLOCK
    turned = routes_rows.T
    names = first_expert + jnp.arange(experts, dtype=jnp.int32)
    hit = turned[None, :, :] == names[:, None, None]
    member = jnp.any(hit, axis=1)
    upper = jnp.triu(jnp.ones((BLOCK, BLOCK), jnp.bfloat16))
    inside = jnp.dot(
        member.astype(jnp.bfloat16).reshape(experts * tiles, BLOCK),
        upper,
        preferred_element_type=jnp.float32,
    ).astype(jnp.int32).reshape(experts, tiles, BLOCK)
    sums = inside[:, :, -1]
    ends = jnp.cumsum(sums, axis=1)
    begins = ends - sums
    place = jnp.where(
        member.reshape(experts, tiles, BLOCK), begins[:, :, None] + inside - 1, -1
    )
    place = jnp.concatenate(
        [place, jnp.full((1, tiles, BLOCK), -1, jnp.int32)], axis=0
    ).reshape(experts + 1, tiles, 1, BLOCK)
    return place, begins, ends


def gate_table(routes_rows, gates_rows, first_expert, experts):
    names = first_expert + jnp.arange(experts, dtype=jnp.int32)
    hit = routes_rows.T[None, :, :] == names[:, None, None]
    table = jnp.sum(jnp.where(hit, gates_rows.astype(jnp.float32).T[None, :, :], 0.0), axis=1)
    return jnp.pad(table, ((0, 128 - experts), (0, 0))).T.astype(jnp.bfloat16)


def gather_tables(begins, ends, slots):
    counts = ends[:, -1]
    parts = jnp.arange(slots // PART, dtype=jnp.int32) * PART
    low = jnp.sum((ends[:, None, :] <= parts[None, :, None]).astype(jnp.int32), axis=2)
    high = jnp.sum((begins[:, None, :] < parts[None, :, None] + PART).astype(jnp.int32), axis=2)
    high = jnp.where(parts[None, :] < counts[:, None], high, low)
    blocks = jnp.maximum(-(-counts // BLOCK), 1)
    return low, high, blocks


def combine_tables(begins, ends, slots):
    experts, tiles = begins.shape
    width = round_up(experts * (BLOCK // PIECE_ROWS + 1), GROUP)
    first = begins // PIECE_ROWS
    amount = jnp.where(ends > begins, (ends - 1) // PIECE_ROWS - first + 1, 0)
    stop = jnp.cumsum(amount, axis=0)
    place = jnp.arange(width, dtype=jnp.int32)
    owner = jnp.sum(
        (stop.T[:, None, :] <= place[None, :, None]).astype(jnp.int32), axis=2
    )
    chosen = owner[:, :, None] == jnp.arange(experts, dtype=jnp.int32)[None, None, :]
    offset = jnp.sum(
        jnp.where(chosen, (first - (stop - amount)).T[:, None, :], 0), axis=2
    )
    valid = owner < experts
    piece = jnp.where(valid, offset + place[None, :], 0)
    source = jnp.where(valid, owner, 0) * (slots // PIECE_ROWS) + piece
    groups = jnp.maximum(-(-stop[-1] // GROUP), 1)
    return owner, piece, source, groups, width


def gather_kernel(sources, with_gates, after, low_ref, high_ref, blocks_ref, place_ref, *rest):
    if with_gates:
        gates_ref, rest = rest[0], rest[1:]
    inputs, rest = rest[:sources], rest[sources + after :]
    if with_gates:
        out_ref, gate_out_ref, held, buffer, gate_buffer, sems, out_sems = rest
    else:
        out_ref, held, buffer, sems, out_sems = rest
    expert = pl.program_id(0)
    share = inputs[0].shape[0]
    slots = out_ref.shape[0] // pl.num_programs(0)

    @pl.when(expert == 0)
    def _():
        copies = [
            pltpu.make_async_copy(ref, held.at[pl.ds(i * share, share)], sems.at[i])
            for i, ref in enumerate(inputs)
        ]
        for copy in copies:
            copy.start()
        for copy in copies:
            copy.wait()

    def copies_of(part, slot):
        start = pl.multiple_of(expert * slots + part * PART, PART)
        made = [
            pltpu.make_async_copy(
                buffer.at[slot], out_ref.at[pl.ds(start, PART)], out_sems.at[0, slot]
            )
        ]
        if with_gates:
            made.append(
                pltpu.make_async_copy(
                    gate_buffer.at[slot], gate_out_ref.at[pl.ds(start, PART)], out_sems.at[1, slot]
                )
            )
        return made

    parts = blocks_ref[expert] * (BLOCK // PART)

    def one(part, carry):
        slot = part % 2

        @pl.when(part >= 2)
        def _():
            for copy in copies_of(part - 2, slot):
                copy.wait()

        buffer[slot] = jnp.zeros(buffer.shape[1:], buffer.dtype)
        if with_gates:
            gate_buffer[slot] = jnp.zeros(gate_buffer.shape[1:], gate_buffer.dtype)
        rows = lax.broadcasted_iota(jnp.int32, (PART, BLOCK), 0) + part * PART

        def step(tile, carry):
            pick = jnp.where(rows == place_ref[expert, tile], 1.0, 0.0).astype(jnp.bfloat16)
            start = pl.multiple_of(tile * BLOCK, BLOCK)
            buffer[slot] += jnp.dot(
                pick, held[pl.ds(start, BLOCK), :], preferred_element_type=jnp.float32
            ).astype(buffer.dtype)
            if with_gates:
                gate_buffer[slot] += jnp.dot(
                    pick, gates_ref[pl.ds(start, BLOCK), :], preferred_element_type=jnp.float32
                )
            return carry

        lax.fori_loop(low_ref[expert, part], high_ref[expert, part], step, 0)
        for copy in copies_of(part, slot):
            copy.start()
        return carry

    lax.fori_loop(0, parts, one, 0)
    for back in (2, 1):
        for copy in copies_of(parts - back, (parts - back) % 2):
            copy.wait()


def gather_rows(tables, place, gates, sources, slots, first, count, after=()):
    low, high, blocks = tables
    low, high, blocks = (t[first : first + count] for t in (low, high, blocks))
    place = place[first : first + count]
    rows = place.shape[1] * BLOCK
    width = sources[0].shape[1]
    with_gates = gates is not None

    def whole(array):
        zeros = (0,) * array.ndim
        return pl.BlockSpec(array.shape, lambda *_: zeros)

    operands = [place] + ([gates] if with_gates else [])
    anywhere = pl.BlockSpec(memory_space=pl.ANY)
    in_specs = [whole(a) for a in operands] + [anywhere] * (len(sources) + len(after))
    out_shape = [jax.ShapeDtypeStruct((count * slots, width), jnp.bfloat16)]
    scratch = [
        pltpu.VMEM((rows, width), jnp.bfloat16),
        pltpu.VMEM((2, PART, width), jnp.bfloat16),
    ]
    if with_gates:
        out_shape.append(jax.ShapeDtypeStruct((count * slots, 128), jnp.float32))
        scratch.append(pltpu.VMEM((2, PART, 128), jnp.float32))
    return pl.pallas_call(
        functools.partial(gather_kernel, len(sources), with_gates, len(after)),
        grid_spec=pltpu.PrefetchScalarGridSpec(
            num_scalar_prefetch=3,
            grid=(count,),
            in_specs=in_specs,
            out_specs=[anywhere] * len(out_shape),
            scratch_shapes=scratch
            + [pltpu.SemaphoreType.DMA((len(sources),)), pltpu.SemaphoreType.DMA((2, 2))],
        ),
        out_shape=out_shape,
        compiler_params=pltpu.CompilerParams(vmem_limit_bytes=VMEM_LIMIT),
    )(low, high, blocks, *operands, *sources, *after)


def expert_kernel(
    first, split, depth, far_first, extra, blocks_ref, misc_ref, x_ref, c_ref, sg_ref, wg_ref,
    wu_ref, wd_ref, *rest
):
    yd_ref = rest[extra]
    rest = rest[extra + 1 :]
    width = x_ref.shape[1]
    if split:
        send_ref, keep_ref = rest[:2]
        rest = rest[2:]
    else:
        grads_ref = rest[0]
        rest = rest[1:]
    total_gu, total_d, x_held, c_held, low_held, gated_held = rest
    expert = first + pl.program_id(0)
    block = pl.program_id(1)
    hidden = wg_ref.shape[2]
    blocks = blocks_ref[expert]
    lanes = lax.broadcasted_iota(jnp.int32, (BLOCK, 128), 1)

    @pl.when(block < blocks)
    def _():
        x = x_ref[...]
        c = c_ref[...]
        gate = jnp.sum(jnp.where(lanes == expert, sg_ref[...], 0.0), axis=1, keepdims=True)
        gate_proj = jnp.dot(x, wg_ref[0], preferred_element_type=jnp.float32)
        up_proj = jnp.dot(x, wu_ref[0], preferred_element_type=jnp.float32)
        pulled = dot_nt(c, wd_ref[0])
        sigmoid = 1.0 / (1.0 + jnp.exp(-gate_proj))
        silu = gate_proj * sigmoid
        activated = (silu * up_proj).astype(jnp.bfloat16).astype(jnp.float32)
        gate_grad = jnp.sum(activated * pulled, axis=1, keepdims=True)
        coarse = gate_grad.astype(jnp.bfloat16).astype(jnp.float32)
        yd_ref[:, 2 * width :] = jnp.where(
            lanes == expert, coarse, jnp.where(lanes == expert + 64, gate_grad - coarse, 0.0)
        ).astype(yd_ref.dtype)
        gated = (gate * activated).astype(jnp.bfloat16)
        yd_ref[:, :width] = jnp.dot(
            gated, wd_ref[0], preferred_element_type=jnp.float32
        ).astype(yd_ref.dtype)
        activated_grad = gate * pulled
        gate_low = (
            activated_grad * up_proj * sigmoid * (1.0 + gate_proj * (1.0 - sigmoid))
        ).astype(jnp.bfloat16)
        up_low = (activated_grad * silu).astype(jnp.bfloat16)
        yd_ref[:, width : 2 * width] = (
            dot_nt(gate_low, wg_ref[0]) + dot_nt(up_low, wu_ref[0])
        ).astype(yd_ref.dtype)
        start = pl.multiple_of((block % 2) * BLOCK, BLOCK)
        held = pl.ds(start, BLOCK)
        x_held[held, :] = x
        c_held[held, :] = c
        low_held[held, :hidden] = gate_low
        low_held[held, hidden:] = up_low
        gated_held[held, :] = gated

    def gather(rows, fresh):
        for begin in range(0, width, BLOCK):
            span = slice(begin, begin + BLOCK)
            for total, left, right in (
                (total_gu, x_held, low_held),
                (total_d, c_held, gated_held),
            ):
                term = dot_tn(left[:rows, span], right[:rows, :])
                total[span, :] = term if fresh else total[span, :] + term

    odd = block % 2 == 1
    last = block == blocks - 1

    @pl.when((block == 0) & last)
    def _():
        gather(BLOCK, True)

    @pl.when((block == 1) & (block < blocks))
    def _():
        gather(2 * BLOCK, True)

    @pl.when((block > 1) & odd & (block < blocks))
    def _():
        gather(2 * BLOCK, False)

    @pl.when((block > 1) & jnp.logical_not(odd) & last)
    def _():
        gather(BLOCK, False)

    @pl.when(block == pl.num_programs(1) - 1)
    def _():
        parts = (
            (total_gu, 0),
            (total_gu, hidden),
            (total_d, 0),
        )
        for which, (ref, column) in enumerate(parts):
            if split:
                side = misc_ref[1 + far_first]
                for high in range(2):
                    for low in range(2):
                        for out, chosen in ((keep_ref, side), (send_ref, 1 - side)):
                            if far_first:
                                start = ((high * 2 + chosen) * 2 + low) * depth
                                place = (high, low, which)
                            else:
                                start = ((high * 2 + low) * 2 + chosen) * depth
                                place = (low, high, which)
                            out[place] = ref[
                                pl.ds(pl.multiple_of(start, 64), depth), pl.ds(column, hidden)
                            ].astype(out.dtype)
            else:
                grads_ref[0, which] = ref[:, pl.ds(column, hidden)].astype(grads_ref.dtype)


def expert_call(
    blocks, misc, x, c, sg, weights, carried, slots, first, count, x_first, c_first, depth,
    far_first=0, after=()
):
    w_gate, w_up, w_down = weights
    experts = blocks.shape[0]
    width = x.shape[1]
    hidden = w_gate.shape[2]
    most = slots // BLOCK
    split = depth is not None

    def rows_index(base):
        def index(expert, block, blocks, misc):
            limit = blocks[first + expert] - 1
            return ((first - base + expert) * most + jnp.minimum(block, limit), 0)

        return index

    def weight_index(expert, block, blocks, misc):
        return (misc[0] + first + expert, 0, 0)

    def grads_index(expert, block, blocks, misc):
        return (0, 0, expert, 0, 0)

    out_shape = [jax.ShapeDtypeStruct((experts * slots, 2 * width + 128), jnp.bfloat16)]
    out_specs = [pl.BlockSpec((BLOCK, 2 * width + 128), rows_index(0))]
    if split:
        out_shape += [jax.ShapeDtypeStruct((2, 2, 3 * count, depth, hidden), jnp.bfloat16)] * 2
        out_specs += [pl.BlockSpec((2, 2, 3, depth, hidden), grads_index)] * 2
    else:
        out_shape += [jax.ShapeDtypeStruct((count, 3, width, hidden), jnp.bfloat16)]
        out_specs += [pl.BlockSpec((1, 3, width, hidden), lambda e, b, *_: (e, 0, 0, 0))]
    operands = [x, c, sg, w_gate, w_up, w_down]
    in_specs = [
        pl.BlockSpec((BLOCK, width), rows_index(x_first)),
        pl.BlockSpec((BLOCK, width), rows_index(c_first)),
        pl.BlockSpec((BLOCK, 128), rows_index(x_first)),
        pl.BlockSpec((1, width, hidden), weight_index),
        pl.BlockSpec((1, width, hidden), weight_index),
        pl.BlockSpec((1, hidden, width), weight_index),
    ]
    aliases = {}
    if carried is not None:
        operands.append(carried)
        aliases = {8: 0}
    operands += list(after)
    extra = len(operands) - 6
    in_specs += [pl.BlockSpec(memory_space=pl.ANY)] * extra
    return pl.pallas_call(
        functools.partial(expert_kernel, first, split, depth, far_first, extra),
        grid_spec=pltpu.PrefetchScalarGridSpec(
            num_scalar_prefetch=2,
            grid=(count, most),
            in_specs=in_specs,
            out_specs=out_specs,
            scratch_shapes=[
                pltpu.VMEM((width, 2 * hidden), jnp.float32),
                pltpu.VMEM((width, hidden), jnp.float32),
                pltpu.VMEM((2 * BLOCK, width), jnp.bfloat16),
                pltpu.VMEM((2 * BLOCK, width), jnp.bfloat16),
                pltpu.VMEM((2 * BLOCK, 2 * hidden), jnp.bfloat16),
                pltpu.VMEM((2 * BLOCK, hidden), jnp.bfloat16),
            ],
        ),
        out_shape=out_shape,
        input_output_aliases=aliases,
        compiler_params=pltpu.CompilerParams(vmem_limit_bytes=VMEM_LIMIT),
    )(blocks, misc, *operands)


def combine_kernel(
    first, owner_ref, piece_ref, source_ref, groups_ref, begin_ref, tile_ref, place_ref, yd_ref, *rest
):
    y_out, dx_out, gate_out, buffer, total, sems = rest[-6:]
    columns = y_out.shape[1]
    step = pl.program_id(0)
    tile = first + step

    head = begin_ref[first]
    final = first + pl.num_programs(0) - 1
    stop = begin_ref[final] + groups_ref[final]

    def copies(place):
        which_tile = tile_ref[place]
        group = place - begin_ref[which_tile]
        slot = (place - head) % DEEP
        made = []
        for i in range(GROUP):
            source = pl.multiple_of(
                source_ref[which_tile, group * GROUP + i] * PIECE_ROWS, PIECE_ROWS
            )
            made.append(
                pltpu.make_async_copy(
                    yd_ref.at[pl.ds(source, PIECE_ROWS)],
                    buffer.at[slot, pl.ds(i * PIECE_ROWS, PIECE_ROWS)],
                    sems.at[slot, i],
                )
            )
        return made

    @pl.when(step == 0)
    def _():
        for ahead in range(DEEP - 1):

            @pl.when(head + ahead < stop)
            def _():
                for copy in copies(head + ahead):
                    copy.start()

    def one(group, carry):
        place = begin_ref[tile] + group
        slot = (place - head) % DEEP

        @pl.when(place + DEEP - 1 < stop)
        def _():
            for copy in copies(place + DEEP - 1):
                copy.start()

        picks = []
        for i in range(GROUP):
            entry = group * GROUP + i
            rows = (
                lax.broadcasted_iota(jnp.int32, (PIECE_ROWS, BLOCK), 0)
                + piece_ref[tile, entry] * PIECE_ROWS
            )
            picks.append(jnp.where(rows == place_ref[owner_ref[tile, entry], step], 1.0, 0.0))
        picked = jnp.concatenate(picks, axis=0).T.astype(jnp.bfloat16)
        for copy in copies(place):
            copy.wait()
        fresh = group == 0
        for begin in range(0, total.shape[1], 640):
            span = slice(begin, begin + 640)
            term = jnp.dot(picked, buffer[slot, :, span], preferred_element_type=jnp.float32)
            total[:, span] = jnp.where(fresh, 0.0, total[:, span]) + term
        return carry

    lax.fori_loop(0, groups_ref[tile], one, 0)
    y_out[...] = total[:, :columns].astype(y_out.dtype)
    dx_out[...] = total[:, columns : 2 * columns].astype(dx_out.dtype)
    gate_out[...] = total[:, 2 * columns :]


def combine_rows(tables, place, yd, first, count, after=()):
    owner, piece, source, groups, width = tables
    ends = jnp.cumsum(groups)
    begin = ends - groups
    most = groups.shape[0] * (width // GROUP)
    tile_of = jnp.minimum(
        jnp.sum((ends[None, :] <= jnp.arange(most)[:, None]).astype(jnp.int32), axis=1),
        groups.shape[0] - 1,
    )
    experts = place.shape[0]
    whole_width = yd.shape[1]
    columns = (whole_width - 128) // 2
    row_block = lambda wide: pl.BlockSpec((BLOCK, wide), lambda t, *_: (t, 0))
    return pl.pallas_call(
        functools.partial(combine_kernel, first),
        grid_spec=pltpu.PrefetchScalarGridSpec(
            num_scalar_prefetch=6,
            grid=(count,),
            in_specs=[pl.BlockSpec((experts, count, 1, BLOCK), lambda *_: (0, first // count, 0, 0))]
            + [pl.BlockSpec(memory_space=pl.ANY)] * (1 + len(after)),
            out_specs=[row_block(columns), row_block(columns), row_block(128)],
            scratch_shapes=[
                pltpu.VMEM((DEEP, GROUP * PIECE_ROWS, whole_width), jnp.bfloat16),
                pltpu.VMEM((BLOCK, whole_width), jnp.float32),
                pltpu.SemaphoreType.DMA((DEEP, GROUP)),
            ],
        ),
        out_shape=[
            jax.ShapeDtypeStruct((count * BLOCK, columns), jnp.bfloat16),
            jax.ShapeDtypeStruct((count * BLOCK, columns), jnp.bfloat16),
            jax.ShapeDtypeStruct((count * BLOCK, 128), jnp.float32),
        ],
        compiler_params=pltpu.CompilerParams(vmem_limit_bytes=VMEM_LIMIT),
    )(owner, piece, source, groups, begin, tile_of, place, yd, *after)


def flip(value, bit):
    size = lax.axis_size("dp")
    return lax.ppermute(value, "dp", [(i, i ^ bit) for i in range(size)])


def swap(value):
    return lax.ppermute(value, "tensor", [(0, 1), (1, 0)])


def order(value, *after):
    return lax.optimization_barrier((value, *after))[0] if after else value


def add_low(left, right):
    return (left.astype(jnp.float32) + right.astype(jnp.float32)).astype(jnp.bfloat16)


def pick_index(value, index, axis):
    return lax.dynamic_index_in_dim(value, index, axis, keepdims=False)


def sum_stage(parts, bit, chosen, after):
    send, keep = parts
    got = order(flip(send, bit), *after)
    return tuple(
        add_low(pick_index(keep, which, 0), pick_index(got, which, 0))
        for which in (1 - chosen, chosen)
    )


class ChipSum:
    def __init__(self, parts, rank, far_first):
        side, low_bit, high_bit = (rank // 2) % 2, (rank // 4) % 2, rank // 8
        self.parts = parts
        self.first = (4, high_bit) if far_first else (2, low_bit)
        self.second = (8, side) if far_first else (4, high_bit)
        self.last = 2 if far_first else 8

    def one(self, *after):
        self.parts = sum_stage(self.parts, *self.first, after)
        return self.parts[0]

    def two(self, *after):
        self.parts = sum_stage(self.parts, *self.second, after)
        return self.parts[0]

    def three(self, *after):
        send, keep = self.parts
        return add_low(keep, order(flip(send, self.last), *after))


def core_sum(value, core):
    rows, columns = value.shape
    value = value.reshape(8, 2, rows // 16, columns)
    got = flip(pick_index(value, 1 - core, 1).astype(jnp.bfloat16), 1)
    return add_low(pick_index(value, core, 1), got)


def plane_sum(total, rank, *after):
    side, low_bit, high_bit = (rank // 2) % 2, (rank // 4) % 2, rank // 8
    part, columns = total.shape[1:]
    total = total.reshape(4, 2, part, columns)
    got = order(flip(pick_index(total, 1 - side, 1), 2), *after)
    total = add_low(pick_index(total, side, 1), got).reshape(2, 2, part, columns)
    got = flip(pick_index(total, 1 - low_bit, 1), 4)
    total = add_low(pick_index(total, low_bit, 1), got)
    got = flip(pick_index(total, 1 - high_bit, 0), 8)
    return pick_index(total, high_bit, 0).astype(jnp.float32) + got.astype(jnp.float32)


def fetch_other(weights, core, side, after=()):
    rows = weights[0].shape[0] // 4
    start = (side * 2 + core) * rows
    own = jnp.concatenate(
        [lax.dynamic_slice_in_dim(w, start, rows, 0) for w in weights], axis=1
    )
    pieces = swap(order(own, *after))
    turned = flip(pieces, 2)
    result = jnp.zeros((4 * rows, own.shape[1]), own.dtype)
    for value, place in (
        (pieces, side * 2 + core),
        (turned, (1 - side) * 2 + core),
        (flip(pieces, 1), side * 2 + 1 - core),
        (flip(turned, 1), (1 - side) * 2 + 1 - core),
    ):
        result = lax.dynamic_update_slice_in_dim(result, value, place * rows, 0)
    return result, own, pieces


ROWS = 256
HALF = 512


def lane_swap(values):
    width = values.shape[1]
    lane = lax.broadcasted_iota(jnp.int32, values.shape, 1) % HD
    ahead = pltpu.roll(values, width - HD // 2, 1)
    behind = pltpu.roll(values, HD // 2, 1)
    return jnp.where(lane < HD // 2, ahead, behind)


def turn_tables(rows):
    cosine, sine = rope_tables(rows, HD)
    return (
        jnp.concatenate([cosine] * 4, axis=1),
        jnp.concatenate([-sine, sine, -sine, sine], axis=1),
    )


def project_kernel(sizes, score_scale, normed_ref, weights_ref, cosine_ref, sine_ref, *outs):
    query_ref, key_ref, value_ref = outs[-3:]
    query_width, key_width = sizes
    projected = jnp.dot(normed_ref[...], weights_ref[...], preferred_element_type=jnp.float32)
    cosine, sine = cosine_ref[...], sine_ref[...]
    for start in range(0, query_width + key_width, 128):
        piece = projected[:, start : start + 128]
        turned = piece * cosine + lane_swap(piece) * sine
        if start < query_width:
            query_ref[:, start : start + 128] = (turned * score_scale).astype(jnp.bfloat16)
        else:
            begin = start - query_width
            key_ref[:, begin : begin + 128] = turned.astype(jnp.bfloat16)
    value_ref[...] = projected[:, query_width + key_width :].astype(jnp.bfloat16)


def project(normed, weights, tables, query_width, key_width, score_scale, after=()):
    rows, depth = normed.shape
    width = weights.shape[1]
    row_spec = lambda columns: pl.BlockSpec((ROWS, columns), lambda i: (i, 0))
    return pl.pallas_call(
        functools.partial(project_kernel, (query_width, key_width), score_scale),
        grid=(rows // ROWS,),
        in_specs=[
            row_spec(depth),
            pl.BlockSpec((depth, width), lambda i: (0, 0)),
            row_spec(128),
            row_spec(128),
        ]
        + [pl.BlockSpec(memory_space=pl.ANY)] * len(after),
        out_specs=[row_spec(query_width), row_spec(key_width), row_spec(key_width)],
        out_shape=[
            jax.ShapeDtypeStruct((rows, query_width), jnp.bfloat16),
            jax.ShapeDtypeStruct((rows, key_width), jnp.bfloat16),
            jax.ShapeDtypeStruct((rows, key_width), jnp.bfloat16),
        ],
        compiler_params=pltpu.CompilerParams(vmem_limit_bytes=VMEM_LIMIT),
    )(normed, weights, *tables, *after)


def attend_kernel(per_pair, query_ref, key_ref, value_ref, limit_ref, *rest):
    out_ref, lse_ref = rest[-2:]
    step = pl.program_id(1)

    def work(keys):
        columns = lax.broadcasted_iota(jnp.int32, (ROWS, HALF), 1) + (keys - HALF)
        allowed = columns <= limit_ref[...]
        lanes = lax.broadcasted_iota(jnp.int32, (ROWS, 128), 1)
        sums = jnp.zeros((ROWS, 128), jnp.float32)
        pieces = []
        for head in range(per_pair):
            group = head // (per_pair // 2)
            query = query_ref[:, head * HD : (head + 1) * HD]
            key = key_ref[:keys, group * HD : (group + 1) * HD]
            value = value_ref[:keys, group * HD : (group + 1) * HD]
            scores = dot_nt(query, key)
            last = jnp.where(allowed, scores[:, keys - HALF :], -1e30)
            scores = last if keys == HALF else jnp.concatenate([scores[:, : keys - HALF], last], 1)
            highest = jnp.max(scores, axis=1, keepdims=True)
            shifted = jnp.exp(scores - highest)
            total = jnp.sum(shifted, axis=1, keepdims=True)
            mixed = jnp.dot(
                shifted.astype(jnp.bfloat16), value, preferred_element_type=jnp.float32
            )
            pieces.append((mixed / total).astype(jnp.bfloat16))
            sums = jnp.where(lanes == head, highest + jnp.log(total), sums)
        out_ref[...] = jnp.concatenate(pieces, axis=1)
        lse_ref[0] = sums

    halfway = pl.num_programs(1) // 2

    @pl.when(step < halfway)
    def _():
        work(HALF)

    @pl.when(step >= halfway)
    def _():
        work(2 * HALF)


def attend(query, key, value, limits, after=()):
    rows, query_width = query.shape
    pairs = key.shape[1] // 128
    wide = query_width // pairs
    return pl.pallas_call(
        functools.partial(attend_kernel, wide // HD),
        grid=(pairs, rows // ROWS),
        in_specs=[
            pl.BlockSpec((ROWS, wide), lambda p, i: (i, p)),
            pl.BlockSpec((rows, 128), lambda p, i: (0, p)),
            pl.BlockSpec((rows, 128), lambda p, i: (0, p)),
            pl.BlockSpec((ROWS, 1), lambda p, i: (i, 0)),
        ]
        + [pl.BlockSpec(memory_space=pl.ANY)] * len(after),
        out_specs=[
            pl.BlockSpec((ROWS, wide), lambda p, i: (i, p)),
            pl.BlockSpec((1, ROWS, 128), lambda p, i: (p, i, 0)),
        ],
        out_shape=[
            jax.ShapeDtypeStruct((rows, query_width), jnp.bfloat16),
            jax.ShapeDtypeStruct((pairs, rows, 128), jnp.float32),
        ],
        compiler_params=pltpu.CompilerParams(vmem_limit_bytes=VMEM_LIMIT),
    )(query, key, value, limits, *after)


def back_kernel(
    per_pair, score_scale, after, query_ref, key_ref, value_ref, turned_key_ref, grad_ref, lse_ref,
    limit_ref, cosine_ref, sine_ref, all_cosine_ref, all_sine_ref, *rest
):
    query_out, key_out, value_out, key_total, value_total = rest[after:]
    step = pl.program_id(1)
    halfway = pl.num_programs(1) // 2

    @pl.when(step == 0)
    def _():
        key_total[...] = jnp.zeros_like(key_total)
        value_total[...] = jnp.zeros_like(value_total)

    def work(keys):
        rows = lax.broadcasted_iota(jnp.int32, (HALF, ROWS), 0) + (keys - HALF)
        allowed = rows <= limit_ref[...]
        made = []
        key_parts, value_parts = [], []
        for group in range(2):
            span = slice(group * HD, (group + 1) * HD)
            key, value = key_ref[:keys, span], value_ref[:keys, span]
            key_part = value_part = 0.0
            for head in range(group * per_pair // 2, (group + 1) * per_pair // 2):
                query = query_ref[:, head * HD : (head + 1) * HD]
                grad = grad_ref[:, head * HD : (head + 1) * HD]
                scores = dot_nt(key, query)
                last = jnp.where(allowed, scores[keys - HALF :], -1e30)
                scores = (
                    last
                    if keys == HALF
                    else jnp.concatenate([scores[: keys - HALF], last], axis=0)
                )
                weights = jnp.exp(scores - lse_ref[0, head : head + 1, :])
                pulled = dot_nt(value, grad)
                inner = jnp.sum(weights * pulled, axis=0, keepdims=True)
                score_low = (weights * (pulled - inner)).astype(jnp.bfloat16)
                value_part += jnp.dot(
                    weights.astype(jnp.bfloat16), grad, preferred_element_type=jnp.float32
                )
                key_part += jnp.dot(score_low, query, preferred_element_type=jnp.float32)
                made.append(
                    jnp.dot(
                        turned_key_ref[0, span, :keys],
                        score_low,
                        preferred_element_type=jnp.float32,
                    )
                )
            key_parts.append(key_part)
            value_parts.append(value_part)
        key_total[:keys] += jnp.concatenate(key_parts, axis=1)
        value_total[:keys] += jnp.concatenate(value_parts, axis=1)
        cosine, sine = cosine_ref[...], sine_ref[...]
        for index in range(per_pair // 2):
            both = jnp.concatenate(made[2 * index : 2 * index + 2], axis=0).T * score_scale
            query_out[:, index * 128 : (index + 1) * 128] = (
                both * cosine - lane_swap(both) * sine
            ).astype(jnp.bfloat16)

    @pl.when(step < halfway)
    def _():
        work(HALF)

    @pl.when(step >= halfway)
    def _():
        work(2 * HALF)

    @pl.when(step == pl.num_programs(1) - 1)
    def _():
        total = key_total[...]
        key_out[...] = (
            total * all_cosine_ref[...] - lane_swap(total) * all_sine_ref[...]
        ).astype(jnp.bfloat16)
        value_out[...] = value_total[...].astype(jnp.bfloat16)


def attend_back(saved, attended_grad, limits, tables, score_scale, chosen, after=()):
    query, key, value, lse = saved
    rows, query_width = query.shape
    pairs = key.shape[1] // 128
    wide = query_width // pairs
    turned_key = key.T.reshape(pairs, 128, rows)
    lse_rows = lse[:, :, :8].transpose(0, 2, 1)
    cosine, sine = tables
    begin, count = chosen
    block = lambda columns: pl.BlockSpec((ROWS, columns), lambda p, i: (i, p + begin))
    whole = pl.BlockSpec((rows, 128), lambda p, i: (0, p + begin))
    block_out = pl.BlockSpec((ROWS, wide), lambda p, i: (i, p))
    whole_out = pl.BlockSpec((rows, 128), lambda p, i: (0, p))
    table = pl.BlockSpec((ROWS, 128), lambda p, i: (i, 0))
    full_table = pl.BlockSpec((rows, 128), lambda p, i: (0, 0))
    return pl.pallas_call(
        functools.partial(back_kernel, wide // HD, score_scale, len(after)),
        grid=(count, rows // ROWS),
        in_specs=[
            block(wide),
            whole,
            whole,
            pl.BlockSpec((1, 128, rows), lambda p, i: (p + begin, 0, 0)),
            block(wide),
            pl.BlockSpec((1, 8, ROWS), lambda p, i: (p + begin, 0, i)),
            pl.BlockSpec((1, ROWS), lambda p, i: (0, i)),
            table,
            table,
            full_table,
            full_table,
        ]
        + [pl.BlockSpec(memory_space=pl.ANY)] * len(after),
        out_specs=[block_out, whole_out, whole_out],
        out_shape=[
            jax.ShapeDtypeStruct((rows, count * wide), jnp.bfloat16),
            jax.ShapeDtypeStruct((rows, count * 128), jnp.bfloat16),
            jax.ShapeDtypeStruct((rows, count * 128), jnp.bfloat16),
        ],
        scratch_shapes=[
            pltpu.VMEM((rows, 128), jnp.float32),
            pltpu.VMEM((rows, 128), jnp.float32),
        ],
        compiler_params=pltpu.CompilerParams(vmem_limit_bytes=VMEM_LIMIT),
    )(
        query, key, value, turned_key, attended_grad, lse_rows, limits.T, cosine, sine, cosine,
        sine, *after,
    )


def piece_limits(starts_row, rows):
    position = jnp.arange(rows, dtype=jnp.int32)
    limits = position
    for index in range(starts_row.shape[0]):
        start = starts_row[index]
        inside = (position >= start) & (position < start + PIECE)
        limits = jnp.where(inside, start + PIECE - 1, limits)
    return limits[:, None]


def slot_table(routes, expert_count, capacity):
    flattened = routes.reshape(-1)
    onehot = (flattened[:, None] == jnp.arange(expert_count, dtype=jnp.int32)[None, :]).astype(
        jnp.int32
    )
    placed = jnp.sum((jnp.cumsum(onehot, axis=0) - 1) * onehot, axis=1)
    entries = jnp.arange(flattened.shape[0], dtype=jnp.int32)
    return (
        jnp.full((expert_count * capacity,), flattened.shape[0], jnp.int32)
        .at[flattened * capacity + placed]
        .set(entries)
    )


def expert_forward(expert_inputs, w_gate, w_up, w_down):
    gate_proj = jnp.einsum(
        "ecd,edf->ecf", expert_inputs, w_gate, preferred_element_type=jnp.float32
    )
    up_proj = jnp.einsum("ecd,edf->ecf", expert_inputs, w_up, preferred_element_type=jnp.float32)
    activated = (gate_proj * jax.nn.sigmoid(gate_proj) * up_proj).astype(jnp.bfloat16)
    returned = jnp.einsum("ecf,efd->ecd", activated, w_down, preferred_element_type=jnp.float32)
    return (gate_proj, up_proj, activated, returned)


def shards_wide(
    tokens,
    norm_gains,
    w_query,
    w_key,
    w_value,
    w_out,
    mix_gains,
    w_router,
    w_gate,
    w_up,
    w_down,
    routes,
    starts,
    cotangent,
):
    share_rows = tokens.shape[0]
    model_width = tokens.shape[1]
    head_width = HD
    query_width = w_query.shape[1]
    key_width = w_key.shape[1]
    heads_here = query_width // head_width
    groups_here = key_width // head_width
    per_group = heads_here // groups_here
    experts_here = w_gate.shape[0]
    group_rows = routes.shape[0]
    choices_count = routes.shape[1]
    sequences_here = starts.shape[0]
    sequence_length = group_rows // sequences_here
    expert_count = w_router.shape[1]
    tensor_rank = lax.axis_index("tensor")
    total_tokens = group_rows * lax.axis_size("dp")
    score_scale = head_width ** (-0.5)
    inputs_share = tokens.astype(jnp.float32)
    normed_share = normalize(inputs_share, norm_gains).astype(jnp.bfloat16)
    normed = lax.all_gather(normed_share, "tensor", axis=0, tiled=True)
    joined_weights = jnp.concatenate([w_query, w_key, w_value], axis=1)
    projected = jnp.dot(normed, joined_weights, preferred_element_type=jnp.float32)
    cosine, sine_table = rope_tables(sequence_length, head_width)
    cosine_rows = jnp.tile(cosine, (sequences_here, 1))
    sine_rows = jnp.tile(sine_table, (sequences_here, 1))
    query_rows = rotate(
        projected[:, :query_width].reshape(group_rows, heads_here, head_width),
        cosine_rows,
        sine_rows,
    ).astype(jnp.bfloat16)
    key_rows = rotate(
        projected[:, query_width : query_width + key_width].reshape(
            group_rows, groups_here, head_width
        ),
        cosine_rows,
        sine_rows,
    ).astype(jnp.bfloat16)
    value_rows = (
        projected[:, query_width + key_width :]
        .astype(jnp.bfloat16)
        .reshape(group_rows, groups_here, head_width)
    )
    attended_parts = []
    logsum_parts = []
    for sequence in range(sequences_here):
        first_row = sequence * sequence_length
        query_block = query_rows[first_row : first_row + sequence_length].reshape(
            sequence_length, groups_here, per_group, head_width
        )
        key_block = key_rows[first_row : first_row + sequence_length]
        value_block = value_rows[first_row : first_row + sequence_length]
        allowed = allowed_pairs(starts[sequence], sequence_length, PIECE)
        scores = scores_of(query_block, key_block, allowed, score_scale)
        highest = jnp.max(scores, axis=-1, keepdims=True)
        shifted = jnp.exp(scores - highest)
        totals = jnp.sum(shifted, axis=-1, keepdims=True)
        weights = (shifted / totals).astype(jnp.bfloat16)
        mixed_values = jnp.einsum(
            "kgqs,skd->qkgd", weights, value_block, preferred_element_type=jnp.float32
        )
        attended_parts.append(
            mixed_values.reshape(sequence_length, query_width).astype(jnp.bfloat16)
        )
        logsum_parts.append(highest + jnp.log(totals))
    attended = jnp.concatenate(attended_parts, axis=0)
    attention_share = lax.psum_scatter(
        jnp.dot(attended, w_out, preferred_element_type=jnp.float32),
        "tensor",
        scatter_dimension=0,
        tiled=True,
    )
    middle_share = inputs_share + attention_share
    mixed_share = normalize(middle_share, mix_gains).astype(jnp.bfloat16)
    share_routes = lax.dynamic_slice_in_dim(routes, tensor_rank * share_rows, share_rows, 0)
    route_onehot = (
        share_routes[:, :, None] == jnp.arange(expert_count, dtype=jnp.int32)[None, None, :]
    ).astype(jnp.float32)
    logits = jnp.dot(mixed_share, w_router, preferred_element_type=jnp.float32)
    probabilities = softmax_rows(logits)
    chosen = jnp.sum(logits[:, None, :] * route_onehot, axis=-1)
    gate_soft = softmax_rows(chosen)
    gate_low = gate_soft.astype(jnp.bfloat16)
    counts, prob_sums = lax.psum(
        (jnp.sum(route_onehot, axis=(0, 1)), jnp.sum(probabilities, axis=0)), ("dp", "tensor")
    )
    fractions = counts / (total_tokens * choices_count)
    balance = expert_count * expert_count * fractions * prob_sums / total_tokens
    mixed_rows, gate_rows = (
        lax.all_gather(mixed_share, "tensor", axis=0, tiled=True),
        lax.all_gather(gate_low, "tensor", axis=0, tiled=True),
    )
    slots_all = slot_table(routes, expert_count, CAP)
    slots = lax.dynamic_slice_in_dim(
        slots_all, tensor_rank * experts_here * CAP, experts_here * CAP, 0
    )
    owners = slots // choices_count
    padded_rows = jnp.concatenate([mixed_rows, jnp.zeros((1, model_width), jnp.bfloat16)], axis=0)
    padded_gates = jnp.concatenate(
        [gate_rows.reshape(-1).astype(jnp.float32), jnp.zeros((1,), jnp.float32)], axis=0
    )
    slot_gates = padded_gates[slots]
    expert_inputs = padded_rows[owners].reshape(experts_here, CAP, model_width)
    gate_proj, up_proj, activated, returned = expert_forward(expert_inputs, w_gate, w_up, w_down)
    returned_flat = returned.reshape(experts_here * CAP, model_width)
    expert_partial = jax.ops.segment_sum(
        slot_gates[:, None] * returned_flat, owners, num_segments=group_rows + 1
    )[:group_rows]
    expert_share = lax.psum_scatter(
        expert_partial.astype(jnp.bfloat16), "tensor", scatter_dimension=0, tiled=True
    ).astype(jnp.float32)
    output_share = (middle_share + expert_share).astype(jnp.bfloat16)
    upstream = cotangent.astype(jnp.float32)
    upstream_rows = lax.all_gather(cotangent, "tensor", axis=0, tiled=True)
    padded_upstream = jnp.concatenate(
        [upstream_rows, jnp.zeros((1, model_width), jnp.bfloat16)], axis=0
    )
    slot_upstream = padded_upstream[owners].astype(jnp.float32)
    slot_cotangent = (
        (slot_gates[:, None] * slot_upstream)
        .astype(jnp.bfloat16)
        .reshape(experts_here, CAP, model_width)
    )
    slot_gate_grad = jnp.sum(slot_upstream * returned_flat, axis=1)
    activated_grad = jnp.einsum(
        "ecd,efd->ecf", slot_cotangent, w_down, preferred_element_type=jnp.float32
    )
    down_grad = jnp.einsum(
        "ecf,ecd->efd", activated, slot_cotangent, preferred_element_type=jnp.float32
    )
    sigmoid_gate = jax.nn.sigmoid(gate_proj)
    gate_proj_low = (
        activated_grad * up_proj * sigmoid_gate * (1.0 + gate_proj * (1.0 - sigmoid_gate))
    ).astype(jnp.bfloat16)
    up_proj_low = (activated_grad * gate_proj * sigmoid_gate).astype(jnp.bfloat16)
    inputs_grad = jnp.einsum(
        "ecf,edf->ecd", gate_proj_low, w_gate, preferred_element_type=jnp.float32
    ) + jnp.einsum("ecf,edf->ecd", up_proj_low, w_up, preferred_element_type=jnp.float32)
    gate_grad = jnp.einsum(
        "ecd,ecf->edf", expert_inputs, gate_proj_low, preferred_element_type=jnp.float32
    )
    up_grad = jnp.einsum(
        "ecd,ecf->edf", expert_inputs, up_proj_low, preferred_element_type=jnp.float32
    )
    mixed_partial = jax.ops.segment_sum(
        inputs_grad.reshape(experts_here * CAP, model_width), owners, num_segments=group_rows + 1
    )[:group_rows]
    gate_partial = jax.ops.segment_sum(
        slot_gate_grad, slots, num_segments=group_rows * choices_count + 1
    )[: group_rows * choices_count].reshape(group_rows, choices_count)
    mixed_grad_share, gates_grad_share = (
        lax.psum_scatter(mixed_partial, "tensor", scatter_dimension=0, tiled=True),
        lax.psum_scatter(gate_partial, "tensor", scatter_dimension=0, tiled=True),
    )
    gate_total, up_total = (
        lax.psum_scatter(
            gate_grad.astype(jnp.bfloat16), "dp", scatter_dimension=1, tiled=True
        ).astype(jnp.float32),
        lax.psum_scatter(
            up_grad.astype(jnp.bfloat16), "dp", scatter_dimension=1, tiled=True
        ).astype(jnp.float32),
    )
    down_total = lax.psum_scatter(
        down_grad.astype(jnp.bfloat16), "dp", scatter_dimension=2, tiled=True
    ).astype(jnp.float32)
    chosen_grad = gate_soft * (
        gates_grad_share - jnp.sum(gate_soft * gates_grad_share, axis=-1, keepdims=True)
    )
    logit_grad = jnp.sum(chosen_grad[:, :, None] * route_onehot, axis=1)
    prob_target = ALPHA * expert_count * fractions / total_tokens
    logit_grad = logit_grad + probabilities * (
        prob_target[None, :] - jnp.sum(probabilities * prob_target[None, :], axis=-1, keepdims=True)
    )
    mixed_float = mixed_share.astype(jnp.float32)
    router_grad = jnp.dot(
        mixed_float.T, logit_grad, precision=HIGHEST, preferred_element_type=jnp.float32
    )
    mixed_grad_share = mixed_grad_share + jnp.dot(
        logit_grad,
        w_router.astype(jnp.float32).T,
        precision=HIGHEST,
        preferred_element_type=jnp.float32,
    )
    mix_pullback = jax.vjp(normalize, middle_share, mix_gains)[1]
    middle_from_norm, mix_gain_grad = mix_pullback(mixed_grad_share)
    middle_grad = upstream + middle_from_norm
    middle_low = middle_grad.astype(jnp.bfloat16)
    middle_rows = lax.all_gather(middle_low, "tensor", axis=0, tiled=True)
    out_grad = contract_rows(attended, middle_rows)
    attended_grad = contract_cols(middle_rows, w_out).astype(jnp.bfloat16)
    query_parts = []
    key_parts = []
    value_parts = []
    for sequence in range(sequences_here):
        first_row = sequence * sequence_length
        query_block = query_rows[first_row : first_row + sequence_length].reshape(
            sequence_length, groups_here, per_group, head_width
        )
        key_block = key_rows[first_row : first_row + sequence_length]
        value_block = value_rows[first_row : first_row + sequence_length]
        allowed = allowed_pairs(starts[sequence], sequence_length, PIECE)
        scores = scores_of(query_block, key_block, allowed, score_scale)
        weights_full = jnp.exp(scores - logsum_parts[sequence])
        weights_low = weights_full.astype(jnp.bfloat16)
        grad_block = attended_grad[first_row : first_row + sequence_length].reshape(
            sequence_length, groups_here, per_group, head_width
        )
        value_parts.append(
            jnp.einsum(
                "kgqs,qkgd->skd", weights_low, grad_block, preferred_element_type=jnp.float32
            )
        )
        weight_grad = jnp.einsum(
            "qkgd,skd->kgqs", grad_block, value_block, preferred_element_type=jnp.float32
        )
        score_low = (
            weights_full
            * (weight_grad - jnp.sum(weights_full * weight_grad, axis=-1, keepdims=True))
        ).astype(jnp.bfloat16)
        query_parts.append(
            jnp.einsum("kgqs,skd->qkgd", score_low, key_block, preferred_element_type=jnp.float32)
            * score_scale
        )
        key_parts.append(
            jnp.einsum("kgqs,qkgd->skd", score_low, query_block, preferred_element_type=jnp.float32)
            * score_scale
        )
    query_grads = (
        rotate(
            jnp.concatenate(query_parts, axis=0).reshape(group_rows, heads_here, head_width),
            cosine_rows,
            -sine_rows,
        )
        .astype(jnp.bfloat16)
        .reshape(group_rows, query_width)
    )
    key_grads = (
        rotate(jnp.concatenate(key_parts, axis=0), cosine_rows, -sine_rows)
        .astype(jnp.bfloat16)
        .reshape(group_rows, key_width)
    )
    value_grads = (
        jnp.concatenate(value_parts, axis=0).astype(jnp.bfloat16).reshape(group_rows, key_width)
    )
    joined_grads = jnp.concatenate([query_grads, key_grads, value_grads], axis=1)
    joined_weight_grad = contract_rows(normed, joined_grads)
    normed_grad_share = lax.psum_scatter(
        contract_cols(joined_grads, joined_weights).astype(jnp.bfloat16),
        "tensor",
        scatter_dimension=0,
        tiled=True,
    ).astype(jnp.float32)
    input_pullback = jax.vjp(normalize, inputs_share, norm_gains)[1]
    input_from_norm, norm_gain_grad = input_pullback(normed_grad_share)
    input_grad_share = middle_grad + input_from_norm
    query_total, key_total, value_total, out_turned = (
        lax.psum_scatter(
            joined_weight_grad[:, :query_width].astype(jnp.bfloat16),
            "dp",
            scatter_dimension=0,
            tiled=True,
        ).astype(jnp.float32),
        lax.psum_scatter(
            joined_weight_grad[:, query_width : query_width + key_width].astype(jnp.bfloat16),
            "dp",
            scatter_dimension=0,
            tiled=True,
        ).astype(jnp.float32),
        lax.psum_scatter(
            joined_weight_grad[:, query_width + key_width :].astype(jnp.bfloat16),
            "dp",
            scatter_dimension=0,
            tiled=True,
        ).astype(jnp.float32),
        lax.psum_scatter(
            out_grad.T.astype(jnp.bfloat16), "dp", scatter_dimension=0, tiled=True
        ).astype(jnp.float32),
    )
    out_total = out_turned.T
    norm_gain_total, mix_gain_total, router_total = lax.psum(
        (norm_gain_grad, mix_gain_grad, router_grad), ("dp", "tensor")
    )
    return (
        output_share,
        balance,
        input_grad_share,
        norm_gain_total,
        query_total,
        key_total,
        value_total,
        out_total,
        mix_gain_total,
        router_total,
        gate_total,
        up_total,
        down_total,
    )


def all_sum(value):
    for bit in (1, 2, 4, 8):
        value = value + flip(value, bit)
    return value + swap(value)


def spread(value):
    across = swap(value)
    return [value, across, flip(value, 1), flip(across, 1)]


CHUNK = 2
FAR_FIRST = -1


def shards_pair(
    tokens,
    norm_gains,
    w_query,
    w_key,
    w_value,
    w_out,
    mix_gains,
    w_router,
    w_gate,
    w_up,
    w_down,
    routes,
    starts,
    cotangent,
):
    share_rows, model_width = tokens.shape
    query_width = w_query.shape[1]
    key_width = w_key.shape[1]
    sizes = (query_width, key_width, HD)
    experts_here = w_gate.shape[0]
    experts = experts_here // 2
    choices_count = routes.shape[1]
    expert_count = w_router.shape[1]
    dp_size = lax.axis_size("dp")
    rank = lax.axis_index("dp")
    core, side = rank % 2, (rank // 2) % 2
    tensor_rank = lax.axis_index("tensor")
    total_tokens = routes.shape[0] * dp_size
    score_scale = HD ** (-0.5)
    depth = model_width // dp_size * 2
    slots = round_up(2 * CAP, BLOCK)

    joined_own = jnp.concatenate([w_query, w_key, w_value], axis=1)
    joined_other, joined_send, joined_piece = fetch_other([w_query, w_key, w_value], core, side)
    out_other, _, out_piece = fetch_other([w_out], core, side, (joined_send,))

    own_routes = lax.dynamic_slice_in_dim(routes, tensor_rank * share_rows, share_rows, 0)
    across_routes = lax.dynamic_slice_in_dim(routes, (1 - tensor_rank) * share_rows, share_rows, 0)
    both_routes = jnp.concatenate([own_routes, across_routes], axis=0)
    group_routes = jnp.concatenate([both_routes, flip(both_routes, 1)], axis=0)
    first_expert = tensor_rank * experts_here + core * experts

    route_onehot = (
        own_routes[:, :, None] == jnp.arange(expert_count, dtype=jnp.int32)[None, None, :]
    ).astype(jnp.float32)
    hops = [jnp.sum(route_onehot, axis=(0, 1))]
    for bit in (1, 2, 4, 8):
        hops.append(hops[-1] + flip(hops[-1], bit))
    counts = hops[-1] + swap(hops[-1])
    cotangent_rows = spread(order(cotangent, joined_piece))

    inputs_share = tokens.astype(jnp.float32)
    normed = normalize(inputs_share, norm_gains).astype(jnp.bfloat16)
    tables = turn_tables(share_rows)
    starts_row = lax.dynamic_index_in_dim(starts, tensor_rank, 0, keepdims=False)
    limits = piece_limits(starts_row, share_rows)

    def half_forward(joined_weights, after=(), later=()):
        query, key, value = project(
            normed, joined_weights, tables, query_width, key_width, score_scale, after
        )
        attended, lse = attend(query, key, value, limits, later)
        return attended, (query, key, value, lse)

    attended_own, saved_own = half_forward(joined_own, (), (joined_piece, hops[1]))
    attended_other, saved_other = half_forward(joined_other, (hops[2],), (hops[3],))
    middle_share = (
        inputs_share
        + jnp.dot(attended_own, w_out, preferred_element_type=jnp.float32)
        + jnp.dot(attended_other, out_other, preferred_element_type=jnp.float32)
    )
    mixed_share = normalize(middle_share, mix_gains).astype(jnp.bfloat16)

    logits = jnp.dot(mixed_share, w_router, preferred_element_type=jnp.float32)
    probabilities = softmax_rows(logits)
    chosen = jnp.sum(logits[:, None, :] * route_onehot, axis=-1)
    gate_soft = softmax_rows(chosen)
    gate_low = gate_soft.astype(jnp.bfloat16)
    fractions = counts / (total_tokens * choices_count)

    group_gates = jnp.concatenate(spread(gate_low), axis=0)
    gates = gate_table(group_routes, group_gates, first_expert, experts)
    place, begins, ends = placement(group_routes, first_expert, experts)
    gather_from = gather_tables(begins, ends, slots)
    blocks = gather_from[2]
    cot_slots = gather_rows(
        gather_from, place, None, cotangent_rows, slots, 0, experts, (hops[4],)
    )[0]
    mixed_across = order(swap(mixed_share), cot_slots)
    mixed_rows = [mixed_share, mixed_across, flip(mixed_share, 1), flip(mixed_across, 1)]
    misc = jnp.stack([core * experts, side, (rank // 4) % 2])
    weights = (w_gate, w_up, w_down)
    first_part = gather_rows(
        gather_from, place, gates, mixed_rows, slots, 0, CHUNK, (cot_slots, counts)
    )
    later_part = None
    carried = None
    chips = []
    for index in range(experts // CHUNK):
        if index == 1:
            later_part = gather_rows(
                gather_from, place, gates, mixed_rows, slots, CHUNK, experts - CHUNK, (carried,)
            )
        (x_slots, slot_gates), x_first = (later_part, CHUNK) if index else (first_part, 0)
        waits = []
        if index == 2:
            waits = [chips[0].one(carried)]
        elif index == 4:
            waits = [chips[0].two(carried)]
        far_first = int(index == FAR_FIRST)
        carried, send, keep = expert_call(
            blocks, misc, x_slots, cot_slots, slot_gates, weights, carried, slots,
            index * CHUNK, CHUNK, x_first, 0, depth, far_first, waits,
        )
        chips.append(ChipSum((send, keep), rank, far_first))
    waits = [chips[1].one(carried)]

    combine_from = combine_tables(begins, ends, slots)
    tiles = place.shape[1] // 4
    names = first_expert + jnp.arange(experts, dtype=jnp.int32)

    def combined(quarter, after):
        y, dx, gate_grads = combine_rows(
            combine_from, place, carried, quarter * tiles, tiles, after
        )
        gate_grads = gate_grads[:, :experts] + gate_grads[:, 64 : 64 + experts]
        rows = group_routes[quarter * share_rows : (quarter + 1) * share_rows]
        hit = rows[:, :, None] == names[None, None, :]
        return y, dx, jnp.sum(jnp.where(hit, gate_grads[:, None, :], 0.0), axis=2)

    far = combined(3, waits)
    far_y, far_dx, far_gg = (flip(value, 1) for value in far)
    cross = combined(1, [far[0]])
    dx_send = add_low(cross[1], far_dx)
    dx_across = swap(dx_send)
    gg_across = swap(cross[2] + far_gg)
    next_door = combined(2, [dx_send, chips[2].one(cross[1])])
    door_y, door_dx, door_gg = (flip(value, 1) for value in next_door)
    y_send = add_low(cross[0], far_y)
    near = combined(0, [next_door[0]])
    y_across = swap(order(y_send, near[0]))
    waits = [chips[1].two(near[0])]
    mixed_grad_share = (
        order(near[1], *waits).astype(jnp.float32)
        + door_dx.astype(jnp.float32)
        + dx_across.astype(jnp.float32)
    )
    gates_grad_share = near[2] + door_gg + gg_across

    upstream = cotangent.astype(jnp.float32)
    chosen_grad = gate_soft * (
        gates_grad_share - jnp.sum(gate_soft * gates_grad_share, axis=-1, keepdims=True)
    )
    logit_grad = jnp.sum(chosen_grad[:, :, None] * route_onehot, axis=1)
    prob_target = ALPHA * expert_count * fractions / total_tokens
    logit_grad = logit_grad + probabilities * (
        prob_target[None, :] - jnp.sum(probabilities * prob_target[None, :], axis=-1, keepdims=True)
    )
    router_grad = jnp.dot(
        mixed_share.astype(jnp.float32).T,
        logit_grad,
        precision=HIGHEST,
        preferred_element_type=jnp.float32,
    )
    mixed_grad_share = mixed_grad_share + jnp.dot(
        logit_grad,
        w_router.astype(jnp.float32).T,
        precision=HIGHEST,
        preferred_element_type=jnp.float32,
    )
    mix_pullback = jax.vjp(normalize, middle_share, mix_gains)[1]
    middle_from_norm, mix_gain_grad = mix_pullback(mixed_grad_share)
    middle_grad = upstream + middle_from_norm
    middle_low = middle_grad.astype(jnp.bfloat16)

    def half_back(saved, out_weights):
        attended_grad = dot_nt(middle_low, out_weights).astype(jnp.bfloat16)

        def part(chosen, after):
            return attend_back(
                saved, attended_grad, limits, tables, score_scale, chosen, after
            )

        return part

    pairs = key_width // 128
    other_grads = jnp.concatenate(
        half_back(saved_other, out_other)(
            (0, pairs), [*waits, chips[3].one(middle_low)]
        ),
        axis=1,
    )
    done = [chips[0].three(other_grads)]
    waits = [chips[2].two(other_grads), *done]
    other_grads = order(other_grads, *waits)
    expert_share = (
        near[0].astype(jnp.float32)
        + door_y.astype(jnp.float32)
        + order(y_across, other_grads).astype(jnp.float32)
    )
    output_share = (middle_share + expert_share).astype(jnp.bfloat16)
    joined_held = core_sum(dot_tn(normed, other_grads), core)
    joined_across = swap(joined_held)
    marked = order(middle_low, other_grads)
    out_held = core_sum(dot_tn(marked, attended_other), core)
    out_across = swap(order(out_held, joined_held))
    out_kept = core_sum(dot_tn(marked, attended_own), core)
    done.append(chips[1].three(joined_held))
    waits = [chips[4].one(joined_held), done[1], joined_held, out_held, out_kept, output_share]
    own_part = half_back(saved_own, w_out)
    front = own_part((0, pairs // 2), waits)
    back = own_part((pairs // 2, pairs - pairs // 2), [joined_across, front[0], chips[3].two(front[0])])
    own_grads = jnp.concatenate(
        [part for both in zip(front, back) for part in both], axis=1
    )
    out_half = add_low(out_kept, order(out_across, own_grads))
    own_weight_grads = dot_tn(normed, own_grads)
    own_held = core_sum(own_weight_grads, core)
    joined_total = plane_sum(add_low(own_held, joined_across), rank)
    out_total = plane_sum(out_half, rank, own_weight_grads)
    done.append(chips[2].three(own_grads))
    chips[4].two(own_grads)
    sums = done + [chips[i].three(own_weight_grads) for i in (3, 4)]
    other_normed = dot_nt(other_grads, joined_other)
    own_normed = dot_nt(order(own_grads, own_held), joined_own)
    input_pullback = jax.vjp(normalize, inputs_share, norm_gains)[1]
    input_from_norm, norm_gain_grad = input_pullback(other_normed + own_normed)
    input_grad_share = middle_grad + input_from_norm
    key_end = query_width + key_width
    small = all_sum(
        jnp.concatenate(
            [jnp.sum(probabilities, axis=0), mix_gain_grad, norm_gain_grad, router_grad.reshape(-1)]
        )
    )
    prob_sums = small[:expert_count]
    mix_gain_total = small[expert_count : expert_count + model_width]
    norm_gain_total = small[expert_count + model_width : expert_count + 2 * model_width]
    router_total = small[expert_count + 2 * model_width :].reshape(router_grad.shape)
    balance = expert_count * expert_count * fractions * prob_sums / total_tokens

    mine = jnp.concatenate(sums, axis=0).reshape(experts, 3, 2, depth // 2, -1)
    theirs = flip(pick_index(mine, 1 - core, 2), 1)
    mine = pick_index(mine, core, 2)
    def placed(kind):
        own_kind, other_kind = mine[:, kind], theirs[:, kind]
        return jnp.where(
            core == 0,
            jnp.concatenate([own_kind, other_kind], axis=0),
            jnp.concatenate([other_kind, own_kind], axis=0),
        ).astype(jnp.float32)

    return (
        output_share,
        balance,
        input_grad_share,
        norm_gain_total,
        joined_total[:, :query_width],
        joined_total[:, query_width:key_end],
        joined_total[:, key_end:],
        out_total.T,
        mix_gain_total,
        router_total,
        placed(0),
        placed(1),
        placed(2).transpose(0, 2, 1),
    )


def solution(mesh):
    sizes = dict(mesh.shape)
    paired = sizes["tensor"] == 2 and sizes["dp"] == 16
    return jax.shard_map(
        shards_pair if paired else shards_wide,
        mesh=mesh,
        in_specs=(
            P(("dp", "tensor"), None),
            P(),
            P(None, "tensor"),
            P(None, "tensor"),
            P(None, "tensor"),
            P("tensor", None),
            P(),
            P(),
            P("tensor", None, None),
            P("tensor", None, None),
            P("tensor", None, None),
            P("dp", None),
            P("dp", None),
            P(("dp", "tensor"), None),
        ),
        out_specs=(
            P(("dp", "tensor"), None),
            P(),
            P(("dp", "tensor"), None),
            P(),
            P("dp", "tensor"),
            P("dp", "tensor"),
            P("dp", "tensor"),
            P("tensor", "dp"),
            P(),
            P(),
            P("tensor", "dp", None),
            P("tensor", "dp", None),
            P("tensor", None, "dp"),
        ),
        check_vma=False,
    )
```

```python
import functools

import jax
import jax.numpy as jnp
from jax import lax
from jax.experimental import pallas as pl
from jax.experimental.pallas import tpu as pltpu
from jax.sharding import PartitionSpec as P

HD = 64
PIECE = 256
CAP = 614


EPSILON = 1e-06
ALPHA = 0.01
HIGHEST = lax.Precision.HIGHEST


def normalize(values, gains):
    return values * lax.rsqrt(jnp.mean(values * values, axis=-1, keepdims=True) + EPSILON) * gains


def softmax_rows(values):
    shifted = jnp.exp(values - jnp.max(values, axis=-1, keepdims=True))
    return shifted / jnp.sum(shifted, axis=-1, keepdims=True)


def contract_rows(left, right):
    return lax.dot_general(
        left, right, (((0,), (0,)), ((), ())), preferred_element_type=jnp.float32
    )


def contract_cols(left, right):
    return lax.dot_general(
        left, right, (((1,), (1,)), ((), ())), preferred_element_type=jnp.float32
    )


def rope_tables(sequence_length, head_width):
    half_width = head_width // 2
    frequency = 10000.0 ** (-(jnp.arange(half_width, dtype=jnp.float32) * 2.0 / head_width))
    angles = jnp.arange(sequence_length, dtype=jnp.float32)[:, None] * frequency[None, :]
    return (jnp.cos(angles), jnp.sin(angles))


def rotate(values, cosine, sine_table):
    half_width = values.shape[-1] // 2
    first_half = values[..., :half_width]
    second_half = values[..., half_width:]
    cosine_rows = cosine[:, None, :]
    sine_rows = sine_table[:, None, :]
    return jnp.concatenate(
        [
            first_half * cosine_rows - second_half * sine_rows,
            second_half * cosine_rows + first_half * sine_rows,
        ],
        axis=-1,
    )


def allowed_pairs(starts_row, sequence_length, piece_length):
    position = jnp.arange(sequence_length, dtype=jnp.int32)
    labels = jnp.full((sequence_length,), -1, jnp.int32)
    for piece_index in range(starts_row.shape[0]):
        inside = (position >= starts_row[piece_index]) & (
            position < starts_row[piece_index] + piece_length
        )
        labels = jnp.where(inside, piece_index, labels)
    causal = position[None, :] <= position[:, None]
    shared = (labels[:, None] == labels[None, :]) & (labels[:, None] >= 0)
    return causal | shared


def scores_of(query_block, key_block, allowed, score_scale):
    raw_scores = (
        jnp.einsum("qkgd,skd->kgqs", query_block, key_block, preferred_element_type=jnp.float32)
        * score_scale
    )
    return jnp.where(allowed, raw_scores, -1e30)


BLOCK = 256
PART = 128
PIECE_ROWS = 32
GROUP = 8
DEEP = 4
VMEM_LIMIT = 60 * 1024 * 1024


def dot_nt(left, right):
    return lax.dot_general(
        left, right, (((1,), (1,)), ((), ())), preferred_element_type=jnp.float32
    )


def dot_tn(left, right):
    return lax.dot_general(
        left, right, (((0,), (0,)), ((), ())), preferred_element_type=jnp.float32
    )


def round_up(value, multiple):
    return -(-value // multiple) * multiple


def placement(routes_rows, first_expert, experts):
    rows = routes_rows.shape[0]
    tiles = rows // BLOCK
    turned = routes_rows.T
    names = first_expert + jnp.arange(experts, dtype=jnp.int32)
    hit = turned[None, :, :] == names[:, None, None]
    member = jnp.any(hit, axis=1)
    upper = jnp.triu(jnp.ones((BLOCK, BLOCK), jnp.bfloat16))
    inside = jnp.dot(
        member.astype(jnp.bfloat16).reshape(experts * tiles, BLOCK),
        upper,
        preferred_element_type=jnp.float32,
    ).astype(jnp.int32).reshape(experts, tiles, BLOCK)
    sums = inside[:, :, -1]
    ends = jnp.cumsum(sums, axis=1)
    begins = ends - sums
    place = jnp.where(
        member.reshape(experts, tiles, BLOCK), begins[:, :, None] + inside - 1, -1
    )
    place = jnp.concatenate(
        [place, jnp.full((1, tiles, BLOCK), -1, jnp.int32)], axis=0
    ).reshape(experts + 1, tiles, 1, BLOCK)
    return place, begins, ends


def gate_table(routes_rows, gates_rows, first_expert, experts):
    names = first_expert + jnp.arange(experts, dtype=jnp.int32)
    hit = routes_rows.T[None, :, :] == names[:, None, None]
    table = jnp.sum(jnp.where(hit, gates_rows.astype(jnp.float32).T[None, :, :], 0.0), axis=1)
    return jnp.pad(table, ((0, 128 - experts), (0, 0))).T.astype(jnp.bfloat16)


def gather_tables(begins, ends, slots):
    counts = ends[:, -1]
    parts = jnp.arange(slots // PART, dtype=jnp.int32) * PART
    low = jnp.sum((ends[:, None, :] <= parts[None, :, None]).astype(jnp.int32), axis=2)
    high = jnp.sum((begins[:, None, :] < parts[None, :, None] + PART).astype(jnp.int32), axis=2)
    high = jnp.where(parts[None, :] < counts[:, None], high, low)
    blocks = jnp.maximum(-(-counts // BLOCK), 1)
    return low, high, blocks


def combine_tables(begins, ends, slots):
    experts, tiles = begins.shape
    width = round_up(experts * (BLOCK // PIECE_ROWS + 1), GROUP)
    first = begins // PIECE_ROWS
    amount = jnp.where(ends > begins, (ends - 1) // PIECE_ROWS - first + 1, 0)
    stop = jnp.cumsum(amount, axis=0)
    place = jnp.arange(width, dtype=jnp.int32)
    owner = jnp.sum(
        (stop.T[:, None, :] <= place[None, :, None]).astype(jnp.int32), axis=2
    )
    chosen = owner[:, :, None] == jnp.arange(experts, dtype=jnp.int32)[None, None, :]
    offset = jnp.sum(
        jnp.where(chosen, (first - (stop - amount)).T[:, None, :], 0), axis=2
    )
    valid = owner < experts
    piece = jnp.where(valid, offset + place[None, :], 0)
    source = jnp.where(valid, owner, 0) * (slots // PIECE_ROWS) + piece
    groups = jnp.maximum(-(-stop[-1] // GROUP), 1)
    return owner, piece, source, groups, width


def gather_kernel(sources, with_gates, after, low_ref, high_ref, blocks_ref, place_ref, *rest):
    if with_gates:
        gates_ref, rest = rest[0], rest[1:]
    inputs, rest = rest[:sources], rest[sources + after :]
    if with_gates:
        out_ref, gate_out_ref, held, buffer, gate_buffer, sems, out_sems = rest
    else:
        out_ref, held, buffer, sems, out_sems = rest
    expert = pl.program_id(0)
    share = inputs[0].shape[0]
    slots = out_ref.shape[0] // pl.num_programs(0)

    @pl.when(expert == 0)
    def _():
        copies = [
            pltpu.make_async_copy(ref, held.at[pl.ds(i * share, share)], sems.at[i])
            for i, ref in enumerate(inputs)
        ]
        for copy in copies:
            copy.start()
        for copy in copies:
            copy.wait()

    def copies_of(part, slot):
        start = pl.multiple_of(expert * slots + part * PART, PART)
        made = [
            pltpu.make_async_copy(
                buffer.at[slot], out_ref.at[pl.ds(start, PART)], out_sems.at[0, slot]
            )
        ]
        if with_gates:
            made.append(
                pltpu.make_async_copy(
                    gate_buffer.at[slot], gate_out_ref.at[pl.ds(start, PART)], out_sems.at[1, slot]
                )
            )
        return made

    parts = blocks_ref[expert] * (BLOCK // PART)

    def one(part, carry):
        slot = part % 2

        @pl.when(part >= 2)
        def _():
            for copy in copies_of(part - 2, slot):
                copy.wait()

        buffer[slot] = jnp.zeros(buffer.shape[1:], buffer.dtype)
        if with_gates:
            gate_buffer[slot] = jnp.zeros(gate_buffer.shape[1:], gate_buffer.dtype)
        rows = lax.broadcasted_iota(jnp.int32, (PART, BLOCK), 0) + part * PART

        def step(tile, carry):
            pick = jnp.where(rows == place_ref[expert, tile], 1.0, 0.0).astype(jnp.bfloat16)
            start = pl.multiple_of(tile * BLOCK, BLOCK)
            buffer[slot] += jnp.dot(
                pick, held[pl.ds(start, BLOCK), :], preferred_element_type=jnp.float32
            ).astype(buffer.dtype)
            if with_gates:
                gate_buffer[slot] += jnp.dot(
                    pick, gates_ref[pl.ds(start, BLOCK), :], preferred_element_type=jnp.float32
                )
            return carry

        lax.fori_loop(low_ref[expert, part], high_ref[expert, part], step, 0)
        for copy in copies_of(part, slot):
            copy.start()
        return carry

    lax.fori_loop(0, parts, one, 0)
    for back in (2, 1):
        for copy in copies_of(parts - back, (parts - back) % 2):
            copy.wait()


def gather_rows(tables, place, gates, sources, slots, first, count, after=()):
    low, high, blocks = tables
    low, high, blocks = (t[first : first + count] for t in (low, high, blocks))
    place = place[first : first + count]
    rows = place.shape[1] * BLOCK
    width = sources[0].shape[1]
    with_gates = gates is not None

    def whole(array):
        zeros = (0,) * array.ndim
        return pl.BlockSpec(array.shape, lambda *_: zeros)

    operands = [place] + ([gates] if with_gates else [])
    anywhere = pl.BlockSpec(memory_space=pl.ANY)
    in_specs = [whole(a) for a in operands] + [anywhere] * (len(sources) + len(after))
    out_shape = [jax.ShapeDtypeStruct((count * slots, width), jnp.bfloat16)]
    scratch = [
        pltpu.VMEM((rows, width), jnp.bfloat16),
        pltpu.VMEM((2, PART, width), jnp.bfloat16),
    ]
    if with_gates:
        out_shape.append(jax.ShapeDtypeStruct((count * slots, 128), jnp.float32))
        scratch.append(pltpu.VMEM((2, PART, 128), jnp.float32))
    return pl.pallas_call(
        functools.partial(gather_kernel, len(sources), with_gates, len(after)),
        grid_spec=pltpu.PrefetchScalarGridSpec(
            num_scalar_prefetch=3,
            grid=(count,),
            in_specs=in_specs,
            out_specs=[anywhere] * len(out_shape),
            scratch_shapes=scratch
            + [pltpu.SemaphoreType.DMA((len(sources),)), pltpu.SemaphoreType.DMA((2, 2))],
        ),
        out_shape=out_shape,
        compiler_params=pltpu.CompilerParams(vmem_limit_bytes=VMEM_LIMIT),
    )(low, high, blocks, *operands, *sources, *after)


def expert_kernel(
    first, split, depth, far_first, extra, blocks_ref, misc_ref, x_ref, c_ref, sg_ref, wg_ref,
    wu_ref, wd_ref, *rest
):
    yd_ref = rest[extra]
    rest = rest[extra + 1 :]
    width = x_ref.shape[1]
    if split:
        send_ref, keep_ref = rest[:2]
        rest = rest[2:]
    else:
        grads_ref = rest[0]
        rest = rest[1:]
    total_gu, total_d, x_held, c_held, low_held, gated_held = rest
    expert = first + pl.program_id(0)
    block = pl.program_id(1)
    hidden = wg_ref.shape[2]
    blocks = blocks_ref[expert]
    lanes = lax.broadcasted_iota(jnp.int32, (BLOCK, 128), 1)

    @pl.when(block < blocks)
    def _():
        x = x_ref[...]
        c = c_ref[...]
        gate = jnp.sum(jnp.where(lanes == expert, sg_ref[...], 0.0), axis=1, keepdims=True)
        gate_proj = jnp.dot(x, wg_ref[0], preferred_element_type=jnp.float32)
        up_proj = jnp.dot(x, wu_ref[0], preferred_element_type=jnp.float32)
        pulled = dot_nt(c, wd_ref[0])
        sigmoid = 1.0 / (1.0 + jnp.exp(-gate_proj))
        silu = gate_proj * sigmoid
        activated = (silu * up_proj).astype(jnp.bfloat16).astype(jnp.float32)
        gate_grad = jnp.sum(activated * pulled, axis=1, keepdims=True)
        coarse = gate_grad.astype(jnp.bfloat16).astype(jnp.float32)
        yd_ref[:, 2 * width :] = jnp.where(
            lanes == expert, coarse, jnp.where(lanes == expert + 64, gate_grad - coarse, 0.0)
        ).astype(yd_ref.dtype)
        gated = (gate * activated).astype(jnp.bfloat16)
        yd_ref[:, :width] = jnp.dot(
            gated, wd_ref[0], preferred_element_type=jnp.float32
        ).astype(yd_ref.dtype)
        activated_grad = gate * pulled
        gate_low = (
            activated_grad * up_proj * sigmoid * (1.0 + gate_proj * (1.0 - sigmoid))
        ).astype(jnp.bfloat16)
        up_low = (activated_grad * silu).astype(jnp.bfloat16)
        yd_ref[:, width : 2 * width] = (
            dot_nt(gate_low, wg_ref[0]) + dot_nt(up_low, wu_ref[0])
        ).astype(yd_ref.dtype)
        start = pl.multiple_of((block % 2) * BLOCK, BLOCK)
        held = pl.ds(start, BLOCK)
        x_held[held, :] = x
        c_held[held, :] = c
        low_held[held, :hidden] = gate_low
        low_held[held, hidden:] = up_low
        gated_held[held, :] = gated

    def gather(rows, fresh):
        for begin in range(0, width, BLOCK):
            span = slice(begin, begin + BLOCK)
            for total, left, right in (
                (total_gu, x_held, low_held),
                (total_d, c_held, gated_held),
            ):
                term = dot_tn(left[:rows, span], right[:rows, :])
                total[span, :] = term if fresh else total[span, :] + term

    odd = block % 2 == 1
    last = block == blocks - 1

    @pl.when((block == 0) & last)
    def _():
        gather(BLOCK, True)

    @pl.when((block == 1) & (block < blocks))
    def _():
        gather(2 * BLOCK, True)

    @pl.when((block > 1) & odd & (block < blocks))
    def _():
        gather(2 * BLOCK, False)

    @pl.when((block > 1) & jnp.logical_not(odd) & last)
    def _():
        gather(BLOCK, False)

    @pl.when(block == pl.num_programs(1) - 1)
    def _():
        parts = (
            (total_gu, 0),
            (total_gu, hidden),
            (total_d, 0),
        )
        for which, (ref, column) in enumerate(parts):
            if split:
                side = misc_ref[1 + far_first]
                for high in range(2):
                    for low in range(2):
                        for out, chosen in ((keep_ref, side), (send_ref, 1 - side)):
                            if far_first:
                                start = ((high * 2 + chosen) * 2 + low) * depth
                                place = (high, low, which)
                            else:
                                start = ((high * 2 + low) * 2 + chosen) * depth
                                place = (low, high, which)
                            out[place] = ref[
                                pl.ds(pl.multiple_of(start, 64), depth), pl.ds(column, hidden)
                            ].astype(out.dtype)
            else:
                grads_ref[0, which] = ref[:, pl.ds(column, hidden)].astype(grads_ref.dtype)


def expert_call(
    blocks, misc, x, c, sg, weights, carried, slots, first, count, x_first, c_first, depth,
    far_first=0, after=()
):
    w_gate, w_up, w_down = weights
    experts = blocks.shape[0]
    width = x.shape[1]
    hidden = w_gate.shape[2]
    most = slots // BLOCK
    split = depth is not None

    def rows_index(base):
        def index(expert, block, blocks, misc):
            limit = blocks[first + expert] - 1
            return ((first - base + expert) * most + jnp.minimum(block, limit), 0)

        return index

    def weight_index(expert, block, blocks, misc):
        return (misc[0] + first + expert, 0, 0)

    def grads_index(expert, block, blocks, misc):
        return (0, 0, expert, 0, 0)

    out_shape = [jax.ShapeDtypeStruct((experts * slots, 2 * width + 128), jnp.bfloat16)]
    out_specs = [pl.BlockSpec((BLOCK, 2 * width + 128), rows_index(0))]
    if split:
        out_shape += [jax.ShapeDtypeStruct((2, 2, 3 * count, depth, hidden), jnp.bfloat16)] * 2
        out_specs += [pl.BlockSpec((2, 2, 3, depth, hidden), grads_index)] * 2
    else:
        out_shape += [jax.ShapeDtypeStruct((count, 3, width, hidden), jnp.bfloat16)]
        out_specs += [pl.BlockSpec((1, 3, width, hidden), lambda e, b, *_: (e, 0, 0, 0))]
    operands = [x, c, sg, w_gate, w_up, w_down]
    in_specs = [
        pl.BlockSpec((BLOCK, width), rows_index(x_first)),
        pl.BlockSpec((BLOCK, width), rows_index(c_first)),
        pl.BlockSpec((BLOCK, 128), rows_index(x_first)),
        pl.BlockSpec((1, width, hidden), weight_index),
        pl.BlockSpec((1, width, hidden), weight_index),
        pl.BlockSpec((1, hidden, width), weight_index),
    ]
    aliases = {}
    if carried is not None:
        operands.append(carried)
        aliases = {8: 0}
    operands += list(after)
    extra = len(operands) - 6
    in_specs += [pl.BlockSpec(memory_space=pl.ANY)] * extra
    return pl.pallas_call(
        functools.partial(expert_kernel, first, split, depth, far_first, extra),
        grid_spec=pltpu.PrefetchScalarGridSpec(
            num_scalar_prefetch=2,
            grid=(count, most),
            in_specs=in_specs,
            out_specs=out_specs,
            scratch_shapes=[
                pltpu.VMEM((width, 2 * hidden), jnp.float32),
                pltpu.VMEM((width, hidden), jnp.float32),
                pltpu.VMEM((2 * BLOCK, width), jnp.bfloat16),
                pltpu.VMEM((2 * BLOCK, width), jnp.bfloat16),
                pltpu.VMEM((2 * BLOCK, 2 * hidden), jnp.bfloat16),
                pltpu.VMEM((2 * BLOCK, hidden), jnp.bfloat16),
            ],
        ),
        out_shape=out_shape,
        input_output_aliases=aliases,
        compiler_params=pltpu.CompilerParams(vmem_limit_bytes=VMEM_LIMIT),
    )(blocks, misc, *operands)


def combine_kernel(
    first, owner_ref, piece_ref, source_ref, groups_ref, begin_ref, tile_ref, place_ref, yd_ref, *rest
):
    y_out, dx_out, gate_out, buffer, total, sems = rest[-6:]
    columns = y_out.shape[1]
    step = pl.program_id(0)
    tile = first + step

    head = begin_ref[first]
    final = first + pl.num_programs(0) - 1
    stop = begin_ref[final] + groups_ref[final]

    def copies(place):
        which_tile = tile_ref[place]
        group = place - begin_ref[which_tile]
        slot = (place - head) % DEEP
        made = []
        for i in range(GROUP):
            source = pl.multiple_of(
                source_ref[which_tile, group * GROUP + i] * PIECE_ROWS, PIECE_ROWS
            )
            made.append(
                pltpu.make_async_copy(
                    yd_ref.at[pl.ds(source, PIECE_ROWS)],
                    buffer.at[slot, pl.ds(i * PIECE_ROWS, PIECE_ROWS)],
                    sems.at[slot, i],
                )
            )
        return made

    @pl.when(step == 0)
    def _():
        for ahead in range(DEEP - 1):

            @pl.when(head + ahead < stop)
            def _():
                for copy in copies(head + ahead):
                    copy.start()

    def one(group, carry):
        place = begin_ref[tile] + group
        slot = (place - head) % DEEP

        @pl.when(place + DEEP - 1 < stop)
        def _():
            for copy in copies(place + DEEP - 1):
                copy.start()

        picks = []
        for i in range(GROUP):
            entry = group * GROUP + i
            rows = (
                lax.broadcasted_iota(jnp.int32, (PIECE_ROWS, BLOCK), 0)
                + piece_ref[tile, entry] * PIECE_ROWS
            )
            picks.append(jnp.where(rows == place_ref[owner_ref[tile, entry], step], 1.0, 0.0))
        picked = jnp.concatenate(picks, axis=0).T.astype(jnp.bfloat16)
        for copy in copies(place):
            copy.wait()
        fresh = group == 0
        for begin in range(0, total.shape[1], 640):
            span = slice(begin, begin + 640)
            term = jnp.dot(picked, buffer[slot, :, span], preferred_element_type=jnp.float32)
            total[:, span] = jnp.where(fresh, 0.0, total[:, span]) + term
        return carry

    lax.fori_loop(0, groups_ref[tile], one, 0)
    y_out[...] = total[:, :columns].astype(y_out.dtype)
    dx_out[...] = total[:, columns : 2 * columns].astype(dx_out.dtype)
    gate_out[...] = total[:, 2 * columns :]


def combine_rows(tables, place, yd, first, count, after=()):
    owner, piece, source, groups, width = tables
    ends = jnp.cumsum(groups)
    begin = ends - groups
    most = groups.shape[0] * (width // GROUP)
    tile_of = jnp.minimum(
        jnp.sum((ends[None, :] <= jnp.arange(most)[:, None]).astype(jnp.int32), axis=1),
        groups.shape[0] - 1,
    )
    experts = place.shape[0]
    whole_width = yd.shape[1]
    columns = (whole_width - 128) // 2
    row_block = lambda wide: pl.BlockSpec((BLOCK, wide), lambda t, *_: (t, 0))
    return pl.pallas_call(
        functools.partial(combine_kernel, first),
        grid_spec=pltpu.PrefetchScalarGridSpec(
            num_scalar_prefetch=6,
            grid=(count,),
            in_specs=[pl.BlockSpec((experts, count, 1, BLOCK), lambda *_: (0, first // count, 0, 0))]
            + [pl.BlockSpec(memory_space=pl.ANY)] * (1 + len(after)),
            out_specs=[row_block(columns), row_block(columns), row_block(128)],
            scratch_shapes=[
                pltpu.VMEM((DEEP, GROUP * PIECE_ROWS, whole_width), jnp.bfloat16),
                pltpu.VMEM((BLOCK, whole_width), jnp.float32),
                pltpu.SemaphoreType.DMA((DEEP, GROUP)),
            ],
        ),
        out_shape=[
            jax.ShapeDtypeStruct((count * BLOCK, columns), jnp.bfloat16),
            jax.ShapeDtypeStruct((count * BLOCK, columns), jnp.bfloat16),
            jax.ShapeDtypeStruct((count * BLOCK, 128), jnp.float32),
        ],
        compiler_params=pltpu.CompilerParams(vmem_limit_bytes=VMEM_LIMIT),
    )(owner, piece, source, groups, begin, tile_of, place, yd, *after)


def flip(value, bit):
    size = lax.axis_size("dp")
    return lax.ppermute(value, "dp", [(i, i ^ bit) for i in range(size)])


def swap(value):
    return lax.ppermute(value, "tensor", [(0, 1), (1, 0)])


def order(value, *after):
    return lax.optimization_barrier((value, *after))[0] if after else value


def add_low(left, right):
    return (left.astype(jnp.float32) + right.astype(jnp.float32)).astype(jnp.bfloat16)


def pick_index(value, index, axis):
    return lax.dynamic_index_in_dim(value, index, axis, keepdims=False)


def sum_stage(parts, bit, chosen, after):
    send, keep = parts
    got = order(flip(send, bit), *after)
    return tuple(
        add_low(pick_index(keep, which, 0), pick_index(got, which, 0))
        for which in (1 - chosen, chosen)
    )


class ChipSum:
    def __init__(self, parts, rank, far_first):
        side, low_bit, high_bit = (rank // 2) % 2, (rank // 4) % 2, rank // 8
        self.parts = parts
        self.first = (4, high_bit) if far_first else (2, low_bit)
        self.second = (8, side) if far_first else (4, high_bit)
        self.last = 2 if far_first else 8

    def one(self, *after):
        self.parts = sum_stage(self.parts, *self.first, after)
        return self.parts[0]

    def two(self, *after):
        self.parts = sum_stage(self.parts, *self.second, after)
        return self.parts[0]

    def three(self, *after):
        send, keep = self.parts
        return add_low(keep, order(flip(send, self.last), *after))


def core_sum(value, core):
    rows, columns = value.shape
    value = value.reshape(8, 2, rows // 16, columns)
    got = flip(pick_index(value, 1 - core, 1).astype(jnp.bfloat16), 1)
    return add_low(pick_index(value, core, 1), got)


def plane_sum(total, rank, marks=((), (), ())):
    side, low_bit, high_bit = (rank // 2) % 2, (rank // 4) % 2, rank // 8
    part, columns = total.shape[1:]
    total = total.reshape(4, 2, part, columns)
    got = order(flip(pick_index(total, 1 - side, 1), 2), *marks[0])
    first = add_low(pick_index(total, side, 1), got).reshape(2, 2, part, columns)
    got = order(flip(pick_index(first, 1 - low_bit, 1), 4), *marks[1])
    second = add_low(pick_index(first, low_bit, 1), got)
    got = order(flip(pick_index(second, 1 - high_bit, 0), 8), *marks[2])
    last = pick_index(second, high_bit, 0).astype(jnp.float32) + got.astype(jnp.float32)
    return last, first, second


def fetch_other(weights, core, side, after=()):
    rows = weights[0].shape[0] // 4
    start = (side * 2 + core) * rows
    own = jnp.concatenate(
        [lax.dynamic_slice_in_dim(w, start, rows, 0) for w in weights], axis=1
    )
    pieces = swap(order(own, *after))
    turned = flip(pieces, 2)
    result = jnp.zeros((4 * rows, own.shape[1]), own.dtype)
    for value, place in (
        (pieces, side * 2 + core),
        (turned, (1 - side) * 2 + core),
        (flip(pieces, 1), side * 2 + 1 - core),
        (flip(turned, 1), (1 - side) * 2 + 1 - core),
    ):
        result = lax.dynamic_update_slice_in_dim(result, value, place * rows, 0)
    return result, own, pieces


ROWS = 256
HALF = 512


def lane_swap(values):
    width = values.shape[1]
    lane = lax.broadcasted_iota(jnp.int32, values.shape, 1) % HD
    ahead = pltpu.roll(values, width - HD // 2, 1)
    behind = pltpu.roll(values, HD // 2, 1)
    return jnp.where(lane < HD // 2, ahead, behind)


def turn_tables(rows):
    cosine, sine = rope_tables(rows, HD)
    return (
        jnp.concatenate([cosine] * 4, axis=1),
        jnp.concatenate([-sine, sine, -sine, sine], axis=1),
    )


def project_kernel(sizes, score_scale, normed_ref, weights_ref, cosine_ref, sine_ref, *outs):
    query_ref, key_ref, value_ref = outs[-3:]
    query_width, key_width = sizes
    projected = jnp.dot(normed_ref[...], weights_ref[...], preferred_element_type=jnp.float32)
    cosine, sine = cosine_ref[...], sine_ref[...]
    for start in range(0, query_width + key_width, 128):
        piece = projected[:, start : start + 128]
        turned = piece * cosine + lane_swap(piece) * sine
        if start < query_width:
            query_ref[:, start : start + 128] = (turned * score_scale).astype(jnp.bfloat16)
        else:
            begin = start - query_width
            key_ref[:, begin : begin + 128] = turned.astype(jnp.bfloat16)
    value_ref[...] = projected[:, query_width + key_width :].astype(jnp.bfloat16)


def project(normed, weights, tables, query_width, key_width, score_scale, after=()):
    rows, depth = normed.shape
    width = weights.shape[1]
    row_spec = lambda columns: pl.BlockSpec((ROWS, columns), lambda i: (i, 0))
    return pl.pallas_call(
        functools.partial(project_kernel, (query_width, key_width), score_scale),
        grid=(rows // ROWS,),
        in_specs=[
            row_spec(depth),
            pl.BlockSpec((depth, width), lambda i: (0, 0)),
            row_spec(128),
            row_spec(128),
        ]
        + [pl.BlockSpec(memory_space=pl.ANY)] * len(after),
        out_specs=[row_spec(query_width), row_spec(key_width), row_spec(key_width)],
        out_shape=[
            jax.ShapeDtypeStruct((rows, query_width), jnp.bfloat16),
            jax.ShapeDtypeStruct((rows, key_width), jnp.bfloat16),
            jax.ShapeDtypeStruct((rows, key_width), jnp.bfloat16),
        ],
        compiler_params=pltpu.CompilerParams(vmem_limit_bytes=VMEM_LIMIT),
    )(normed, weights, *tables, *after)


def attend_kernel(per_pair, query_ref, key_ref, value_ref, limit_ref, *rest):
    out_ref, lse_ref = rest[-2:]
    step = pl.program_id(1)

    def work(keys):
        columns = lax.broadcasted_iota(jnp.int32, (ROWS, HALF), 1) + (keys - HALF)
        allowed = columns <= limit_ref[...]
        lanes = lax.broadcasted_iota(jnp.int32, (ROWS, 128), 1)
        sums = jnp.zeros((ROWS, 128), jnp.float32)
        pieces = []
        for head in range(per_pair):
            group = head // (per_pair // 2)
            query = query_ref[:, head * HD : (head + 1) * HD]
            key = key_ref[:keys, group * HD : (group + 1) * HD]
            value = value_ref[:keys, group * HD : (group + 1) * HD]
            scores = dot_nt(query, key)
            last = jnp.where(allowed, scores[:, keys - HALF :], -1e30)
            scores = last if keys == HALF else jnp.concatenate([scores[:, : keys - HALF], last], 1)
            highest = jnp.max(scores, axis=1, keepdims=True)
            shifted = jnp.exp(scores - highest)
            total = jnp.sum(shifted, axis=1, keepdims=True)
            mixed = jnp.dot(
                shifted.astype(jnp.bfloat16), value, preferred_element_type=jnp.float32
            )
            pieces.append((mixed / total).astype(jnp.bfloat16))
            sums = jnp.where(lanes == head, highest + jnp.log(total), sums)
        out_ref[...] = jnp.concatenate(pieces, axis=1)
        lse_ref[0] = sums

    halfway = pl.num_programs(1) // 2

    @pl.when(step < halfway)
    def _():
        work(HALF)

    @pl.when(step >= halfway)
    def _():
        work(2 * HALF)


def attend(query, key, value, limits, after=()):
    rows, query_width = query.shape
    pairs = key.shape[1] // 128
    wide = query_width // pairs
    return pl.pallas_call(
        functools.partial(attend_kernel, wide // HD),
        grid=(pairs, rows // ROWS),
        in_specs=[
            pl.BlockSpec((ROWS, wide), lambda p, i: (i, p)),
            pl.BlockSpec((rows, 128), lambda p, i: (0, p)),
            pl.BlockSpec((rows, 128), lambda p, i: (0, p)),
            pl.BlockSpec((ROWS, 1), lambda p, i: (i, 0)),
        ]
        + [pl.BlockSpec(memory_space=pl.ANY)] * len(after),
        out_specs=[
            pl.BlockSpec((ROWS, wide), lambda p, i: (i, p)),
            pl.BlockSpec((1, ROWS, 128), lambda p, i: (p, i, 0)),
        ],
        out_shape=[
            jax.ShapeDtypeStruct((rows, query_width), jnp.bfloat16),
            jax.ShapeDtypeStruct((pairs, rows, 128), jnp.float32),
        ],
        compiler_params=pltpu.CompilerParams(vmem_limit_bytes=VMEM_LIMIT),
    )(query, key, value, limits, *after)


def back_kernel(
    per_pair, score_scale, after, query_ref, key_ref, value_ref, turned_key_ref, grad_ref, lse_ref,
    limit_ref, cosine_ref, sine_ref, all_cosine_ref, all_sine_ref, *rest
):
    query_out, key_out, value_out, key_total, value_total = rest[after:]
    step = pl.program_id(1)
    halfway = pl.num_programs(1) // 2

    @pl.when(step == 0)
    def _():
        key_total[...] = jnp.zeros_like(key_total)
        value_total[...] = jnp.zeros_like(value_total)

    def work(keys):
        rows = lax.broadcasted_iota(jnp.int32, (HALF, ROWS), 0) + (keys - HALF)
        allowed = rows <= limit_ref[...]
        made = []
        key_parts, value_parts = [], []
        for group in range(2):
            span = slice(group * HD, (group + 1) * HD)
            key, value = key_ref[:keys, span], value_ref[:keys, span]
            key_part = value_part = 0.0
            for head in range(group * per_pair // 2, (group + 1) * per_pair // 2):
                query = query_ref[:, head * HD : (head + 1) * HD]
                grad = grad_ref[:, head * HD : (head + 1) * HD]
                scores = dot_nt(key, query)
                last = jnp.where(allowed, scores[keys - HALF :], -1e30)
                scores = (
                    last
                    if keys == HALF
                    else jnp.concatenate([scores[: keys - HALF], last], axis=0)
                )
                weights = jnp.exp(scores - lse_ref[0, head : head + 1, :])
                pulled = dot_nt(value, grad)
                inner = jnp.sum(weights * pulled, axis=0, keepdims=True)
                score_low = (weights * (pulled - inner)).astype(jnp.bfloat16)
                value_part += jnp.dot(
                    weights.astype(jnp.bfloat16), grad, preferred_element_type=jnp.float32
                )
                key_part += jnp.dot(score_low, query, preferred_element_type=jnp.float32)
                made.append(
                    jnp.dot(
                        turned_key_ref[0, span, :keys],
                        score_low,
                        preferred_element_type=jnp.float32,
                    )
                )
            key_parts.append(key_part)
            value_parts.append(value_part)
        key_total[:keys] += jnp.concatenate(key_parts, axis=1)
        value_total[:keys] += jnp.concatenate(value_parts, axis=1)
        cosine, sine = cosine_ref[...], sine_ref[...]
        for index in range(per_pair // 2):
            both = jnp.concatenate(made[2 * index : 2 * index + 2], axis=0).T * score_scale
            query_out[:, index * 128 : (index + 1) * 128] = (
                both * cosine - lane_swap(both) * sine
            ).astype(jnp.bfloat16)

    @pl.when(step < halfway)
    def _():
        work(HALF)

    @pl.when(step >= halfway)
    def _():
        work(2 * HALF)

    @pl.when(step == pl.num_programs(1) - 1)
    def _():
        total = key_total[...]
        key_out[...] = (
            total * all_cosine_ref[...] - lane_swap(total) * all_sine_ref[...]
        ).astype(jnp.bfloat16)
        value_out[...] = value_total[...].astype(jnp.bfloat16)


def attend_back(saved, attended_grad, limits, tables, score_scale, chosen, after=()):
    query, key, value, lse = saved
    rows, query_width = query.shape
    pairs = key.shape[1] // 128
    wide = query_width // pairs
    turned_key = key.T.reshape(pairs, 128, rows)
    lse_rows = lse[:, :, :8].transpose(0, 2, 1)
    cosine, sine = tables
    begin, count = chosen
    block = lambda columns: pl.BlockSpec((ROWS, columns), lambda p, i: (i, p + begin))
    whole = pl.BlockSpec((rows, 128), lambda p, i: (0, p + begin))
    block_out = pl.BlockSpec((ROWS, wide), lambda p, i: (i, p))
    whole_out = pl.BlockSpec((rows, 128), lambda p, i: (0, p))
    table = pl.BlockSpec((ROWS, 128), lambda p, i: (i, 0))
    full_table = pl.BlockSpec((rows, 128), lambda p, i: (0, 0))
    return pl.pallas_call(
        functools.partial(back_kernel, wide // HD, score_scale, len(after)),
        grid=(count, rows // ROWS),
        in_specs=[
            block(wide),
            whole,
            whole,
            pl.BlockSpec((1, 128, rows), lambda p, i: (p + begin, 0, 0)),
            block(wide),
            pl.BlockSpec((1, 8, ROWS), lambda p, i: (p + begin, 0, i)),
            pl.BlockSpec((1, ROWS), lambda p, i: (0, i)),
            table,
            table,
            full_table,
            full_table,
        ]
        + [pl.BlockSpec(memory_space=pl.ANY)] * len(after),
        out_specs=[block_out, whole_out, whole_out],
        out_shape=[
            jax.ShapeDtypeStruct((rows, count * wide), jnp.bfloat16),
            jax.ShapeDtypeStruct((rows, count * 128), jnp.bfloat16),
            jax.ShapeDtypeStruct((rows, count * 128), jnp.bfloat16),
        ],
        scratch_shapes=[
            pltpu.VMEM((rows, 128), jnp.float32),
            pltpu.VMEM((rows, 128), jnp.float32),
        ],
        compiler_params=pltpu.CompilerParams(vmem_limit_bytes=VMEM_LIMIT),
    )(
        query, key, value, turned_key, attended_grad, lse_rows, limits.T, cosine, sine, cosine,
        sine, *after,
    )


def piece_limits(starts_row, rows):
    position = jnp.arange(rows, dtype=jnp.int32)
    limits = position
    for index in range(starts_row.shape[0]):
        start = starts_row[index]
        inside = (position >= start) & (position < start + PIECE)
        limits = jnp.where(inside, start + PIECE - 1, limits)
    return limits[:, None]


def slot_table(routes, expert_count, capacity):
    flattened = routes.reshape(-1)
    onehot = (flattened[:, None] == jnp.arange(expert_count, dtype=jnp.int32)[None, :]).astype(
        jnp.int32
    )
    placed = jnp.sum((jnp.cumsum(onehot, axis=0) - 1) * onehot, axis=1)
    entries = jnp.arange(flattened.shape[0], dtype=jnp.int32)
    return (
        jnp.full((expert_count * capacity,), flattened.shape[0], jnp.int32)
        .at[flattened * capacity + placed]
        .set(entries)
    )


def expert_forward(expert_inputs, w_gate, w_up, w_down):
    gate_proj = jnp.einsum(
        "ecd,edf->ecf", expert_inputs, w_gate, preferred_element_type=jnp.float32
    )
    up_proj = jnp.einsum("ecd,edf->ecf", expert_inputs, w_up, preferred_element_type=jnp.float32)
    activated = (gate_proj * jax.nn.sigmoid(gate_proj) * up_proj).astype(jnp.bfloat16)
    returned = jnp.einsum("ecf,efd->ecd", activated, w_down, preferred_element_type=jnp.float32)
    return (gate_proj, up_proj, activated, returned)


def shards_wide(
    tokens,
    norm_gains,
    w_query,
    w_key,
    w_value,
    w_out,
    mix_gains,
    w_router,
    w_gate,
    w_up,
    w_down,
    routes,
    starts,
    cotangent,
):
    share_rows = tokens.shape[0]
    model_width = tokens.shape[1]
    head_width = HD
    query_width = w_query.shape[1]
    key_width = w_key.shape[1]
    heads_here = query_width // head_width
    groups_here = key_width // head_width
    per_group = heads_here // groups_here
    experts_here = w_gate.shape[0]
    group_rows = routes.shape[0]
    choices_count = routes.shape[1]
    sequences_here = starts.shape[0]
    sequence_length = group_rows // sequences_here
    expert_count = w_router.shape[1]
    tensor_rank = lax.axis_index("tensor")
    total_tokens = group_rows * lax.axis_size("dp")
    score_scale = head_width ** (-0.5)
    inputs_share = tokens.astype(jnp.float32)
    normed_share = normalize(inputs_share, norm_gains).astype(jnp.bfloat16)
    normed = lax.all_gather(normed_share, "tensor", axis=0, tiled=True)
    joined_weights = jnp.concatenate([w_query, w_key, w_value], axis=1)
    projected = jnp.dot(normed, joined_weights, preferred_element_type=jnp.float32)
    cosine, sine_table = rope_tables(sequence_length, head_width)
    cosine_rows = jnp.tile(cosine, (sequences_here, 1))
    sine_rows = jnp.tile(sine_table, (sequences_here, 1))
    query_rows = rotate(
        projected[:, :query_width].reshape(group_rows, heads_here, head_width),
        cosine_rows,
        sine_rows,
    ).astype(jnp.bfloat16)
    key_rows = rotate(
        projected[:, query_width : query_width + key_width].reshape(
            group_rows, groups_here, head_width
        ),
        cosine_rows,
        sine_rows,
    ).astype(jnp.bfloat16)
    value_rows = (
        projected[:, query_width + key_width :]
        .astype(jnp.bfloat16)
        .reshape(group_rows, groups_here, head_width)
    )
    attended_parts = []
    logsum_parts = []
    for sequence in range(sequences_here):
        first_row = sequence * sequence_length
        query_block = query_rows[first_row : first_row + sequence_length].reshape(
            sequence_length, groups_here, per_group, head_width
        )
        key_block = key_rows[first_row : first_row + sequence_length]
        value_block = value_rows[first_row : first_row + sequence_length]
        allowed = allowed_pairs(starts[sequence], sequence_length, PIECE)
        scores = scores_of(query_block, key_block, allowed, score_scale)
        highest = jnp.max(scores, axis=-1, keepdims=True)
        shifted = jnp.exp(scores - highest)
        totals = jnp.sum(shifted, axis=-1, keepdims=True)
        weights = (shifted / totals).astype(jnp.bfloat16)
        mixed_values = jnp.einsum(
            "kgqs,skd->qkgd", weights, value_block, preferred_element_type=jnp.float32
        )
        attended_parts.append(
            mixed_values.reshape(sequence_length, query_width).astype(jnp.bfloat16)
        )
        logsum_parts.append(highest + jnp.log(totals))
    attended = jnp.concatenate(attended_parts, axis=0)
    attention_share = lax.psum_scatter(
        jnp.dot(attended, w_out, preferred_element_type=jnp.float32),
        "tensor",
        scatter_dimension=0,
        tiled=True,
    )
    middle_share = inputs_share + attention_share
    mixed_share = normalize(middle_share, mix_gains).astype(jnp.bfloat16)
    share_routes = lax.dynamic_slice_in_dim(routes, tensor_rank * share_rows, share_rows, 0)
    route_onehot = (
        share_routes[:, :, None] == jnp.arange(expert_count, dtype=jnp.int32)[None, None, :]
    ).astype(jnp.float32)
    logits = jnp.dot(mixed_share, w_router, preferred_element_type=jnp.float32)
    probabilities = softmax_rows(logits)
    chosen = jnp.sum(logits[:, None, :] * route_onehot, axis=-1)
    gate_soft = softmax_rows(chosen)
    gate_low = gate_soft.astype(jnp.bfloat16)
    counts, prob_sums = lax.psum(
        (jnp.sum(route_onehot, axis=(0, 1)), jnp.sum(probabilities, axis=0)), ("dp", "tensor")
    )
    fractions = counts / (total_tokens * choices_count)
    balance = expert_count * expert_count * fractions * prob_sums / total_tokens
    mixed_rows, gate_rows = (
        lax.all_gather(mixed_share, "tensor", axis=0, tiled=True),
        lax.all_gather(gate_low, "tensor", axis=0, tiled=True),
    )
    slots_all = slot_table(routes, expert_count, CAP)
    slots = lax.dynamic_slice_in_dim(
        slots_all, tensor_rank * experts_here * CAP, experts_here * CAP, 0
    )
    owners = slots // choices_count
    padded_rows = jnp.concatenate([mixed_rows, jnp.zeros((1, model_width), jnp.bfloat16)], axis=0)
    padded_gates = jnp.concatenate(
        [gate_rows.reshape(-1).astype(jnp.float32), jnp.zeros((1,), jnp.float32)], axis=0
    )
    slot_gates = padded_gates[slots]
    expert_inputs = padded_rows[owners].reshape(experts_here, CAP, model_width)
    gate_proj, up_proj, activated, returned = expert_forward(expert_inputs, w_gate, w_up, w_down)
    returned_flat = returned.reshape(experts_here * CAP, model_width)
    expert_partial = jax.ops.segment_sum(
        slot_gates[:, None] * returned_flat, owners, num_segments=group_rows + 1
    )[:group_rows]
    expert_share = lax.psum_scatter(
        expert_partial.astype(jnp.bfloat16), "tensor", scatter_dimension=0, tiled=True
    ).astype(jnp.float32)
    output_share = (middle_share + expert_share).astype(jnp.bfloat16)
    upstream = cotangent.astype(jnp.float32)
    upstream_rows = lax.all_gather(cotangent, "tensor", axis=0, tiled=True)
    padded_upstream = jnp.concatenate(
        [upstream_rows, jnp.zeros((1, model_width), jnp.bfloat16)], axis=0
    )
    slot_upstream = padded_upstream[owners].astype(jnp.float32)
    slot_cotangent = (
        (slot_gates[:, None] * slot_upstream)
        .astype(jnp.bfloat16)
        .reshape(experts_here, CAP, model_width)
    )
    slot_gate_grad = jnp.sum(slot_upstream * returned_flat, axis=1)
    activated_grad = jnp.einsum(
        "ecd,efd->ecf", slot_cotangent, w_down, preferred_element_type=jnp.float32
    )
    down_grad = jnp.einsum(
        "ecf,ecd->efd", activated, slot_cotangent, preferred_element_type=jnp.float32
    )
    sigmoid_gate = jax.nn.sigmoid(gate_proj)
    gate_proj_low = (
        activated_grad * up_proj * sigmoid_gate * (1.0 + gate_proj * (1.0 - sigmoid_gate))
    ).astype(jnp.bfloat16)
    up_proj_low = (activated_grad * gate_proj * sigmoid_gate).astype(jnp.bfloat16)
    inputs_grad = jnp.einsum(
        "ecf,edf->ecd", gate_proj_low, w_gate, preferred_element_type=jnp.float32
    ) + jnp.einsum("ecf,edf->ecd", up_proj_low, w_up, preferred_element_type=jnp.float32)
    gate_grad = jnp.einsum(
        "ecd,ecf->edf", expert_inputs, gate_proj_low, preferred_element_type=jnp.float32
    )
    up_grad = jnp.einsum(
        "ecd,ecf->edf", expert_inputs, up_proj_low, preferred_element_type=jnp.float32
    )
    mixed_partial = jax.ops.segment_sum(
        inputs_grad.reshape(experts_here * CAP, model_width), owners, num_segments=group_rows + 1
    )[:group_rows]
    gate_partial = jax.ops.segment_sum(
        slot_gate_grad, slots, num_segments=group_rows * choices_count + 1
    )[: group_rows * choices_count].reshape(group_rows, choices_count)
    mixed_grad_share, gates_grad_share = (
        lax.psum_scatter(mixed_partial, "tensor", scatter_dimension=0, tiled=True),
        lax.psum_scatter(gate_partial, "tensor", scatter_dimension=0, tiled=True),
    )
    gate_total, up_total = (
        lax.psum_scatter(
            gate_grad.astype(jnp.bfloat16), "dp", scatter_dimension=1, tiled=True
        ).astype(jnp.float32),
        lax.psum_scatter(
            up_grad.astype(jnp.bfloat16), "dp", scatter_dimension=1, tiled=True
        ).astype(jnp.float32),
    )
    down_total = lax.psum_scatter(
        down_grad.astype(jnp.bfloat16), "dp", scatter_dimension=2, tiled=True
    ).astype(jnp.float32)
    chosen_grad = gate_soft * (
        gates_grad_share - jnp.sum(gate_soft * gates_grad_share, axis=-1, keepdims=True)
    )
    logit_grad = jnp.sum(chosen_grad[:, :, None] * route_onehot, axis=1)
    prob_target = ALPHA * expert_count * fractions / total_tokens
    logit_grad = logit_grad + probabilities * (
        prob_target[None, :] - jnp.sum(probabilities * prob_target[None, :], axis=-1, keepdims=True)
    )
    mixed_float = mixed_share.astype(jnp.float32)
    router_grad = jnp.dot(
        mixed_float.T, logit_grad, precision=HIGHEST, preferred_element_type=jnp.float32
    )
    mixed_grad_share = mixed_grad_share + jnp.dot(
        logit_grad,
        w_router.astype(jnp.float32).T,
        precision=HIGHEST,
        preferred_element_type=jnp.float32,
    )
    mix_pullback = jax.vjp(normalize, middle_share, mix_gains)[1]
    middle_from_norm, mix_gain_grad = mix_pullback(mixed_grad_share)
    middle_grad = upstream + middle_from_norm
    middle_low = middle_grad.astype(jnp.bfloat16)
    middle_rows = lax.all_gather(middle_low, "tensor", axis=0, tiled=True)
    out_grad = contract_rows(attended, middle_rows)
    attended_grad = contract_cols(middle_rows, w_out).astype(jnp.bfloat16)
    query_parts = []
    key_parts = []
    value_parts = []
    for sequence in range(sequences_here):
        first_row = sequence * sequence_length
        query_block = query_rows[first_row : first_row + sequence_length].reshape(
            sequence_length, groups_here, per_group, head_width
        )
        key_block = key_rows[first_row : first_row + sequence_length]
        value_block = value_rows[first_row : first_row + sequence_length]
        allowed = allowed_pairs(starts[sequence], sequence_length, PIECE)
        scores = scores_of(query_block, key_block, allowed, score_scale)
        weights_full = jnp.exp(scores - logsum_parts[sequence])
        weights_low = weights_full.astype(jnp.bfloat16)
        grad_block = attended_grad[first_row : first_row + sequence_length].reshape(
            sequence_length, groups_here, per_group, head_width
        )
        value_parts.append(
            jnp.einsum(
                "kgqs,qkgd->skd", weights_low, grad_block, preferred_element_type=jnp.float32
            )
        )
        weight_grad = jnp.einsum(
            "qkgd,skd->kgqs", grad_block, value_block, preferred_element_type=jnp.float32
        )
        score_low = (
            weights_full
            * (weight_grad - jnp.sum(weights_full * weight_grad, axis=-1, keepdims=True))
        ).astype(jnp.bfloat16)
        query_parts.append(
            jnp.einsum("kgqs,skd->qkgd", score_low, key_block, preferred_element_type=jnp.float32)
            * score_scale
        )
        key_parts.append(
            jnp.einsum("kgqs,qkgd->skd", score_low, query_block, preferred_element_type=jnp.float32)
            * score_scale
        )
    query_grads = (
        rotate(
            jnp.concatenate(query_parts, axis=0).reshape(group_rows, heads_here, head_width),
            cosine_rows,
            -sine_rows,
        )
        .astype(jnp.bfloat16)
        .reshape(group_rows, query_width)
    )
    key_grads = (
        rotate(jnp.concatenate(key_parts, axis=0), cosine_rows, -sine_rows)
        .astype(jnp.bfloat16)
        .reshape(group_rows, key_width)
    )
    value_grads = (
        jnp.concatenate(value_parts, axis=0).astype(jnp.bfloat16).reshape(group_rows, key_width)
    )
    joined_grads = jnp.concatenate([query_grads, key_grads, value_grads], axis=1)
    joined_weight_grad = contract_rows(normed, joined_grads)
    normed_grad_share = lax.psum_scatter(
        contract_cols(joined_grads, joined_weights).astype(jnp.bfloat16),
        "tensor",
        scatter_dimension=0,
        tiled=True,
    ).astype(jnp.float32)
    input_pullback = jax.vjp(normalize, inputs_share, norm_gains)[1]
    input_from_norm, norm_gain_grad = input_pullback(normed_grad_share)
    input_grad_share = middle_grad + input_from_norm
    query_total, key_total, value_total, out_turned = (
        lax.psum_scatter(
            joined_weight_grad[:, :query_width].astype(jnp.bfloat16),
            "dp",
            scatter_dimension=0,
            tiled=True,
        ).astype(jnp.float32),
        lax.psum_scatter(
            joined_weight_grad[:, query_width : query_width + key_width].astype(jnp.bfloat16),
            "dp",
            scatter_dimension=0,
            tiled=True,
        ).astype(jnp.float32),
        lax.psum_scatter(
            joined_weight_grad[:, query_width + key_width :].astype(jnp.bfloat16),
            "dp",
            scatter_dimension=0,
            tiled=True,
        ).astype(jnp.float32),
        lax.psum_scatter(
            out_grad.T.astype(jnp.bfloat16), "dp", scatter_dimension=0, tiled=True
        ).astype(jnp.float32),
    )
    out_total = out_turned.T
    norm_gain_total, mix_gain_total, router_total = lax.psum(
        (norm_gain_grad, mix_gain_grad, router_grad), ("dp", "tensor")
    )
    return (
        output_share,
        balance,
        input_grad_share,
        norm_gain_total,
        query_total,
        key_total,
        value_total,
        out_total,
        mix_gain_total,
        router_total,
        gate_total,
        up_total,
        down_total,
    )


def all_sum(value):
    for bit in (1, 2, 4, 8):
        value = value + flip(value, bit)
    return value + swap(value)


def spread(value):
    across = swap(value)
    return [value, across, flip(value, 1), flip(across, 1)]


CHUNK = 2
FAR_FIRST = -1


def shards_pair(
    tokens,
    norm_gains,
    w_query,
    w_key,
    w_value,
    w_out,
    mix_gains,
    w_router,
    w_gate,
    w_up,
    w_down,
    routes,
    starts,
    cotangent,
):
    share_rows, model_width = tokens.shape
    query_width = w_query.shape[1]
    key_width = w_key.shape[1]
    sizes = (query_width, key_width, HD)
    experts_here = w_gate.shape[0]
    experts = experts_here // 2
    choices_count = routes.shape[1]
    expert_count = w_router.shape[1]
    dp_size = lax.axis_size("dp")
    rank = lax.axis_index("dp")
    core, side = rank % 2, (rank // 2) % 2
    tensor_rank = lax.axis_index("tensor")
    total_tokens = routes.shape[0] * dp_size
    score_scale = HD ** (-0.5)
    depth = model_width // dp_size * 2
    slots = round_up(2 * CAP, BLOCK)

    joined_own = jnp.concatenate([w_query, w_key, w_value], axis=1)
    joined_other, joined_send, joined_piece = fetch_other([w_query, w_key, w_value], core, side)
    out_other, _, out_piece = fetch_other([w_out], core, side, (joined_send,))

    own_routes = lax.dynamic_slice_in_dim(routes, tensor_rank * share_rows, share_rows, 0)
    across_routes = lax.dynamic_slice_in_dim(routes, (1 - tensor_rank) * share_rows, share_rows, 0)
    both_routes = jnp.concatenate([own_routes, across_routes], axis=0)
    group_routes = jnp.concatenate([both_routes, flip(both_routes, 1)], axis=0)
    first_expert = tensor_rank * experts_here + core * experts

    route_onehot = (
        own_routes[:, :, None] == jnp.arange(expert_count, dtype=jnp.int32)[None, None, :]
    ).astype(jnp.float32)
    hops = [jnp.sum(route_onehot, axis=(0, 1))]
    for bit in (1, 2, 4, 8):
        hops.append(hops[-1] + flip(hops[-1], bit))
    counts = hops[-1] + swap(hops[-1])
    cotangent_rows = spread(order(cotangent, joined_piece))

    inputs_share = tokens.astype(jnp.float32)
    normed = normalize(inputs_share, norm_gains).astype(jnp.bfloat16)
    tables = turn_tables(share_rows)
    starts_row = lax.dynamic_index_in_dim(starts, tensor_rank, 0, keepdims=False)
    limits = piece_limits(starts_row, share_rows)

    def half_forward(joined_weights, after=(), later=()):
        query, key, value = project(
            normed, joined_weights, tables, query_width, key_width, score_scale, after
        )
        attended, lse = attend(query, key, value, limits, later)
        return attended, (query, key, value, lse)

    attended_own, saved_own = half_forward(joined_own, (), (joined_piece,))
    attended_other, saved_other = half_forward(joined_other, (hops[1],), (hops[2],))
    middle_share = (
        inputs_share
        + jnp.dot(attended_own, w_out, preferred_element_type=jnp.float32)
        + jnp.dot(attended_other, out_other, preferred_element_type=jnp.float32)
    )
    mixed_share = normalize(middle_share, mix_gains).astype(jnp.bfloat16)

    logits = jnp.dot(mixed_share, w_router, preferred_element_type=jnp.float32)
    probabilities = softmax_rows(logits)
    chosen = jnp.sum(logits[:, None, :] * route_onehot, axis=-1)
    gate_soft = softmax_rows(chosen)
    gate_low = gate_soft.astype(jnp.bfloat16)
    fractions = counts / (total_tokens * choices_count)

    group_gates = jnp.concatenate(spread(gate_low), axis=0)
    gates = gate_table(group_routes, group_gates, first_expert, experts)
    place, begins, ends = placement(group_routes, first_expert, experts)
    gather_from = gather_tables(begins, ends, slots)
    blocks = gather_from[2]
    cot_slots = gather_rows(
        gather_from, place, None, cotangent_rows, slots, 0, experts, (hops[3],)
    )[0]
    mixed_across = order(swap(mixed_share), cot_slots)
    mixed_rows = [mixed_share, mixed_across, flip(mixed_share, 1), flip(mixed_across, 1)]
    misc = jnp.stack([core * experts, side, (rank // 4) % 2])
    weights = (w_gate, w_up, w_down)
    first_part = gather_rows(
        gather_from, place, gates, mixed_rows, slots, 0, CHUNK, (cot_slots, hops[4])
    )
    later_part = None
    carried = None
    chips = []
    for index in range(experts // CHUNK):
        if index == 1:
            later_part = gather_rows(
                gather_from, place, gates, mixed_rows, slots, CHUNK, experts - CHUNK, (carried, counts)
            )
        (x_slots, slot_gates), x_first = (later_part, CHUNK) if index else (first_part, 0)
        waits = []
        if index == 2:
            waits = [chips[0].one(carried)]
        elif index == 3:
            waits = [chips[0].two(carried)]
        elif index == 4:
            waits = [chips[1].one(carried)]
        far_first = int(index == FAR_FIRST)
        carried, send, keep = expert_call(
            blocks, misc, x_slots, cot_slots, slot_gates, weights, carried, slots,
            index * CHUNK, CHUNK, x_first, 0, depth, far_first, waits,
        )
        chips.append(ChipSum((send, keep), rank, far_first))
    done = [chips[0].three(carried)]
    waits = [chips[1].two(carried), done[0]]

    combine_from = combine_tables(begins, ends, slots)
    tiles = place.shape[1] // 4
    names = first_expert + jnp.arange(experts, dtype=jnp.int32)

    def combined(quarter, after):
        y, dx, gate_grads = combine_rows(
            combine_from, place, carried, quarter * tiles, tiles, after
        )
        gate_grads = gate_grads[:, :experts] + gate_grads[:, 64 : 64 + experts]
        rows = group_routes[quarter * share_rows : (quarter + 1) * share_rows]
        hit = rows[:, :, None] == names[None, None, :]
        return y, dx, jnp.sum(jnp.where(hit, gate_grads[:, None, :], 0.0), axis=2)

    far = combined(3, waits)
    far_y, far_dx, far_gg = (flip(value, 1) for value in far)
    cross = combined(1, [far[0]])
    dx_send = add_low(cross[1], far_dx)
    dx_across = swap(dx_send)
    gg_across = swap(cross[2] + far_gg)
    next_door = combined(2, [dx_send, chips[2].one(cross[1])])
    door_y, door_dx, door_gg = (flip(value, 1) for value in next_door)
    y_send = add_low(cross[0], far_y)
    near = combined(0, [next_door[0]])
    y_across = swap(order(y_send, near[0]))
    mixed_grad_share = (
        near[1].astype(jnp.float32)
        + door_dx.astype(jnp.float32)
        + dx_across.astype(jnp.float32)
    )
    gates_grad_share = near[2] + door_gg + gg_across

    upstream = cotangent.astype(jnp.float32)
    chosen_grad = gate_soft * (
        gates_grad_share - jnp.sum(gate_soft * gates_grad_share, axis=-1, keepdims=True)
    )
    logit_grad = jnp.sum(chosen_grad[:, :, None] * route_onehot, axis=1)
    prob_target = ALPHA * expert_count * fractions / total_tokens
    logit_grad = logit_grad + probabilities * (
        prob_target[None, :] - jnp.sum(probabilities * prob_target[None, :], axis=-1, keepdims=True)
    )
    router_grad = jnp.dot(
        mixed_share.astype(jnp.float32).T,
        logit_grad,
        precision=HIGHEST,
        preferred_element_type=jnp.float32,
    )
    mixed_grad_share = mixed_grad_share + jnp.dot(
        logit_grad,
        w_router.astype(jnp.float32).T,
        precision=HIGHEST,
        preferred_element_type=jnp.float32,
    )
    mix_pullback = jax.vjp(normalize, middle_share, mix_gains)[1]
    middle_from_norm, mix_gain_grad = mix_pullback(mixed_grad_share)
    middle_grad = upstream + middle_from_norm
    middle_low = middle_grad.astype(jnp.bfloat16)

    def half_back(saved, out_weights):
        attended_grad = dot_nt(middle_low, out_weights).astype(jnp.bfloat16)

        def part(chosen, after):
            return attend_back(
                saved, attended_grad, limits, tables, score_scale, chosen, after
            )

        return part

    early = [
        jnp.concatenate(
            [jnp.sum(probabilities, axis=0), mix_gain_grad, router_grad.reshape(-1)]
        )
    ]
    early.append(early[-1] + order(flip(early[-1], 1), middle_low))
    middle_sum = chips[3].one(middle_low)
    chips[4].parts = (order(chips[4].parts[0], middle_sum), chips[4].parts[1])
    pairs = key_width // 128
    other_grads = jnp.concatenate(
        half_back(saved_other, out_other)(
            (0, pairs), [early[1], middle_sum]
        ),
        axis=1,
    )
    waits = [chips[2].two(other_grads)]
    other_grads = order(other_grads, *waits)
    expert_share = (
        near[0].astype(jnp.float32)
        + door_y.astype(jnp.float32)
        + order(y_across, other_grads).astype(jnp.float32)
    )
    output_share = (middle_share + expert_share).astype(jnp.bfloat16)
    joined_held = core_sum(dot_tn(normed, other_grads), core)
    joined_across = swap(joined_held)
    marked = order(middle_low, other_grads)
    out_held = core_sum(dot_tn(marked, attended_other), core)
    out_across = swap(order(out_held, joined_held))
    out_kept = core_sum(dot_tn(marked, attended_own), core)
    done.append(chips[1].three(joined_held))
    early.append(early[-1] + order(flip(early[-1], 2), joined_held))
    waits = [early[2], chips[4].one(joined_held), done[1], joined_held, out_held, out_kept, output_share]
    own_part = half_back(saved_own, w_out)
    front = own_part((0, pairs // 2), waits)
    back = own_part((pairs // 2, pairs - pairs // 2), [joined_across, front[0], chips[3].two(front[0])])
    early.append(early[-1] + order(flip(early[-1], 4), back[0]))
    early.append(early[-1] + flip(early[-1], 8))
    own_grads = jnp.concatenate(
        [part for both in zip(front, back) for part in both], axis=1
    )
    out_half = add_low(out_kept, order(out_across, own_grads))
    own_weight_grads = dot_tn(normed, own_grads)
    own_held = core_sum(own_weight_grads, core)
    joined_half = add_low(own_held, joined_across)
    joined_total, joined_first, joined_second = plane_sum(joined_half, rank)
    out_total, _, _ = plane_sum(
        out_half, rank, ((joined_half,), (joined_first,), (joined_second,))
    )
    done.append(chips[2].three(joined_half))
    chips[4].two(joined_half)
    sums = done + [chips[i].three(joined_first) for i in (3, 4)]
    other_normed = dot_nt(other_grads, joined_other)
    own_normed = dot_nt(order(own_grads, own_held), joined_own)
    input_pullback = jax.vjp(normalize, inputs_share, norm_gains)[1]
    input_from_norm, norm_gain_grad = input_pullback(other_normed + own_normed)
    input_grad_share = middle_grad + input_from_norm
    key_end = query_width + key_width
    small = early[-1] + swap(early[-1])
    prob_sums = small[:expert_count]
    mix_gain_total = small[expert_count : expert_count + model_width]
    router_total = small[expert_count + model_width :].reshape(router_grad.shape)
    norm_gain_total = all_sum(norm_gain_grad)
    balance = expert_count * expert_count * fractions * prob_sums / total_tokens

    mine = jnp.concatenate(sums, axis=0).reshape(experts, 3, 2, depth // 2, -1)
    theirs = flip(pick_index(mine, 1 - core, 2), 1)
    mine = pick_index(mine, core, 2)
    def placed(kind):
        own_kind, other_kind = mine[:, kind], theirs[:, kind]
        return jnp.where(
            core == 0,
            jnp.concatenate([own_kind, other_kind], axis=0),
            jnp.concatenate([other_kind, own_kind], axis=0),
        ).astype(jnp.float32)

    return (
        output_share,
        balance,
        input_grad_share,
        norm_gain_total,
        joined_total[:, :query_width],
        joined_total[:, query_width:key_end],
        joined_total[:, key_end:],
        out_total.T,
        mix_gain_total,
        router_total,
        placed(0),
        placed(1),
        placed(2).transpose(0, 2, 1),
    )


def solution(mesh):
    sizes = dict(mesh.shape)
    paired = sizes["tensor"] == 2 and sizes["dp"] == 16
    return jax.shard_map(
        shards_pair if paired else shards_wide,
        mesh=mesh,
        in_specs=(
            P(("dp", "tensor"), None),
            P(),
            P(None, "tensor"),
            P(None, "tensor"),
            P(None, "tensor"),
            P("tensor", None),
            P(),
            P(),
            P("tensor", None, None),
            P("tensor", None, None),
            P("tensor", None, None),
            P("dp", None),
            P("dp", None),
            P(("dp", "tensor"), None),
        ),
        out_specs=(
            P(("dp", "tensor"), None),
            P(),
            P(("dp", "tensor"), None),
            P(),
            P("dp", "tensor"),
            P("dp", "tensor"),
            P("dp", "tensor"),
            P("tensor", "dp"),
            P(),
            P(),
            P("tensor", "dp", None),
            P("tensor", "dp", None),
            P("tensor", None, "dp"),
        ),
        check_vma=False,
    )
```

```python
import functools

import jax
import jax.numpy as jnp
from jax import lax
from jax.experimental import pallas as pl
from jax.experimental.pallas import tpu as pltpu
from jax.sharding import PartitionSpec as P

HD = 64
PIECE = 256
CAP = 614


EPSILON = 1e-06
ALPHA = 0.01
HIGHEST = lax.Precision.HIGHEST


def normalize(values, gains):
    return values * lax.rsqrt(jnp.mean(values * values, axis=-1, keepdims=True) + EPSILON) * gains


def softmax_rows(values):
    shifted = jnp.exp(values - jnp.max(values, axis=-1, keepdims=True))
    return shifted / jnp.sum(shifted, axis=-1, keepdims=True)


def contract_rows(left, right):
    return lax.dot_general(
        left, right, (((0,), (0,)), ((), ())), preferred_element_type=jnp.float32
    )


def contract_cols(left, right):
    return lax.dot_general(
        left, right, (((1,), (1,)), ((), ())), preferred_element_type=jnp.float32
    )


def rope_tables(sequence_length, head_width):
    half_width = head_width // 2
    frequency = 10000.0 ** (-(jnp.arange(half_width, dtype=jnp.float32) * 2.0 / head_width))
    angles = jnp.arange(sequence_length, dtype=jnp.float32)[:, None] * frequency[None, :]
    return (jnp.cos(angles), jnp.sin(angles))


def rotate(values, cosine, sine_table):
    half_width = values.shape[-1] // 2
    first_half = values[..., :half_width]
    second_half = values[..., half_width:]
    cosine_rows = cosine[:, None, :]
    sine_rows = sine_table[:, None, :]
    return jnp.concatenate(
        [
            first_half * cosine_rows - second_half * sine_rows,
            second_half * cosine_rows + first_half * sine_rows,
        ],
        axis=-1,
    )


def allowed_pairs(starts_row, sequence_length, piece_length):
    position = jnp.arange(sequence_length, dtype=jnp.int32)
    labels = jnp.full((sequence_length,), -1, jnp.int32)
    for piece_index in range(starts_row.shape[0]):
        inside = (position >= starts_row[piece_index]) & (
            position < starts_row[piece_index] + piece_length
        )
        labels = jnp.where(inside, piece_index, labels)
    causal = position[None, :] <= position[:, None]
    shared = (labels[:, None] == labels[None, :]) & (labels[:, None] >= 0)
    return causal | shared


def scores_of(query_block, key_block, allowed, score_scale):
    raw_scores = (
        jnp.einsum("qkgd,skd->kgqs", query_block, key_block, preferred_element_type=jnp.float32)
        * score_scale
    )
    return jnp.where(allowed, raw_scores, -1e30)


BLOCK = 256
PART = 128
PIECE_ROWS = 32
GROUP = 8
DEEP = 4
VMEM_LIMIT = 60 * 1024 * 1024


def dot_nt(left, right):
    return lax.dot_general(
        left, right, (((1,), (1,)), ((), ())), preferred_element_type=jnp.float32
    )


def dot_tn(left, right):
    return lax.dot_general(
        left, right, (((0,), (0,)), ((), ())), preferred_element_type=jnp.float32
    )


def round_up(value, multiple):
    return -(-value // multiple) * multiple


def placement(routes_rows, first_expert, experts):
    rows = routes_rows.shape[0]
    tiles = rows // BLOCK
    turned = routes_rows.T
    names = first_expert + jnp.arange(experts, dtype=jnp.int32)
    hit = turned[None, :, :] == names[:, None, None]
    member = jnp.any(hit, axis=1)
    upper = jnp.triu(jnp.ones((BLOCK, BLOCK), jnp.bfloat16))
    inside = jnp.dot(
        member.astype(jnp.bfloat16).reshape(experts * tiles, BLOCK),
        upper,
        preferred_element_type=jnp.float32,
    ).astype(jnp.int32).reshape(experts, tiles, BLOCK)
    sums = inside[:, :, -1]
    ends = jnp.cumsum(sums, axis=1)
    begins = ends - sums
    place = jnp.where(
        member.reshape(experts, tiles, BLOCK), begins[:, :, None] + inside - 1, -1
    )
    place = jnp.concatenate(
        [place, jnp.full((1, tiles, BLOCK), -1, jnp.int32)], axis=0
    ).reshape(experts + 1, tiles, 1, BLOCK)
    return place, begins, ends


def gate_table(routes_rows, gates_rows, first_expert, experts):
    names = first_expert + jnp.arange(experts, dtype=jnp.int32)
    hit = routes_rows.T[None, :, :] == names[:, None, None]
    table = jnp.sum(jnp.where(hit, gates_rows.astype(jnp.float32).T[None, :, :], 0.0), axis=1)
    return jnp.pad(table, ((0, 128 - experts), (0, 0))).T.astype(jnp.bfloat16)


def gather_tables(begins, ends, slots):
    counts = ends[:, -1]
    parts = jnp.arange(slots // PART, dtype=jnp.int32) * PART
    low = jnp.sum((ends[:, None, :] <= parts[None, :, None]).astype(jnp.int32), axis=2)
    high = jnp.sum((begins[:, None, :] < parts[None, :, None] + PART).astype(jnp.int32), axis=2)
    high = jnp.where(parts[None, :] < counts[:, None], high, low)
    blocks = jnp.maximum(-(-counts // BLOCK), 1)
    return low, high, blocks


def combine_tables(begins, ends, slots):
    experts, tiles = begins.shape
    width = round_up(experts * (BLOCK // PIECE_ROWS + 1), GROUP)
    first = begins // PIECE_ROWS
    amount = jnp.where(ends > begins, (ends - 1) // PIECE_ROWS - first + 1, 0)
    stop = jnp.cumsum(amount, axis=0)
    place = jnp.arange(width, dtype=jnp.int32)
    owner = jnp.sum(
        (stop.T[:, None, :] <= place[None, :, None]).astype(jnp.int32), axis=2
    )
    chosen = owner[:, :, None] == jnp.arange(experts, dtype=jnp.int32)[None, None, :]
    offset = jnp.sum(
        jnp.where(chosen, (first - (stop - amount)).T[:, None, :], 0), axis=2
    )
    valid = owner < experts
    piece = jnp.where(valid, offset + place[None, :], 0)
    source = jnp.where(valid, owner, 0) * (slots // PIECE_ROWS) + piece
    groups = jnp.maximum(-(-stop[-1] // GROUP), 1)
    return owner, piece, source, groups, width


def gather_kernel(sources, with_gates, after, low_ref, high_ref, blocks_ref, place_ref, *rest):
    if with_gates:
        gates_ref, rest = rest[0], rest[1:]
    inputs, rest = rest[:sources], rest[sources + after :]
    if with_gates:
        out_ref, gate_out_ref, held, buffer, gate_buffer, sems, out_sems = rest
    else:
        out_ref, held, buffer, sems, out_sems = rest
    expert = pl.program_id(0)
    share = inputs[0].shape[0]
    slots = out_ref.shape[0] // pl.num_programs(0)

    @pl.when(expert == 0)
    def _():
        copies = [
            pltpu.make_async_copy(ref, held.at[pl.ds(i * share, share)], sems.at[i])
            for i, ref in enumerate(inputs)
        ]
        for copy in copies:
            copy.start()
        for copy in copies:
            copy.wait()

    def copies_of(part, slot):
        start = pl.multiple_of(expert * slots + part * PART, PART)
        made = [
            pltpu.make_async_copy(
                buffer.at[slot], out_ref.at[pl.ds(start, PART)], out_sems.at[0, slot]
            )
        ]
        if with_gates:
            made.append(
                pltpu.make_async_copy(
                    gate_buffer.at[slot], gate_out_ref.at[pl.ds(start, PART)], out_sems.at[1, slot]
                )
            )
        return made

    parts = blocks_ref[expert] * (BLOCK // PART)

    def one(part, carry):
        slot = part % 2

        @pl.when(part >= 2)
        def _():
            for copy in copies_of(part - 2, slot):
                copy.wait()

        buffer[slot] = jnp.zeros(buffer.shape[1:], buffer.dtype)
        if with_gates:
            gate_buffer[slot] = jnp.zeros(gate_buffer.shape[1:], gate_buffer.dtype)
        rows = lax.broadcasted_iota(jnp.int32, (PART, BLOCK), 0) + part * PART

        def step(tile, carry):
            pick = jnp.where(rows == place_ref[expert, tile], 1.0, 0.0).astype(jnp.bfloat16)
            start = pl.multiple_of(tile * BLOCK, BLOCK)
            buffer[slot] += jnp.dot(
                pick, held[pl.ds(start, BLOCK), :], preferred_element_type=jnp.float32
            ).astype(buffer.dtype)
            if with_gates:
                gate_buffer[slot] += jnp.dot(
                    pick, gates_ref[pl.ds(start, BLOCK), :], preferred_element_type=jnp.float32
                )
            return carry

        lax.fori_loop(low_ref[expert, part], high_ref[expert, part], step, 0)
        for copy in copies_of(part, slot):
            copy.start()
        return carry

    lax.fori_loop(0, parts, one, 0)
    for back in (2, 1):
        for copy in copies_of(parts - back, (parts - back) % 2):
            copy.wait()


def gather_rows(tables, place, gates, sources, slots, first, count, after=()):
    low, high, blocks = tables
    low, high, blocks = (t[first : first + count] for t in (low, high, blocks))
    place = place[first : first + count]
    rows = place.shape[1] * BLOCK
    width = sources[0].shape[1]
    with_gates = gates is not None

    def whole(array):
        zeros = (0,) * array.ndim
        return pl.BlockSpec(array.shape, lambda *_: zeros)

    operands = [place] + ([gates] if with_gates else [])
    anywhere = pl.BlockSpec(memory_space=pl.ANY)
    in_specs = [whole(a) for a in operands] + [anywhere] * (len(sources) + len(after))
    out_shape = [jax.ShapeDtypeStruct((count * slots, width), jnp.bfloat16)]
    scratch = [
        pltpu.VMEM((rows, width), jnp.bfloat16),
        pltpu.VMEM((2, PART, width), jnp.bfloat16),
    ]
    if with_gates:
        out_shape.append(jax.ShapeDtypeStruct((count * slots, 128), jnp.float32))
        scratch.append(pltpu.VMEM((2, PART, 128), jnp.float32))
    return pl.pallas_call(
        functools.partial(gather_kernel, len(sources), with_gates, len(after)),
        grid_spec=pltpu.PrefetchScalarGridSpec(
            num_scalar_prefetch=3,
            grid=(count,),
            in_specs=in_specs,
            out_specs=[anywhere] * len(out_shape),
            scratch_shapes=scratch
            + [pltpu.SemaphoreType.DMA((len(sources),)), pltpu.SemaphoreType.DMA((2, 2))],
        ),
        out_shape=out_shape,
        compiler_params=pltpu.CompilerParams(vmem_limit_bytes=VMEM_LIMIT),
    )(low, high, blocks, *operands, *sources, *after)


def expert_kernel(
    first, split, depth, far_first, extra, blocks_ref, misc_ref, x_ref, c_ref, sg_ref, wg_ref,
    wu_ref, wd_ref, *rest
):
    yd_ref = rest[extra]
    rest = rest[extra + 1 :]
    width = x_ref.shape[1]
    if split:
        send_ref, keep_ref = rest[:2]
        rest = rest[2:]
    else:
        grads_ref = rest[0]
        rest = rest[1:]
    total_gu, total_d, x_held, c_held, low_held, gated_held = rest
    expert = first + pl.program_id(0)
    block = pl.program_id(1)
    hidden = wg_ref.shape[2]
    blocks = blocks_ref[expert]
    lanes = lax.broadcasted_iota(jnp.int32, (BLOCK, 128), 1)

    @pl.when(block < blocks)
    def _():
        x = x_ref[...]
        c = c_ref[...]
        gate = jnp.sum(jnp.where(lanes == expert, sg_ref[...], 0.0), axis=1, keepdims=True)
        gate_proj = jnp.dot(x, wg_ref[0], preferred_element_type=jnp.float32)
        up_proj = jnp.dot(x, wu_ref[0], preferred_element_type=jnp.float32)
        pulled = dot_nt(c, wd_ref[0])
        sigmoid = 1.0 / (1.0 + jnp.exp(-gate_proj))
        silu = gate_proj * sigmoid
        activated = (silu * up_proj).astype(jnp.bfloat16).astype(jnp.float32)
        gate_grad = jnp.sum(activated * pulled, axis=1, keepdims=True)
        coarse = gate_grad.astype(jnp.bfloat16).astype(jnp.float32)
        yd_ref[:, 2 * width :] = jnp.where(
            lanes == expert, coarse, jnp.where(lanes == expert + 64, gate_grad - coarse, 0.0)
        ).astype(yd_ref.dtype)
        gated = (gate * activated).astype(jnp.bfloat16)
        yd_ref[:, :width] = jnp.dot(
            gated, wd_ref[0], preferred_element_type=jnp.float32
        ).astype(yd_ref.dtype)
        activated_grad = gate * pulled
        gate_low = (
            activated_grad * up_proj * sigmoid * (1.0 + gate_proj * (1.0 - sigmoid))
        ).astype(jnp.bfloat16)
        up_low = (activated_grad * silu).astype(jnp.bfloat16)
        yd_ref[:, width : 2 * width] = (
            dot_nt(gate_low, wg_ref[0]) + dot_nt(up_low, wu_ref[0])
        ).astype(yd_ref.dtype)
        start = pl.multiple_of((block % 2) * BLOCK, BLOCK)
        held = pl.ds(start, BLOCK)
        x_held[held, :] = x
        c_held[held, :] = c
        low_held[held, :hidden] = gate_low
        low_held[held, hidden:] = up_low
        gated_held[held, :] = gated

    def gather(rows, fresh):
        for begin in range(0, width, BLOCK):
            span = slice(begin, begin + BLOCK)
            for total, left, right in (
                (total_gu, x_held, low_held),
                (total_d, c_held, gated_held),
            ):
                term = dot_tn(left[:rows, span], right[:rows, :])
                total[span, :] = term if fresh else total[span, :] + term

    odd = block % 2 == 1
    last = block == blocks - 1

    @pl.when((block == 0) & last)
    def _():
        gather(BLOCK, True)

    @pl.when((block == 1) & (block < blocks))
    def _():
        gather(2 * BLOCK, True)

    @pl.when((block > 1) & odd & (block < blocks))
    def _():
        gather(2 * BLOCK, False)

    @pl.when((block > 1) & jnp.logical_not(odd) & last)
    def _():
        gather(BLOCK, False)

    @pl.when(block == pl.num_programs(1) - 1)
    def _():
        parts = (
            (total_gu, 0),
            (total_gu, hidden),
            (total_d, 0),
        )
        for which, (ref, column) in enumerate(parts):
            if split:
                side = misc_ref[1 + far_first]
                for high in range(2):
                    for low in range(2):
                        for out, chosen in ((keep_ref, side), (send_ref, 1 - side)):
                            if far_first:
                                start = ((high * 2 + chosen) * 2 + low) * depth
                                place = (high, low, which)
                            else:
                                start = ((high * 2 + low) * 2 + chosen) * depth
                                place = (low, high, which)
                            out[place] = ref[
                                pl.ds(pl.multiple_of(start, 64), depth), pl.ds(column, hidden)
                            ].astype(out.dtype)
            else:
                grads_ref[0, which] = ref[:, pl.ds(column, hidden)].astype(grads_ref.dtype)


def expert_call(
    blocks, misc, x, c, sg, weights, carried, slots, first, count, x_first, c_first, depth,
    far_first=0, after=()
):
    w_gate, w_up, w_down = weights
    experts = blocks.shape[0]
    width = x.shape[1]
    hidden = w_gate.shape[2]
    most = slots // BLOCK
    split = depth is not None

    def rows_index(base):
        def index(expert, block, blocks, misc):
            limit = blocks[first + expert] - 1
            return ((first - base + expert) * most + jnp.minimum(block, limit), 0)

        return index

    def weight_index(expert, block, blocks, misc):
        return (misc[0] + first + expert, 0, 0)

    def grads_index(expert, block, blocks, misc):
        return (0, 0, expert, 0, 0)

    out_shape = [jax.ShapeDtypeStruct((experts * slots, 2 * width + 128), jnp.bfloat16)]
    out_specs = [pl.BlockSpec((BLOCK, 2 * width + 128), rows_index(0))]
    if split:
        out_shape += [jax.ShapeDtypeStruct((2, 2, 3 * count, depth, hidden), jnp.bfloat16)] * 2
        out_specs += [pl.BlockSpec((2, 2, 3, depth, hidden), grads_index)] * 2
    else:
        out_shape += [jax.ShapeDtypeStruct((count, 3, width, hidden), jnp.bfloat16)]
        out_specs += [pl.BlockSpec((1, 3, width, hidden), lambda e, b, *_: (e, 0, 0, 0))]
    operands = [x, c, sg, w_gate, w_up, w_down]
    in_specs = [
        pl.BlockSpec((BLOCK, width), rows_index(x_first)),
        pl.BlockSpec((BLOCK, width), rows_index(c_first)),
        pl.BlockSpec((BLOCK, 128), rows_index(x_first)),
        pl.BlockSpec((1, width, hidden), weight_index),
        pl.BlockSpec((1, width, hidden), weight_index),
        pl.BlockSpec((1, hidden, width), weight_index),
    ]
    aliases = {}
    if carried is not None:
        operands.append(carried)
        aliases = {8: 0}
    operands += list(after)
    extra = len(operands) - 6
    in_specs += [pl.BlockSpec(memory_space=pl.ANY)] * extra
    return pl.pallas_call(
        functools.partial(expert_kernel, first, split, depth, far_first, extra),
        grid_spec=pltpu.PrefetchScalarGridSpec(
            num_scalar_prefetch=2,
            grid=(count, most),
            in_specs=in_specs,
            out_specs=out_specs,
            scratch_shapes=[
                pltpu.VMEM((width, 2 * hidden), jnp.float32),
                pltpu.VMEM((width, hidden), jnp.float32),
                pltpu.VMEM((2 * BLOCK, width), jnp.bfloat16),
                pltpu.VMEM((2 * BLOCK, width), jnp.bfloat16),
                pltpu.VMEM((2 * BLOCK, 2 * hidden), jnp.bfloat16),
                pltpu.VMEM((2 * BLOCK, hidden), jnp.bfloat16),
            ],
        ),
        out_shape=out_shape,
        input_output_aliases=aliases,
        compiler_params=pltpu.CompilerParams(vmem_limit_bytes=VMEM_LIMIT),
    )(blocks, misc, *operands)


def combine_kernel(
    first, owner_ref, piece_ref, source_ref, groups_ref, begin_ref, tile_ref, place_ref, yd_ref, *rest
):
    y_out, dx_out, gate_out, buffer, total, sems = rest[-6:]
    columns = y_out.shape[1]
    step = pl.program_id(0)
    tile = first + step

    head = begin_ref[first]
    final = first + pl.num_programs(0) - 1
    stop = begin_ref[final] + groups_ref[final]

    def copies(place):
        which_tile = tile_ref[place]
        group = place - begin_ref[which_tile]
        slot = (place - head) % DEEP
        made = []
        for i in range(GROUP):
            source = pl.multiple_of(
                source_ref[which_tile, group * GROUP + i] * PIECE_ROWS, PIECE_ROWS
            )
            made.append(
                pltpu.make_async_copy(
                    yd_ref.at[pl.ds(source, PIECE_ROWS)],
                    buffer.at[slot, pl.ds(i * PIECE_ROWS, PIECE_ROWS)],
                    sems.at[slot, i],
                )
            )
        return made

    @pl.when(step == 0)
    def _():
        for ahead in range(DEEP - 1):

            @pl.when(head + ahead < stop)
            def _():
                for copy in copies(head + ahead):
                    copy.start()

    def one(group, carry):
        place = begin_ref[tile] + group
        slot = (place - head) % DEEP

        @pl.when(place + DEEP - 1 < stop)
        def _():
            for copy in copies(place + DEEP - 1):
                copy.start()

        picks = []
        for i in range(GROUP):
            entry = group * GROUP + i
            rows = (
                lax.broadcasted_iota(jnp.int32, (PIECE_ROWS, BLOCK), 0)
                + piece_ref[tile, entry] * PIECE_ROWS
            )
            picks.append(jnp.where(rows == place_ref[owner_ref[tile, entry], step], 1.0, 0.0))
        picked = jnp.concatenate(picks, axis=0).T.astype(jnp.bfloat16)
        for copy in copies(place):
            copy.wait()
        fresh = group == 0
        for begin in range(0, total.shape[1], 640):
            span = slice(begin, begin + 640)
            term = jnp.dot(picked, buffer[slot, :, span], preferred_element_type=jnp.float32)
            total[:, span] = jnp.where(fresh, 0.0, total[:, span]) + term
        return carry

    lax.fori_loop(0, groups_ref[tile], one, 0)
    y_out[...] = total[:, :columns].astype(y_out.dtype)
    dx_out[...] = total[:, columns : 2 * columns].astype(dx_out.dtype)
    gate_out[...] = total[:, 2 * columns :]


def combine_rows(tables, place, yd, first, count, after=()):
    owner, piece, source, groups, width = tables
    ends = jnp.cumsum(groups)
    begin = ends - groups
    most = groups.shape[0] * (width // GROUP)
    tile_of = jnp.minimum(
        jnp.sum((ends[None, :] <= jnp.arange(most)[:, None]).astype(jnp.int32), axis=1),
        groups.shape[0] - 1,
    )
    experts = place.shape[0]
    whole_width = yd.shape[1]
    columns = (whole_width - 128) // 2
    row_block = lambda wide: pl.BlockSpec((BLOCK, wide), lambda t, *_: (t, 0))
    return pl.pallas_call(
        functools.partial(combine_kernel, first),
        grid_spec=pltpu.PrefetchScalarGridSpec(
            num_scalar_prefetch=6,
            grid=(count,),
            in_specs=[pl.BlockSpec((experts, count, 1, BLOCK), lambda *_: (0, first // count, 0, 0))]
            + [pl.BlockSpec(memory_space=pl.ANY)] * (1 + len(after)),
            out_specs=[row_block(columns), row_block(columns), row_block(128)],
            scratch_shapes=[
                pltpu.VMEM((DEEP, GROUP * PIECE_ROWS, whole_width), jnp.bfloat16),
                pltpu.VMEM((BLOCK, whole_width), jnp.float32),
                pltpu.SemaphoreType.DMA((DEEP, GROUP)),
            ],
        ),
        out_shape=[
            jax.ShapeDtypeStruct((count * BLOCK, columns), jnp.bfloat16),
            jax.ShapeDtypeStruct((count * BLOCK, columns), jnp.bfloat16),
            jax.ShapeDtypeStruct((count * BLOCK, 128), jnp.float32),
        ],
        compiler_params=pltpu.CompilerParams(vmem_limit_bytes=VMEM_LIMIT),
    )(owner, piece, source, groups, begin, tile_of, place, yd, *after)


def flip(value, bit):
    size = lax.axis_size("dp")
    return lax.ppermute(value, "dp", [(i, i ^ bit) for i in range(size)])


def swap(value):
    return lax.ppermute(value, "tensor", [(0, 1), (1, 0)])


def order(value, *after):
    return lax.optimization_barrier((value, *after))[0] if after else value


def add_low(left, right):
    return (left.astype(jnp.float32) + right.astype(jnp.float32)).astype(jnp.bfloat16)


def pick_index(value, index, axis):
    return lax.dynamic_index_in_dim(value, index, axis, keepdims=False)


def sum_stage(parts, bit, chosen, after):
    send, keep = parts
    got = order(flip(send, bit), *after)
    return tuple(
        add_low(pick_index(keep, which, 0), pick_index(got, which, 0))
        for which in (1 - chosen, chosen)
    )


class ChipSum:
    def __init__(self, parts, rank, far_first):
        side, low_bit, high_bit = (rank // 2) % 2, (rank // 4) % 2, rank // 8
        self.parts = parts
        self.first = (4, high_bit) if far_first else (2, low_bit)
        self.second = (8, side) if far_first else (4, high_bit)
        self.last = 2 if far_first else 8

    def one(self, *after):
        self.parts = sum_stage(self.parts, *self.first, after)
        return self.parts[0]

    def two(self, *after):
        self.parts = sum_stage(self.parts, *self.second, after)
        return self.parts[0]

    def three(self, *after):
        send, keep = self.parts
        return add_low(keep, order(flip(send, self.last), *after))


def core_sum(value, core):
    rows, columns = value.shape
    value = value.reshape(8, 2, rows // 16, columns)
    got = flip(pick_index(value, 1 - core, 1).astype(jnp.bfloat16), 1)
    return add_low(pick_index(value, core, 1), got)


def plane_sum(total, rank, *after):
    side, low_bit, high_bit = (rank // 2) % 2, (rank // 4) % 2, rank // 8
    part, columns = total.shape[1:]
    total = total.reshape(4, 2, part, columns)
    got = order(flip(pick_index(total, 1 - side, 1), 2), *after)
    total = add_low(pick_index(total, side, 1), got).reshape(2, 2, part, columns)
    got = flip(pick_index(total, 1 - low_bit, 1), 4)
    total = add_low(pick_index(total, low_bit, 1), got)
    got = flip(pick_index(total, 1 - high_bit, 0), 8)
    return pick_index(total, high_bit, 0).astype(jnp.float32) + got.astype(jnp.float32)


def fetch_other(weights, core, side, after=()):
    rows = weights[0].shape[0] // 4
    start = (side * 2 + core) * rows
    own = jnp.concatenate(
        [lax.dynamic_slice_in_dim(w, start, rows, 0) for w in weights], axis=1
    )
    pieces = swap(order(own, *after))
    turned = flip(pieces, 2)
    result = jnp.zeros((4 * rows, own.shape[1]), own.dtype)
    for value, place in (
        (pieces, side * 2 + core),
        (turned, (1 - side) * 2 + core),
        (flip(pieces, 1), side * 2 + 1 - core),
        (flip(turned, 1), (1 - side) * 2 + 1 - core),
    ):
        result = lax.dynamic_update_slice_in_dim(result, value, place * rows, 0)
    return result, own, pieces


ROWS = 256
HALF = 512


def lane_swap(values):
    width = values.shape[1]
    lane = lax.broadcasted_iota(jnp.int32, values.shape, 1) % HD
    ahead = pltpu.roll(values, width - HD // 2, 1)
    behind = pltpu.roll(values, HD // 2, 1)
    return jnp.where(lane < HD // 2, ahead, behind)


def turn_tables(rows):
    cosine, sine = rope_tables(rows, HD)
    return (
        jnp.concatenate([cosine] * 4, axis=1),
        jnp.concatenate([-sine, sine, -sine, sine], axis=1),
    )


def project_kernel(sizes, score_scale, normed_ref, weights_ref, cosine_ref, sine_ref, *outs):
    query_ref, key_ref, value_ref = outs[-3:]
    query_width, key_width = sizes
    projected = jnp.dot(normed_ref[...], weights_ref[...], preferred_element_type=jnp.float32)
    cosine, sine = cosine_ref[...], sine_ref[...]
    for start in range(0, query_width + key_width, 128):
        piece = projected[:, start : start + 128]
        turned = piece * cosine + lane_swap(piece) * sine
        if start < query_width:
            query_ref[:, start : start + 128] = (turned * score_scale).astype(jnp.bfloat16)
        else:
            begin = start - query_width
            key_ref[:, begin : begin + 128] = turned.astype(jnp.bfloat16)
    value_ref[...] = projected[:, query_width + key_width :].astype(jnp.bfloat16)


def project(normed, weights, tables, query_width, key_width, score_scale, after=()):
    rows, depth = normed.shape
    width = weights.shape[1]
    row_spec = lambda columns: pl.BlockSpec((ROWS, columns), lambda i: (i, 0))
    return pl.pallas_call(
        functools.partial(project_kernel, (query_width, key_width), score_scale),
        grid=(rows // ROWS,),
        in_specs=[
            row_spec(depth),
            pl.BlockSpec((depth, width), lambda i: (0, 0)),
            row_spec(128),
            row_spec(128),
        ]
        + [pl.BlockSpec(memory_space=pl.ANY)] * len(after),
        out_specs=[row_spec(query_width), row_spec(key_width), row_spec(key_width)],
        out_shape=[
            jax.ShapeDtypeStruct((rows, query_width), jnp.bfloat16),
            jax.ShapeDtypeStruct((rows, key_width), jnp.bfloat16),
            jax.ShapeDtypeStruct((rows, key_width), jnp.bfloat16),
        ],
        compiler_params=pltpu.CompilerParams(vmem_limit_bytes=VMEM_LIMIT),
    )(normed, weights, *tables, *after)


def attend_kernel(per_pair, query_ref, key_ref, value_ref, limit_ref, *rest):
    out_ref, lse_ref = rest[-2:]
    step = pl.program_id(1)

    def work(keys):
        columns = lax.broadcasted_iota(jnp.int32, (ROWS, HALF), 1) + (keys - HALF)
        allowed = columns <= limit_ref[...]
        lanes = lax.broadcasted_iota(jnp.int32, (ROWS, 128), 1)
        sums = jnp.zeros((ROWS, 128), jnp.float32)
        pieces = []
        for head in range(per_pair):
            group = head // (per_pair // 2)
            query = query_ref[:, head * HD : (head + 1) * HD]
            key = key_ref[:keys, group * HD : (group + 1) * HD]
            value = value_ref[:keys, group * HD : (group + 1) * HD]
            scores = dot_nt(query, key)
            last = jnp.where(allowed, scores[:, keys - HALF :], -1e30)
            scores = last if keys == HALF else jnp.concatenate([scores[:, : keys - HALF], last], 1)
            highest = jnp.max(scores, axis=1, keepdims=True)
            shifted = jnp.exp(scores - highest)
            total = jnp.sum(shifted, axis=1, keepdims=True)
            mixed = jnp.dot(
                shifted.astype(jnp.bfloat16), value, preferred_element_type=jnp.float32
            )
            pieces.append((mixed / total).astype(jnp.bfloat16))
            sums = jnp.where(lanes == head, highest + jnp.log(total), sums)
        out_ref[...] = jnp.concatenate(pieces, axis=1)
        lse_ref[0] = sums

    halfway = pl.num_programs(1) // 2

    @pl.when(step < halfway)
    def _():
        work(HALF)

    @pl.when(step >= halfway)
    def _():
        work(2 * HALF)


def attend(query, key, value, limits, after=()):
    rows, query_width = query.shape
    pairs = key.shape[1] // 128
    wide = query_width // pairs
    return pl.pallas_call(
        functools.partial(attend_kernel, wide // HD),
        grid=(pairs, rows // ROWS),
        in_specs=[
            pl.BlockSpec((ROWS, wide), lambda p, i: (i, p)),
            pl.BlockSpec((rows, 128), lambda p, i: (0, p)),
            pl.BlockSpec((rows, 128), lambda p, i: (0, p)),
            pl.BlockSpec((ROWS, 1), lambda p, i: (i, 0)),
        ]
        + [pl.BlockSpec(memory_space=pl.ANY)] * len(after),
        out_specs=[
            pl.BlockSpec((ROWS, wide), lambda p, i: (i, p)),
            pl.BlockSpec((1, ROWS, 128), lambda p, i: (p, i, 0)),
        ],
        out_shape=[
            jax.ShapeDtypeStruct((rows, query_width), jnp.bfloat16),
            jax.ShapeDtypeStruct((pairs, rows, 128), jnp.float32),
        ],
        compiler_params=pltpu.CompilerParams(vmem_limit_bytes=VMEM_LIMIT),
    )(query, key, value, limits, *after)


def back_kernel(
    per_pair, score_scale, after, query_ref, key_ref, value_ref, turned_key_ref, grad_ref, lse_ref,
    limit_ref, cosine_ref, sine_ref, all_cosine_ref, all_sine_ref, *rest
):
    query_out, key_out, value_out, key_total, value_total = rest[after:]
    step = pl.program_id(1)
    halfway = pl.num_programs(1) // 2

    @pl.when(step == 0)
    def _():
        key_total[...] = jnp.zeros_like(key_total)
        value_total[...] = jnp.zeros_like(value_total)

    def work(keys):
        rows = lax.broadcasted_iota(jnp.int32, (HALF, ROWS), 0) + (keys - HALF)
        allowed = rows <= limit_ref[...]
        made = []
        key_parts, value_parts = [], []
        for group in range(2):
            span = slice(group * HD, (group + 1) * HD)
            key, value = key_ref[:keys, span], value_ref[:keys, span]
            key_part = value_part = 0.0
            for head in range(group * per_pair // 2, (group + 1) * per_pair // 2):
                query = query_ref[:, head * HD : (head + 1) * HD]
                grad = grad_ref[:, head * HD : (head + 1) * HD]
                scores = dot_nt(key, query)
                last = jnp.where(allowed, scores[keys - HALF :], -1e30)
                scores = (
                    last
                    if keys == HALF
                    else jnp.concatenate([scores[: keys - HALF], last], axis=0)
                )
                weights = jnp.exp(scores - lse_ref[0, head : head + 1, :])
                pulled = dot_nt(value, grad)
                inner = jnp.sum(weights * pulled, axis=0, keepdims=True)
                score_low = (weights * (pulled - inner)).astype(jnp.bfloat16)
                value_part += jnp.dot(
                    weights.astype(jnp.bfloat16), grad, preferred_element_type=jnp.float32
                )
                key_part += jnp.dot(score_low, query, preferred_element_type=jnp.float32)
                made.append(
                    jnp.dot(
                        turned_key_ref[0, span, :keys],
                        score_low,
                        preferred_element_type=jnp.float32,
                    )
                )
            key_parts.append(key_part)
            value_parts.append(value_part)
        key_total[:keys] += jnp.concatenate(key_parts, axis=1)
        value_total[:keys] += jnp.concatenate(value_parts, axis=1)
        cosine, sine = cosine_ref[...], sine_ref[...]
        for index in range(per_pair // 2):
            both = jnp.concatenate(made[2 * index : 2 * index + 2], axis=0).T * score_scale
            query_out[:, index * 128 : (index + 1) * 128] = (
                both * cosine - lane_swap(both) * sine
            ).astype(jnp.bfloat16)

    @pl.when(step < halfway)
    def _():
        work(HALF)

    @pl.when(step >= halfway)
    def _():
        work(2 * HALF)

    @pl.when(step == pl.num_programs(1) - 1)
    def _():
        total = key_total[...]
        key_out[...] = (
            total * all_cosine_ref[...] - lane_swap(total) * all_sine_ref[...]
        ).astype(jnp.bfloat16)
        value_out[...] = value_total[...].astype(jnp.bfloat16)


def attend_back(saved, attended_grad, limits, tables, score_scale, chosen, after=()):
    query, key, value, lse = saved
    rows, query_width = query.shape
    pairs = key.shape[1] // 128
    wide = query_width // pairs
    turned_key = key.T.reshape(pairs, 128, rows)
    lse_rows = lse[:, :, :8].transpose(0, 2, 1)
    cosine, sine = tables
    begin, count = chosen
    block = lambda columns: pl.BlockSpec((ROWS, columns), lambda p, i: (i, p + begin))
    whole = pl.BlockSpec((rows, 128), lambda p, i: (0, p + begin))
    block_out = pl.BlockSpec((ROWS, wide), lambda p, i: (i, p))
    whole_out = pl.BlockSpec((rows, 128), lambda p, i: (0, p))
    table = pl.BlockSpec((ROWS, 128), lambda p, i: (i, 0))
    full_table = pl.BlockSpec((rows, 128), lambda p, i: (0, 0))
    return pl.pallas_call(
        functools.partial(back_kernel, wide // HD, score_scale, len(after)),
        grid=(count, rows // ROWS),
        in_specs=[
            block(wide),
            whole,
            whole,
            pl.BlockSpec((1, 128, rows), lambda p, i: (p + begin, 0, 0)),
            block(wide),
            pl.BlockSpec((1, 8, ROWS), lambda p, i: (p + begin, 0, i)),
            pl.BlockSpec((1, ROWS), lambda p, i: (0, i)),
            table,
            table,
            full_table,
            full_table,
        ]
        + [pl.BlockSpec(memory_space=pl.ANY)] * len(after),
        out_specs=[block_out, whole_out, whole_out],
        out_shape=[
            jax.ShapeDtypeStruct((rows, count * wide), jnp.bfloat16),
            jax.ShapeDtypeStruct((rows, count * 128), jnp.bfloat16),
            jax.ShapeDtypeStruct((rows, count * 128), jnp.bfloat16),
        ],
        scratch_shapes=[
            pltpu.VMEM((rows, 128), jnp.float32),
            pltpu.VMEM((rows, 128), jnp.float32),
        ],
        compiler_params=pltpu.CompilerParams(vmem_limit_bytes=VMEM_LIMIT),
    )(
        query, key, value, turned_key, attended_grad, lse_rows, limits.T, cosine, sine, cosine,
        sine, *after,
    )


def piece_limits(starts_row, rows):
    position = jnp.arange(rows, dtype=jnp.int32)
    limits = position
    for index in range(starts_row.shape[0]):
        start = starts_row[index]
        inside = (position >= start) & (position < start + PIECE)
        limits = jnp.where(inside, start + PIECE - 1, limits)
    return limits[:, None]


def slot_table(routes, expert_count, capacity):
    flattened = routes.reshape(-1)
    onehot = (flattened[:, None] == jnp.arange(expert_count, dtype=jnp.int32)[None, :]).astype(
        jnp.int32
    )
    placed = jnp.sum((jnp.cumsum(onehot, axis=0) - 1) * onehot, axis=1)
    entries = jnp.arange(flattened.shape[0], dtype=jnp.int32)
    return (
        jnp.full((expert_count * capacity,), flattened.shape[0], jnp.int32)
        .at[flattened * capacity + placed]
        .set(entries)
    )


def expert_forward(expert_inputs, w_gate, w_up, w_down):
    gate_proj = jnp.einsum(
        "ecd,edf->ecf", expert_inputs, w_gate, preferred_element_type=jnp.float32
    )
    up_proj = jnp.einsum("ecd,edf->ecf", expert_inputs, w_up, preferred_element_type=jnp.float32)
    activated = (gate_proj * jax.nn.sigmoid(gate_proj) * up_proj).astype(jnp.bfloat16)
    returned = jnp.einsum("ecf,efd->ecd", activated, w_down, preferred_element_type=jnp.float32)
    return (gate_proj, up_proj, activated, returned)


def shards_wide(
    tokens,
    norm_gains,
    w_query,
    w_key,
    w_value,
    w_out,
    mix_gains,
    w_router,
    w_gate,
    w_up,
    w_down,
    routes,
    starts,
    cotangent,
):
    share_rows = tokens.shape[0]
    model_width = tokens.shape[1]
    head_width = HD
    query_width = w_query.shape[1]
    key_width = w_key.shape[1]
    heads_here = query_width // head_width
    groups_here = key_width // head_width
    per_group = heads_here // groups_here
    experts_here = w_gate.shape[0]
    group_rows = routes.shape[0]
    choices_count = routes.shape[1]
    sequences_here = starts.shape[0]
    sequence_length = group_rows // sequences_here
    expert_count = w_router.shape[1]
    tensor_rank = lax.axis_index("tensor")
    total_tokens = group_rows * lax.axis_size("dp")
    score_scale = head_width ** (-0.5)
    inputs_share = tokens.astype(jnp.float32)
    normed_share = normalize(inputs_share, norm_gains).astype(jnp.bfloat16)
    normed = lax.all_gather(normed_share, "tensor", axis=0, tiled=True)
    joined_weights = jnp.concatenate([w_query, w_key, w_value], axis=1)
    projected = jnp.dot(normed, joined_weights, preferred_element_type=jnp.float32)
    cosine, sine_table = rope_tables(sequence_length, head_width)
    cosine_rows = jnp.tile(cosine, (sequences_here, 1))
    sine_rows = jnp.tile(sine_table, (sequences_here, 1))
    query_rows = rotate(
        projected[:, :query_width].reshape(group_rows, heads_here, head_width),
        cosine_rows,
        sine_rows,
    ).astype(jnp.bfloat16)
    key_rows = rotate(
        projected[:, query_width : query_width + key_width].reshape(
            group_rows, groups_here, head_width
        ),
        cosine_rows,
        sine_rows,
    ).astype(jnp.bfloat16)
    value_rows = (
        projected[:, query_width + key_width :]
        .astype(jnp.bfloat16)
        .reshape(group_rows, groups_here, head_width)
    )
    attended_parts = []
    logsum_parts = []
    for sequence in range(sequences_here):
        first_row = sequence * sequence_length
        query_block = query_rows[first_row : first_row + sequence_length].reshape(
            sequence_length, groups_here, per_group, head_width
        )
        key_block = key_rows[first_row : first_row + sequence_length]
        value_block = value_rows[first_row : first_row + sequence_length]
        allowed = allowed_pairs(starts[sequence], sequence_length, PIECE)
        scores = scores_of(query_block, key_block, allowed, score_scale)
        highest = jnp.max(scores, axis=-1, keepdims=True)
        shifted = jnp.exp(scores - highest)
        totals = jnp.sum(shifted, axis=-1, keepdims=True)
        weights = (shifted / totals).astype(jnp.bfloat16)
        mixed_values = jnp.einsum(
            "kgqs,skd->qkgd", weights, value_block, preferred_element_type=jnp.float32
        )
        attended_parts.append(
            mixed_values.reshape(sequence_length, query_width).astype(jnp.bfloat16)
        )
        logsum_parts.append(highest + jnp.log(totals))
    attended = jnp.concatenate(attended_parts, axis=0)
    attention_share = lax.psum_scatter(
        jnp.dot(attended, w_out, preferred_element_type=jnp.float32),
        "tensor",
        scatter_dimension=0,
        tiled=True,
    )
    middle_share = inputs_share + attention_share
    mixed_share = normalize(middle_share, mix_gains).astype(jnp.bfloat16)
    share_routes = lax.dynamic_slice_in_dim(routes, tensor_rank * share_rows, share_rows, 0)
    route_onehot = (
        share_routes[:, :, None] == jnp.arange(expert_count, dtype=jnp.int32)[None, None, :]
    ).astype(jnp.float32)
    logits = jnp.dot(mixed_share, w_router, preferred_element_type=jnp.float32)
    probabilities = softmax_rows(logits)
    chosen = jnp.sum(logits[:, None, :] * route_onehot, axis=-1)
    gate_soft = softmax_rows(chosen)
    gate_low = gate_soft.astype(jnp.bfloat16)
    counts, prob_sums = lax.psum(
        (jnp.sum(route_onehot, axis=(0, 1)), jnp.sum(probabilities, axis=0)), ("dp", "tensor")
    )
    fractions = counts / (total_tokens * choices_count)
    balance = expert_count * expert_count * fractions * prob_sums / total_tokens
    mixed_rows, gate_rows = (
        lax.all_gather(mixed_share, "tensor", axis=0, tiled=True),
        lax.all_gather(gate_low, "tensor", axis=0, tiled=True),
    )
    slots_all = slot_table(routes, expert_count, CAP)
    slots = lax.dynamic_slice_in_dim(
        slots_all, tensor_rank * experts_here * CAP, experts_here * CAP, 0
    )
    owners = slots // choices_count
    padded_rows = jnp.concatenate([mixed_rows, jnp.zeros((1, model_width), jnp.bfloat16)], axis=0)
    padded_gates = jnp.concatenate(
        [gate_rows.reshape(-1).astype(jnp.float32), jnp.zeros((1,), jnp.float32)], axis=0
    )
    slot_gates = padded_gates[slots]
    expert_inputs = padded_rows[owners].reshape(experts_here, CAP, model_width)
    gate_proj, up_proj, activated, returned = expert_forward(expert_inputs, w_gate, w_up, w_down)
    returned_flat = returned.reshape(experts_here * CAP, model_width)
    expert_partial = jax.ops.segment_sum(
        slot_gates[:, None] * returned_flat, owners, num_segments=group_rows + 1
    )[:group_rows]
    expert_share = lax.psum_scatter(
        expert_partial.astype(jnp.bfloat16), "tensor", scatter_dimension=0, tiled=True
    ).astype(jnp.float32)
    output_share = (middle_share + expert_share).astype(jnp.bfloat16)
    upstream = cotangent.astype(jnp.float32)
    upstream_rows = lax.all_gather(cotangent, "tensor", axis=0, tiled=True)
    padded_upstream = jnp.concatenate(
        [upstream_rows, jnp.zeros((1, model_width), jnp.bfloat16)], axis=0
    )
    slot_upstream = padded_upstream[owners].astype(jnp.float32)
    slot_cotangent = (
        (slot_gates[:, None] * slot_upstream)
        .astype(jnp.bfloat16)
        .reshape(experts_here, CAP, model_width)
    )
    slot_gate_grad = jnp.sum(slot_upstream * returned_flat, axis=1)
    activated_grad = jnp.einsum(
        "ecd,efd->ecf", slot_cotangent, w_down, preferred_element_type=jnp.float32
    )
    down_grad = jnp.einsum(
        "ecf,ecd->efd", activated, slot_cotangent, preferred_element_type=jnp.float32
    )
    sigmoid_gate = jax.nn.sigmoid(gate_proj)
    gate_proj_low = (
        activated_grad * up_proj * sigmoid_gate * (1.0 + gate_proj * (1.0 - sigmoid_gate))
    ).astype(jnp.bfloat16)
    up_proj_low = (activated_grad * gate_proj * sigmoid_gate).astype(jnp.bfloat16)
    inputs_grad = jnp.einsum(
        "ecf,edf->ecd", gate_proj_low, w_gate, preferred_element_type=jnp.float32
    ) + jnp.einsum("ecf,edf->ecd", up_proj_low, w_up, preferred_element_type=jnp.float32)
    gate_grad = jnp.einsum(
        "ecd,ecf->edf", expert_inputs, gate_proj_low, preferred_element_type=jnp.float32
    )
    up_grad = jnp.einsum(
        "ecd,ecf->edf", expert_inputs, up_proj_low, preferred_element_type=jnp.float32
    )
    mixed_partial = jax.ops.segment_sum(
        inputs_grad.reshape(experts_here * CAP, model_width), owners, num_segments=group_rows + 1
    )[:group_rows]
    gate_partial = jax.ops.segment_sum(
        slot_gate_grad, slots, num_segments=group_rows * choices_count + 1
    )[: group_rows * choices_count].reshape(group_rows, choices_count)
    mixed_grad_share, gates_grad_share = (
        lax.psum_scatter(mixed_partial, "tensor", scatter_dimension=0, tiled=True),
        lax.psum_scatter(gate_partial, "tensor", scatter_dimension=0, tiled=True),
    )
    gate_total, up_total = (
        lax.psum_scatter(
            gate_grad.astype(jnp.bfloat16), "dp", scatter_dimension=1, tiled=True
        ).astype(jnp.float32),
        lax.psum_scatter(
            up_grad.astype(jnp.bfloat16), "dp", scatter_dimension=1, tiled=True
        ).astype(jnp.float32),
    )
    down_total = lax.psum_scatter(
        down_grad.astype(jnp.bfloat16), "dp", scatter_dimension=2, tiled=True
    ).astype(jnp.float32)
    chosen_grad = gate_soft * (
        gates_grad_share - jnp.sum(gate_soft * gates_grad_share, axis=-1, keepdims=True)
    )
    logit_grad = jnp.sum(chosen_grad[:, :, None] * route_onehot, axis=1)
    prob_target = ALPHA * expert_count * fractions / total_tokens
    logit_grad = logit_grad + probabilities * (
        prob_target[None, :] - jnp.sum(probabilities * prob_target[None, :], axis=-1, keepdims=True)
    )
    mixed_float = mixed_share.astype(jnp.float32)
    router_grad = jnp.dot(
        mixed_float.T, logit_grad, precision=HIGHEST, preferred_element_type=jnp.float32
    )
    mixed_grad_share = mixed_grad_share + jnp.dot(
        logit_grad,
        w_router.astype(jnp.float32).T,
        precision=HIGHEST,
        preferred_element_type=jnp.float32,
    )
    mix_pullback = jax.vjp(normalize, middle_share, mix_gains)[1]
    middle_from_norm, mix_gain_grad = mix_pullback(mixed_grad_share)
    middle_grad = upstream + middle_from_norm
    middle_low = middle_grad.astype(jnp.bfloat16)
    middle_rows = lax.all_gather(middle_low, "tensor", axis=0, tiled=True)
    out_grad = contract_rows(attended, middle_rows)
    attended_grad = contract_cols(middle_rows, w_out).astype(jnp.bfloat16)
    query_parts = []
    key_parts = []
    value_parts = []
    for sequence in range(sequences_here):
        first_row = sequence * sequence_length
        query_block = query_rows[first_row : first_row + sequence_length].reshape(
            sequence_length, groups_here, per_group, head_width
        )
        key_block = key_rows[first_row : first_row + sequence_length]
        value_block = value_rows[first_row : first_row + sequence_length]
        allowed = allowed_pairs(starts[sequence], sequence_length, PIECE)
        scores = scores_of(query_block, key_block, allowed, score_scale)
        weights_full = jnp.exp(scores - logsum_parts[sequence])
        weights_low = weights_full.astype(jnp.bfloat16)
        grad_block = attended_grad[first_row : first_row + sequence_length].reshape(
            sequence_length, groups_here, per_group, head_width
        )
        value_parts.append(
            jnp.einsum(
                "kgqs,qkgd->skd", weights_low, grad_block, preferred_element_type=jnp.float32
            )
        )
        weight_grad = jnp.einsum(
            "qkgd,skd->kgqs", grad_block, value_block, preferred_element_type=jnp.float32
        )
        score_low = (
            weights_full
            * (weight_grad - jnp.sum(weights_full * weight_grad, axis=-1, keepdims=True))
        ).astype(jnp.bfloat16)
        query_parts.append(
            jnp.einsum("kgqs,skd->qkgd", score_low, key_block, preferred_element_type=jnp.float32)
            * score_scale
        )
        key_parts.append(
            jnp.einsum("kgqs,qkgd->skd", score_low, query_block, preferred_element_type=jnp.float32)
            * score_scale
        )
    query_grads = (
        rotate(
            jnp.concatenate(query_parts, axis=0).reshape(group_rows, heads_here, head_width),
            cosine_rows,
            -sine_rows,
        )
        .astype(jnp.bfloat16)
        .reshape(group_rows, query_width)
    )
    key_grads = (
        rotate(jnp.concatenate(key_parts, axis=0), cosine_rows, -sine_rows)
        .astype(jnp.bfloat16)
        .reshape(group_rows, key_width)
    )
    value_grads = (
        jnp.concatenate(value_parts, axis=0).astype(jnp.bfloat16).reshape(group_rows, key_width)
    )
    joined_grads = jnp.concatenate([query_grads, key_grads, value_grads], axis=1)
    joined_weight_grad = contract_rows(normed, joined_grads)
    normed_grad_share = lax.psum_scatter(
        contract_cols(joined_grads, joined_weights).astype(jnp.bfloat16),
        "tensor",
        scatter_dimension=0,
        tiled=True,
    ).astype(jnp.float32)
    input_pullback = jax.vjp(normalize, inputs_share, norm_gains)[1]
    input_from_norm, norm_gain_grad = input_pullback(normed_grad_share)
    input_grad_share = middle_grad + input_from_norm
    query_total, key_total, value_total, out_turned = (
        lax.psum_scatter(
            joined_weight_grad[:, :query_width].astype(jnp.bfloat16),
            "dp",
            scatter_dimension=0,
            tiled=True,
        ).astype(jnp.float32),
        lax.psum_scatter(
            joined_weight_grad[:, query_width : query_width + key_width].astype(jnp.bfloat16),
            "dp",
            scatter_dimension=0,
            tiled=True,
        ).astype(jnp.float32),
        lax.psum_scatter(
            joined_weight_grad[:, query_width + key_width :].astype(jnp.bfloat16),
            "dp",
            scatter_dimension=0,
            tiled=True,
        ).astype(jnp.float32),
        lax.psum_scatter(
            out_grad.T.astype(jnp.bfloat16), "dp", scatter_dimension=0, tiled=True
        ).astype(jnp.float32),
    )
    out_total = out_turned.T
    norm_gain_total, mix_gain_total, router_total = lax.psum(
        (norm_gain_grad, mix_gain_grad, router_grad), ("dp", "tensor")
    )
    return (
        output_share,
        balance,
        input_grad_share,
        norm_gain_total,
        query_total,
        key_total,
        value_total,
        out_total,
        mix_gain_total,
        router_total,
        gate_total,
        up_total,
        down_total,
    )


def all_sum(value):
    for bit in (1, 2, 4, 8):
        value = value + flip(value, bit)
    return value + swap(value)


def spread(value):
    across = swap(value)
    return [value, across, flip(value, 1), flip(across, 1)]


CHUNK = 2
FAR_FIRST = -1


def shards_pair(
    tokens,
    norm_gains,
    w_query,
    w_key,
    w_value,
    w_out,
    mix_gains,
    w_router,
    w_gate,
    w_up,
    w_down,
    routes,
    starts,
    cotangent,
):
    share_rows, model_width = tokens.shape
    query_width = w_query.shape[1]
    key_width = w_key.shape[1]
    sizes = (query_width, key_width, HD)
    experts_here = w_gate.shape[0]
    experts = experts_here // 2
    choices_count = routes.shape[1]
    expert_count = w_router.shape[1]
    dp_size = lax.axis_size("dp")
    rank = lax.axis_index("dp")
    core, side = rank % 2, (rank // 2) % 2
    tensor_rank = lax.axis_index("tensor")
    total_tokens = routes.shape[0] * dp_size
    score_scale = HD ** (-0.5)
    depth = model_width // dp_size * 2
    slots = round_up(2 * CAP, BLOCK)

    joined_own = jnp.concatenate([w_query, w_key, w_value], axis=1)
    joined_other, joined_send, joined_piece = fetch_other([w_query, w_key, w_value], core, side)
    out_other, _, out_piece = fetch_other([w_out], core, side, (joined_send,))

    own_routes = lax.dynamic_slice_in_dim(routes, tensor_rank * share_rows, share_rows, 0)
    across_routes = lax.dynamic_slice_in_dim(routes, (1 - tensor_rank) * share_rows, share_rows, 0)
    both_routes = jnp.concatenate([own_routes, across_routes], axis=0)
    group_routes = jnp.concatenate([both_routes, flip(both_routes, 1)], axis=0)
    first_expert = tensor_rank * experts_here + core * experts

    route_onehot = (
        own_routes[:, :, None] == jnp.arange(expert_count, dtype=jnp.int32)[None, None, :]
    ).astype(jnp.float32)
    hops = [jnp.sum(route_onehot, axis=(0, 1))]
    for bit in (1, 2, 4, 8):
        hops.append(hops[-1] + flip(hops[-1], bit))
    counts = hops[-1] + swap(hops[-1])
    cotangent_rows = spread(order(cotangent, joined_piece))

    inputs_share = tokens.astype(jnp.float32)
    normed = normalize(inputs_share, norm_gains).astype(jnp.bfloat16)
    tables = turn_tables(share_rows)
    starts_row = lax.dynamic_index_in_dim(starts, tensor_rank, 0, keepdims=False)
    limits = piece_limits(starts_row, share_rows)

    def half_forward(joined_weights, after=(), later=()):
        query, key, value = project(
            normed, joined_weights, tables, query_width, key_width, score_scale, after
        )
        attended, lse = attend(query, key, value, limits, later)
        return attended, (query, key, value, lse)

    attended_own, saved_own = half_forward(joined_own, (), (joined_piece, hops[1]))
    attended_other, saved_other = half_forward(joined_other, (hops[2],), (hops[3],))
    middle_share = (
        inputs_share
        + jnp.dot(attended_own, w_out, preferred_element_type=jnp.float32)
        + jnp.dot(attended_other, out_other, preferred_element_type=jnp.float32)
    )
    mixed_share = normalize(middle_share, mix_gains).astype(jnp.bfloat16)

    logits = jnp.dot(mixed_share, w_router, preferred_element_type=jnp.float32)
    probabilities = softmax_rows(logits)
    chosen = jnp.sum(logits[:, None, :] * route_onehot, axis=-1)
    gate_soft = softmax_rows(chosen)
    gate_low = gate_soft.astype(jnp.bfloat16)
    fractions = counts / (total_tokens * choices_count)

    group_gates = jnp.concatenate(spread(gate_low), axis=0)
    gates = gate_table(group_routes, group_gates, first_expert, experts)
    place, begins, ends = placement(group_routes, first_expert, experts)
    gather_from = gather_tables(begins, ends, slots)
    blocks = gather_from[2]
    cot_slots = gather_rows(
        gather_from, place, None, cotangent_rows, slots, 0, experts, (hops[4],)
    )[0]
    mixed_across = order(swap(mixed_share), cot_slots)
    mixed_rows = [mixed_share, mixed_across, flip(mixed_share, 1), flip(mixed_across, 1)]
    misc = jnp.stack([core * experts, side, (rank // 4) % 2])
    weights = (w_gate, w_up, w_down)
    first_part = gather_rows(
        gather_from, place, gates, mixed_rows, slots, 0, CHUNK, (cot_slots, counts)
    )
    later_part = None
    carried = None
    chips = []
    for index in range(experts // CHUNK):
        if index == 1:
            later_part = gather_rows(
                gather_from, place, gates, mixed_rows, slots, CHUNK, experts - CHUNK, (carried,)
            )
        (x_slots, slot_gates), x_first = (later_part, CHUNK) if index else (first_part, 0)
        waits = []
        if index == 2:
            waits = [chips[0].one(carried)]
        elif index == 3:
            waits = [chips[0].two(carried)]
        elif index == 4:
            waits = [chips[1].one(carried)]
        far_first = int(index == FAR_FIRST)
        carried, send, keep = expert_call(
            blocks, misc, x_slots, cot_slots, slot_gates, weights, carried, slots,
            index * CHUNK, CHUNK, x_first, 0, depth, far_first, waits,
        )
        chips.append(ChipSum((send, keep), rank, far_first))
    done = [chips[0].three(carried)]
    waits = [chips[1].two(carried), done[0]]

    combine_from = combine_tables(begins, ends, slots)
    tiles = place.shape[1] // 4
    names = first_expert + jnp.arange(experts, dtype=jnp.int32)

    def combined(quarter, after):
        y, dx, gate_grads = combine_rows(
            combine_from, place, carried, quarter * tiles, tiles, after
        )
        gate_grads = gate_grads[:, :experts] + gate_grads[:, 64 : 64 + experts]
        rows = group_routes[quarter * share_rows : (quarter + 1) * share_rows]
        hit = rows[:, :, None] == names[None, None, :]
        return y, dx, jnp.sum(jnp.where(hit, gate_grads[:, None, :], 0.0), axis=2)

    far = combined(3, waits)
    far_y, far_dx, far_gg = (flip(value, 1) for value in far)
    cross = combined(1, [far[0]])
    dx_send = add_low(cross[1], far_dx)
    dx_across = swap(dx_send)
    gg_across = swap(cross[2] + far_gg)
    next_door = combined(2, [dx_send, chips[2].one(cross[1])])
    door_y, door_dx, door_gg = (flip(value, 1) for value in next_door)
    y_send = add_low(cross[0], far_y)
    near = combined(0, [next_door[0]])
    y_across = swap(order(y_send, near[0]))
    mixed_grad_share = (
        near[1].astype(jnp.float32)
        + door_dx.astype(jnp.float32)
        + dx_across.astype(jnp.float32)
    )
    gates_grad_share = near[2] + door_gg + gg_across

    upstream = cotangent.astype(jnp.float32)
    chosen_grad = gate_soft * (
        gates_grad_share - jnp.sum(gate_soft * gates_grad_share, axis=-1, keepdims=True)
    )
    logit_grad = jnp.sum(chosen_grad[:, :, None] * route_onehot, axis=1)
    prob_target = ALPHA * expert_count * fractions / total_tokens
    logit_grad = logit_grad + probabilities * (
        prob_target[None, :] - jnp.sum(probabilities * prob_target[None, :], axis=-1, keepdims=True)
    )
    router_grad = jnp.dot(
        mixed_share.astype(jnp.float32).T,
        logit_grad,
        precision=HIGHEST,
        preferred_element_type=jnp.float32,
    )
    mixed_grad_share = mixed_grad_share + jnp.dot(
        logit_grad,
        w_router.astype(jnp.float32).T,
        precision=HIGHEST,
        preferred_element_type=jnp.float32,
    )
    mix_pullback = jax.vjp(normalize, middle_share, mix_gains)[1]
    middle_from_norm, mix_gain_grad = mix_pullback(mixed_grad_share)
    middle_grad = upstream + middle_from_norm
    middle_low = middle_grad.astype(jnp.bfloat16)

    def half_back(saved, out_weights):
        attended_grad = dot_nt(middle_low, out_weights).astype(jnp.bfloat16)

        def part(chosen, after):
            return attend_back(
                saved, attended_grad, limits, tables, score_scale, chosen, after
            )

        return part

    pairs = key_width // 128
    other_grads = jnp.concatenate(
        half_back(saved_other, out_other)(
            (0, pairs), [chips[3].one(middle_low)]
        ),
        axis=1,
    )
    waits = [chips[2].two(other_grads)]
    other_grads = order(other_grads, *waits)
    expert_share = (
        near[0].astype(jnp.float32)
        + door_y.astype(jnp.float32)
        + order(y_across, other_grads).astype(jnp.float32)
    )
    output_share = (middle_share + expert_share).astype(jnp.bfloat16)
    joined_held = core_sum(dot_tn(normed, other_grads), core)
    joined_across = swap(joined_held)
    marked = order(middle_low, other_grads)
    out_held = core_sum(dot_tn(marked, attended_other), core)
    out_across = swap(order(out_held, joined_held))
    out_kept = core_sum(dot_tn(marked, attended_own), core)
    done.append(chips[1].three(joined_held))
    waits = [chips[4].one(joined_held), done[1], joined_held, out_held, out_kept, output_share]
    own_part = half_back(saved_own, w_out)
    front = own_part((0, pairs // 2), waits)
    back = own_part((pairs // 2, pairs - pairs // 2), [joined_across, front[0], chips[3].two(front[0])])
    own_grads = jnp.concatenate(
        [part for both in zip(front, back) for part in both], axis=1
    )
    out_half = add_low(out_kept, order(out_across, own_grads))
    own_weight_grads = dot_tn(normed, own_grads)
    own_held = core_sum(own_weight_grads, core)
    half = jnp.concatenate([add_low(own_held, joined_across), out_half], axis=-1)
    both_total = plane_sum(half, rank)
    joined_total = both_total[:, : query_width + 2 * key_width]
    out_total = both_total[:, query_width + 2 * key_width :]
    done.append(chips[2].three(half))
    chips[4].two(half)
    sums = done + [chips[i].three(half) for i in (3, 4)]
    other_normed = dot_nt(other_grads, joined_other)
    own_normed = dot_nt(order(own_grads, half), joined_own)
    input_pullback = jax.vjp(normalize, inputs_share, norm_gains)[1]
    input_from_norm, norm_gain_grad = input_pullback(other_normed + own_normed)
    input_grad_share = middle_grad + input_from_norm
    key_end = query_width + key_width
    small = all_sum(
        jnp.concatenate(
            [jnp.sum(probabilities, axis=0), mix_gain_grad, norm_gain_grad, router_grad.reshape(-1)]
        )
    )
    prob_sums = small[:expert_count]
    mix_gain_total = small[expert_count : expert_count + model_width]
    norm_gain_total = small[expert_count + model_width : expert_count + 2 * model_width]
    router_total = small[expert_count + 2 * model_width :].reshape(router_grad.shape)
    balance = expert_count * expert_count * fractions * prob_sums / total_tokens

    mine = jnp.concatenate(sums, axis=0).reshape(experts, 3, 2, depth // 2, -1)
    theirs = flip(pick_index(mine, 1 - core, 2), 1)
    mine = pick_index(mine, core, 2)
    def placed(kind):
        own_kind, other_kind = mine[:, kind], theirs[:, kind]
        return jnp.where(
            core == 0,
            jnp.concatenate([own_kind, other_kind], axis=0),
            jnp.concatenate([other_kind, own_kind], axis=0),
        ).astype(jnp.float32)

    return (
        output_share,
        balance,
        input_grad_share,
        norm_gain_total,
        joined_total[:, :query_width],
        joined_total[:, query_width:key_end],
        joined_total[:, key_end:],
        out_total.T,
        mix_gain_total,
        router_total,
        placed(0),
        placed(1),
        placed(2).transpose(0, 2, 1),
    )


def solution(mesh):
    sizes = dict(mesh.shape)
    paired = sizes["tensor"] == 2 and sizes["dp"] == 16
    return jax.shard_map(
        shards_pair if paired else shards_wide,
        mesh=mesh,
        in_specs=(
            P(("dp", "tensor"), None),
            P(),
            P(None, "tensor"),
            P(None, "tensor"),
            P(None, "tensor"),
            P("tensor", None),
            P(),
            P(),
            P("tensor", None, None),
            P("tensor", None, None),
            P("tensor", None, None),
            P("dp", None),
            P("dp", None),
            P(("dp", "tensor"), None),
        ),
        out_specs=(
            P(("dp", "tensor"), None),
            P(),
            P(("dp", "tensor"), None),
            P(),
            P("dp", "tensor"),
            P("dp", "tensor"),
            P("dp", "tensor"),
            P("tensor", "dp"),
            P(),
            P(),
            P("tensor", "dp", None),
            P("tensor", "dp", None),
            P("tensor", None, "dp"),
        ),
        check_vma=False,
    )
```

```python
import functools

import jax
import jax.numpy as jnp
from jax import lax
from jax.experimental import pallas as pl
from jax.experimental.pallas import tpu as pltpu
from jax.sharding import PartitionSpec as P

HD = 64
PIECE = 256
CAP = 614


EPSILON = 1e-06
ALPHA = 0.01
HIGHEST = lax.Precision.HIGHEST


def normalize(values, gains):
    return values * lax.rsqrt(jnp.mean(values * values, axis=-1, keepdims=True) + EPSILON) * gains


def softmax_rows(values):
    shifted = jnp.exp(values - jnp.max(values, axis=-1, keepdims=True))
    return shifted / jnp.sum(shifted, axis=-1, keepdims=True)


def contract_rows(left, right):
    return lax.dot_general(
        left, right, (((0,), (0,)), ((), ())), preferred_element_type=jnp.float32
    )


def contract_cols(left, right):
    return lax.dot_general(
        left, right, (((1,), (1,)), ((), ())), preferred_element_type=jnp.float32
    )


def rope_tables(sequence_length, head_width):
    half_width = head_width // 2
    frequency = 10000.0 ** (-(jnp.arange(half_width, dtype=jnp.float32) * 2.0 / head_width))
    angles = jnp.arange(sequence_length, dtype=jnp.float32)[:, None] * frequency[None, :]
    return (jnp.cos(angles), jnp.sin(angles))


def rotate(values, cosine, sine_table):
    half_width = values.shape[-1] // 2
    first_half = values[..., :half_width]
    second_half = values[..., half_width:]
    cosine_rows = cosine[:, None, :]
    sine_rows = sine_table[:, None, :]
    return jnp.concatenate(
        [
            first_half * cosine_rows - second_half * sine_rows,
            second_half * cosine_rows + first_half * sine_rows,
        ],
        axis=-1,
    )


def allowed_pairs(starts_row, sequence_length, piece_length):
    position = jnp.arange(sequence_length, dtype=jnp.int32)
    labels = jnp.full((sequence_length,), -1, jnp.int32)
    for piece_index in range(starts_row.shape[0]):
        inside = (position >= starts_row[piece_index]) & (
            position < starts_row[piece_index] + piece_length
        )
        labels = jnp.where(inside, piece_index, labels)
    causal = position[None, :] <= position[:, None]
    shared = (labels[:, None] == labels[None, :]) & (labels[:, None] >= 0)
    return causal | shared


def scores_of(query_block, key_block, allowed, score_scale):
    raw_scores = (
        jnp.einsum("qkgd,skd->kgqs", query_block, key_block, preferred_element_type=jnp.float32)
        * score_scale
    )
    return jnp.where(allowed, raw_scores, -1e30)


BLOCK = 256
PART = 128
PIECE_ROWS = 32
GROUP = 8
DEEP = 4
VMEM_LIMIT = 60 * 1024 * 1024


def dot_nt(left, right):
    return lax.dot_general(
        left, right, (((1,), (1,)), ((), ())), preferred_element_type=jnp.float32
    )


def dot_tn(left, right):
    return lax.dot_general(
        left, right, (((0,), (0,)), ((), ())), preferred_element_type=jnp.float32
    )


def round_up(value, multiple):
    return -(-value // multiple) * multiple


def placement(routes_rows, first_expert, experts):
    rows = routes_rows.shape[0]
    tiles = rows // BLOCK
    turned = routes_rows.T
    names = first_expert + jnp.arange(experts, dtype=jnp.int32)
    hit = turned[None, :, :] == names[:, None, None]
    member = jnp.any(hit, axis=1)
    upper = jnp.triu(jnp.ones((BLOCK, BLOCK), jnp.bfloat16))
    inside = jnp.dot(
        member.astype(jnp.bfloat16).reshape(experts * tiles, BLOCK),
        upper,
        preferred_element_type=jnp.float32,
    ).astype(jnp.int32).reshape(experts, tiles, BLOCK)
    sums = inside[:, :, -1]
    ends = jnp.cumsum(sums, axis=1)
    begins = ends - sums
    place = jnp.where(
        member.reshape(experts, tiles, BLOCK), begins[:, :, None] + inside - 1, -1
    )
    place = jnp.concatenate(
        [place, jnp.full((1, tiles, BLOCK), -1, jnp.int32)], axis=0
    ).reshape(experts + 1, tiles, 1, BLOCK)
    return place, begins, ends


def gate_table(routes_rows, gates_rows, first_expert, experts):
    names = first_expert + jnp.arange(experts, dtype=jnp.int32)
    hit = routes_rows.T[None, :, :] == names[:, None, None]
    table = jnp.sum(jnp.where(hit, gates_rows.astype(jnp.float32).T[None, :, :], 0.0), axis=1)
    return jnp.pad(table, ((0, 128 - experts), (0, 0))).T.astype(jnp.bfloat16)


def gather_tables(begins, ends, slots):
    counts = ends[:, -1]
    parts = jnp.arange(slots // PART, dtype=jnp.int32) * PART
    low = jnp.sum((ends[:, None, :] <= parts[None, :, None]).astype(jnp.int32), axis=2)
    high = jnp.sum((begins[:, None, :] < parts[None, :, None] + PART).astype(jnp.int32), axis=2)
    high = jnp.where(parts[None, :] < counts[:, None], high, low)
    blocks = jnp.maximum(-(-counts // BLOCK), 1)
    return low, high, blocks


def combine_tables(begins, ends, slots):
    experts, tiles = begins.shape
    width = round_up(experts * (BLOCK // PIECE_ROWS + 1), GROUP)
    first = begins // PIECE_ROWS
    amount = jnp.where(ends > begins, (ends - 1) // PIECE_ROWS - first + 1, 0)
    stop = jnp.cumsum(amount, axis=0)
    place = jnp.arange(width, dtype=jnp.int32)
    owner = jnp.sum(
        (stop.T[:, None, :] <= place[None, :, None]).astype(jnp.int32), axis=2
    )
    chosen = owner[:, :, None] == jnp.arange(experts, dtype=jnp.int32)[None, None, :]
    offset = jnp.sum(
        jnp.where(chosen, (first - (stop - amount)).T[:, None, :], 0), axis=2
    )
    valid = owner < experts
    piece = jnp.where(valid, offset + place[None, :], 0)
    source = jnp.where(valid, owner, 0) * (slots // PIECE_ROWS) + piece
    groups = jnp.maximum(-(-stop[-1] // GROUP), 1)
    return owner, piece, source, groups, width


def gather_kernel(sources, with_gates, after, low_ref, high_ref, blocks_ref, place_ref, *rest):
    if with_gates:
        gates_ref, rest = rest[0], rest[1:]
    inputs, rest = rest[:sources], rest[sources + after :]
    if with_gates:
        out_ref, gate_out_ref, held, buffer, gate_buffer, sems, out_sems = rest
    else:
        out_ref, held, buffer, sems, out_sems = rest
    expert = pl.program_id(0)
    share = inputs[0].shape[0]
    slots = out_ref.shape[0] // pl.num_programs(0)

    @pl.when(expert == 0)
    def _():
        copies = [
            pltpu.make_async_copy(ref, held.at[pl.ds(i * share, share)], sems.at[i])
            for i, ref in enumerate(inputs)
        ]
        for copy in copies:
            copy.start()
        for copy in copies:
            copy.wait()

    def copies_of(part, slot):
        start = pl.multiple_of(expert * slots + part * PART, PART)
        made = [
            pltpu.make_async_copy(
                buffer.at[slot], out_ref.at[pl.ds(start, PART)], out_sems.at[0, slot]
            )
        ]
        if with_gates:
            made.append(
                pltpu.make_async_copy(
                    gate_buffer.at[slot], gate_out_ref.at[pl.ds(start, PART)], out_sems.at[1, slot]
                )
            )
        return made

    parts = blocks_ref[expert] * (BLOCK // PART)

    def one(part, carry):
        slot = part % 2

        @pl.when(part >= 2)
        def _():
            for copy in copies_of(part - 2, slot):
                copy.wait()

        buffer[slot] = jnp.zeros(buffer.shape[1:], buffer.dtype)
        if with_gates:
            gate_buffer[slot] = jnp.zeros(gate_buffer.shape[1:], gate_buffer.dtype)
        rows = lax.broadcasted_iota(jnp.int32, (PART, BLOCK), 0) + part * PART

        def step(tile, carry):
            pick = jnp.where(rows == place_ref[expert, tile], 1.0, 0.0).astype(jnp.bfloat16)
            start = pl.multiple_of(tile * BLOCK, BLOCK)
            buffer[slot] += jnp.dot(
                pick, held[pl.ds(start, BLOCK), :], preferred_element_type=jnp.float32
            ).astype(buffer.dtype)
            if with_gates:
                gate_buffer[slot] += jnp.dot(
                    pick, gates_ref[pl.ds(start, BLOCK), :], preferred_element_type=jnp.float32
                )
            return carry

        lax.fori_loop(low_ref[expert, part], high_ref[expert, part], step, 0)
        for copy in copies_of(part, slot):
            copy.start()
        return carry

    lax.fori_loop(0, parts, one, 0)
    for back in (2, 1):
        for copy in copies_of(parts - back, (parts - back) % 2):
            copy.wait()


def gather_rows(tables, place, gates, sources, slots, first, count, after=()):
    low, high, blocks = tables
    low, high, blocks = (t[first : first + count] for t in (low, high, blocks))
    place = place[first : first + count]
    rows = place.shape[1] * BLOCK
    width = sources[0].shape[1]
    with_gates = gates is not None

    def whole(array):
        zeros = (0,) * array.ndim
        return pl.BlockSpec(array.shape, lambda *_: zeros)

    operands = [place] + ([gates] if with_gates else [])
    anywhere = pl.BlockSpec(memory_space=pl.ANY)
    in_specs = [whole(a) for a in operands] + [anywhere] * (len(sources) + len(after))
    out_shape = [jax.ShapeDtypeStruct((count * slots, width), jnp.bfloat16)]
    scratch = [
        pltpu.VMEM((rows, width), jnp.bfloat16),
        pltpu.VMEM((2, PART, width), jnp.bfloat16),
    ]
    if with_gates:
        out_shape.append(jax.ShapeDtypeStruct((count * slots, 128), jnp.float32))
        scratch.append(pltpu.VMEM((2, PART, 128), jnp.float32))
    return pl.pallas_call(
        functools.partial(gather_kernel, len(sources), with_gates, len(after)),
        grid_spec=pltpu.PrefetchScalarGridSpec(
            num_scalar_prefetch=3,
            grid=(count,),
            in_specs=in_specs,
            out_specs=[anywhere] * len(out_shape),
            scratch_shapes=scratch
            + [pltpu.SemaphoreType.DMA((len(sources),)), pltpu.SemaphoreType.DMA((2, 2))],
        ),
        out_shape=out_shape,
        compiler_params=pltpu.CompilerParams(vmem_limit_bytes=VMEM_LIMIT),
    )(low, high, blocks, *operands, *sources, *after)


def expert_kernel(
    first, split, depth, far_first, extra, blocks_ref, misc_ref, x_ref, c_ref, sg_ref, wg_ref,
    wu_ref, wd_ref, *rest
):
    yd_ref = rest[extra]
    rest = rest[extra + 1 :]
    width = x_ref.shape[1]
    if split:
        send_ref, keep_ref = rest[:2]
        rest = rest[2:]
    else:
        grads_ref = rest[0]
        rest = rest[1:]
    total_gu, total_d, x_held, c_held, low_held, gated_held = rest
    expert = first + pl.program_id(0)
    block = pl.program_id(1)
    hidden = wg_ref.shape[2]
    blocks = blocks_ref[expert]
    lanes = lax.broadcasted_iota(jnp.int32, (BLOCK, 128), 1)

    @pl.when(block < blocks)
    def _():
        x = x_ref[...]
        c = c_ref[...]
        gate = jnp.sum(jnp.where(lanes == expert, sg_ref[...], 0.0), axis=1, keepdims=True)
        gate_proj = jnp.dot(x, wg_ref[0], preferred_element_type=jnp.float32)
        up_proj = jnp.dot(x, wu_ref[0], preferred_element_type=jnp.float32)
        pulled = dot_nt(c, wd_ref[0])
        sigmoid = 1.0 / (1.0 + jnp.exp(-gate_proj))
        silu = gate_proj * sigmoid
        activated = (silu * up_proj).astype(jnp.bfloat16).astype(jnp.float32)
        gate_grad = jnp.sum(activated * pulled, axis=1, keepdims=True)
        coarse = gate_grad.astype(jnp.bfloat16).astype(jnp.float32)
        yd_ref[:, 2 * width :] = jnp.where(
            lanes == expert, coarse, jnp.where(lanes == expert + 64, gate_grad - coarse, 0.0)
        ).astype(yd_ref.dtype)
        gated = (gate * activated).astype(jnp.bfloat16)
        yd_ref[:, :width] = jnp.dot(
            gated, wd_ref[0], preferred_element_type=jnp.float32
        ).astype(yd_ref.dtype)
        activated_grad = gate * pulled
        gate_low = (
            activated_grad * up_proj * sigmoid * (1.0 + gate_proj * (1.0 - sigmoid))
        ).astype(jnp.bfloat16)
        up_low = (activated_grad * silu).astype(jnp.bfloat16)
        yd_ref[:, width : 2 * width] = (
            dot_nt(gate_low, wg_ref[0]) + dot_nt(up_low, wu_ref[0])
        ).astype(yd_ref.dtype)
        start = pl.multiple_of((block % 2) * BLOCK, BLOCK)
        held = pl.ds(start, BLOCK)
        x_held[held, :] = x
        c_held[held, :] = c
        low_held[held, :hidden] = gate_low
        low_held[held, hidden:] = up_low
        gated_held[held, :] = gated

    def gather(rows, fresh):
        for begin in range(0, width, BLOCK):
            span = slice(begin, begin + BLOCK)
            for total, left, right in (
                (total_gu, x_held, low_held),
                (total_d, c_held, gated_held),
            ):
                term = dot_tn(left[:rows, span], right[:rows, :])
                total[span, :] = term if fresh else total[span, :] + term

    odd = block % 2 == 1
    last = block == blocks - 1

    @pl.when((block == 0) & last)
    def _():
        gather(BLOCK, True)

    @pl.when((block == 1) & (block < blocks))
    def _():
        gather(2 * BLOCK, True)

    @pl.when((block > 1) & odd & (block < blocks))
    def _():
        gather(2 * BLOCK, False)

    @pl.when((block > 1) & jnp.logical_not(odd) & last)
    def _():
        gather(BLOCK, False)

    @pl.when(block == pl.num_programs(1) - 1)
    def _():
        parts = (
            (total_gu, 0),
            (total_gu, hidden),
            (total_d, 0),
        )
        for which, (ref, column) in enumerate(parts):
            if split:
                side = misc_ref[1 + far_first]
                for high in range(2):
                    for low in range(2):
                        for out, chosen in ((keep_ref, side), (send_ref, 1 - side)):
                            if far_first:
                                start = ((high * 2 + chosen) * 2 + low) * depth
                                place = (high, low, which)
                            else:
                                start = ((high * 2 + low) * 2 + chosen) * depth
                                place = (low, high, which)
                            out[place] = ref[
                                pl.ds(pl.multiple_of(start, 64), depth), pl.ds(column, hidden)
                            ].astype(out.dtype)
            else:
                grads_ref[0, which] = ref[:, pl.ds(column, hidden)].astype(grads_ref.dtype)


def expert_call(
    blocks, misc, x, c, sg, weights, carried, slots, first, count, x_first, c_first, depth,
    far_first=0, after=()
):
    w_gate, w_up, w_down = weights
    experts = blocks.shape[0]
    width = x.shape[1]
    hidden = w_gate.shape[2]
    most = slots // BLOCK
    split = depth is not None

    def rows_index(base):
        def index(expert, block, blocks, misc):
            limit = blocks[first + expert] - 1
            return ((first - base + expert) * most + jnp.minimum(block, limit), 0)

        return index

    def weight_index(expert, block, blocks, misc):
        return (misc[0] + first + expert, 0, 0)

    def grads_index(expert, block, blocks, misc):
        return (0, 0, expert, 0, 0)

    out_shape = [jax.ShapeDtypeStruct((experts * slots, 2 * width + 128), jnp.bfloat16)]
    out_specs = [pl.BlockSpec((BLOCK, 2 * width + 128), rows_index(0))]
    if split:
        out_shape += [jax.ShapeDtypeStruct((2, 2, 3 * count, depth, hidden), jnp.bfloat16)] * 2
        out_specs += [pl.BlockSpec((2, 2, 3, depth, hidden), grads_index)] * 2
    else:
        out_shape += [jax.ShapeDtypeStruct((count, 3, width, hidden), jnp.bfloat16)]
        out_specs += [pl.BlockSpec((1, 3, width, hidden), lambda e, b, *_: (e, 0, 0, 0))]
    operands = [x, c, sg, w_gate, w_up, w_down]
    in_specs = [
        pl.BlockSpec((BLOCK, width), rows_index(x_first)),
        pl.BlockSpec((BLOCK, width), rows_index(c_first)),
        pl.BlockSpec((BLOCK, 128), rows_index(x_first)),
        pl.BlockSpec((1, width, hidden), weight_index),
        pl.BlockSpec((1, width, hidden), weight_index),
        pl.BlockSpec((1, hidden, width), weight_index),
    ]
    aliases = {}
    if carried is not None:
        operands.append(carried)
        aliases = {8: 0}
    operands += list(after)
    extra = len(operands) - 6
    in_specs += [pl.BlockSpec(memory_space=pl.ANY)] * extra
    return pl.pallas_call(
        functools.partial(expert_kernel, first, split, depth, far_first, extra),
        grid_spec=pltpu.PrefetchScalarGridSpec(
            num_scalar_prefetch=2,
            grid=(count, most),
            in_specs=in_specs,
            out_specs=out_specs,
            scratch_shapes=[
                pltpu.VMEM((width, 2 * hidden), jnp.float32),
                pltpu.VMEM((width, hidden), jnp.float32),
                pltpu.VMEM((2 * BLOCK, width), jnp.bfloat16),
                pltpu.VMEM((2 * BLOCK, width), jnp.bfloat16),
                pltpu.VMEM((2 * BLOCK, 2 * hidden), jnp.bfloat16),
                pltpu.VMEM((2 * BLOCK, hidden), jnp.bfloat16),
            ],
        ),
        out_shape=out_shape,
        input_output_aliases=aliases,
        compiler_params=pltpu.CompilerParams(vmem_limit_bytes=VMEM_LIMIT),
    )(blocks, misc, *operands)


def combine_kernel(
    first, owner_ref, piece_ref, source_ref, groups_ref, begin_ref, tile_ref, place_ref, yd_ref, *rest
):
    y_out, dx_out, gate_out, buffer, total, sems = rest[-6:]
    columns = y_out.shape[1]
    step = pl.program_id(0)
    tile = first + step

    head = begin_ref[first]
    final = first + pl.num_programs(0) - 1
    stop = begin_ref[final] + groups_ref[final]

    def copies(place):
        which_tile = tile_ref[place]
        group = place - begin_ref[which_tile]
        slot = (place - head) % DEEP
        made = []
        for i in range(GROUP):
            source = pl.multiple_of(
                source_ref[which_tile, group * GROUP + i] * PIECE_ROWS, PIECE_ROWS
            )
            made.append(
                pltpu.make_async_copy(
                    yd_ref.at[pl.ds(source, PIECE_ROWS)],
                    buffer.at[slot, pl.ds(i * PIECE_ROWS, PIECE_ROWS)],
                    sems.at[slot, i],
                )
            )
        return made

    @pl.when(step == 0)
    def _():
        for ahead in range(DEEP - 1):

            @pl.when(head + ahead < stop)
            def _():
                for copy in copies(head + ahead):
                    copy.start()

    def one(group, carry):
        place = begin_ref[tile] + group
        slot = (place - head) % DEEP

        @pl.when(place + DEEP - 1 < stop)
        def _():
            for copy in copies(place + DEEP - 1):
                copy.start()

        picks = []
        for i in range(GROUP):
            entry = group * GROUP + i
            rows = (
                lax.broadcasted_iota(jnp.int32, (PIECE_ROWS, BLOCK), 0)
                + piece_ref[tile, entry] * PIECE_ROWS
            )
            picks.append(jnp.where(rows == place_ref[owner_ref[tile, entry], step], 1.0, 0.0))
        picked = jnp.concatenate(picks, axis=0).T.astype(jnp.bfloat16)
        for copy in copies(place):
            copy.wait()
        fresh = group == 0
        for begin in range(0, total.shape[1], 640):
            span = slice(begin, begin + 640)
            term = jnp.dot(picked, buffer[slot, :, span], preferred_element_type=jnp.float32)
            total[:, span] = jnp.where(fresh, 0.0, total[:, span]) + term
        return carry

    lax.fori_loop(0, groups_ref[tile], one, 0)
    y_out[...] = total[:, :columns].astype(y_out.dtype)
    dx_out[...] = total[:, columns : 2 * columns].astype(dx_out.dtype)
    gate_out[...] = total[:, 2 * columns :]


def combine_rows(tables, place, yd, first, count, after=()):
    owner, piece, source, groups, width = tables
    ends = jnp.cumsum(groups)
    begin = ends - groups
    most = groups.shape[0] * (width // GROUP)
    tile_of = jnp.minimum(
        jnp.sum((ends[None, :] <= jnp.arange(most)[:, None]).astype(jnp.int32), axis=1),
        groups.shape[0] - 1,
    )
    experts = place.shape[0]
    whole_width = yd.shape[1]
    columns = (whole_width - 128) // 2
    row_block = lambda wide: pl.BlockSpec((BLOCK, wide), lambda t, *_: (t, 0))
    return pl.pallas_call(
        functools.partial(combine_kernel, first),
        grid_spec=pltpu.PrefetchScalarGridSpec(
            num_scalar_prefetch=6,
            grid=(count,),
            in_specs=[pl.BlockSpec((experts, count, 1, BLOCK), lambda *_: (0, first // count, 0, 0))]
            + [pl.BlockSpec(memory_space=pl.ANY)] * (1 + len(after)),
            out_specs=[row_block(columns), row_block(columns), row_block(128)],
            scratch_shapes=[
                pltpu.VMEM((DEEP, GROUP * PIECE_ROWS, whole_width), jnp.bfloat16),
                pltpu.VMEM((BLOCK, whole_width), jnp.float32),
                pltpu.SemaphoreType.DMA((DEEP, GROUP)),
            ],
        ),
        out_shape=[
            jax.ShapeDtypeStruct((count * BLOCK, columns), jnp.bfloat16),
            jax.ShapeDtypeStruct((count * BLOCK, columns), jnp.bfloat16),
            jax.ShapeDtypeStruct((count * BLOCK, 128), jnp.float32),
        ],
        compiler_params=pltpu.CompilerParams(vmem_limit_bytes=VMEM_LIMIT),
    )(owner, piece, source, groups, begin, tile_of, place, yd, *after)


def flip(value, bit):
    size = lax.axis_size("dp")
    return lax.ppermute(value, "dp", [(i, i ^ bit) for i in range(size)])


def swap(value):
    return lax.ppermute(value, "tensor", [(0, 1), (1, 0)])


def order(value, *after):
    return lax.optimization_barrier((value, *after))[0] if after else value


def add_low(left, right):
    return (left.astype(jnp.float32) + right.astype(jnp.float32)).astype(jnp.bfloat16)


def pick_index(value, index, axis):
    return lax.dynamic_index_in_dim(value, index, axis, keepdims=False)


def sum_stage(parts, bit, chosen, after):
    send, keep = parts
    got = order(flip(send, bit), *after)
    return tuple(
        add_low(pick_index(keep, which, 0), pick_index(got, which, 0))
        for which in (1 - chosen, chosen)
    )


class ChipSum:
    def __init__(self, parts, rank, far_first):
        side, low_bit, high_bit = (rank // 2) % 2, (rank // 4) % 2, rank // 8
        self.parts = parts
        self.first = (4, high_bit) if far_first else (2, low_bit)
        self.second = (8, side) if far_first else (4, high_bit)
        self.last = 2 if far_first else 8

    def one(self, *after):
        self.parts = sum_stage(self.parts, *self.first, after)
        return self.parts[0]

    def two(self, *after):
        self.parts = sum_stage(self.parts, *self.second, after)
        return self.parts[0]

    def three(self, *after):
        send, keep = self.parts
        return add_low(keep, order(flip(send, self.last), *after))


def core_sum(value, core):
    rows, columns = value.shape
    value = value.reshape(8, 2, rows // 16, columns)
    got = flip(pick_index(value, 1 - core, 1).astype(jnp.bfloat16), 1)
    return add_low(pick_index(value, core, 1), got)


def plane_sum(total, rank, *after):
    side, low_bit, high_bit = (rank // 2) % 2, (rank // 4) % 2, rank // 8
    part, columns = total.shape[1:]
    total = total.reshape(4, 2, part, columns)
    got = order(flip(pick_index(total, 1 - side, 1), 2), *after)
    total = add_low(pick_index(total, side, 1), got).reshape(2, 2, part, columns)
    got = flip(pick_index(total, 1 - low_bit, 1), 4)
    total = add_low(pick_index(total, low_bit, 1), got)
    got = flip(pick_index(total, 1 - high_bit, 0), 8)
    return pick_index(total, high_bit, 0).astype(jnp.float32) + got.astype(jnp.float32)


def fetch_other(weights, core, side, after=()):
    rows = weights[0].shape[0] // 4
    start = (side * 2 + core) * rows
    own = jnp.concatenate(
        [lax.dynamic_slice_in_dim(w, start, rows, 0) for w in weights], axis=1
    )
    pieces = swap(order(own, *after))
    turned = flip(pieces, 2)
    result = jnp.zeros((4 * rows, own.shape[1]), own.dtype)
    for value, place in (
        (pieces, side * 2 + core),
        (turned, (1 - side) * 2 + core),
        (flip(pieces, 1), side * 2 + 1 - core),
        (flip(turned, 1), (1 - side) * 2 + 1 - core),
    ):
        result = lax.dynamic_update_slice_in_dim(result, value, place * rows, 0)
    return result, own, pieces


ROWS = 256
HALF = 512


def lane_swap(values):
    width = values.shape[1]
    lane = lax.broadcasted_iota(jnp.int32, values.shape, 1) % HD
    ahead = pltpu.roll(values, width - HD // 2, 1)
    behind = pltpu.roll(values, HD // 2, 1)
    return jnp.where(lane < HD // 2, ahead, behind)


def turn_tables(rows):
    cosine, sine = rope_tables(rows, HD)
    return (
        jnp.concatenate([cosine] * 4, axis=1),
        jnp.concatenate([-sine, sine, -sine, sine], axis=1),
    )


def project_kernel(sizes, score_scale, normed_ref, weights_ref, cosine_ref, sine_ref, *outs):
    query_ref, key_ref, value_ref = outs[-3:]
    query_width, key_width = sizes
    projected = jnp.dot(normed_ref[...], weights_ref[...], preferred_element_type=jnp.float32)
    cosine, sine = cosine_ref[...], sine_ref[...]
    for start in range(0, query_width + key_width, 128):
        piece = projected[:, start : start + 128]
        turned = piece * cosine + lane_swap(piece) * sine
        if start < query_width:
            query_ref[:, start : start + 128] = (turned * score_scale).astype(jnp.bfloat16)
        else:
            begin = start - query_width
            key_ref[:, begin : begin + 128] = turned.astype(jnp.bfloat16)
    value_ref[...] = projected[:, query_width + key_width :].astype(jnp.bfloat16)


def project(normed, weights, tables, query_width, key_width, score_scale, after=()):
    rows, depth = normed.shape
    width = weights.shape[1]
    row_spec = lambda columns: pl.BlockSpec((ROWS, columns), lambda i: (i, 0))
    return pl.pallas_call(
        functools.partial(project_kernel, (query_width, key_width), score_scale),
        grid=(rows // ROWS,),
        in_specs=[
            row_spec(depth),
            pl.BlockSpec((depth, width), lambda i: (0, 0)),
            row_spec(128),
            row_spec(128),
        ]
        + [pl.BlockSpec(memory_space=pl.ANY)] * len(after),
        out_specs=[row_spec(query_width), row_spec(key_width), row_spec(key_width)],
        out_shape=[
            jax.ShapeDtypeStruct((rows, query_width), jnp.bfloat16),
            jax.ShapeDtypeStruct((rows, key_width), jnp.bfloat16),
            jax.ShapeDtypeStruct((rows, key_width), jnp.bfloat16),
        ],
        compiler_params=pltpu.CompilerParams(vmem_limit_bytes=VMEM_LIMIT),
    )(normed, weights, *tables, *after)


def attend_kernel(per_pair, query_ref, key_ref, value_ref, limit_ref, *rest):
    out_ref, lse_ref = rest[-2:]
    step = pl.program_id(1)

    def work(keys):
        columns = lax.broadcasted_iota(jnp.int32, (ROWS, HALF), 1) + (keys - HALF)
        allowed = columns <= limit_ref[...]
        lanes = lax.broadcasted_iota(jnp.int32, (ROWS, 128), 1)
        sums = jnp.zeros((ROWS, 128), jnp.float32)
        pieces = []
        for head in range(per_pair):
            group = head // (per_pair // 2)
            query = query_ref[:, head * HD : (head + 1) * HD]
            key = key_ref[:keys, group * HD : (group + 1) * HD]
            value = value_ref[:keys, group * HD : (group + 1) * HD]
            scores = dot_nt(query, key)
            last = jnp.where(allowed, scores[:, keys - HALF :], -1e30)
            scores = last if keys == HALF else jnp.concatenate([scores[:, : keys - HALF], last], 1)
            highest = jnp.max(scores, axis=1, keepdims=True)
            shifted = jnp.exp(scores - highest)
            total = jnp.sum(shifted, axis=1, keepdims=True)
            mixed = jnp.dot(
                shifted.astype(jnp.bfloat16), value, preferred_element_type=jnp.float32
            )
            pieces.append((mixed / total).astype(jnp.bfloat16))
            sums = jnp.where(lanes == head, highest + jnp.log(total), sums)
        out_ref[...] = jnp.concatenate(pieces, axis=1)
        lse_ref[0] = sums

    halfway = pl.num_programs(1) // 2

    @pl.when(step < halfway)
    def _():
        work(HALF)

    @pl.when(step >= halfway)
    def _():
        work(2 * HALF)


def attend(query, key, value, limits, after=()):
    rows, query_width = query.shape
    pairs = key.shape[1] // 128
    wide = query_width // pairs
    return pl.pallas_call(
        functools.partial(attend_kernel, wide // HD),
        grid=(pairs, rows // ROWS),
        in_specs=[
            pl.BlockSpec((ROWS, wide), lambda p, i: (i, p)),
            pl.BlockSpec((rows, 128), lambda p, i: (0, p)),
            pl.BlockSpec((rows, 128), lambda p, i: (0, p)),
            pl.BlockSpec((ROWS, 1), lambda p, i: (i, 0)),
        ]
        + [pl.BlockSpec(memory_space=pl.ANY)] * len(after),
        out_specs=[
            pl.BlockSpec((ROWS, wide), lambda p, i: (i, p)),
            pl.BlockSpec((1, ROWS, 128), lambda p, i: (p, i, 0)),
        ],
        out_shape=[
            jax.ShapeDtypeStruct((rows, query_width), jnp.bfloat16),
            jax.ShapeDtypeStruct((pairs, rows, 128), jnp.float32),
        ],
        compiler_params=pltpu.CompilerParams(vmem_limit_bytes=VMEM_LIMIT),
    )(query, key, value, limits, *after)


def back_kernel(
    per_pair, score_scale, after, query_ref, key_ref, value_ref, turned_key_ref, grad_ref, lse_ref,
    limit_ref, cosine_ref, sine_ref, all_cosine_ref, all_sine_ref, *rest
):
    query_out, key_out, value_out, key_total, value_total = rest[after:]
    step = pl.program_id(1)
    halfway = pl.num_programs(1) // 2

    @pl.when(step == 0)
    def _():
        key_total[...] = jnp.zeros_like(key_total)
        value_total[...] = jnp.zeros_like(value_total)

    def work(keys):
        rows = lax.broadcasted_iota(jnp.int32, (HALF, ROWS), 0) + (keys - HALF)
        allowed = rows <= limit_ref[...]
        made = []
        key_parts, value_parts = [], []
        for group in range(2):
            span = slice(group * HD, (group + 1) * HD)
            key, value = key_ref[:keys, span], value_ref[:keys, span]
            key_part = value_part = 0.0
            for head in range(group * per_pair // 2, (group + 1) * per_pair // 2):
                query = query_ref[:, head * HD : (head + 1) * HD]
                grad = grad_ref[:, head * HD : (head + 1) * HD]
                scores = dot_nt(key, query)
                last = jnp.where(allowed, scores[keys - HALF :], -1e30)
                scores = (
                    last
                    if keys == HALF
                    else jnp.concatenate([scores[: keys - HALF], last], axis=0)
                )
                weights = jnp.exp(scores - lse_ref[0, head : head + 1, :])
                pulled = dot_nt(value, grad)
                inner = jnp.sum(weights * pulled, axis=0, keepdims=True)
                score_low = (weights * (pulled - inner)).astype(jnp.bfloat16)
                value_part += jnp.dot(
                    weights.astype(jnp.bfloat16), grad, preferred_element_type=jnp.float32
                )
                key_part += jnp.dot(score_low, query, preferred_element_type=jnp.float32)
                made.append(
                    jnp.dot(
                        turned_key_ref[0, span, :keys],
                        score_low,
                        preferred_element_type=jnp.float32,
                    )
                )
            key_parts.append(key_part)
            value_parts.append(value_part)
        key_total[:keys] += jnp.concatenate(key_parts, axis=1)
        value_total[:keys] += jnp.concatenate(value_parts, axis=1)
        cosine, sine = cosine_ref[...], sine_ref[...]
        for index in range(per_pair // 2):
            both = jnp.concatenate(made[2 * index : 2 * index + 2], axis=0).T * score_scale
            query_out[:, index * 128 : (index + 1) * 128] = (
                both * cosine - lane_swap(both) * sine
            ).astype(jnp.bfloat16)

    @pl.when(step < halfway)
    def _():
        work(HALF)

    @pl.when(step >= halfway)
    def _():
        work(2 * HALF)

    @pl.when(step == pl.num_programs(1) - 1)
    def _():
        total = key_total[...]
        key_out[...] = (
            total * all_cosine_ref[...] - lane_swap(total) * all_sine_ref[...]
        ).astype(jnp.bfloat16)
        value_out[...] = value_total[...].astype(jnp.bfloat16)


def attend_back(saved, attended_grad, limits, tables, score_scale, chosen, after=()):
    query, key, value, lse = saved
    rows, query_width = query.shape
    pairs = key.shape[1] // 128
    wide = query_width // pairs
    turned_key = key.T.reshape(pairs, 128, rows)
    lse_rows = lse[:, :, :8].transpose(0, 2, 1)
    cosine, sine = tables
    begin, count = chosen
    block = lambda columns: pl.BlockSpec((ROWS, columns), lambda p, i: (i, p + begin))
    whole = pl.BlockSpec((rows, 128), lambda p, i: (0, p + begin))
    block_out = pl.BlockSpec((ROWS, wide), lambda p, i: (i, p))
    whole_out = pl.BlockSpec((rows, 128), lambda p, i: (0, p))
    table = pl.BlockSpec((ROWS, 128), lambda p, i: (i, 0))
    full_table = pl.BlockSpec((rows, 128), lambda p, i: (0, 0))
    return pl.pallas_call(
        functools.partial(back_kernel, wide // HD, score_scale, len(after)),
        grid=(count, rows // ROWS),
        in_specs=[
            block(wide),
            whole,
            whole,
            pl.BlockSpec((1, 128, rows), lambda p, i: (p + begin, 0, 0)),
            block(wide),
            pl.BlockSpec((1, 8, ROWS), lambda p, i: (p + begin, 0, i)),
            pl.BlockSpec((1, ROWS), lambda p, i: (0, i)),
            table,
            table,
            full_table,
            full_table,
        ]
        + [pl.BlockSpec(memory_space=pl.ANY)] * len(after),
        out_specs=[block_out, whole_out, whole_out],
        out_shape=[
            jax.ShapeDtypeStruct((rows, count * wide), jnp.bfloat16),
            jax.ShapeDtypeStruct((rows, count * 128), jnp.bfloat16),
            jax.ShapeDtypeStruct((rows, count * 128), jnp.bfloat16),
        ],
        scratch_shapes=[
            pltpu.VMEM((rows, 128), jnp.float32),
            pltpu.VMEM((rows, 128), jnp.float32),
        ],
        compiler_params=pltpu.CompilerParams(vmem_limit_bytes=VMEM_LIMIT),
    )(
        query, key, value, turned_key, attended_grad, lse_rows, limits.T, cosine, sine, cosine,
        sine, *after,
    )


def piece_limits(starts_row, rows):
    position = jnp.arange(rows, dtype=jnp.int32)
    limits = position
    for index in range(starts_row.shape[0]):
        start = starts_row[index]
        inside = (position >= start) & (position < start + PIECE)
        limits = jnp.where(inside, start + PIECE - 1, limits)
    return limits[:, None]


def slot_table(routes, expert_count, capacity):
    flattened = routes.reshape(-1)
    onehot = (flattened[:, None] == jnp.arange(expert_count, dtype=jnp.int32)[None, :]).astype(
        jnp.int32
    )
    placed = jnp.sum((jnp.cumsum(onehot, axis=0) - 1) * onehot, axis=1)
    entries = jnp.arange(flattened.shape[0], dtype=jnp.int32)
    return (
        jnp.full((expert_count * capacity,), flattened.shape[0], jnp.int32)
        .at[flattened * capacity + placed]
        .set(entries)
    )


def expert_forward(expert_inputs, w_gate, w_up, w_down):
    gate_proj = jnp.einsum(
        "ecd,edf->ecf", expert_inputs, w_gate, preferred_element_type=jnp.float32
    )
    up_proj = jnp.einsum("ecd,edf->ecf", expert_inputs, w_up, preferred_element_type=jnp.float32)
    activated = (gate_proj * jax.nn.sigmoid(gate_proj) * up_proj).astype(jnp.bfloat16)
    returned = jnp.einsum("ecf,efd->ecd", activated, w_down, preferred_element_type=jnp.float32)
    return (gate_proj, up_proj, activated, returned)


def shards_wide(
    tokens,
    norm_gains,
    w_query,
    w_key,
    w_value,
    w_out,
    mix_gains,
    w_router,
    w_gate,
    w_up,
    w_down,
    routes,
    starts,
    cotangent,
):
    share_rows = tokens.shape[0]
    model_width = tokens.shape[1]
    head_width = HD
    query_width = w_query.shape[1]
    key_width = w_key.shape[1]
    heads_here = query_width // head_width
    groups_here = key_width // head_width
    per_group = heads_here // groups_here
    experts_here = w_gate.shape[0]
    group_rows = routes.shape[0]
    choices_count = routes.shape[1]
    sequences_here = starts.shape[0]
    sequence_length = group_rows // sequences_here
    expert_count = w_router.shape[1]
    tensor_rank = lax.axis_index("tensor")
    total_tokens = group_rows * lax.axis_size("dp")
    score_scale = head_width ** (-0.5)
    inputs_share = tokens.astype(jnp.float32)
    normed_share = normalize(inputs_share, norm_gains).astype(jnp.bfloat16)
    normed = lax.all_gather(normed_share, "tensor", axis=0, tiled=True)
    joined_weights = jnp.concatenate([w_query, w_key, w_value], axis=1)
    projected = jnp.dot(normed, joined_weights, preferred_element_type=jnp.float32)
    cosine, sine_table = rope_tables(sequence_length, head_width)
    cosine_rows = jnp.tile(cosine, (sequences_here, 1))
    sine_rows = jnp.tile(sine_table, (sequences_here, 1))
    query_rows = rotate(
        projected[:, :query_width].reshape(group_rows, heads_here, head_width),
        cosine_rows,
        sine_rows,
    ).astype(jnp.bfloat16)
    key_rows = rotate(
        projected[:, query_width : query_width + key_width].reshape(
            group_rows, groups_here, head_width
        ),
        cosine_rows,
        sine_rows,
    ).astype(jnp.bfloat16)
    value_rows = (
        projected[:, query_width + key_width :]
        .astype(jnp.bfloat16)
        .reshape(group_rows, groups_here, head_width)
    )
    attended_parts = []
    logsum_parts = []
    for sequence in range(sequences_here):
        first_row = sequence * sequence_length
        query_block = query_rows[first_row : first_row + sequence_length].reshape(
            sequence_length, groups_here, per_group, head_width
        )
        key_block = key_rows[first_row : first_row + sequence_length]
        value_block = value_rows[first_row : first_row + sequence_length]
        allowed = allowed_pairs(starts[sequence], sequence_length, PIECE)
        scores = scores_of(query_block, key_block, allowed, score_scale)
        highest = jnp.max(scores, axis=-1, keepdims=True)
        shifted = jnp.exp(scores - highest)
        totals = jnp.sum(shifted, axis=-1, keepdims=True)
        weights = (shifted / totals).astype(jnp.bfloat16)
        mixed_values = jnp.einsum(
            "kgqs,skd->qkgd", weights, value_block, preferred_element_type=jnp.float32
        )
        attended_parts.append(
            mixed_values.reshape(sequence_length, query_width).astype(jnp.bfloat16)
        )
        logsum_parts.append(highest + jnp.log(totals))
    attended = jnp.concatenate(attended_parts, axis=0)
    attention_share = lax.psum_scatter(
        jnp.dot(attended, w_out, preferred_element_type=jnp.float32),
        "tensor",
        scatter_dimension=0,
        tiled=True,
    )
    middle_share = inputs_share + attention_share
    mixed_share = normalize(middle_share, mix_gains).astype(jnp.bfloat16)
    share_routes = lax.dynamic_slice_in_dim(routes, tensor_rank * share_rows, share_rows, 0)
    route_onehot = (
        share_routes[:, :, None] == jnp.arange(expert_count, dtype=jnp.int32)[None, None, :]
    ).astype(jnp.float32)
    logits = jnp.dot(mixed_share, w_router, preferred_element_type=jnp.float32)
    probabilities = softmax_rows(logits)
    chosen = jnp.sum(logits[:, None, :] * route_onehot, axis=-1)
    gate_soft = softmax_rows(chosen)
    gate_low = gate_soft.astype(jnp.bfloat16)
    counts, prob_sums = lax.psum(
        (jnp.sum(route_onehot, axis=(0, 1)), jnp.sum(probabilities, axis=0)), ("dp", "tensor")
    )
    fractions = counts / (total_tokens * choices_count)
    balance = expert_count * expert_count * fractions * prob_sums / total_tokens
    mixed_rows, gate_rows = (
        lax.all_gather(mixed_share, "tensor", axis=0, tiled=True),
        lax.all_gather(gate_low, "tensor", axis=0, tiled=True),
    )
    slots_all = slot_table(routes, expert_count, CAP)
    slots = lax.dynamic_slice_in_dim(
        slots_all, tensor_rank * experts_here * CAP, experts_here * CAP, 0
    )
    owners = slots // choices_count
    padded_rows = jnp.concatenate([mixed_rows, jnp.zeros((1, model_width), jnp.bfloat16)], axis=0)
    padded_gates = jnp.concatenate(
        [gate_rows.reshape(-1).astype(jnp.float32), jnp.zeros((1,), jnp.float32)], axis=0
    )
    slot_gates = padded_gates[slots]
    expert_inputs = padded_rows[owners].reshape(experts_here, CAP, model_width)
    gate_proj, up_proj, activated, returned = expert_forward(expert_inputs, w_gate, w_up, w_down)
    returned_flat = returned.reshape(experts_here * CAP, model_width)
    expert_partial = jax.ops.segment_sum(
        slot_gates[:, None] * returned_flat, owners, num_segments=group_rows + 1
    )[:group_rows]
    expert_share = lax.psum_scatter(
        expert_partial.astype(jnp.bfloat16), "tensor", scatter_dimension=0, tiled=True
    ).astype(jnp.float32)
    output_share = (middle_share + expert_share).astype(jnp.bfloat16)
    upstream = cotangent.astype(jnp.float32)
    upstream_rows = lax.all_gather(cotangent, "tensor", axis=0, tiled=True)
    padded_upstream = jnp.concatenate(
        [upstream_rows, jnp.zeros((1, model_width), jnp.bfloat16)], axis=0
    )
    slot_upstream = padded_upstream[owners].astype(jnp.float32)
    slot_cotangent = (
        (slot_gates[:, None] * slot_upstream)
        .astype(jnp.bfloat16)
        .reshape(experts_here, CAP, model_width)
    )
    slot_gate_grad = jnp.sum(slot_upstream * returned_flat, axis=1)
    activated_grad = jnp.einsum(
        "ecd,efd->ecf", slot_cotangent, w_down, preferred_element_type=jnp.float32
    )
    down_grad = jnp.einsum(
        "ecf,ecd->efd", activated, slot_cotangent, preferred_element_type=jnp.float32
    )
    sigmoid_gate = jax.nn.sigmoid(gate_proj)
    gate_proj_low = (
        activated_grad * up_proj * sigmoid_gate * (1.0 + gate_proj * (1.0 - sigmoid_gate))
    ).astype(jnp.bfloat16)
    up_proj_low = (activated_grad * gate_proj * sigmoid_gate).astype(jnp.bfloat16)
    inputs_grad = jnp.einsum(
        "ecf,edf->ecd", gate_proj_low, w_gate, preferred_element_type=jnp.float32
    ) + jnp.einsum("ecf,edf->ecd", up_proj_low, w_up, preferred_element_type=jnp.float32)
    gate_grad = jnp.einsum(
        "ecd,ecf->edf", expert_inputs, gate_proj_low, preferred_element_type=jnp.float32
    )
    up_grad = jnp.einsum(
        "ecd,ecf->edf", expert_inputs, up_proj_low, preferred_element_type=jnp.float32
    )
    mixed_partial = jax.ops.segment_sum(
        inputs_grad.reshape(experts_here * CAP, model_width), owners, num_segments=group_rows + 1
    )[:group_rows]
    gate_partial = jax.ops.segment_sum(
        slot_gate_grad, slots, num_segments=group_rows * choices_count + 1
    )[: group_rows * choices_count].reshape(group_rows, choices_count)
    mixed_grad_share, gates_grad_share = (
        lax.psum_scatter(mixed_partial, "tensor", scatter_dimension=0, tiled=True),
        lax.psum_scatter(gate_partial, "tensor", scatter_dimension=0, tiled=True),
    )
    gate_total, up_total = (
        lax.psum_scatter(
            gate_grad.astype(jnp.bfloat16), "dp", scatter_dimension=1, tiled=True
        ).astype(jnp.float32),
        lax.psum_scatter(
            up_grad.astype(jnp.bfloat16), "dp", scatter_dimension=1, tiled=True
        ).astype(jnp.float32),
    )
    down_total = lax.psum_scatter(
        down_grad.astype(jnp.bfloat16), "dp", scatter_dimension=2, tiled=True
    ).astype(jnp.float32)
    chosen_grad = gate_soft * (
        gates_grad_share - jnp.sum(gate_soft * gates_grad_share, axis=-1, keepdims=True)
    )
    logit_grad = jnp.sum(chosen_grad[:, :, None] * route_onehot, axis=1)
    prob_target = ALPHA * expert_count * fractions / total_tokens
    logit_grad = logit_grad + probabilities * (
        prob_target[None, :] - jnp.sum(probabilities * prob_target[None, :], axis=-1, keepdims=True)
    )
    mixed_float = mixed_share.astype(jnp.float32)
    router_grad = jnp.dot(
        mixed_float.T, logit_grad, precision=HIGHEST, preferred_element_type=jnp.float32
    )
    mixed_grad_share = mixed_grad_share + jnp.dot(
        logit_grad,
        w_router.astype(jnp.float32).T,
        precision=HIGHEST,
        preferred_element_type=jnp.float32,
    )
    mix_pullback = jax.vjp(normalize, middle_share, mix_gains)[1]
    middle_from_norm, mix_gain_grad = mix_pullback(mixed_grad_share)
    middle_grad = upstream + middle_from_norm
    middle_low = middle_grad.astype(jnp.bfloat16)
    middle_rows = lax.all_gather(middle_low, "tensor", axis=0, tiled=True)
    out_grad = contract_rows(attended, middle_rows)
    attended_grad = contract_cols(middle_rows, w_out).astype(jnp.bfloat16)
    query_parts = []
    key_parts = []
    value_parts = []
    for sequence in range(sequences_here):
        first_row = sequence * sequence_length
        query_block = query_rows[first_row : first_row + sequence_length].reshape(
            sequence_length, groups_here, per_group, head_width
        )
        key_block = key_rows[first_row : first_row + sequence_length]
        value_block = value_rows[first_row : first_row + sequence_length]
        allowed = allowed_pairs(starts[sequence], sequence_length, PIECE)
        scores = scores_of(query_block, key_block, allowed, score_scale)
        weights_full = jnp.exp(scores - logsum_parts[sequence])
        weights_low = weights_full.astype(jnp.bfloat16)
        grad_block = attended_grad[first_row : first_row + sequence_length].reshape(
            sequence_length, groups_here, per_group, head_width
        )
        value_parts.append(
            jnp.einsum(
                "kgqs,qkgd->skd", weights_low, grad_block, preferred_element_type=jnp.float32
            )
        )
        weight_grad = jnp.einsum(
            "qkgd,skd->kgqs", grad_block, value_block, preferred_element_type=jnp.float32
        )
        score_low = (
            weights_full
            * (weight_grad - jnp.sum(weights_full * weight_grad, axis=-1, keepdims=True))
        ).astype(jnp.bfloat16)
        query_parts.append(
            jnp.einsum("kgqs,skd->qkgd", score_low, key_block, preferred_element_type=jnp.float32)
            * score_scale
        )
        key_parts.append(
            jnp.einsum("kgqs,qkgd->skd", score_low, query_block, preferred_element_type=jnp.float32)
            * score_scale
        )
    query_grads = (
        rotate(
            jnp.concatenate(query_parts, axis=0).reshape(group_rows, heads_here, head_width),
            cosine_rows,
            -sine_rows,
        )
        .astype(jnp.bfloat16)
        .reshape(group_rows, query_width)
    )
    key_grads = (
        rotate(jnp.concatenate(key_parts, axis=0), cosine_rows, -sine_rows)
        .astype(jnp.bfloat16)
        .reshape(group_rows, key_width)
    )
    value_grads = (
        jnp.concatenate(value_parts, axis=0).astype(jnp.bfloat16).reshape(group_rows, key_width)
    )
    joined_grads = jnp.concatenate([query_grads, key_grads, value_grads], axis=1)
    joined_weight_grad = contract_rows(normed, joined_grads)
    normed_grad_share = lax.psum_scatter(
        contract_cols(joined_grads, joined_weights).astype(jnp.bfloat16),
        "tensor",
        scatter_dimension=0,
        tiled=True,
    ).astype(jnp.float32)
    input_pullback = jax.vjp(normalize, inputs_share, norm_gains)[1]
    input_from_norm, norm_gain_grad = input_pullback(normed_grad_share)
    input_grad_share = middle_grad + input_from_norm
    query_total, key_total, value_total, out_turned = (
        lax.psum_scatter(
            joined_weight_grad[:, :query_width].astype(jnp.bfloat16),
            "dp",
            scatter_dimension=0,
            tiled=True,
        ).astype(jnp.float32),
        lax.psum_scatter(
            joined_weight_grad[:, query_width : query_width + key_width].astype(jnp.bfloat16),
            "dp",
            scatter_dimension=0,
            tiled=True,
        ).astype(jnp.float32),
        lax.psum_scatter(
            joined_weight_grad[:, query_width + key_width :].astype(jnp.bfloat16),
            "dp",
            scatter_dimension=0,
            tiled=True,
        ).astype(jnp.float32),
        lax.psum_scatter(
            out_grad.T.astype(jnp.bfloat16), "dp", scatter_dimension=0, tiled=True
        ).astype(jnp.float32),
    )
    out_total = out_turned.T
    norm_gain_total, mix_gain_total, router_total = lax.psum(
        (norm_gain_grad, mix_gain_grad, router_grad), ("dp", "tensor")
    )
    return (
        output_share,
        balance,
        input_grad_share,
        norm_gain_total,
        query_total,
        key_total,
        value_total,
        out_total,
        mix_gain_total,
        router_total,
        gate_total,
        up_total,
        down_total,
    )


def all_sum(value):
    for bit in (1, 2, 4, 8):
        value = value + flip(value, bit)
    return value + swap(value)


def spread(value):
    across = swap(value)
    return [value, across, flip(value, 1), flip(across, 1)]


CHUNK = 2
FAR_FIRST = -1


def shards_pair(
    tokens,
    norm_gains,
    w_query,
    w_key,
    w_value,
    w_out,
    mix_gains,
    w_router,
    w_gate,
    w_up,
    w_down,
    routes,
    starts,
    cotangent,
):
    share_rows, model_width = tokens.shape
    query_width = w_query.shape[1]
    key_width = w_key.shape[1]
    sizes = (query_width, key_width, HD)
    experts_here = w_gate.shape[0]
    experts = experts_here // 2
    choices_count = routes.shape[1]
    expert_count = w_router.shape[1]
    dp_size = lax.axis_size("dp")
    rank = lax.axis_index("dp")
    core, side = rank % 2, (rank // 2) % 2
    tensor_rank = lax.axis_index("tensor")
    total_tokens = routes.shape[0] * dp_size
    score_scale = HD ** (-0.5)
    depth = model_width // dp_size * 2
    slots = round_up(2 * CAP, BLOCK)

    joined_own = jnp.concatenate([w_query, w_key, w_value], axis=1)
    joined_other, joined_send, joined_piece = fetch_other([w_query, w_key, w_value], core, side)
    out_other, _, out_piece = fetch_other([w_out], core, side, (joined_send,))

    own_routes = lax.dynamic_slice_in_dim(routes, tensor_rank * share_rows, share_rows, 0)
    across_routes = lax.dynamic_slice_in_dim(routes, (1 - tensor_rank) * share_rows, share_rows, 0)
    both_routes = jnp.concatenate([own_routes, across_routes], axis=0)
    group_routes = jnp.concatenate([both_routes, flip(both_routes, 1)], axis=0)
    first_expert = tensor_rank * experts_here + core * experts

    route_onehot = (
        own_routes[:, :, None] == jnp.arange(expert_count, dtype=jnp.int32)[None, None, :]
    ).astype(jnp.float32)
    hops = [jnp.sum(route_onehot, axis=(0, 1))]
    for bit in (1, 2, 4, 8):
        hops.append(hops[-1] + flip(hops[-1], bit))
    counts = hops[-1] + swap(hops[-1])
    cotangent_rows = spread(order(cotangent, joined_piece))

    inputs_share = tokens.astype(jnp.float32)
    normed = normalize(inputs_share, norm_gains).astype(jnp.bfloat16)
    tables = turn_tables(share_rows)
    starts_row = lax.dynamic_index_in_dim(starts, tensor_rank, 0, keepdims=False)
    limits = piece_limits(starts_row, share_rows)

    def half_forward(joined_weights, after=(), later=()):
        query, key, value = project(
            normed, joined_weights, tables, query_width, key_width, score_scale, after
        )
        attended, lse = attend(query, key, value, limits, later)
        return attended, (query, key, value, lse)

    attended_own, saved_own = half_forward(joined_own, (), (joined_piece, hops[1]))
    attended_other, saved_other = half_forward(joined_other, (hops[2],), (hops[3],))
    middle_share = (
        inputs_share
        + jnp.dot(attended_own, w_out, preferred_element_type=jnp.float32)
        + jnp.dot(attended_other, out_other, preferred_element_type=jnp.float32)
    )
    mixed_share = normalize(middle_share, mix_gains).astype(jnp.bfloat16)

    logits = jnp.dot(mixed_share, w_router, preferred_element_type=jnp.float32)
    probabilities = softmax_rows(logits)
    chosen = jnp.sum(logits[:, None, :] * route_onehot, axis=-1)
    gate_soft = softmax_rows(chosen)
    gate_low = gate_soft.astype(jnp.bfloat16)
    fractions = counts / (total_tokens * choices_count)

    group_gates = jnp.concatenate(spread(gate_low), axis=0)
    gates = gate_table(group_routes, group_gates, first_expert, experts)
    place, begins, ends = placement(group_routes, first_expert, experts)
    gather_from = gather_tables(begins, ends, slots)
    blocks = gather_from[2]
    cot_slots = gather_rows(
        gather_from, place, None, cotangent_rows, slots, 0, experts, (hops[4],)
    )[0]
    mixed_across = order(swap(mixed_share), cot_slots)
    mixed_rows = [mixed_share, mixed_across, flip(mixed_share, 1), flip(mixed_across, 1)]
    misc = jnp.stack([core * experts, side, (rank // 4) % 2])
    weights = (w_gate, w_up, w_down)
    first_part = gather_rows(
        gather_from, place, gates, mixed_rows, slots, 0, CHUNK, (cot_slots, counts)
    )
    later_part = None
    carried = None
    chips = []
    for index in range(experts // CHUNK):
        if index == 1:
            later_part = gather_rows(
                gather_from, place, gates, mixed_rows, slots, CHUNK, experts - CHUNK, (carried,)
            )
        (x_slots, slot_gates), x_first = (later_part, CHUNK) if index else (first_part, 0)
        waits = []
        if index == 2:
            waits = [chips[0].one(carried)]
        elif index == 3:
            waits = [chips[0].two(carried)]
        elif index == 4:
            waits = [chips[1].one(carried)]
        far_first = int(index == FAR_FIRST)
        carried, send, keep = expert_call(
            blocks, misc, x_slots, cot_slots, slot_gates, weights, carried, slots,
            index * CHUNK, CHUNK, x_first, 0, depth, far_first, waits,
        )
        chips.append(ChipSum((send, keep), rank, far_first))
    done = [chips[0].three(carried)]
    waits = [chips[1].two(carried), done[0]]

    combine_from = combine_tables(begins, ends, slots)
    tiles = place.shape[1] // 4
    names = first_expert + jnp.arange(experts, dtype=jnp.int32)

    def combined(quarter, after):
        y, dx, gate_grads = combine_rows(
            combine_from, place, carried, quarter * tiles, tiles, after
        )
        gate_grads = gate_grads[:, :experts] + gate_grads[:, 64 : 64 + experts]
        rows = group_routes[quarter * share_rows : (quarter + 1) * share_rows]
        hit = rows[:, :, None] == names[None, None, :]
        return y, dx, jnp.sum(jnp.where(hit, gate_grads[:, None, :], 0.0), axis=2)

    far = combined(3, waits)
    far_y, far_dx, far_gg = (flip(value, 1) for value in far)
    cross = combined(1, [far[0]])
    dx_send = add_low(cross[1], far_dx)
    dx_across = swap(dx_send)
    gg_across = swap(cross[2] + far_gg)
    next_door = combined(2, [dx_send, chips[2].one(cross[1])])
    door_y, door_dx, door_gg = (flip(value, 1) for value in next_door)
    y_send = add_low(cross[0], far_y)
    near = combined(0, [next_door[0]])
    y_across = swap(order(y_send, near[0]))
    mixed_grad_share = (
        near[1].astype(jnp.float32)
        + door_dx.astype(jnp.float32)
        + dx_across.astype(jnp.float32)
    )
    gates_grad_share = near[2] + door_gg + gg_across

    upstream = cotangent.astype(jnp.float32)
    chosen_grad = gate_soft * (
        gates_grad_share - jnp.sum(gate_soft * gates_grad_share, axis=-1, keepdims=True)
    )
    logit_grad = jnp.sum(chosen_grad[:, :, None] * route_onehot, axis=1)
    prob_target = ALPHA * expert_count * fractions / total_tokens
    logit_grad = logit_grad + probabilities * (
        prob_target[None, :] - jnp.sum(probabilities * prob_target[None, :], axis=-1, keepdims=True)
    )
    router_grad = jnp.dot(
        mixed_share.astype(jnp.float32).T,
        logit_grad,
        precision=HIGHEST,
        preferred_element_type=jnp.float32,
    )
    mixed_grad_share = mixed_grad_share + jnp.dot(
        logit_grad,
        w_router.astype(jnp.float32).T,
        precision=HIGHEST,
        preferred_element_type=jnp.float32,
    )
    mix_pullback = jax.vjp(normalize, middle_share, mix_gains)[1]
    middle_from_norm, mix_gain_grad = mix_pullback(mixed_grad_share)
    middle_grad = upstream + middle_from_norm
    middle_low = middle_grad.astype(jnp.bfloat16)

    def half_back(saved, out_weights):
        attended_grad = dot_nt(middle_low, out_weights).astype(jnp.bfloat16)

        def part(chosen, after):
            return attend_back(
                saved, attended_grad, limits, tables, score_scale, chosen, after
            )

        return part

    pairs = key_width // 128
    other_grads = jnp.concatenate(
        half_back(saved_other, out_other)(
            (0, pairs), [chips[3].one(middle_low)]
        ),
        axis=1,
    )
    waits = [chips[2].two(other_grads)]
    other_grads = order(other_grads, *waits)
    expert_share = (
        near[0].astype(jnp.float32)
        + door_y.astype(jnp.float32)
        + order(y_across, other_grads).astype(jnp.float32)
    )
    output_share = (middle_share + expert_share).astype(jnp.bfloat16)
    joined_held = core_sum(dot_tn(normed, other_grads), core)
    joined_across = swap(joined_held)
    marked = order(middle_low, other_grads)
    out_held = core_sum(dot_tn(marked, attended_other), core)
    out_across = swap(order(out_held, joined_held))
    out_kept = core_sum(dot_tn(marked, attended_own), core)
    done.append(chips[1].three(joined_held))
    waits = [chips[4].one(joined_held), done[1], joined_held, out_held, out_kept, output_share]
    own_part = half_back(saved_own, w_out)
    front = own_part((0, pairs // 2), waits)
    back = own_part((pairs // 2, pairs - pairs // 2), [joined_across, front[0], chips[3].two(front[0])])
    own_grads = jnp.concatenate(
        [part for both in zip(front, back) for part in both], axis=1
    )
    out_half = add_low(out_kept, order(out_across, own_grads))
    own_weight_grads = dot_tn(normed, own_grads)
    own_held = core_sum(own_weight_grads, core)
    half = jnp.concatenate([add_low(own_held, joined_across), out_half], axis=-1)
    both_total = plane_sum(half, rank)
    joined_total = both_total[:, : query_width + 2 * key_width]
    out_total = both_total[:, query_width + 2 * key_width :]
    done.append(chips[2].three(half))
    chips[4].two(own_grads)
    other_normed = dot_nt(other_grads, joined_other)
    own_normed = dot_nt(order(own_grads, half), joined_own)
    input_pullback = jax.vjp(normalize, inputs_share, norm_gains)[1]
    input_from_norm, norm_gain_grad = input_pullback(other_normed + own_normed)
    input_grad_share = middle_grad + input_from_norm
    sums = done + [chips[i].three(norm_gain_grad) for i in (3, 4)]
    key_end = query_width + key_width
    small = all_sum(
        jnp.concatenate(
            [jnp.sum(probabilities, axis=0), mix_gain_grad, norm_gain_grad, router_grad.reshape(-1)]
        )
    )
    prob_sums = small[:expert_count]
    mix_gain_total = small[expert_count : expert_count + model_width]
    norm_gain_total = small[expert_count + model_width : expert_count + 2 * model_width]
    router_total = small[expert_count + 2 * model_width :].reshape(router_grad.shape)
    balance = expert_count * expert_count * fractions * prob_sums / total_tokens

    mine = jnp.concatenate(sums, axis=0).reshape(experts, 3, 2, depth // 2, -1)
    theirs = flip(pick_index(mine, 1 - core, 2), 1)
    mine = pick_index(mine, core, 2)
    def placed(kind):
        own_kind, other_kind = mine[:, kind], theirs[:, kind]
        return jnp.where(
            core == 0,
            jnp.concatenate([own_kind, other_kind], axis=0),
            jnp.concatenate([other_kind, own_kind], axis=0),
        ).astype(jnp.float32)

    return (
        output_share,
        balance,
        input_grad_share,
        norm_gain_total,
        joined_total[:, :query_width],
        joined_total[:, query_width:key_end],
        joined_total[:, key_end:],
        out_total.T,
        mix_gain_total,
        router_total,
        placed(0),
        placed(1),
        placed(2).transpose(0, 2, 1),
    )


def solution(mesh):
    sizes = dict(mesh.shape)
    paired = sizes["tensor"] == 2 and sizes["dp"] == 16
    return jax.shard_map(
        shards_pair if paired else shards_wide,
        mesh=mesh,
        in_specs=(
            P(("dp", "tensor"), None),
            P(),
            P(None, "tensor"),
            P(None, "tensor"),
            P(None, "tensor"),
            P("tensor", None),
            P(),
            P(),
            P("tensor", None, None),
            P("tensor", None, None),
            P("tensor", None, None),
            P("dp", None),
            P("dp", None),
            P(("dp", "tensor"), None),
        ),
        out_specs=(
            P(("dp", "tensor"), None),
            P(),
            P(("dp", "tensor"), None),
            P(),
            P("dp", "tensor"),
            P("dp", "tensor"),
            P("dp", "tensor"),
            P("tensor", "dp"),
            P(),
            P(),
            P("tensor", "dp", None),
            P("tensor", "dp", None),
            P("tensor", None, "dp"),
        ),
        check_vma=False,
    )
```
